32 devices in a mesh: groups: 2 (over x), row: 8 (over z, y), col: 2 (over core).
Axes of the slice: x: 2, y: 2, z: 4, core: 2. Of those that a mesh axis runs over, the one named last changes fastest.
Arguments:
- positions: float32 [32768, 384], P(('groups', 'row', 'col')), parts along dimension 0, may hold values from -1 to 1
- momenta: float32 [32768, 384], P(('groups', 'row', 'col')), parts along dimension 0, may hold values from -3 to 3
- tile_values: bfloat16 [3072, 128, 128], P(('groups', 'row', 'col')), parts along dimension 0, may hold values from -0.19921875 to 0.19921875
- tile_rows: int32 [3072], P(('groups', 'row', 'col')), parts along dimension 0, may hold values from 0 to 7
- tile_cols: int32 [3072], P(('groups', 'row', 'col')), parts along dimension 0, may hold values from 0 to 23
- tile_count: int32 [32], P(('groups', 'row', 'col')), parts along dimension 0, may hold values from 24 to 96, as said below
- channel_coupling: bfloat16 [48, 48], replicated, may hold values from -0.875 to 0.875
Outputs:
- new_positions: float32 [32768, 384], P(('groups', 'row', 'col')), parts along dimension 0
- new_momenta: float32 [32768, 384], P(('groups', 'row', 'col')), parts along dimension 0
- energy: float32 [16], P('groups'), parts along dimension 0
The draws below stay inside these ranges and needn't reach their ends.
There are 2 independent parts, one for each index of `groups`. The reference program is written for one: setup_inputs(seed, part) draws one part's arguments, and reference() takes and returns one part's arrays. A program takes and returns all parts, laid end to end along the dimension named above; an argument that names none is the same for every part. Nothing has to cross between parts.
Inputs may be any that keep to these rules, and one draw needn't show every extreme that they name: tile_count[b] is the number of live slots of block b; slots at or past it are ignored; some block has exactly 96 live slots.
All inputs are finite; a program needn't handle non-finite values.
Results may differ from the reference program's by a relative error of at most 0.00079.
Values may be sent and summed in bfloat16 or wider, within the bound.
No kernel may reach another device: no remote copies, remote signals or barrier semaphores. Data moves between devices by JAX's collectives and lax.ppermute only.
A program may use at most 64 MiB of HBM per device.

```python
import jax
import jax.numpy as jnp
from jax import lax

CH = 48
REP = 8
TILE = 128
STEPS = 2
TPD = 8
MAXT = 96
BLOCKS = 16
CELLS = 16384
ALLT = 1536


def draw_tile_count(key, part):
    counts = jax.random.randint(key, (BLOCKS,), MAXT // 4, MAXT + 1)
    chosen = jax.random.randint(jax.random.fold_in(key, 17), (), 0, BLOCKS)
    return jnp.where(jnp.arange(BLOCKS) == chosen, MAXT, counts).astype(jnp.int32)


def plant(result, rng, least, high):
    longest = result.shape.index(max(result.shape))
    spots = []
    for shift in (0, 1):
        where = [jax.random.randint(jax.random.fold_in(rng, axis), (), 0, length) for axis, length in enumerate(result.shape)]
        where[longest] = (where[longest] + shift) % result.shape[longest]
        spots.append(tuple(where))
    return result.at[spots[0]].set(least).at[spots[1]].set(high)


def steps_of(key, dims, shards, least, high):
    factor_of = 1.0
    for position, parts in shards:
        heights = jax.random.uniform(jax.random.fold_in(jax.random.fold_in(key, 6), position), (parts,), jnp.float32, least / len(shards), high / len(shards))
        factor_of = factor_of * jnp.repeat(jnp.exp(heights), dims[position] // parts).reshape((-1,) + (1,) * (len(dims) - 1 - position))
    return factor_of


def bell_draw(own_key, extent, scale, bound, split=(), held_as=jnp.bfloat16):
    entries = scale * jax.random.normal(own_key, extent, jnp.float32)
    if split:
        entries = entries * steps_of(own_key, extent, split, -0.22, 0.18)
    return jnp.clip(entries, -bound, bound).astype(held_as)


def setup_inputs(seed: int = 0, part: int = 0) -> dict:
    seeds = jax.random.split(jax.random.key(seed), 8)
    part_splits = jax.random.split(jax.random.fold_in(seeds[7], part), 8)
    positions = jnp.clip(jax.random.uniform(part_splits[0], (CELLS, REP * CH), jnp.float32, -1.0, 1.0) * steps_of(part_splits[0], (CELLS, REP * CH), ((0, 16),), -0.4, 0.0), -1.0, 1.0)
    momenta = bell_draw(part_splits[1], (CELLS, REP * CH), 0.5, 3.0, ((0, 16),), jnp.float32)
    tile_values = bell_draw(part_splits[2], (ALLT, TILE, TILE), 0.03, 0.19921875, ((0, 16),))
    tile_rows = plant(jax.random.randint(part_splits[3], (ALLT,), 0, TPD), jax.random.fold_in(part_splits[3], 1), 0, TPD - 1).astype(jnp.int32)
    tile_cols = plant(jax.random.randint(part_splits[4], (ALLT,), 0, 3 * TPD), jax.random.fold_in(part_splits[4], 1), 0, (3 * TPD) - 1).astype(jnp.int32)
    tile_count = draw_tile_count(jax.random.fold_in(jax.random.fold_in(seeds[7], part), 71), part)
    channel_coupling = bell_draw(seeds[6], (CH, CH), CH ** -0.5, 0.875)
    return {"positions": positions, "momenta": momenta, "tile_values": tile_values, "tile_rows": tile_rows, "tile_cols": tile_cols, "tile_count": tile_count, "channel_coupling": channel_coupling}


def plan_field(rounded, tile_values, tile_rows, tile_cols, tile_count):
    width = rounded.shape[1]
    source_tiles = rounded.reshape(BLOCKS * TPD, TILE, width).astype(jnp.float32)
    values = tile_values.reshape(BLOCKS, MAXT, TILE, TILE)
    rows = tile_rows.reshape(BLOCKS, MAXT)
    cols = tile_cols.reshape(BLOCKS, MAXT)

    def one_block(index):
        block = index.astype(jnp.int32)
        source_index = (block * TPD - TPD + cols[block]) % (BLOCKS * TPD)
        sources = source_tiles[source_index]
        products = jnp.einsum('sij,sjk->sik', values[block].astype(jnp.float32), sources, precision=lax.Precision.HIGHEST)
        live = jnp.arange(MAXT, dtype=jnp.int32) < tile_count[block]
        place = ((rows[block][None, :] == jnp.arange(TPD, dtype=jnp.int32)[:, None]) & live[None, :]).astype(jnp.float32)
        return jnp.einsum('ts,sik->tik', place, products, precision=lax.Precision.HIGHEST)
    fields = lax.map(one_block, jnp.arange(BLOCKS, dtype=jnp.int32))
    return fields.reshape(BLOCKS * TPD * TILE, width)

def reference(positions, momenta, tile_values, tile_rows, tile_cols, tile_count, channel_coupling):
    x_state = positions
    y_state = momenta
    coupling = channel_coupling.astype(jnp.float32)
    energy = jnp.zeros((REP,), jnp.float32)
    for step in range(STEPS):
        rounded = x_state.astype(jnp.bfloat16)
        field = plan_field(rounded, tile_values, tile_rows, tile_cols, tile_count)
        interference = field.astype(jnp.bfloat16).astype(jnp.float32).reshape(CELLS, REP, CH)
        mixed = jnp.einsum('crb,ba->cra', interference, coupling, precision=lax.Precision.HIGHEST).reshape(CELLS, REP * CH)
        totals = lax.optimization_barrier(jnp.sum(x_state.reshape(CELLS, REP, CH), axis=2, keepdims=True))
        penalty = jnp.broadcast_to(0.02 * (totals - (2.0 - CH)), (CELLS, REP, CH)).reshape(CELLS, REP * CH)
        detune = 1.0 - (step + 1.0) / (STEPS + 1.0)
        y_state = y_state + 0.5 * (-detune * x_state - 0.4 * (mixed + penalty))
        if step == STEPS - 1:
            weighted = rounded.astype(jnp.float32) * mixed
            energy = lax.optimization_barrier(jnp.sum(weighted.reshape(CELLS, REP, CH), axis=(0, 2))) / jnp.sqrt(jnp.float32(CELLS * CH))
        x_state = jnp.clip(x_state + 0.5 * y_state, -1.0, 1.0)
    return (x_state, y_state, energy)
```

```python
import functools

import jax
import jax.numpy as jnp
from jax import lax
from jax.experimental import pallas as pl
from jax.experimental.pallas import tpu as pltpu
from jax.sharding import PartitionSpec as P

STEPS = 2
LANES = 128
UNROLL = 16
VMEM_LIMIT = 40 * 1024 * 1024

SMEM_SPEC = pl.BlockSpec(memory_space=pltpu.SMEM)
VMEM_SPEC = pl.BlockSpec(memory_space=pltpu.VMEM)
ANY_SPEC = pl.BlockSpec(memory_space=pl.ANY)


def params():
    return pltpu.CompilerParams(vmem_limit_bytes=VMEM_LIMIT)


def cost(flops, moved):
    return pl.CostEstimate(flops=int(flops), bytes_accessed=int(moved), transcendentals=0)


def lanes(group):
    return slice(group * LANES, (group + 1) * LANES)


def spanned(group, channels, width):
    first = group * LANES // channels * channels
    last = -(-(group + 1) * LANES // channels) * channels
    return list(range(first // LANES, -(-min(last, width) // LANES)))


def round_group(positions, group):
    cells = positions.shape[0]

    def body(x_ref, out_ref):
        out_ref[...] = x_ref[...].astype(jnp.bfloat16)

    return pl.pallas_call(
        body,
        grid=(1,),
        in_specs=[pl.BlockSpec((cells, LANES), lambda i: (0, group))],
        out_specs=pl.BlockSpec((cells, LANES), lambda i: (0, 0)),
        out_shape=jax.ShapeDtypeStruct((cells, LANES), jnp.bfloat16),
        compiler_params=params(),
        cost_estimate=cost(0, cells * LANES * 6),
        name="round_group",
    )(positions)


def base_values(xs, ys, same, step, channels):
    groups = len(xs)
    cells = xs[0].shape[0]
    width = groups * LANES
    detune = 1.0 - (step + 1.0) / (STEPS + 1.0)

    def body(*refs):
        x_refs, y_refs = refs[:groups], refs[groups : 2 * groups]
        same_ref, out_refs = refs[2 * groups], refs[2 * groups + 1 :]
        high = [r[...].astype(jnp.bfloat16) for r in x_refs]
        low = [
            (r[...] - h.astype(jnp.float32)).astype(jnp.bfloat16) for r, h in zip(x_refs, high)
        ]
        for g in range(groups):
            near = spanned(g, channels, width)
            part = slice(near[0] * LANES, (near[-1] + 1) * LANES)
            ones = same_ref[part, lanes(g)]
            totals = jnp.dot(
                jnp.concatenate([high[n] for n in near], axis=1),
                ones,
                preferred_element_type=jnp.float32,
            ) + jnp.dot(
                jnp.concatenate([low[n] for n in near], axis=1),
                ones,
                preferred_element_type=jnp.float32,
            )
            penalty = 0.02 * (totals - (2.0 - channels))
            out_refs[g][...] = y_refs[g][...] + 0.5 * (
                -detune * x_refs[g][...] - 0.4 * penalty
            )

    return pl.pallas_call(
        body,
        in_specs=[VMEM_SPEC] * (2 * groups + 1),
        out_specs=[VMEM_SPEC] * groups,
        out_shape=[jax.ShapeDtypeStruct((cells, LANES), jnp.float32)] * groups,
        compiler_params=params(),
        cost_estimate=cost(4 * cells * width * width, cells * width * 12),
        name="base_values",
    )(*xs, *ys, same)


def field_into(rows, cols, count, tiles, parts, field, window):
    slots, tile, _ = tiles.shape
    spare = field.shape[0] - 1
    per = window.shape[0] // len(parts)
    for k, part in enumerate(parts):
        window[k * per : (k + 1) * per] = part[...].reshape(per, tile, LANES)
    field[...] = jnp.zeros_like(field)
    live = count[0]

    def some(start, unroll):
        for u in range(unroll):
            slot = start + u
            row = jnp.where(slot < live, rows[slot], spare)
            field[row] += jnp.dot(
                tiles[slot], window[cols[slot]], preferred_element_type=jnp.float32
            )

    whole = slots // UNROLL

    def body(i, carry):
        some(i * UNROLL, UNROLL)
        return carry

    lax.fori_loop(0, whole, body, 0)
    some(whole * UNROLL, slots - whole * UNROLL)


def stage(
    slot_args,
    parts,
    others,
    updates,
    mixing,
    channels,
    field_group,
    final,
):
    rows, cols, count, tiles = slot_args
    slots, tile, _ = tiles.shape
    cells = parts[0].shape[0]
    width = mixing.shape[0]
    keys = sorted(others)
    per = cells // tile

    def body(*refs):
        refs = list(refs)
        rows_ref, cols_ref, count_ref, tiles_ref = refs[:4]
        part_refs = refs[4:7]
        refs = refs[7:]
        other_refs = dict(zip(keys, refs[: len(keys)]))
        refs = refs[len(keys) :]
        mixing_ref, refs = refs[0], refs[1:]
        update_refs = [refs[i * 3 : i * 3 + 3] for i in range(len(updates))]
        refs = refs[3 * len(updates) :]
        out_refs, (field, window) = refs[:-2], refs[-2:]
        field_into(rows_ref, cols_ref, count_ref, tiles_ref, part_refs, field, window)
        own = field[:per].reshape(cells, LANES).astype(jnp.bfloat16)
        out_refs[0][...] = own
        out_refs = out_refs[1:]
        for i, (group, *_) in enumerate(updates):
            base_ref, x_ref, rounded_ref = update_refs[i]
            x_out, y_out, last_out = out_refs[3 * i : 3 * i + 3]
            near = spanned(group, channels, width)
            part = slice(near[0] * LANES, (near[-1] + 1) * LANES)
            mixed = jnp.dot(
                jnp.concatenate(
                    [own if n == field_group else other_refs[n][...] for n in near], axis=1
                ),
                mixing_ref[part, lanes(group)],
                preferred_element_type=jnp.float32,
            )
            y_new = base_ref[...] - 0.2 * mixed
            x_new = jnp.clip(x_ref[...] + 0.5 * y_new, -1.0, 1.0)
            y_out[...] = y_new
            x_out[...] = x_new
            if final:
                weighted = rounded_ref[...].astype(jnp.float32) * mixed
                last_out[...] = jnp.sum(weighted, axis=0, keepdims=True)
            else:
                last_out[...] = x_new.astype(jnp.bfloat16)

    f32 = jax.ShapeDtypeStruct((cells, LANES), jnp.float32)
    b16 = jax.ShapeDtypeStruct((cells, LANES), jnp.bfloat16)
    lane = jax.ShapeDtypeStruct((1, LANES), jnp.float32)
    shapes = [b16]
    for _ in updates:
        shapes += [f32, f32, lane if final else b16]
    flat = [a for _, *arrays in updates for a in arrays]
    outs = pl.pallas_call(
        body,
        in_specs=[SMEM_SPEC] * 3 + [VMEM_SPEC] * (5 + len(keys) + len(flat)),
        out_specs=[VMEM_SPEC] * len(shapes),
        out_shape=shapes,
        scratch_shapes=[
            pltpu.VMEM((per + 1, tile, LANES), jnp.float32),
            pltpu.VMEM((3 * per, tile, LANES), jnp.bfloat16),
        ],
        compiler_params=params(),
        cost_estimate=cost(8 * slots * tile * tile * LANES, slots * tile * tile * 2),
        name="stage",
    )(rows, cols, count, tiles, *parts, *[others[k] for k in keys], mixing, *flat)
    return outs[0], [outs[1 + 3 * i : 4 + 3 * i] for i in range(len(updates))]


def local(positions, momenta, tile_values, tile_rows, tile_cols, tile_count, channel_coupling):
    cells, width = positions.shape
    channels = channel_coupling.shape[0]
    replicas = width // channels
    groups = width // LANES
    ring = lax.axis_size("row") * lax.axis_size("col")
    eye = jnp.eye(replicas, dtype=jnp.bfloat16)
    mixing = (eye[:, None, :, None] * channel_coupling[None, :, None, :]).reshape(width, width)
    same = jnp.repeat(jnp.repeat(eye, channels, axis=0), channels, axis=1)
    slot_args = (tile_rows, tile_cols, tile_count, tile_values)
    ahead = [(i, (i + 1) % ring) for i in range(ring)]
    back = [((i + 1) % ring, i) for i in range(ring)]

    def exchange(mine):
        return [
            lax.ppermute(mine, ("row", "col"), ahead),
            mine,
            lax.ppermute(mine, ("row", "col"), back),
        ]

    ready = {g: [] for g in range(groups)}
    for g in range(groups):
        ready[max(spanned(g, channels, width))].append(g)

    xs = [positions[:, lanes(g)] for g in range(groups)]
    ys = [momenta[:, lanes(g)] for g in range(groups)]
    rounded = [round_group(positions, g) for g in range(groups)]
    energies = [None] * groups
    for step in range(STEPS):
        final = step == STEPS - 1
        windows = [exchange(r) for r in rounded]
        bases = base_values(xs, ys, same, step, channels)
        interference = {}
        new_x, new_y, new_r = [None] * groups, [None] * groups, [None] * groups
        for g in range(groups):
            todo = ready[g]
            needed = {n for t in todo for n in spanned(t, channels, width)} - {g}
            interference[g], done = stage(
                slot_args,
                windows[g],
                {n: interference[n] for n in needed},
                [(t, bases[t], xs[t], rounded[t]) for t in todo],
                mixing,
                channels,
                g,
                final,
            )
            for t, (x, y, r) in zip(todo, done):
                new_x[t], new_y[t], new_r[t] = x, y, r
        xs, ys = new_x, new_y
        if final:
            energies = new_r
        else:
            rounded = new_r
    partial = jnp.concatenate(energies, axis=1).reshape(replicas, channels).sum(axis=1)
    size = 1
    while size < ring:
        partial = partial + lax.ppermute(
            partial, ("row", "col"), [(i, i ^ size) for i in range(ring)]
        )
        size *= 2
    energy = partial / jnp.sqrt(jnp.float32(cells * ring * channels))
    return (jnp.concatenate(xs, axis=1), jnp.concatenate(ys, axis=1), energy)


def solution(mesh):
    cells = P(("groups", "row", "col"), None)
    slots = P(("groups", "row", "col"))
    return jax.shard_map(
        local,
        mesh=mesh,
        in_specs=(cells, cells, P(("groups", "row", "col"), None, None), slots, slots, slots, P()),
        out_specs=(cells, cells, P("groups")),
        check_vma=False,
    )
```

```python
import jax
import jax.numpy as jnp
import ml_dtypes
import numpy as np
from jax import lax
from jax.experimental import pallas as pl
from jax.experimental.pallas import tpu as pltpu
from jax.sharding import PartitionSpec as P

STEPS = 2
LANES = 128
UNROLL = 16
VMEM_LIMIT = 40 * 1024 * 1024
F32 = jnp.float32
BF16 = jnp.bfloat16

SMEM = pl.BlockSpec(memory_space=pltpu.SMEM)
VMEM = pl.BlockSpec(memory_space=pltpu.VMEM)
HBM = pl.BlockSpec(memory_space=pltpu.HBM)


def params():
    return pltpu.CompilerParams(vmem_limit_bytes=VMEM_LIMIT)


def cost(flops, moved):
    return pl.CostEstimate(flops=int(flops), bytes_accessed=int(moved), transcendentals=0)


def shape(rows, columns, dtype):
    return jax.ShapeDtypeStruct((rows, columns), dtype)


def lanes(group):
    return slice(group * LANES, (group + 1) * LANES)


def spanned(group, channels, width):
    first = group * LANES // channels * channels
    last = -(-(group + 1) * LANES // channels) * channels
    return list(range(first // LANES, -(-min(last, width) // LANES)))


def span_lanes(near):
    return slice(near[0] * LANES, (near[-1] + 1) * LANES)


def detune(step):
    return 1.0 - (step + 1.0) / (STEPS + 1.0)


def round_first(positions):
    cells = positions.shape[0]

    def body(x_ref, out_ref, buf, sem):
        copy = pltpu.make_async_copy(x_ref.at[:, lanes(0)], buf, sem)
        copy.start()
        copy.wait()
        out_ref[...] = buf[...].astype(BF16)

    return pl.pallas_call(
        body,
        in_specs=[HBM],
        out_specs=VMEM,
        out_shape=shape(cells, LANES, BF16),
        scratch_shapes=[pltpu.VMEM((cells, LANES), F32), pltpu.SemaphoreType.DMA],
        compiler_params=params(),
        cost_estimate=cost(0, cells * LANES * 6),
        name="round_first",
    )(positions)


def totals_of(high, low, same, near, group):
    ones = same[span_lanes(near), lanes(group)]
    return jnp.dot(
        jnp.concatenate([high[n] for n in near], axis=1), ones, preferred_element_type=F32
    ) + jnp.dot(jnp.concatenate([low[n] for n in near], axis=1), ones, preferred_element_type=F32)


def base_of(x, y, totals, step, channels):
    penalty = 0.02 * (totals - (2.0 - channels))
    return y + 0.5 * (-detune(step) * x - 0.4 * penalty)


def split(x):
    high = x.astype(BF16)
    return high, (x - high.astype(F32)).astype(BF16)


def prepare(positions, momenta, same, spread, coupling, emit):
    cells, width = positions.shape
    channels = coupling.shape[0]
    groups = width // LANES

    def body(x_ref, y_ref, same_ref, spread_ref, coupling_ref, *outs):
        mixing_out, base_outs, round_outs = outs[0], outs[1 : 1 + groups], outs[1 + groups :]
        x = [x_ref[:, lanes(g)] for g in range(groups)]
        parts = [split(v) for v in x]
        for out, g in zip(round_outs, emit):
            out[...] = parts[g][0]
        tall = jnp.dot(
            spread_ref[...], coupling_ref[...], preferred_element_type=F32
        ).astype(BF16)
        wide = lax.dot_general(
            tall, spread_ref[...], (((1,), (1,)), ((), ())), preferred_element_type=F32
        )
        mixing_out[...] = (wide * same_ref[...].astype(F32)).astype(BF16)
        for g in range(groups):
            near = spanned(g, channels, width)
            totals = totals_of([p[0] for p in parts], [p[1] for p in parts], same_ref, near, g)
            base_outs[g][...] = base_of(x[g], y_ref[:, lanes(g)], totals, 0, channels)

    outs = pl.pallas_call(
        body,
        in_specs=[VMEM] * 5,
        out_specs=[VMEM] * (1 + groups + len(emit)),
        out_shape=[shape(width, width, BF16)]
        + [shape(cells, LANES, F32)] * groups
        + [shape(cells, LANES, BF16)] * len(emit),
        compiler_params=params(),
        cost_estimate=cost(4 * cells * width * width, cells * width * 12),
        name="prepare",
    )(positions, momenta, same, spread, coupling)
    return outs[0], outs[1 : 1 + groups], outs[1 + groups :]


def field_into(rows, cols, count, tiles, parts, field, window):
    slots, tile, _ = tiles.shape
    spare = field.shape[0] - 1
    per = window.shape[0] // len(parts)
    for k, part in enumerate(parts):
        window[k * per : (k + 1) * per] = part[...].reshape(per, tile, LANES)
    field[...] = jnp.zeros_like(field)
    live = count[0]

    def some(start, unroll):
        for u in range(unroll):
            slot = start + u
            row = jnp.where(slot < live, rows[slot], spare)
            field[row] += jnp.dot(tiles[slot], window[cols[slot]], preferred_element_type=F32)

    whole = slots // UNROLL

    def body(i, carry):
        some(i * UNROLL, UNROLL)
        return carry

    lax.fori_loop(0, whole, body, 0)
    some(whole * UNROLL, slots - whole * UNROLL)


def stage(
    slot_args, channels, mixing, group, parts, before=(), after=(), mix=(), rounds=(), name="stage"
):
    rows, cols, count, tiles = slot_args
    slots, tile, _ = tiles.shape
    cells = parts[0].shape[0]
    width = mixing.shape[0]
    per = cells // tile
    arrays, shapes = [], []

    def take(array):
        for i, held in enumerate(arrays):
            if held is array:
                return i
        arrays.append(array)
        return len(arrays) - 1

    def give(*kinds):
        shapes.extend(shape(n, LANES, kind) for n, kind in kinds)
        return list(range(len(shapes) - len(kinds), len(shapes)))

    def near_fields(t, fields):
        near = spanned(t, channels, width)
        return [None if fields[n] is None else take(fields[n]) for n in near]

    part_ids = [take(p) for p in parts]
    mixing_id = take(mixing)
    (own_out,) = give((cells, BF16))
    jobs = [
        [
            (t, near_fields(t, fields), take(base), take(x), where, give(*[(cells, k) for k in (F32, F32, BF16)]))
            for t, fields, base, x, where in todo
        ]
        for todo in (before, after)
    ]
    mix_jobs = [
        (t, near_fields(t, fields), take(rounded), give((cells, F32), (1, F32)))
        for t, fields, rounded in mix
    ]
    round_jobs = [(take(x), where, give((cells, BF16))) for x, where in rounds]
    n_in, n_out = len(arrays), len(shapes)

    def body(rows_ref, cols_ref, count_ref, tiles_ref, *refs):
        ins, outs, (field, window) = refs[:n_in], refs[n_in : n_in + n_out], refs[n_in + n_out :]

        def mixed_of(t, ids, own):
            near = spanned(t, channels, width)
            return jnp.dot(
                jnp.concatenate([own if i is None else ins[i][...] for i in ids], axis=1),
                ins[mixing_id][span_lanes(near), lanes(t)],
                preferred_element_type=F32,
            )

        def update(job, own):
            t, ids, base, x, where, (x_out, y_out, r_out) = job
            y_new = ins[base][...] - 0.2 * mixed_of(t, ids, own)
            x_new = jnp.clip(ins[x][:, where] + 0.5 * y_new, -1.0, 1.0)
            outs[x_out][...] = x_new
            outs[y_out][...] = y_new
            outs[r_out][...] = x_new.astype(BF16)

        for job in jobs[0]:
            update(job, None)
        for x, where, (out,) in round_jobs:
            outs[out][...] = ins[x][:, where].astype(BF16)
        field_into(
            rows_ref, cols_ref, count_ref, tiles_ref, [ins[i] for i in part_ids], field, window
        )
        own = field[:per].reshape(cells, LANES).astype(BF16)
        outs[own_out][...] = own
        for job in jobs[1]:
            update(job, own)
        for t, ids, rounded, (mixed_out, energy_out) in mix_jobs:
            mixed = mixed_of(t, ids, own)
            outs[mixed_out][...] = mixed
            outs[energy_out][...] = jnp.sum(
                ins[rounded][...].astype(F32) * mixed, axis=0, keepdims=True
            )

    outs = pl.pallas_call(
        body,
        in_specs=[SMEM] * 3 + [VMEM] * (1 + n_in),
        out_specs=[VMEM] * n_out,
        out_shape=shapes,
        scratch_shapes=[
            pltpu.VMEM((per + 1, tile, LANES), F32),
            pltpu.VMEM((3 * per, tile, LANES), BF16),
        ],
        compiler_params=params(),
        cost_estimate=cost(8 * slots * tile * tile * LANES, slots * tile * tile * 2),
        name=name,
    )(rows, cols, count, tiles, *arrays)
    return (
        outs[own_out],
        [[outs[i] for i in job[-1]] for job in jobs[0] + jobs[1]],
        [[outs[i] for i in job[-1]] for job in mix_jobs],
        [outs[job[-1][0]] for job in round_jobs],
    )


def finish(xs, ys, mixed, same, channels):
    groups = len(xs)
    cells = xs[0].shape[0]
    width = groups * LANES
    block = cells // 4 if cells % 64 == 0 else cells

    def body(*refs):
        x_refs, y_refs, mixed_refs = [refs[i * groups : (i + 1) * groups] for i in range(3)]
        same_ref, x_out, y_out = refs[3 * groups :]
        x = [r[...] for r in x_refs]
        parts = [split(v) for v in x]
        for g in range(groups):
            near = spanned(g, channels, width)
            totals = totals_of([p[0] for p in parts], [p[1] for p in parts], same_ref, near, g)
            base = base_of(x[g], y_refs[g][...], totals, STEPS - 1, channels)
            y_new = base - 0.2 * mixed_refs[g][...]
            y_out[:, lanes(g)] = y_new
            x_out[:, lanes(g)] = jnp.clip(x[g] + 0.5 * y_new, -1.0, 1.0)

    part = pl.BlockSpec((block, LANES), lambda i: (i, 0))
    full = pl.BlockSpec((block, width), lambda i: (i, 0))
    return pl.pallas_call(
        body,
        grid=(cells // block,),
        in_specs=[part] * (3 * groups) + [pl.BlockSpec((width, width), lambda i: (0, 0))],
        out_specs=[full, full],
        out_shape=[shape(cells, width, F32)] * 2,
        compiler_params=params(),
        cost_estimate=cost(4 * cells * width * width, cells * width * 12),
        name="finish",
    )(*xs, *ys, *mixed, same)


def sum_over_ring(value, ring):
    if ring & (ring - 1):
        return lax.psum(value, ("row", "col"))
    size = 1
    while size < ring:
        digits = (1, 2, 3) if 4 * size <= ring else (1,)
        value = value + sum(
            lax.ppermute(value, ("row", "col"), [(i, i ^ (size * d)) for i in range(ring)])
            for d in digits
        )
        size *= len(digits) + 1
    return value


def local(positions, momenta, tile_values, tile_rows, tile_cols, tile_count, channel_coupling):
    cells, width = positions.shape
    channels = channel_coupling.shape[0]
    replicas = width // channels
    groups = width // LANES
    ring = lax.axis_size("row") * lax.axis_size("col")
    where = np.arange(width)
    same = (where[:, None] // channels == where[None] // channels).astype(ml_dtypes.bfloat16)
    spread = (where[:, None] % channels == np.arange(channels)[None]).astype(ml_dtypes.bfloat16)
    slot_args = (tile_rows, tile_cols, tile_count, tile_values)
    ahead = [(i, (i + 1) % ring) for i in range(ring)]
    back = [((i + 1) % ring, i) for i in range(ring)]

    def exchange(mine):
        return [
            lax.ppermute(mine, ("row", "col"), ahead),
            mine,
            lax.ppermute(mine, ("row", "col"), back),
        ]

    ready = {g: [] for g in range(groups)}
    for g in range(groups):
        ready[max(spanned(g, channels, width))].append(g)

    def fields_for(t, known, own):
        return {n: None if n == own else known[n] for n in spanned(t, channels, width)}

    first = round_first(positions)
    windows = [exchange(first)]
    emit = [1] if groups > 1 else []
    mixing, bases, early = prepare(positions, momenta, same, spread, channel_coupling, emit)
    windows += [exchange(r) for r in early]
    known, state, waiting = {}, {}, []
    for g in range(groups):
        waiting += ready[g]
        now, waiting = waiting[:1], waiting[1:]
        coming = [len(windows)] if len(windows) < groups else []
        known[g], updated, _, rounded = stage(
            slot_args,
            channels,
            mixing,
            g,
            windows[g],
            after=[(t, fields_for(t, known, g), bases[t], positions, lanes(t)) for t in now],
            rounds=[(positions, lanes(c)) for c in coming],
            name=f"first_{g}",
        )
        state.update(zip(now, updated))
        windows += [exchange(r) for r in rounded]
    new_windows = {t: exchange(state[t][2]) for t in state}
    last_known, mixed, energies = {}, {}, {}
    for g in range(groups):
        now, waiting = waiting[:1], waiting[1:]
        last_known[g], updated, mixes, _ = stage(
            slot_args,
            channels,
            mixing,
            g,
            new_windows[g],
            before=[(t, fields_for(t, known, None), bases[t], positions, lanes(t)) for t in now],
            mix=[(t, fields_for(t, last_known, g), state[t][2]) for t in ready[g]],
            name=f"second_{g}",
        )
        for t, new in zip(now, updated):
            state[t] = new
            new_windows[t] = exchange(new[2])
        for t, (field, energy) in zip(ready[g], mixes):
            mixed[t], energies[t] = field, energy
    partial = jnp.concatenate([energies[g] for g in range(groups)], axis=1)
    partial = partial.reshape(replicas, channels).sum(axis=1)
    energy = sum_over_ring(partial, ring) / jnp.sqrt(jnp.float32(cells * ring * channels))
    x_new, y_new = finish(
        [state[g][0] for g in range(groups)],
        [state[g][1] for g in range(groups)],
        [mixed[g] for g in range(groups)],
        same,
        channels,
    )
    return (x_new, y_new, energy)


def solution(mesh):
    cells = P(("groups", "row", "col"), None)
    slots = P(("groups", "row", "col"))
    return jax.shard_map(
        local,
        mesh=mesh,
        in_specs=(cells, cells, P(("groups", "row", "col"), None, None), slots, slots, slots, P()),
        out_specs=(cells, cells, P("groups")),
        check_vma=False,
    )
```

```python
import jax
import jax.numpy as jnp
import ml_dtypes
import numpy as np
from jax import lax
from jax.experimental import pallas as pl
from jax.experimental.pallas import tpu as pltpu
from jax.sharding import PartitionSpec as P

STEPS = 2
LANES = 128
UNROLL = 4
VMEM_LIMIT = 14 * 1024 * 1024
F32 = jnp.float32
BF16 = jnp.bfloat16
RING = ("row", "col")

SMEM = pl.BlockSpec(memory_space=pltpu.SMEM)
VMEM = pl.BlockSpec(memory_space=pltpu.VMEM)
ANY = pl.BlockSpec(memory_space=pl.ANY)


def params():
    return pltpu.CompilerParams(vmem_limit_bytes=VMEM_LIMIT)


def cost(flops, moved):
    return pl.CostEstimate(flops=int(flops) // 1000, bytes_accessed=int(moved) // 1000, transcendentals=0)


def shape(rows, columns, dtype):
    return jax.ShapeDtypeStruct((rows, columns), dtype)


def in_hbm(array):
    return pltpu.with_memory_space_constraint(array, pltpu.HBM)


def lanes(group):
    return slice(group * LANES, (group + 1) * LANES)


def spanned(group, channels, width):
    first = group * LANES // channels * channels
    last = -(-(group + 1) * LANES // channels) * channels
    return list(range(first // LANES, -(-min(last, width) // LANES)))


def span_lanes(near):
    return slice(near[0] * LANES, (near[-1] + 1) * LANES)


def detune(step):
    return 1.0 - (step + 1.0) / (STEPS + 1.0)


def split(x):
    high = x.astype(BF16)
    return high, (x - high.astype(F32)).astype(BF16)


def totals_of(parts, same, group, channels, width):
    near = spanned(group, channels, width)
    ones = same[span_lanes(near), lanes(group)]
    return sum(
        jnp.dot(
            jnp.concatenate([parts[n][k] for n in near], axis=1), ones, preferred_element_type=F32
        )
        for k in range(2)
    )


def base_of(x, y, totals, step, channels):
    penalty = 0.02 * (totals - (2.0 - channels))
    return y + 0.5 * (-detune(step) * x - 0.4 * penalty)


def mixed_of(fields, mixing, group, channels):
    near = spanned(group, channels, mixing.shape[0])
    return jnp.dot(
        jnp.concatenate([fields[n] for n in near], axis=1),
        mixing[span_lanes(near), lanes(group)],
        preferred_element_type=F32,
    )


def round_first(positions):
    cells = positions.shape[0]

    def body(x_ref, out_ref, buf, sem):
        copy = pltpu.make_async_copy(x_ref.at[:, lanes(0)], buf, sem)
        copy.start()
        copy.wait()
        out_ref[...] = buf[...].astype(BF16)

    return pl.pallas_call(
        body,
        in_specs=[ANY],
        out_specs=VMEM,
        out_shape=shape(cells, LANES, BF16),
        scratch_shapes=[pltpu.VMEM((cells, LANES), F32), pltpu.SemaphoreType.DMA],
        compiler_params=params(),
        cost_estimate=cost(0, cells * LANES * 6),
        name="round_first",
    )(in_hbm(positions))


def round_all(positions, after):
    def body(x_ref, _, out_ref):
        out_ref[...] = x_ref[...].astype(BF16)

    return pl.pallas_call(
        body,
        in_specs=[VMEM, ANY],
        out_specs=VMEM,
        out_shape=shape(*positions.shape, BF16),
        compiler_params=params(),
        cost_estimate=cost(0, positions.size * 6),
        name="round_all",
    )(positions, after)


def section(slots, per):
    turn = 2 * UNROLL
    return -(-(slots + per) // turn) * turn


def make_lists(rows, cols, count, odd, slot_list, col_list, row_list, turns, held, per, size):
    for k in range(2 * per):
        held[k] = -1

    def visit(slot, totals):
        near_pairs, far_pairs = totals
        row, col = rows[slot], cols[slot]
        third = jnp.where(col >= 2 * per, 2, jnp.where(col >= per, 1, 0))
        tile = col - third * per
        far = third == jnp.where(odd, 2, 0)
        tile = jnp.where(far | (third == 1), tile, tile + per)
        key = row + jnp.where(far, per, 0)
        pair = jnp.where(far, far_pairs + size // 2, near_pairs)
        other = held[key]
        full = other >= 0
        slot_list[2 * pair] = other // 64
        col_list[2 * pair] = other % 64
        slot_list[2 * pair + 1] = slot
        col_list[2 * pair + 1] = tile
        row_list[pair] = row
        held[key] = jnp.where(full, -1, slot * 64 + tile)
        one = full.astype(jnp.int32)
        return near_pairs + jnp.where(far, 0, one), far_pairs + jnp.where(far, one, 0)

    def left(key, pairs, start, zero):
        other = held[key]
        pair = pairs + start
        row_list[pair] = key % per
        slot_list[2 * pair] = other // 64
        col_list[2 * pair] = other % 64
        slot_list[2 * pair + 1] = 0
        col_list[2 * pair + 1] = zero
        return pairs + (other >= 0).astype(jnp.int32)

    totals = lax.fori_loop(0, count[0], visit, (jnp.int32(0), jnp.int32(0)))
    for part, (start, zero) in enumerate(((0, 2 * per), (size // 2, per))):
        pairs = totals[part]
        for k in range(per):
            pairs = left(part * per + k, pairs, start, zero)
        whole = (pairs + UNROLL - 1) // UNROLL

        def pad(pair, carry, start=start, zero=zero):
            row_list[start + pair] = per
            for e in range(2):
                slot_list[2 * (start + pair) + e] = 0
                col_list[2 * (start + pair) + e] = zero
            return carry

        lax.fori_loop(pairs, whole * UNROLL, pad, 0)
        turns[part] = whole


def prepare(positions, momenta, same, spread, coupling, rows, cols, count, odd, slots, tile, emit):
    cells, width = positions.shape
    channels = coupling.shape[0]
    groups = width // LANES
    per = cells // tile
    size = section(slots, per)

    def body(rows_ref, cols_ref, count_ref, odd_ref, x_ref, y_ref, same_ref, spread_ref, coupling_ref, *refs):
        slot_list, col_list, row_list, turns, mixing_out = refs[:5]
        base_outs = refs[5 : 5 + groups]
        round_outs = refs[5 + groups : 5 + groups + len(emit)]
        held, momenta_buf, sem = refs[5 + groups + len(emit) :]
        copy = pltpu.make_async_copy(y_ref, momenta_buf, sem)
        copy.start()
        x = [x_ref[:, lanes(g)] for g in range(groups)]
        parts = [split(v) for v in x]
        for out, g in zip(round_outs, emit):
            out[...] = parts[g][0]
        make_lists(
            rows_ref, cols_ref, count_ref, odd_ref[0] == 1, slot_list, col_list, row_list, turns, held, per, size
        )
        tall = jnp.dot(spread_ref[...], coupling_ref[...], preferred_element_type=F32).astype(BF16)
        wide = lax.dot_general(
            tall, spread_ref[...], (((1,), (1,)), ((), ())), preferred_element_type=F32
        )
        mixing_out[...] = (wide * same_ref[...].astype(F32)).astype(BF16)
        copy.wait()
        for g in range(groups):
            totals = totals_of(parts, same_ref, g, channels, width)
            base_outs[g][...] = base_of(x[g], momenta_buf[:, lanes(g)], totals, 0, channels)

    i32 = jnp.int32
    lists = [
        jax.ShapeDtypeStruct((2 * size,), i32),
        jax.ShapeDtypeStruct((2 * size,), i32),
        jax.ShapeDtypeStruct((size,), i32),
        jax.ShapeDtypeStruct((2,), i32),
    ]
    outs = pl.pallas_call(
        body,
        in_specs=[SMEM] * 4 + [VMEM, ANY] + [VMEM] * 3,
        out_specs=[SMEM] * 4 + [VMEM] * (1 + groups + len(emit)),
        out_shape=lists
        + [shape(width, width, BF16)]
        + [shape(cells, LANES, F32)] * groups
        + [shape(cells, LANES, BF16)] * len(emit),
        scratch_shapes=[
            pltpu.SMEM((2 * per,), i32),
            pltpu.VMEM((cells, width), F32),
            pltpu.SemaphoreType.DMA,
        ],
        compiler_params=params(),
        cost_estimate=cost(4 * cells * width * width, cells * width * 12),
        name="prepare",
    )(rows, cols, count, odd, positions, in_hbm(momenta), same, spread, coupling)
    return outs[:4], outs[4], outs[5 : 5 + groups], outs[5 + groups :]


def add_pairs(part, lists, tiles, field, window, size):
    slot_list, col_list, row_list, turns = lists

    def turn(i, carry):
        for u in range(UNROLL):
            pair = part * (size // 2) + i * UNROLL + u
            left = jnp.concatenate([tiles[slot_list[2 * pair + e]] for e in range(2)], axis=1)
            right = jnp.concatenate([window[col_list[2 * pair + e]] for e in range(2)], axis=0)
            field[row_list[pair]] += jnp.dot(left, right, preferred_element_type=F32)
        return carry

    lax.fori_loop(0, turns[part], turn, 0)


def near_fields(lists, tiles, own, other, far_part, emit, name):
    slots, tile, _ = tiles.shape
    cells, width = own.shape
    groups = width // LANES
    per = cells // tile
    size = section(slots, per)

    def body(*refs):
        list_refs, (tiles_ref, own_ref, other_ref, part_ref), refs = refs[:4], refs[4:8], refs[8:]
        field_outs, round_outs = refs[:groups], refs[groups : groups + len(emit)]
        field, window = refs[groups + len(emit) :]
        for out, g in zip(round_outs, emit):
            out[...] = own_ref[:, lanes(g)]
        window[:per] = own_ref[...].reshape(per, tile, width)
        window[per : 2 * per] = other_ref[...].reshape(per, tile, width)
        window[2 * per] = jnp.zeros((tile, width), BF16)
        field[:per, :, lanes(0)] = part_ref[...].reshape(per, tile, LANES)
        if groups > 1:
            field[:per, :, LANES:] = jnp.zeros((per, tile, width - LANES), F32)
        add_pairs(0, list_refs, tiles_ref, field, window, size)
        for g, out in enumerate(field_outs):
            out[...] = field[:per, :, lanes(g)].reshape(cells, LANES).astype(out.dtype)

    outs = pl.pallas_call(
        body,
        in_specs=[SMEM] * 4 + [VMEM] * 4,
        out_specs=[VMEM] * (groups + len(emit)),
        out_shape=[shape(cells, LANES, BF16)]
        + [shape(cells, LANES, F32)] * (groups - 1)
        + [shape(cells, LANES, BF16)] * len(emit),
        scratch_shapes=[
            pltpu.VMEM((per + 1, tile, width), F32),
            pltpu.VMEM((2 * per + 1, tile, width), BF16),
        ],
        compiler_params=params(),
        cost_estimate=cost(2 * slots * tile * tile * width, slots * tile * tile * 2),
        name=name,
    )(*lists, tiles, own, other, far_part)
    return outs[:groups], outs[groups:]


def far_first_group(lists, tiles, far, name):
    slots, tile, _ = tiles.shape
    cells = far.shape[0]
    per = cells // tile
    size = section(slots, per)

    def body(*refs):
        list_refs, (tiles_ref, far_ref, out_ref, field, window) = refs[:4], refs[4:]
        window[:per] = far_ref[...].reshape(per, tile, LANES)
        window[per] = jnp.zeros((tile, LANES), BF16)
        field[:per] = jnp.zeros((per, tile, LANES), F32)
        add_pairs(1, list_refs, tiles_ref, field, window, size)
        out_ref[...] = field[:per].reshape(cells, LANES)

    return pl.pallas_call(
        body,
        in_specs=[SMEM] * 4 + [VMEM] * 2,
        out_specs=VMEM,
        out_shape=shape(cells, LANES, F32),
        scratch_shapes=[
            pltpu.VMEM((per + 1, tile, LANES), F32),
            pltpu.VMEM((per + 1, tile, LANES), BF16),
        ],
        compiler_params=params(),
        cost_estimate=cost(2 * slots * tile * tile * LANES, slots * tile * tile * 2),
        name=name,
    )(*lists, tiles, far)


def far_fields(lists, tiles, group, near, far, extra, outs_of, work, name):
    slots, tile, _ = tiles.shape
    cells = near.shape[0]
    per = cells // tile
    size = section(slots, per)

    def body(*refs):
        list_refs, (tiles_ref, near_ref, far_ref), refs = refs[:4], refs[4:7], refs[7:]
        extra_refs, out_refs = refs[: len(extra)], refs[len(extra) : -2]
        field, window = refs[-2:]
        window[:per] = far_ref[...].reshape(per, tile, LANES)
        window[per] = jnp.zeros((tile, LANES), BF16)
        field[:per] = near_ref[...].reshape(per, tile, LANES)
        add_pairs(1, list_refs, tiles_ref, field, window, size)
        own = field[:per].reshape(cells, LANES).astype(BF16)
        out_refs[0][...] = own
        work(own, extra_refs, out_refs[1:])

    shapes = [shape(cells, LANES, BF16)] + outs_of
    outs = pl.pallas_call(
        body,
        in_specs=[SMEM] * 4 + [VMEM] * (3 + len(extra)),
        out_specs=[VMEM] * len(shapes),
        out_shape=shapes,
        scratch_shapes=[
            pltpu.VMEM((per + 1, tile, LANES), F32),
            pltpu.VMEM((per + 1, tile, LANES), BF16),
        ],
        compiler_params=params(),
        cost_estimate=cost(2 * slots * tile * tile * LANES, slots * tile * tile * 2),
        name=name,
    )(*lists, tiles, near, far, *extra)
    return outs[0], outs[1:]


def finish(xs, bases, mixed):
    groups = len(xs)
    cells = xs[0].shape[0]
    width = groups * LANES
    blocks = 4 if cells % 32 == 0 else 1
    block = cells // blocks

    def body(*refs):
        x_refs, base_refs, mixed_refs = [refs[i * groups : (i + 1) * groups] for i in range(3)]
        x_out, y_out, x_buf, y_buf, sems = refs[3 * groups :]
        copies = []
        for b in range(blocks):
            rows = slice(b * block, (b + 1) * block)
            for g in range(groups):
                y_new = base_refs[g][rows, :] - 0.2 * mixed_refs[g][rows, :]
                y_buf[rows, lanes(g)] = y_new
                x_buf[rows, lanes(g)] = jnp.clip(x_refs[g][rows, :] + 0.5 * y_new, -1.0, 1.0)
            for k, (buf, out) in enumerate(((y_buf, y_out), (x_buf, x_out))):
                copies.append(pltpu.make_async_copy(buf.at[rows], out.at[rows], sems.at[b, k]))
                copies[-1].start()
        for copy in copies:
            copy.wait()

    return pl.pallas_call(
        body,
        in_specs=[VMEM] * (3 * groups),
        out_specs=[ANY, ANY],
        out_shape=[shape(cells, width, F32)] * 2,
        scratch_shapes=[
            pltpu.VMEM((cells, width), F32),
            pltpu.VMEM((cells, width), F32),
            pltpu.SemaphoreType.DMA((blocks, 2)),
        ],
        compiler_params=params(),
        cost_estimate=cost(0, cells * width * 20),
        name="finish",
    )(*xs, *bases, *mixed)


def local(positions, momenta, tile_values, tile_rows, tile_cols, tile_count, channel_coupling):
    cells, width = positions.shape
    slots, tile, _ = tile_values.shape
    channels = channel_coupling.shape[0]
    replicas = width // channels
    groups = width // LANES
    ring = lax.axis_size("row") * lax.axis_size("col")
    where = np.arange(width)
    same = (where[:, None] // channels == where[None] // channels).astype(ml_dtypes.bfloat16)
    spread = (where[:, None] % channels == np.arange(channels)[None]).astype(ml_dtypes.bfloat16)
    odd = jnp.full((1,), lax.axis_index(RING) % 2, jnp.int32)
    on_chip = [(i, i ^ 1) for i in range(ring)]
    off_chip = [(i, (i + 1) % ring if i % 2 else (i - 1) % ring) for i in range(ring)]

    def far_swap(mine):
        return lax.ppermute(mine, RING, off_chip)

    def near_swap(mine):
        return lax.ppermute(mine, RING, on_chip)

    ready = {g: [] for g in range(groups)}
    for g in range(groups):
        ready[max(max(spanned(g, channels, width)), 1)].append(g)

    late = list(range(2, groups))
    first = round_first(positions)
    far = {0: far_swap(first)}
    own = round_all(positions, first)
    other = near_swap(own)
    lists, mixing, bases, early = prepare(
        positions,
        momenta,
        same,
        spread,
        channel_coupling,
        tile_rows,
        tile_cols,
        tile_count,
        odd,
        slots,
        tile,
        [1] if groups > 1 else [],
    )
    for g, mine in zip(range(1, 2), early):
        far[g] = far_swap(mine)
    part = far_first_group(lists, tile_values, far[0], "far_first_0")
    near, sent = near_fields(lists, tile_values, own, other, part, late, "near_first")
    for g, mine in zip(late, sent):
        far[g] = far_swap(mine)

    fields, xs, ys, rounded, new_far = {0: near[0]}, {}, {}, {}, {}
    for g in range(1, groups):
        todo = ready[g]
        known = sorted({n for t in todo for n in spanned(t, channels, width)} - {g})
        done = sorted(rounded)
        last = g == groups - 1
        extra = [mixing] + [fields[n] for n in known]
        if todo:
            extra += [positions] + [bases[t] for t in todo]
        if last:
            extra += [rounded[t] for t in done]
        outs = []
        for _ in todo:
            outs += [shape(cells, LANES, F32), shape(cells, LANES, F32), shape(cells, LANES, BF16)]
        if last:
            outs += [shape(cells, width, BF16)]

        def work(own_field, ins, out_refs, g=g, todo=todo, known=known, done=done, last=last):
            held = {n: ins[1 + i][...] for i, n in enumerate(known)}
            held[g] = own_field
            x_ref, base_refs = ins[1 + len(known) : 2 + len(known)], ins[2 + len(known) :]
            for i, t in enumerate(todo):
                y_new = base_refs[i][...] - 0.2 * mixed_of(held, ins[0], t, channels)
                x_new = jnp.clip(x_ref[0][:, lanes(t)] + 0.5 * y_new, -1.0, 1.0)
                out_refs[3 * i][...] = x_new
                out_refs[3 * i + 1][...] = y_new
                r_new = x_new.astype(BF16)
                out_refs[3 * i + 2][...] = r_new
                if last:
                    out_refs[-1][:, lanes(t)] = r_new
            if last:
                for t, ref in zip(done, ins[len(ins) - len(done) :]):
                    out_refs[-1][:, lanes(t)] = ref[...]

        fields[g], results = far_fields(
            lists, tile_values, g, near[g], far[g], extra, outs, work, f"far_first_{g}"
        )
        for i, t in enumerate(todo):
            xs[t], ys[t], rounded[t] = results[3 * i : 3 * i + 3]
            if t not in late:
                new_far[t] = far_swap(rounded[t])
        if last:
            own = results[-1]

    other = near_swap(own)
    part = far_first_group(lists, tile_values, new_far[0], "far_second_0")
    near, sent = near_fields(lists, tile_values, own, other, part, late, "near_second")
    for g, mine in zip(late, sent):
        new_far[g] = far_swap(mine)
    last_fields, mixed, energies, last_bases = {0: near[0]}, {}, {}, []
    for g in range(1, groups):
        todo = ready[g]
        known = sorted({n for t in todo for n in spanned(t, channels, width)} - {g})
        done = sorted(energies)
        last = g == groups - 1
        extra = [mixing] + [last_fields[n] for n in known] + [rounded[t] for t in todo]
        if last:
            extra += [energies[t] for t in done]
        rebase = g == 1
        if rebase:
            extra += [same] + [xs[n] for n in range(groups)] + [ys[n] for n in range(groups)]
        outs = []
        for _ in todo:
            outs += [shape(cells, LANES, F32), shape(1, LANES, F32)]
        if last:
            outs += [shape(ring, LANES, F32)]
        if rebase:
            outs += [shape(cells, LANES, F32)] * groups

        def work(
            own_field, ins, out_refs, g=g, todo=todo, known=known, done=done, last=last, rebase=rebase
        ):
            held = {n: ins[1 + i][...] for i, n in enumerate(known)}
            held[g] = own_field
            rounded_refs = ins[1 + len(known) : 1 + len(known) + len(todo)]
            sums = {}
            for i, t in enumerate(todo):
                value = mixed_of(held, ins[0], t, channels)
                out_refs[2 * i][...] = value
                sums[t] = jnp.sum(rounded_refs[i][...].astype(F32) * value, axis=0, keepdims=True)
                out_refs[2 * i + 1][...] = sums[t]
            if last:
                for t, ref in zip(done, ins[len(ins) - len(done) :]):
                    sums[t] = ref[...]
                row = jnp.concatenate([sums[t] for t in range(groups)], axis=1)
                lane = lax.broadcasted_iota(jnp.int32, (1, width), 1)
                place = lax.broadcasted_iota(jnp.int32, (1, LANES), 1)
                total = jnp.zeros((1, LANES), F32)
                for r in range(replicas):
                    inside = (lane >= r * channels) & (lane < (r + 1) * channels)
                    value = jnp.sum(jnp.where(inside, row, 0.0), axis=1, keepdims=True)
                    total = jnp.where(place == r, value, total)
                out_refs[-1][...] = jnp.broadcast_to(total, (ring, LANES))
            if rebase:
                same_ref = ins[-1 - 2 * groups]
                x = [ref[...] for ref in ins[-2 * groups : -groups]]
                parts = [split(v) for v in x]
                for n in range(groups):
                    totals = totals_of(parts, same_ref, n, channels, width)
                    y = ins[len(ins) - groups + n][...]
                    out_refs[len(out_refs) - groups + n][...] = base_of(
                        x[n], y, totals, STEPS - 1, channels
                    )

        last_fields[g], results = far_fields(
            lists, tile_values, g, near[g], new_far[g], extra, outs, work, f"far_second_{g}"
        )
        for i, t in enumerate(todo):
            mixed[t], energies[t] = results[2 * i : 2 * i + 2]
        if rebase:
            last_bases = results[len(results) - groups :]
        if last:
            partial = results[2 * len(todo)]

    everyone = lax.all_to_all(partial, RING, 0, 0, tiled=True)
    energy = jnp.sum(everyone, axis=0)[:replicas] / jnp.sqrt(jnp.float32(cells * ring * channels))
    x_new, y_new = finish(
        [xs[g] for g in range(groups)], last_bases, [mixed[g] for g in range(groups)]
    )
    return (x_new, y_new, energy)


def solution(mesh):
    cells = P(("groups", "row", "col"), None)
    slots = P(("groups", "row", "col"))
    return jax.shard_map(
        local,
        mesh=mesh,
        in_specs=(cells, cells, P(("groups", "row", "col"), None, None), slots, slots, slots, P()),
        out_specs=(cells, cells, P("groups")),
        check_vma=False,
    )
```

```python
import jax
import jax.numpy as jnp
import ml_dtypes
import numpy as np
from jax import lax
from jax.experimental import pallas as pl
from jax.experimental.pallas import tpu as pltpu
from jax.sharding import PartitionSpec as P

STEPS = 2
LANES = 128
LONG, SHORT = 16, 4
VMEM_LIMIT = 14 * 1024 * 1024
F32 = jnp.float32
BF16 = jnp.bfloat16
RING = ("row", "col")


def cost(flops, moved):
    return pl.CostEstimate(
        flops=int(flops) // 1000, bytes_accessed=int(moved) // 1000, transcendentals=0
    )


def call(body, ins, outs, scratch, name, work=0):
    return pl.pallas_call(
        body,
        in_specs=[pl.BlockSpec(memory_space=pl.ANY if s is pltpu.HBM else s) for _, s in ins],
        out_specs=[pl.BlockSpec(memory_space=pl.ANY if s is pltpu.HBM else s) for *_, s in outs],
        out_shape=[
            jax.ShapeDtypeStruct(dims, kind) if s is pltpu.HBM else s(dims, kind)
            for dims, kind, s in outs
        ],
        scratch_shapes=scratch,
        compiler_params=pltpu.CompilerParams(vmem_limit_bytes=VMEM_LIMIT),
        cost_estimate=cost(work, work),
        name=name,
    )(*[pltpu.with_memory_space_constraint(a, s) for a, s in ins])


def vmem(*arrays):
    return [(a, pltpu.VMEM) for a in arrays]


def lanes(group):
    return slice(group * LANES, (group + 1) * LANES)


def spanned(group, channels, width):
    first = group * LANES // channels * channels
    last = -(-(group + 1) * LANES // channels) * channels
    return list(range(first // LANES, -(-min(last, width) // LANES)))


def span_lanes(near):
    return slice(near[0] * LANES, (near[-1] + 1) * LANES)


def split(x):
    high = x.astype(BF16)
    return high, (x - high.astype(F32)).astype(BF16)


def bases_into(outs, xs, ys, same, step, channels):
    groups = len(xs)
    width = groups * LANES
    detune = 1.0 - (step + 1.0) / (STEPS + 1.0)
    parts = [split(x) for x in xs]
    for g in range(groups):
        near = spanned(g, channels, width)
        ones = same[span_lanes(near), lanes(g)]
        totals = sum(
            jnp.dot(
                jnp.concatenate([parts[n][k] for n in near], axis=1),
                ones,
                preferred_element_type=F32,
            )
            for k in range(2)
        )
        penalty = 0.02 * (totals - (2.0 - channels))
        outs[g][...] = ys[g] + 0.5 * (-detune * xs[g] - 0.4 * penalty)


def mixed_of(fields, mixing, group, channels):
    near = spanned(group, channels, mixing.shape[0])
    return jnp.dot(
        jnp.concatenate([fields[n] for n in near], axis=1),
        mixing[span_lanes(near), lanes(group)],
        preferred_element_type=F32,
    )


def round_first(positions):
    cells = positions.shape[0]

    def body(x_ref, out_ref, buf, sem):
        copy = pltpu.make_async_copy(x_ref.at[:, lanes(0)], buf, sem)
        copy.start()
        copy.wait()
        out_ref[...] = buf[...].astype(BF16)

    return call(
        body,
        [(positions, pltpu.HBM)],
        [((cells, LANES), BF16, pltpu.VMEM)],
        [pltpu.VMEM((cells, LANES), F32), pltpu.SemaphoreType.DMA],
        "round_first",
    )[0]


def round_rest(positions, after):
    cells, width = positions.shape
    groups = width // LANES

    def body(x_ref, _, *outs):
        for g in range(1, groups):
            outs[g - 1][...] = x_ref[:, lanes(g)].astype(BF16)

    return call(
        body,
        vmem(positions, after),
        [((cells, LANES), BF16, pltpu.VMEM)] * (groups - 1),
        [],
        "round_rest",
    )


def section(slots, per):
    return -(-(slots + per) // (2 * SHORT)) * SHORT


def make_lists(rows, cols, count, mixing_parts, sent, slots, tile, cells, ring_index):
    per = cells // tile
    pairs = section(slots, per)
    same, spread, coupling = mixing_parts
    width = same.shape[0]

    def body(rows_ref, cols_ref, count_ref, same_ref, spread_ref, coupling_ref, sent_ref, list_ref, mixing_ref, copy_ref, held):
        odd = lax.rem(ring_index(), 2) == 1
        copy_ref[...] = sent_ref[...]
        tall = jnp.dot(spread_ref[...], coupling_ref[...], preferred_element_type=F32).astype(BF16)
        wide = lax.dot_general(
            tall, spread_ref[...], (((1,), (1,)), ((), ())), preferred_element_type=F32
        )
        mixing_ref[...] = (wide * same_ref[...].astype(F32)).astype(BF16)
        for k in range(2 * per):
            held[k] = -1
        far_third = jnp.where(odd, 2, 0)

        def visit(slot, totals):
            near_pairs, far_pairs = totals
            row, col = rows_ref[slot], cols_ref[slot]
            third = jnp.where(col >= 2 * per, 2, jnp.where(col >= per, 1, 0))
            source = col - third * per
            far = third == far_third
            source = jnp.where(far | (third == 1), source, source + per)
            key = row + jnp.where(far, per, 0)
            place = 2 * jnp.where(far, far_pairs + pairs, near_pairs)
            entry = slot * 65536 + source * 256 + row
            other = held[key]
            full = other >= 0
            list_ref[place] = other
            list_ref[place + 1] = entry
            held[key] = jnp.where(full, -1, entry)
            one = full.astype(jnp.int32)
            far_one = jnp.where(far, one, 0)
            return near_pairs + one - far_one, far_pairs + far_one

        totals = lax.fori_loop(0, count_ref[0], visit, (jnp.int32(0), jnp.int32(0)))
        for part, zero in enumerate((2 * per, per)):
            total = totals[part]
            start = part * pairs
            for k in range(per):
                other = held[part * per + k]
                list_ref[2 * (start + total)] = other
                list_ref[2 * (start + total) + 1] = zero * 256 + k
                total = total + (other >= 0).astype(jnp.int32)
            short_turns = (total + SHORT - 1) // SHORT

            def pad(pair, carry, start=start, zero=zero):
                for e in range(2):
                    list_ref[2 * (start + pair) + e] = zero * 256 + per
                return carry

            lax.fori_loop(total, short_turns * SHORT, pad, 0)
            list_ref[4 * pairs + 2 * part] = short_turns // (LONG // SHORT)
            list_ref[4 * pairs + 2 * part + 1] = short_turns % (LONG // SHORT)

    return call(
        body,
        [(rows, pltpu.SMEM), (cols, pltpu.SMEM), (count, pltpu.SMEM)]
        + vmem(same, spread, coupling, sent),
        [
            ((4 * pairs + 4 + 2,), jnp.int32, pltpu.SMEM),
            ((width, width), BF16, pltpu.VMEM),
            (sent.shape, BF16, pltpu.VMEM),
        ],
        [pltpu.SMEM((2 * per,), jnp.int32)],
        "make_lists",
    )


def add_pairs(part, list_ref, tiles, field, window, pairs):
    def turn(first, length):
        for u in range(length):
            place = 2 * (part * pairs + first + u)
            entries = [list_ref[place + e] for e in range(2)]
            left = jnp.concatenate([tiles[n >> 16] for n in entries], axis=1)
            right = jnp.concatenate([window[(n >> 8) & 255] for n in entries], axis=0)
            field[entries[1] & 255] += jnp.dot(left, right, preferred_element_type=F32)

    def long(i, carry):
        turn(i * LONG, LONG)
        return carry

    def short(i, carry):
        turn(long_turns * LONG + i * SHORT, SHORT)
        return carry

    long_turns = list_ref[4 * pairs + 2 * part]
    lax.fori_loop(0, long_turns, long, 0)
    lax.fori_loop(0, list_ref[4 * pairs + 2 * part + 1], short, 0)


def near_fields(lists, tiles, owns, others, far_part, sent, name):
    slots, tile, _ = tiles.shape
    cells = owns[0].shape[0]
    groups = len(owns)
    width = groups * LANES
    per = cells // tile
    pairs = section(slots, per)

    def body(list_ref, tiles_ref, *refs):
        own_refs, other_refs, refs = refs[:groups], refs[groups : 2 * groups], refs[2 * groups :]
        part_ref, sent_refs, refs = refs[0], refs[1 : 1 + len(sent)], refs[1 + len(sent) :]
        field_outs, copy_outs, (field, window) = refs[:groups], refs[groups:-2], refs[-2:]
        for out, ref in zip(copy_outs, sent_refs):
            out[...] = ref[...]
        for g in range(groups):
            window[:per, :, lanes(g)] = own_refs[g][...].reshape(per, tile, LANES)
            window[per : 2 * per, :, lanes(g)] = other_refs[g][...].reshape(per, tile, LANES)
        window[2 * per] = jnp.zeros((tile, width), BF16)
        field[:per, :, lanes(0)] = part_ref[...].reshape(per, tile, LANES)
        if groups > 1:
            field[:per, :, LANES:] = jnp.zeros((per, tile, width - LANES), F32)
        add_pairs(0, list_ref, tiles_ref, field, window, pairs)
        for g, out in enumerate(field_outs):
            out[...] = field[:per, :, lanes(g)].reshape(cells, LANES).astype(out.dtype)

    outs = call(
        body,
        [(lists, pltpu.SMEM)] + vmem(tiles, *owns, *others, far_part, *sent),
        [((cells, LANES), BF16 if g == 0 else F32, pltpu.VMEM) for g in range(groups)]
        + [((cells, LANES), BF16, pltpu.VMEM)] * len(sent),
        [
            pltpu.VMEM((per + 1, tile, width), F32),
            pltpu.VMEM((2 * per + 1, tile, width), BF16),
        ],
        name,
    )
    return outs[:groups], outs[groups:]


def far_fields(lists, tiles, near, far, extra, outs_of, work, name):
    slots, tile, _ = tiles.shape
    cells = far.shape[0]
    per = cells // tile
    pairs = section(slots, per)
    start = [] if near is None else [near]

    def body(list_ref, tiles_ref, far_ref, *refs):
        near_refs, refs = refs[: len(start)], refs[len(start) :]
        extra_refs, out_refs, (field, window) = refs[: len(extra)], refs[len(extra) : -2], refs[-2:]
        window[:per] = far_ref[...].reshape(per, tile, LANES)
        window[per] = jnp.zeros((tile, LANES), BF16)
        if start:
            field[:per] = near_refs[0][...].reshape(per, tile, LANES)
        else:
            field[:per] = jnp.zeros((per, tile, LANES), F32)
        add_pairs(1, list_ref, tiles_ref, field, window, pairs)
        work(field[:per].reshape(cells, LANES), extra_refs, out_refs)

    return call(
        body,
        [(lists, pltpu.SMEM)] + vmem(tiles, far, *start, *extra),
        [(*out, pltpu.VMEM) for out in outs_of],
        [
            pltpu.VMEM((per + 1, tile, LANES), F32),
            pltpu.VMEM((per + 1, tile, LANES), BF16),
        ],
        name,
    )


def bases(xs, ys, same, step, channels, after, name):
    cells = xs[0].shape[0]
    groups = same.shape[0] // LANES

    def body(*refs):
        x_refs, y_refs = refs[: len(xs)], refs[len(xs) : 2 * len(xs)]
        if len(xs) == 1:
            x, y = [[r[0][:, lanes(g)] for g in range(groups)] for r in (x_refs, y_refs)]
        else:
            x, y = [[r[...] for r in refs_of] for refs_of in (x_refs, y_refs)]
        bases_into(refs[2 * len(xs) + 2 :], x, y, refs[2 * len(xs)], step, channels)

    return call(
        body,
        vmem(*xs, *ys, same, after),
        [((cells, LANES), F32, pltpu.VMEM)] * groups,
        [],
        name,
    )


def assemble(xs, ys):
    groups = len(xs)
    cells = xs[0].shape[0]
    width = groups * LANES

    def body(*refs):
        outs, sems = refs[2 * groups : -1], refs[-1]
        copies = [
            pltpu.make_async_copy(
                refs[k * groups + g], outs[k].at[:, lanes(g)], sems.at[k * groups + g]
            )
            for g in range(groups)
            for k in range(2)
        ]
        for copy in copies:
            copy.start()
        for copy in copies:
            copy.wait()

    return call(
        body,
        vmem(*xs, *ys),
        [((cells, width), F32, pltpu.HBM)] * 2,
        [pltpu.SemaphoreType.DMA((2 * groups,))],
        "assemble",
    )


def local(positions, momenta, tile_values, tile_rows, tile_cols, tile_count, channel_coupling):
    cells, width = positions.shape
    slots, tile, _ = tile_values.shape
    channels = channel_coupling.shape[0]
    replicas = width // channels
    groups = width // LANES
    ring = lax.axis_size("row") * lax.axis_size("col")
    where = np.arange(width)
    same = jnp.asarray((where[:, None] // channels == where[None] // channels).astype(ml_dtypes.bfloat16))
    spread = jnp.asarray((where[:, None] % channels == np.arange(channels)[None]).astype(ml_dtypes.bfloat16))
    on_chip = [(i, i ^ 1) for i in range(ring)]
    off_chip = [(i, (i + 1) % ring if i % 2 else (i - 1) % ring) for i in range(ring)]
    wide = (cells, LANES)

    def ring_index():
        return lax.axis_index("row") * lax.axis_size("col") + lax.axis_index("col")

    def far_swap(mine):
        return lax.ppermute(mine, RING, off_chip)

    def near_swap(mine):
        return lax.ppermute(mine, RING, on_chip)

    ready = {g: [] for g in range(groups)}
    for g in range(groups):
        ready[max(max(spanned(g, channels, width)), 1)].append(g)

    def keep(field, _, outs):
        outs[0][...] = field

    owns = [round_first(positions)]
    far = {0: far_swap(owns[0])}
    owns += round_rest(positions, owns[0])
    others = [near_swap(r) for r in owns]
    lists, mixing, sent = make_lists(
        tile_rows, tile_cols, tile_count, (same, spread, channel_coupling), owns[1], slots, tile, cells, ring_index
    )
    far[1] = far_swap(sent)
    (part,) = far_fields(lists, tile_values, None, far[0], [], [(wide, F32)], keep, "far_first_0")
    near, sent = near_fields(lists, tile_values, owns, others, part, owns[2:], "near_first")
    for g in range(2, groups):
        far[g] = far_swap(sent[g - 2])
    base = bases([positions], [momenta], same, 0, channels, near[-1], "base_first")

    fields, xs, ys, rounded, new_far = {0: near[0]}, {}, {}, {}, {}
    for g in range(1, groups):
        todo = ready[g]
        known = sorted({n for t in todo for n in spanned(t, channels, width)} - {g})

        def work(field, ins, outs, g=g, todo=todo, known=known):
            own = field.astype(BF16)
            outs[0][...] = own
            held = {n: ins[1 + i][...] for i, n in enumerate(known)}
            held[g] = own
            x_ref, base_refs = ins[1 + len(known)], ins[2 + len(known) :]
            for i, t in enumerate(todo):
                y_new = base_refs[i][...] - 0.2 * mixed_of(held, ins[0], t, channels)
                x_new = jnp.clip(x_ref[:, lanes(t)] + 0.5 * y_new, -1.0, 1.0)
                outs[1 + 3 * i][...] = x_new
                outs[2 + 3 * i][...] = y_new
                outs[3 + 3 * i][...] = x_new.astype(BF16)

        fields[g], *results = far_fields(
            lists,
            tile_values,
            near[g],
            far[g],
            [mixing] + [fields[n] for n in known] + [positions] + [base[t] for t in todo],
            [(wide, BF16)] + [(wide, F32), (wide, F32), (wide, BF16)] * len(todo),
            work,
            f"far_first_{g}",
        )
        for i, t in enumerate(todo):
            xs[t], ys[t], rounded[t] = results[3 * i : 3 * i + 3]
            if t < 2:
                new_far[t] = far_swap(rounded[t])

    owns = [rounded[g] for g in range(groups)]
    others = [near_swap(r) for r in owns]
    (part,) = far_fields(
        lists, tile_values, None, new_far[0], [], [(wide, F32)], keep, "far_second_0"
    )
    near, sent = near_fields(lists, tile_values, owns, others, part, owns[2:], "near_second")
    for g in range(2, groups):
        new_far[g] = far_swap(sent[g - 2])
    base = bases(
        [xs[g] for g in range(groups)],
        [ys[g] for g in range(groups)],
        same,
        1,
        channels,
        near[-1],
        "base_second",
    )
    fields, last_x, last_y, energies = {0: near[0]}, {}, {}, {}
    for g in range(1, groups):
        todo = ready[g]
        known = sorted({n for t in todo for n in spanned(t, channels, width)} - {g})
        done = sorted(energies)
        last = g == groups - 1

        def work(field, ins, outs, g=g, todo=todo, known=known, done=done, last=last):
            own = field.astype(BF16)
            held = {n: ins[1 + i][...] for i, n in enumerate(known)}
            held[g] = own
            ins_of = ins[1 + len(known) :]
            sums = {}
            for i, t in enumerate(todo):
                base_ref, x_ref, rounded_ref = ins_of[3 * i : 3 * i + 3]
                mixed = mixed_of(held, ins[0], t, channels)
                y_new = base_ref[...] - 0.2 * mixed
                outs[1 + 3 * i][...] = jnp.clip(x_ref[...] + 0.5 * y_new, -1.0, 1.0)
                outs[2 + 3 * i][...] = y_new
                sums[t] = jnp.sum(rounded_ref[...].astype(F32) * mixed, axis=0, keepdims=True)
                outs[3 + 3 * i][...] = sums[t]
            if not last:
                outs[0][...] = own
                return
            for t, ref in zip(done, ins_of[3 * len(todo) :]):
                sums[t] = ref[...]
            row = jnp.concatenate([sums[t] for t in range(groups)], axis=1)
            lane = lax.broadcasted_iota(jnp.int32, (1, width), 1)
            place = lax.broadcasted_iota(jnp.int32, (1, LANES), 1)
            total = jnp.zeros((1, LANES), F32)
            for r in range(replicas):
                inside = (lane >= r * channels) & (lane < (r + 1) * channels)
                value = jnp.sum(jnp.where(inside, row, 0.0), axis=1, keepdims=True)
                total = jnp.where(place == r, value, total)
            outs[0][...] = jnp.broadcast_to(total, (ring, LANES))

        first, *results = far_fields(
            lists,
            tile_values,
            near[g],
            new_far[g],
            [mixing]
            + [fields[n] for n in known]
            + [a for t in todo for a in (base[t], xs[t], rounded[t])]
            + ([energies[t] for t in done] if last else []),
            [((ring, LANES), F32) if last else (wide, BF16)]
            + [(wide, F32), (wide, F32), ((1, LANES), F32)] * len(todo),
            work,
            f"far_second_{g}",
        )
        if last:
            partial = first
        else:
            fields[g] = first
        for i, t in enumerate(todo):
            last_x[t], last_y[t], energies[t] = results[3 * i : 3 * i + 3]

    everyone = lax.all_to_all(partial, RING, 0, 0, tiled=True)
    energy = jnp.sum(everyone, axis=0)[:replicas] / jnp.sqrt(jnp.float32(cells * ring * channels))
    x_new, y_new = assemble(
        [last_x[g] for g in range(groups)], [last_y[g] for g in range(groups)]
    )
    return (x_new, y_new, energy)


def solution(mesh):
    cells = P(("groups", "row", "col"), None)
    slots = P(("groups", "row", "col"))
    return jax.shard_map(
        local,
        mesh=mesh,
        in_specs=(cells, cells, P(("groups", "row", "col"), None, None), slots, slots, slots, P()),
        out_specs=(cells, cells, P("groups")),
        check_vma=False,
    )
```

```python
import jax
import jax.numpy as jnp
import ml_dtypes
import numpy as np
from jax import lax
from jax.experimental import pallas as pl
from jax.experimental.pallas import tpu as pltpu
from jax.sharding import PartitionSpec as P

STEPS = 2
LANES = 128
LONG, SHORT = 16, 4
VMEM_LIMIT = 14 * 1024 * 1024
NEAR_FLOPS = 10**10
F32 = jnp.float32
BF16 = jnp.bfloat16
RING = ("row", "col")


def call(body, ins, outs, scratch, name, flops=0):
    return pl.pallas_call(
        body,
        in_specs=[pl.BlockSpec(memory_space=pl.ANY if s is pltpu.HBM else s) for _, s in ins],
        out_specs=[pl.BlockSpec(memory_space=pl.ANY if s is pltpu.HBM else s) for *_, s in outs],
        out_shape=[
            jax.ShapeDtypeStruct(dims, kind) if s is pltpu.HBM else s(dims, kind)
            for dims, kind, s in outs
        ],
        scratch_shapes=scratch,
        compiler_params=pltpu.CompilerParams(vmem_limit_bytes=VMEM_LIMIT),
        cost_estimate=pl.CostEstimate(
            flops=int(flops) or 1000, bytes_accessed=1000, transcendentals=0
        ),
        name=name,
    )(*[pltpu.with_memory_space_constraint(a, s) for a, s in ins])


def vmem(*arrays):
    return [(a, pltpu.VMEM) for a in arrays]


def lanes(group):
    return slice(group * LANES, (group + 1) * LANES)


def spanned(group, channels, width):
    first = group * LANES // channels * channels
    last = -(-(group + 1) * LANES // channels) * channels
    return list(range(first // LANES, -(-min(last, width) // LANES)))


def span_lanes(near):
    return slice(near[0] * LANES, (near[-1] + 1) * LANES)


def split(x):
    high = x.astype(BF16)
    return high, (x - high.astype(F32)).astype(BF16)


def bases_into(outs, xs, ys, same, step, channels):
    groups = len(xs)
    width = groups * LANES
    detune = 1.0 - (step + 1.0) / (STEPS + 1.0)
    parts = [split(x) for x in xs]
    for g in range(groups):
        near = spanned(g, channels, width)
        ones = same[span_lanes(near), lanes(g)]
        totals = sum(
            jnp.dot(
                jnp.concatenate([parts[n][k] for n in near], axis=1),
                ones,
                preferred_element_type=F32,
            )
            for k in range(2)
        )
        penalty = 0.02 * (totals - (2.0 - channels))
        outs[g][...] = ys[g] + 0.5 * (-detune * xs[g] - 0.4 * penalty)


def mixed_of(fields, mixing, group, channels):
    near = spanned(group, channels, mixing.shape[0])
    return jnp.dot(
        jnp.concatenate([fields[n] for n in near], axis=1),
        mixing[span_lanes(near), lanes(group)],
        preferred_element_type=F32,
    )


def load_first(positions, groups_of):
    cells = positions.shape[0]
    n = len(groups_of)

    def body(x_ref, *refs):
        x_outs, r_outs, sent, sems = refs[:n], refs[n : 2 * n], refs[2 * n], refs[-1]
        copies = [
            pltpu.make_async_copy(x_ref.at[:, lanes(g)], x_outs[i], sems.at[i])
            for i, g in enumerate(groups_of)
        ]
        for copy in copies:
            copy.start()
        for i, copy in enumerate(copies):
            copy.wait()
            rounded = x_outs[i][...].astype(BF16)
            r_outs[i][...] = rounded
            sent[:, lanes(i)] = rounded

    outs = call(
        body,
        [(positions, pltpu.HBM)],
        [((cells, LANES), F32, pltpu.VMEM)] * n
        + [((cells, LANES), BF16, pltpu.VMEM)] * n
        + [((cells, n * LANES), BF16, pltpu.VMEM)],
        [pltpu.SemaphoreType.DMA((n,))],
        "load_first",
    )
    return outs[:n], outs[n : 2 * n], outs[2 * n]


def section(slots, per):
    return -(-(slots + per) // (2 * SHORT)) * SHORT


def make_lists(rows, cols, count, positions, groups_of, after, slots, tile, ring_index):
    cells = positions.shape[0]
    per = cells // tile
    pairs = section(slots, per)
    n = len(groups_of)

    def body(rows_hbm, cols_hbm, count_hbm, x_ref, _, list_ref, *refs):
        x_outs, r_outs = refs[:n], refs[n : 2 * n]
        rows_ref, cols_ref, count_ref, held, sems = refs[2 * n :]
        copies = [
            pltpu.make_async_copy(*ends, sems.at[k])
            for k, ends in enumerate(
                [(rows_hbm, rows_ref), (cols_hbm, cols_ref), (count_hbm, count_ref)]
                + [(x_ref.at[:, lanes(g)], x_outs[i]) for i, g in enumerate(groups_of)]
            )
        ]
        for copy in copies:
            copy.start()
        for k in range(2 * per):
            held[k] = -1
        far_third = jnp.where(lax.rem(ring_index(), 2) == 1, 2, 0)
        for copy in copies[:3]:
            copy.wait()

        def visit(slot, totals):
            near_pairs, far_pairs = totals
            row, col = rows_ref[slot], cols_ref[slot]
            third = jnp.where(col >= 2 * per, 2, jnp.where(col >= per, 1, 0))
            source = col - third * per
            far = third == far_third
            source = jnp.where(far | (third == 1), source, source + per)
            key = row + jnp.where(far, per, 0)
            place = 2 * jnp.where(far, far_pairs + pairs, near_pairs)
            entry = slot * 65536 + source * 256 + row
            other = held[key]
            full = other >= 0
            list_ref[place] = other
            list_ref[place + 1] = entry
            held[key] = jnp.where(full, -1, entry)
            one = full.astype(jnp.int32)
            far_one = jnp.where(far, one, 0)
            return near_pairs + one - far_one, far_pairs + far_one

        totals = lax.fori_loop(0, count_ref[0], visit, (jnp.int32(0), jnp.int32(0)))
        for part, zero in enumerate((2 * per, per)):
            total = totals[part]
            start = part * pairs
            for k in range(per):
                other = held[part * per + k]
                list_ref[2 * (start + total)] = other
                list_ref[2 * (start + total) + 1] = zero * 256 + k
                total = total + (other >= 0).astype(jnp.int32)
            short_turns = (total + SHORT - 1) // SHORT

            def pad(pair, carry, start=start, zero=zero):
                for e in range(2):
                    list_ref[2 * (start + pair) + e] = zero * 256 + per
                return carry

            lax.fori_loop(total, short_turns * SHORT, pad, 0)
            list_ref[4 * pairs + 2 * part] = short_turns // (LONG // SHORT)
            list_ref[4 * pairs + 2 * part + 1] = short_turns % (LONG // SHORT)
        for i, copy in enumerate(copies[3:]):
            copy.wait()
            r_outs[i][...] = x_outs[i][...].astype(BF16)

    outs = call(
        body,
        [(a, pl.ANY) for a in (rows, cols, count)] + [(positions, pltpu.HBM)] + vmem(after),
        [((4 * pairs + 4 + 2,), jnp.int32, pltpu.SMEM)]
        + [((cells, LANES), F32, pltpu.VMEM)] * n
        + [((cells, LANES), BF16, pltpu.VMEM)] * n,
        [
            pltpu.SMEM(rows.shape, jnp.int32),
            pltpu.SMEM(cols.shape, jnp.int32),
            pltpu.SMEM(count.shape, jnp.int32),
            pltpu.SMEM((2 * per,), jnp.int32),
            pltpu.SemaphoreType.DMA((3 + n,)),
        ],
        "make_lists",
    )
    return outs[0], outs[1 : 1 + n], outs[1 + n :]


def add_pairs(part, list_ref, tiles, field, window, pairs):
    def turn(first, length):
        for u in range(length):
            place = 2 * (part * pairs + first + u)
            entries = [list_ref[place + e] for e in range(2)]
            left = jnp.concatenate([tiles[n >> 16] for n in entries], axis=1)
            right = jnp.concatenate([window[(n >> 8) & 255] for n in entries], axis=0)
            field[entries[1] & 255] += jnp.dot(left, right, preferred_element_type=F32)

    def long(i, carry):
        turn(i * LONG, LONG)
        return carry

    def short(i, carry):
        turn(long_turns * LONG + i * SHORT, SHORT)
        return carry

    long_turns = list_ref[4 * pairs + 2 * part]
    lax.fori_loop(0, long_turns, long, 0)
    lax.fori_loop(0, list_ref[4 * pairs + 2 * part + 1], short, 0)


def near_fields(lists, tiles, owns, others, far_part, sent, after, flops, name):
    slots, tile, _ = tiles.shape
    cells = owns[0].shape[0]
    groups = len(owns)
    width = groups * LANES
    per = cells // tile
    pairs = section(slots, per)
    start = [] if far_part is None else [far_part]

    def body(list_ref, tiles_ref, *refs):
        own_refs, other_refs, refs = refs[:groups], refs[groups : 2 * groups], refs[2 * groups :]
        start_refs, refs = refs[: len(start)], refs[len(start) :]
        sent_refs, refs = refs[: len(sent)], refs[len(sent) + len(after) :]
        field_outs, sent_outs, (field, window) = refs[:groups], refs[groups:-2], refs[-2:]
        for out, ref in zip(sent_outs, sent_refs):
            out[...] = ref[...]
        for g in range(groups):
            window[:per, :, lanes(g)] = own_refs[g][...].reshape(per, tile, LANES)
            window[per : 2 * per, :, lanes(g)] = other_refs[g][...].reshape(per, tile, LANES)
        window[2 * per] = jnp.zeros((tile, width), BF16)
        field[:per] = jnp.zeros((per, tile, width), F32)
        for ref in start_refs:
            field[:per, :, lanes(0)] = ref[...].reshape(per, tile, LANES)
        add_pairs(0, list_ref, tiles_ref, field, window, pairs)
        for g, out in enumerate(field_outs):
            out[...] = field[:per, :, lanes(g)].reshape(cells, LANES).astype(out.dtype)

    outs = call(
        body,
        [(lists, pltpu.SMEM)] + vmem(tiles, *owns, *others, *start, *sent, *after),
        [
            ((cells, LANES), BF16 if start and g == 0 else F32, pltpu.VMEM)
            for g in range(groups)
        ]
        + [(a.shape, BF16, pltpu.VMEM) for a in sent],
        [
            pltpu.VMEM((per + 1, tile, width), F32),
            pltpu.VMEM((2 * per + 1, tile, width), BF16),
        ],
        name,
        flops,
    )
    return outs[:groups], outs[groups:]


def far_fields(lists, tiles, nears, far, extra, outs_of, work, name, flops=0):
    slots, tile, _ = tiles.shape
    cells, width = far.shape
    per = cells // tile
    pairs = section(slots, per)
    n = width // LANES
    m = len(nears)

    def body(list_ref, tiles_ref, far_ref, *refs):
        near_refs, extra_refs = refs[:m], refs[m : m + len(extra)]
        out_refs, (field, window) = refs[m + len(extra) : -2], refs[-2:]
        window[:per] = far_ref[...].reshape(per, tile, width)
        window[per] = jnp.zeros((tile, width), BF16)
        if not near_refs:
            field[:per] = jnp.zeros((per, tile, width), F32)
        for i, ref in enumerate(near_refs):
            field[:per, :, lanes(i)] = ref[...].reshape(per, tile, LANES)
        add_pairs(1, list_ref, tiles_ref, field, window, pairs)
        work([field[:per, :, lanes(i)].reshape(cells, LANES) for i in range(n)], extra_refs, out_refs)

    return call(
        body,
        [(lists, pltpu.SMEM)] + vmem(tiles, far, *nears, *extra),
        [(*out, pltpu.VMEM) for out in outs_of],
        [pltpu.VMEM((per + 1, tile, width), F32), pltpu.VMEM((per + 1, tile, width), BF16)],
        name,
        flops,
    )


def first_base(xs, momenta, same, spread, coupling, channels):
    cells, width = momenta.shape
    groups = len(xs)

    def body(*refs):
        x_refs, (y_ref, same_ref, spread_ref, coupling_ref) = refs[:groups], refs[groups : groups + 4]
        outs = refs[groups + 4 :]
        tall = jnp.dot(spread_ref[...], coupling_ref[...], preferred_element_type=F32).astype(BF16)
        wide = lax.dot_general(
            tall, spread_ref[...], (((1,), (1,)), ((), ())), preferred_element_type=F32
        )
        outs[groups][...] = (wide * same_ref[...].astype(F32)).astype(BF16)
        x = [ref[...] for ref in x_refs]
        y = [y_ref[:, lanes(g)] for g in range(groups)]
        bases_into(outs[:groups], x, y, same_ref, 0, channels)

    outs = call(
        body,
        vmem(*xs, momenta, same, spread, coupling),
        [((cells, LANES), F32, pltpu.VMEM)] * groups + [((width, width), BF16, pltpu.VMEM)],
        [],
        "first_base",
    )
    return outs[:groups], outs[groups]


def second_base(xs, ys, same, channels):
    groups = len(xs)

    def body(*refs):
        x = [ref[...] for ref in refs[:groups]]
        y = [ref[...] for ref in refs[groups : 2 * groups]]
        bases_into(refs[2 * groups + 1 :], x, y, refs[2 * groups], 1, channels)

    return call(
        body,
        vmem(*xs, *ys, same),
        [(xs[0].shape, F32, pltpu.VMEM)] * groups,
        [],
        "second_base",
    )


def finish(xs, bases, mixed):
    groups = len(xs)
    cells = xs[0].shape[0]
    width = groups * LANES

    def body(*refs):
        x_refs, base_refs, mixed_refs = [refs[k * groups : (k + 1) * groups] for k in range(3)]
        x_out, y_out, x_buf, y_buf, sems = refs[3 * groups :]
        copies = []
        for g in range(groups):
            y_new = base_refs[g][...] - 0.2 * mixed_refs[g][...]
            y_buf[g] = y_new
            x_buf[g] = jnp.clip(x_refs[g][...] + 0.5 * y_new, -1.0, 1.0)
            for k, (buf, out) in enumerate(((y_buf, y_out), (x_buf, x_out))):
                copies.append(
                    pltpu.make_async_copy(buf.at[g], out.at[:, lanes(g)], sems.at[g, k])
                )
                copies[-1].start()
        for copy in copies:
            copy.wait()

    return call(
        body,
        vmem(*xs, *bases, *mixed),
        [((cells, width), F32, pltpu.HBM)] * 2,
        [
            pltpu.VMEM((groups, cells, LANES), F32),
            pltpu.VMEM((groups, cells, LANES), F32),
            pltpu.SemaphoreType.DMA((groups, 2)),
        ],
        "finish",
    )


def local(positions, momenta, tile_values, tile_rows, tile_cols, tile_count, channel_coupling):
    cells, width = positions.shape
    slots, tile, _ = tile_values.shape
    channels = channel_coupling.shape[0]
    replicas = width // channels
    groups = width // LANES
    ring = lax.axis_size("row") * lax.axis_size("col")
    where = np.arange(width)
    same = jnp.asarray(
        (where[:, None] // channels == where[None] // channels).astype(ml_dtypes.bfloat16)
    )
    spread = jnp.asarray(
        (where[:, None] % channels == np.arange(channels)[None]).astype(ml_dtypes.bfloat16)
    )
    on_chip = [(i, i ^ 1) for i in range(ring)]
    off_chip = [(i, (i + 1) % ring if i % 2 else (i - 1) % ring) for i in range(ring)]
    wide = (cells, LANES)
    every = list(range(groups))
    first_pieces = [every[:-1], every[-1:]]
    second_pieces = [every[:1], every[1:]]

    def ring_index():
        return lax.axis_index("row") * lax.axis_size("col") + lax.axis_index("col")

    def far_swap(mine):
        return lax.ppermute(mine, RING, off_chip)

    def near_swap(mine):
        return lax.ppermute(mine, RING, on_chip)

    def ready(piece, done):
        return [
            t for t in every if t not in done and max(spanned(t, channels, width)) <= piece[-1]
        ]

    def keep(done, _, outs):
        outs[0][...] = done[0]

    def needed(todo, piece):
        return sorted({n for t in todo for n in spanned(t, channels, width)} - set(piece))

    xs, owns, sent = load_first(positions, first_pieces[0])
    fars = [far_swap(sent)]
    lists, more_x, more_own = make_lists(
        tile_rows, tile_cols, tile_count, positions, first_pieces[1], sent, slots, tile, ring_index
    )
    xs, owns = [*xs, *more_x], [*owns, *more_own]
    others = [near_swap(r) for r in owns]
    base, mixing = first_base(xs, momenta, same, spread, channel_coupling, channels)
    near, sent = near_fields(
        lists, tile_values, owns, others, None, more_own, [mixing], 0, "near_first"
    )
    fars.append(far_swap(sent[0]))

    fields, new_x, new_y, rounded, new_fars = {}, {}, {}, {}, []
    for p, piece in enumerate(first_pieces):
        todo = ready(piece, new_x)
        known = needed(todo, piece)
        going = second_pieces[p]
        assert going == todo
        last = p == len(first_pieces) - 1

        def work(done, ins, outs, piece=piece, todo=todo, known=known, last=last):
            held = {n: ins[1 + i][...] for i, n in enumerate(known)}
            done = [field.astype(BF16) for field in done]
            held.update(zip(piece, done))
            rest = ins[1 + len(known) :]
            for i, t in enumerate(todo):
                y_new = rest[2 * i][...] - 0.2 * mixed_of(held, ins[0], t, channels)
                x_new = jnp.clip(rest[2 * i + 1][...] + 0.5 * y_new, -1.0, 1.0)
                r_new = x_new.astype(BF16)
                outs[3 * i][...] = x_new
                outs[3 * i + 1][...] = y_new
                outs[3 * i + 2][...] = r_new
                outs[3 * len(todo)][:, lanes(i)] = r_new
            if not last:
                for i, field in enumerate(done):
                    outs[3 * len(todo) + 1 + i][...] = field

        results = far_fields(
            lists,
            tile_values,
            [near[n] for n in piece],
            fars[p],
            [mixing] + [fields[n] for n in known] + [a for t in todo for a in (base[t], xs[t])],
            [(wide, F32), (wide, F32), (wide, BF16)] * len(todo)
            + [((cells, len(todo) * LANES), BF16)]
            + ([] if last else [(wide, BF16)] * len(piece)),
            work,
            f"far_first_{p}",
        )
        for i, t in enumerate(todo):
            new_x[t], new_y[t], rounded[t] = results[3 * i : 3 * i + 3]
        new_fars.append(far_swap(results[3 * len(todo)]))
        fields.update(zip(piece, results[3 * len(todo) + 1 :]))

    xs, ys, owns = [[of[g] for g in every] for of in (new_x, new_y, rounded)]
    others = [near_swap(r) for r in owns]
    (part,) = far_fields(
        lists, tile_values, [], new_fars[0], [], [(wide, F32)], keep, "far_second_0", NEAR_FLOPS
    )
    near, _ = near_fields(
        lists, tile_values, owns, others, part, [], [], NEAR_FLOPS, "near_second"
    )
    base = second_base(xs, ys, same, channels)
    piece = second_pieces[1]

    def last_work(done, ins, outs):
        held = {n: field.astype(BF16) for n, field in zip(piece, done)}
        held[0] = ins[1][...]
        sums = []
        for t in every:
            value = mixed_of(held, ins[0], t, channels)
            outs[t][...] = value
            sums.append(jnp.sum(ins[2 + t][...].astype(F32) * value, axis=0, keepdims=True))
        row = jnp.concatenate(sums, axis=1)
        lane = lax.broadcasted_iota(jnp.int32, (1, width), 1)
        place = lax.broadcasted_iota(jnp.int32, (1, LANES), 1)
        total = jnp.zeros((1, LANES), F32)
        for r in range(replicas):
            inside = (lane >= r * channels) & (lane < (r + 1) * channels)
            value = jnp.sum(jnp.where(inside, row, 0.0), axis=1, keepdims=True)
            total = jnp.where(place == r, value, total)
        outs[groups][...] = jnp.broadcast_to(total, (ring, LANES))

    *mixed, partial = far_fields(
        lists,
        tile_values,
        near[1:],
        new_fars[1],
        [mixing, near[0]] + owns,
        [(wide, F32)] * groups + [((ring, LANES), F32)],
        last_work,
        "far_second_1",
    )

    everyone = lax.all_to_all(partial, RING, 0, 0, tiled=True)
    energy = jnp.sum(everyone, axis=0)[:replicas] / jnp.sqrt(jnp.float32(cells * ring * channels))
    x_new, y_new = finish(xs, base, mixed)
    return (x_new, y_new, energy)


def solution(mesh):
    cells = P(("groups", "row", "col"), None)
    slots = P(("groups", "row", "col"))
    return jax.shard_map(
        local,
        mesh=mesh,
        in_specs=(cells, cells, P(("groups", "row", "col"), None, None), slots, slots, slots, P()),
        out_specs=(cells, cells, P("groups")),
        check_vma=False,
    )
```

```python
import jax
import jax.numpy as jnp
import ml_dtypes
import numpy as np
from jax import lax
from jax.experimental import pallas as pl
from jax.experimental.pallas import tpu as pltpu
from jax.sharding import PartitionSpec as P

STEPS = 2
LANES = 128
LONG, SHORT = 16, 4
VMEM_LIMIT = 14 * 1024 * 1024
NEAR_FLOPS = 4 * 10**9
F32 = jnp.float32
BF16 = jnp.bfloat16
RING = ("row", "col")


def call(body, ins, outs, scratch, name, flops=0):
    return pl.pallas_call(
        body,
        in_specs=[pl.BlockSpec(memory_space=pl.ANY if s is pltpu.HBM else s) for _, s in ins],
        out_specs=[pl.BlockSpec(memory_space=pl.ANY if s is pltpu.HBM else s) for *_, s in outs],
        out_shape=[
            jax.ShapeDtypeStruct(dims, kind) if s is pltpu.HBM else s(dims, kind)
            for dims, kind, s in outs
        ],
        scratch_shapes=scratch,
        compiler_params=pltpu.CompilerParams(vmem_limit_bytes=VMEM_LIMIT),
        cost_estimate=pl.CostEstimate(
            flops=int(flops) or 1000, bytes_accessed=1000, transcendentals=0
        ),
        name=name,
    )(*[pltpu.with_memory_space_constraint(a, s) for a, s in ins])


def vmem(*arrays):
    return [(a, pltpu.VMEM) for a in arrays]


def lanes(group):
    return slice(group * LANES, (group + 1) * LANES)


def spanned(group, channels, width):
    first = group * LANES // channels * channels
    last = -(-(group + 1) * LANES // channels) * channels
    return list(range(first // LANES, -(-min(last, width) // LANES)))


def span_lanes(near):
    return slice(near[0] * LANES, (near[-1] + 1) * LANES)


def split(x):
    high = x.astype(BF16)
    return high, (x - high.astype(F32)).astype(BF16)


def bases_into(outs, xs, ys, same, step, channels):
    groups = len(xs)
    width = groups * LANES
    detune = 1.0 - (step + 1.0) / (STEPS + 1.0)
    parts = [split(x) for x in xs]
    for g in range(groups):
        near = spanned(g, channels, width)
        ones = same[span_lanes(near), lanes(g)]
        totals = sum(
            jnp.dot(
                jnp.concatenate([parts[n][k] for n in near], axis=1),
                ones,
                preferred_element_type=F32,
            )
            for k in range(2)
        )
        penalty = 0.02 * (totals - (2.0 - channels))
        outs[g][...] = ys[g] + 0.5 * (-detune * xs[g] - 0.4 * penalty)


def mixed_of(fields, mixing, group, channels):
    near = spanned(group, channels, mixing.shape[0])
    return jnp.dot(
        jnp.concatenate([fields[n] for n in near], axis=1),
        mixing[span_lanes(near), lanes(group)],
        preferred_element_type=F32,
    )


def load_first(positions, groups_of):
    cells = positions.shape[0]
    n = len(groups_of)

    def body(x_ref, *refs):
        x_outs, r_outs, sent, sems = refs[:n], refs[n : 2 * n], refs[2 * n], refs[-1]
        copies = [
            pltpu.make_async_copy(x_ref.at[:, lanes(g)], x_outs[i], sems.at[i])
            for i, g in enumerate(groups_of)
        ]
        for copy in copies:
            copy.start()
        for i, copy in enumerate(copies):
            copy.wait()
            rounded = x_outs[i][...].astype(BF16)
            r_outs[i][...] = rounded
            sent[:, lanes(i)] = rounded

    outs = call(
        body,
        [(positions, pltpu.HBM)],
        [((cells, LANES), F32, pltpu.VMEM)] * n
        + [((cells, LANES), BF16, pltpu.VMEM)] * n
        + [((cells, n * LANES), BF16, pltpu.VMEM)],
        [pltpu.SemaphoreType.DMA((n,))],
        "load_first",
    )
    return outs[:n], outs[n : 2 * n], outs[2 * n]


def section(slots, per):
    return -(-(slots + per) // (2 * SHORT)) * SHORT


def make_lists(rows, cols, count, positions, groups_of, after, slots, tile, ring_index):
    cells = positions.shape[0]
    per = cells // tile
    pairs = section(slots, per)
    n = len(groups_of)

    def body(rows_hbm, cols_hbm, count_hbm, x_ref, _, list_ref, *refs):
        x_outs, r_outs = refs[:n], refs[n : 2 * n]
        rows_ref, cols_ref, count_ref, held, sems = refs[2 * n :]
        copies = [
            pltpu.make_async_copy(*ends, sems.at[k])
            for k, ends in enumerate(
                [(rows_hbm, rows_ref), (cols_hbm, cols_ref), (count_hbm, count_ref)]
                + [(x_ref.at[:, lanes(g)], x_outs[i]) for i, g in enumerate(groups_of)]
            )
        ]
        for copy in copies:
            copy.start()
        for k in range(2 * per):
            held[k] = -1
        far_third = jnp.where(lax.rem(ring_index(), 2) == 1, 2, 0)
        for copy in copies[:3]:
            copy.wait()

        def visit(slot, totals):
            near_pairs, far_pairs = totals
            row, col = rows_ref[slot], cols_ref[slot]
            third = jnp.where(col >= 2 * per, 2, jnp.where(col >= per, 1, 0))
            source = col - third * per
            far = third == far_third
            source = jnp.where(far | (third == 1), source, source + per)
            key = row + jnp.where(far, per, 0)
            place = 2 * jnp.where(far, far_pairs + pairs, near_pairs)
            entry = slot * 65536 + source * 256 + row
            other = held[key]
            full = other >= 0
            list_ref[place] = other
            list_ref[place + 1] = entry
            held[key] = jnp.where(full, -1, entry)
            one = full.astype(jnp.int32)
            far_one = jnp.where(far, one, 0)
            return near_pairs + one - far_one, far_pairs + far_one

        totals = lax.fori_loop(0, count_ref[0], visit, (jnp.int32(0), jnp.int32(0)))
        for part, zero in enumerate((2 * per, per)):
            total = totals[part]
            start = part * pairs
            for k in range(per):
                other = held[part * per + k]
                list_ref[2 * (start + total)] = other
                list_ref[2 * (start + total) + 1] = zero * 256 + k
                total = total + (other >= 0).astype(jnp.int32)
            short_turns = (total + SHORT - 1) // SHORT

            def pad(pair, carry, start=start, zero=zero):
                for e in range(2):
                    list_ref[2 * (start + pair) + e] = zero * 256 + per
                return carry

            lax.fori_loop(total, short_turns * SHORT, pad, 0)
            list_ref[4 * pairs + 2 * part] = short_turns // (LONG // SHORT)
            list_ref[4 * pairs + 2 * part + 1] = short_turns % (LONG // SHORT)
        for i, copy in enumerate(copies[3:]):
            copy.wait()
            r_outs[i][...] = x_outs[i][...].astype(BF16)

    outs = call(
        body,
        [(a, pl.ANY) for a in (rows, cols, count)] + [(positions, pltpu.HBM)] + vmem(after),
        [((4 * pairs + 4 + 2,), jnp.int32, pltpu.SMEM)]
        + [((cells, LANES), F32, pltpu.VMEM)] * n
        + [((cells, LANES), BF16, pltpu.VMEM)] * n,
        [
            pltpu.SMEM(rows.shape, jnp.int32),
            pltpu.SMEM(cols.shape, jnp.int32),
            pltpu.SMEM(count.shape, jnp.int32),
            pltpu.SMEM((2 * per,), jnp.int32),
            pltpu.SemaphoreType.DMA((3 + n,)),
        ],
        "make_lists",
    )
    return outs[0], outs[1 : 1 + n], outs[1 + n :]


def add_pairs(part, list_ref, tiles, field, window, pairs):
    def turn(first, length):
        for u in range(length):
            place = 2 * (part * pairs + first + u)
            entries = [list_ref[place + e] for e in range(2)]
            left = jnp.concatenate([tiles[n >> 16] for n in entries], axis=1)
            right = jnp.concatenate([window[(n >> 8) & 255] for n in entries], axis=0)
            field[entries[1] & 255] += jnp.dot(left, right, preferred_element_type=F32)

    def long(i, carry):
        turn(i * LONG, LONG)
        return carry

    def short(i, carry):
        turn(long_turns * LONG + i * SHORT, SHORT)
        return carry

    long_turns = list_ref[4 * pairs + 2 * part]
    lax.fori_loop(0, long_turns, long, 0)
    lax.fori_loop(0, list_ref[4 * pairs + 2 * part + 1], short, 0)


def near_fields(lists, tiles, owns, others, far_part, sent, after, flops, name):
    slots, tile, _ = tiles.shape
    cells = owns[0].shape[0]
    groups = len(owns)
    width = groups * LANES
    per = cells // tile
    pairs = section(slots, per)
    start = [] if far_part is None else [far_part]

    def body(list_ref, tiles_ref, *refs):
        own_refs, other_refs, refs = refs[:groups], refs[groups : 2 * groups], refs[2 * groups :]
        start_refs, refs = refs[: len(start)], refs[len(start) :]
        sent_refs, refs = refs[: len(sent)], refs[len(sent) + len(after) :]
        field_outs, sent_outs, (field, window) = refs[:groups], refs[groups:-2], refs[-2:]
        for out, ref in zip(sent_outs, sent_refs):
            out[...] = ref[...]
        for g in range(groups):
            window[:per, :, lanes(g)] = own_refs[g][...].reshape(per, tile, LANES)
            window[per : 2 * per, :, lanes(g)] = other_refs[g][...].reshape(per, tile, LANES)
        window[2 * per] = jnp.zeros((tile, width), BF16)
        field[:per] = jnp.zeros((per, tile, width), F32)
        for ref in start_refs:
            field[:per, :, lanes(0)] = ref[...].reshape(per, tile, LANES)
        add_pairs(0, list_ref, tiles_ref, field, window, pairs)
        for g, out in enumerate(field_outs):
            out[...] = field[:per, :, lanes(g)].reshape(cells, LANES).astype(out.dtype)

    outs = call(
        body,
        [(lists, pltpu.SMEM)] + vmem(tiles, *owns, *others, *start, *sent, *after),
        [
            ((cells, LANES), BF16 if start and g == 0 else F32, pltpu.VMEM)
            for g in range(groups)
        ]
        + [(a.shape, BF16, pltpu.VMEM) for a in sent],
        [
            pltpu.VMEM((per + 1, tile, width), F32),
            pltpu.VMEM((2 * per + 1, tile, width), BF16),
        ],
        name,
        flops,
    )
    return outs[:groups], outs[groups:]


def far_fields(lists, tiles, nears, far, extra, outs_of, work, name, flops=0):
    slots, tile, _ = tiles.shape
    cells, width = far.shape
    per = cells // tile
    pairs = section(slots, per)
    n = width // LANES
    m = len(nears)

    def body(list_ref, tiles_ref, far_ref, *refs):
        near_refs, extra_refs = refs[:m], refs[m : m + len(extra)]
        out_refs, (field, window) = refs[m + len(extra) : -2], refs[-2:]
        window[:per] = far_ref[...].reshape(per, tile, width)
        window[per] = jnp.zeros((tile, width), BF16)
        if not near_refs:
            field[:per] = jnp.zeros((per, tile, width), F32)
        for i, ref in enumerate(near_refs):
            field[:per, :, lanes(i)] = ref[...].reshape(per, tile, LANES)
        add_pairs(1, list_ref, tiles_ref, field, window, pairs)
        work([field[:per, :, lanes(i)].reshape(cells, LANES) for i in range(n)], extra_refs, out_refs)

    return call(
        body,
        [(lists, pltpu.SMEM)] + vmem(tiles, far, *nears, *extra),
        [(*out, pltpu.VMEM) for out in outs_of],
        [pltpu.VMEM((per + 1, tile, width), F32), pltpu.VMEM((per + 1, tile, width), BF16)],
        name,
        flops,
    )


def first_base(xs, momenta, same, spread, coupling, channels):
    cells, width = momenta.shape
    groups = len(xs)

    def body(*refs):
        x_refs, (y_ref, same_ref, spread_ref, coupling_ref) = refs[:groups], refs[groups : groups + 4]
        outs = refs[groups + 4 :]
        tall = jnp.dot(spread_ref[...], coupling_ref[...], preferred_element_type=F32).astype(BF16)
        wide = lax.dot_general(
            tall, spread_ref[...], (((1,), (1,)), ((), ())), preferred_element_type=F32
        )
        outs[groups][...] = (wide * same_ref[...].astype(F32)).astype(BF16)
        x = [ref[...] for ref in x_refs]
        y = [y_ref[:, lanes(g)] for g in range(groups)]
        bases_into(outs[:groups], x, y, same_ref, 0, channels)

    outs = call(
        body,
        vmem(*xs, momenta, same, spread, coupling),
        [((cells, LANES), F32, pltpu.VMEM)] * groups + [((width, width), BF16, pltpu.VMEM)],
        [],
        "first_base",
    )
    return outs[:groups], outs[groups]


def second_base(xs, ys, same, channels):
    groups = len(xs)

    def body(*refs):
        x = [ref[...] for ref in refs[:groups]]
        y = [ref[...] for ref in refs[groups : 2 * groups]]
        bases_into(refs[2 * groups + 1 :], x, y, refs[2 * groups], 1, channels)

    return call(
        body,
        vmem(*xs, *ys, same),
        [(xs[0].shape, F32, pltpu.VMEM)] * groups,
        [],
        "second_base",
    )


def finish(xs, bases, mixed):
    groups = len(xs)
    cells = xs[0].shape[0]
    width = groups * LANES

    def body(*refs):
        x_refs, base_refs, mixed_refs = [refs[k * groups : (k + 1) * groups] for k in range(3)]
        x_out, y_out, x_buf, y_buf, sems = refs[3 * groups :]
        copies = []
        for g in range(groups):
            y_new = base_refs[g][...] - 0.2 * mixed_refs[g][...]
            y_buf[g] = y_new
            x_buf[g] = jnp.clip(x_refs[g][...] + 0.5 * y_new, -1.0, 1.0)
            for k, (buf, out) in enumerate(((y_buf, y_out), (x_buf, x_out))):
                copies.append(
                    pltpu.make_async_copy(buf.at[g], out.at[:, lanes(g)], sems.at[g, k])
                )
                copies[-1].start()
        for copy in copies:
            copy.wait()

    return call(
        body,
        vmem(*xs, *bases, *mixed),
        [((cells, width), F32, pltpu.HBM)] * 2,
        [
            pltpu.VMEM((groups, cells, LANES), F32),
            pltpu.VMEM((groups, cells, LANES), F32),
            pltpu.SemaphoreType.DMA((groups, 2)),
        ],
        "finish",
    )


def local(positions, momenta, tile_values, tile_rows, tile_cols, tile_count, channel_coupling):
    cells, width = positions.shape
    slots, tile, _ = tile_values.shape
    channels = channel_coupling.shape[0]
    replicas = width // channels
    groups = width // LANES
    ring = lax.axis_size("row") * lax.axis_size("col")
    where = np.arange(width)
    same = jnp.asarray(
        (where[:, None] // channels == where[None] // channels).astype(ml_dtypes.bfloat16)
    )
    spread = jnp.asarray(
        (where[:, None] % channels == np.arange(channels)[None]).astype(ml_dtypes.bfloat16)
    )
    on_chip = [(i, i ^ 1) for i in range(ring)]
    off_chip = [(i, (i + 1) % ring if i % 2 else (i - 1) % ring) for i in range(ring)]
    wide = (cells, LANES)
    every = list(range(groups))
    first_pieces = [every[:-1], every[-1:]]
    second_pieces = [every[:1], every[1:]]

    def ring_index():
        return lax.axis_index("row") * lax.axis_size("col") + lax.axis_index("col")

    def far_swap(mine):
        return lax.ppermute(mine, RING, off_chip)

    def near_swap(mine):
        return lax.ppermute(mine, RING, on_chip)

    def ready(piece, done):
        return [
            t for t in every if t not in done and max(spanned(t, channels, width)) <= piece[-1]
        ]

    def keep(done, _, outs):
        outs[0][...] = done[0]

    def needed(todo, piece):
        return sorted({n for t in todo for n in spanned(t, channels, width)} - set(piece))

    xs, owns, sent = load_first(positions, first_pieces[0])
    fars = [far_swap(sent)]
    lists, more_x, more_own = make_lists(
        tile_rows, tile_cols, tile_count, positions, first_pieces[1], sent, slots, tile, ring_index
    )
    xs, owns = [*xs, *more_x], [*owns, *more_own]
    others = [near_swap(r) for r in owns]
    base, mixing = first_base(xs, momenta, same, spread, channel_coupling, channels)
    near, sent = near_fields(
        lists, tile_values, owns, others, None, more_own, [mixing], 0, "near_first"
    )
    fars.append(far_swap(sent[0]))

    fields, new_x, new_y, rounded, new_fars = {}, {}, {}, {}, []
    for p, piece in enumerate(first_pieces):
        todo = ready(piece, new_x)
        known = needed(todo, piece)
        going = second_pieces[p]
        assert going == todo
        last = p == len(first_pieces) - 1

        def work(done, ins, outs, piece=piece, todo=todo, known=known, last=last):
            held = {n: ins[1 + i][...] for i, n in enumerate(known)}
            done = [field.astype(BF16) for field in done]
            held.update(zip(piece, done))
            rest = ins[1 + len(known) :]
            for i, t in enumerate(todo):
                y_new = rest[2 * i][...] - 0.2 * mixed_of(held, ins[0], t, channels)
                x_new = jnp.clip(rest[2 * i + 1][...] + 0.5 * y_new, -1.0, 1.0)
                r_new = x_new.astype(BF16)
                outs[3 * i][...] = x_new
                outs[3 * i + 1][...] = y_new
                outs[3 * i + 2][...] = r_new
                outs[3 * len(todo)][:, lanes(i)] = r_new
            if not last:
                for i, field in enumerate(done):
                    outs[3 * len(todo) + 1 + i][...] = field

        results = far_fields(
            lists,
            tile_values,
            [near[n] for n in piece],
            fars[p],
            [mixing] + [fields[n] for n in known] + [a for t in todo for a in (base[t], xs[t])],
            [(wide, F32), (wide, F32), (wide, BF16)] * len(todo)
            + [((cells, len(todo) * LANES), BF16)]
            + ([] if last else [(wide, BF16)] * len(piece)),
            work,
            f"far_first_{p}",
        )
        for i, t in enumerate(todo):
            new_x[t], new_y[t], rounded[t] = results[3 * i : 3 * i + 3]
        new_fars.append(far_swap(results[3 * len(todo)]))
        fields.update(zip(piece, results[3 * len(todo) + 1 :]))

    xs, ys, owns = [[of[g] for g in every] for of in (new_x, new_y, rounded)]
    others = [near_swap(r) for r in owns]
    (part,) = far_fields(
        lists, tile_values, [], new_fars[0], [], [(wide, F32)], keep, "far_second_0", NEAR_FLOPS
    )
    near, _ = near_fields(lists, tile_values, owns, others, part, [], [], 0, "near_second")
    base = second_base(xs, ys, same, channels)
    piece = second_pieces[1]

    def last_work(done, ins, outs):
        held = {n: field.astype(BF16) for n, field in zip(piece, done)}
        held[0] = ins[1][...]
        sums = []
        for t in every:
            value = mixed_of(held, ins[0], t, channels)
            outs[t][...] = value
            sums.append(jnp.sum(ins[2 + t][...].astype(F32) * value, axis=0, keepdims=True))
        row = jnp.concatenate(sums, axis=1)
        lane = lax.broadcasted_iota(jnp.int32, (1, width), 1)
        place = lax.broadcasted_iota(jnp.int32, (1, LANES), 1)
        total = jnp.zeros((1, LANES), F32)
        for r in range(replicas):
            inside = (lane >= r * channels) & (lane < (r + 1) * channels)
            value = jnp.sum(jnp.where(inside, row, 0.0), axis=1, keepdims=True)
            total = jnp.where(place == r, value, total)
        outs[groups][...] = jnp.broadcast_to(total, (ring, LANES))

    *mixed, partial = far_fields(
        lists,
        tile_values,
        near[1:],
        new_fars[1],
        [mixing, near[0], *owns, base[0]],
        [(wide, F32)] * groups + [((ring, LANES), F32)],
        last_work,
        "far_second_1",
    )

    everyone = lax.all_to_all(partial, RING, 0, 0, tiled=True)
    energy = jnp.sum(everyone, axis=0)[:replicas] / jnp.sqrt(jnp.float32(cells * ring * channels))
    x_new, y_new = finish(xs, base, mixed)
    return (x_new, y_new, energy)


def solution(mesh):
    cells = P(("groups", "row", "col"), None)
    slots = P(("groups", "row", "col"))
    return jax.shard_map(
        local,
        mesh=mesh,
        in_specs=(cells, cells, P(("groups", "row", "col"), None, None), slots, slots, slots, P()),
        out_specs=(cells, cells, P("groups")),
        check_vma=False,
    )
```

```python
import jax
import jax.numpy as jnp
import ml_dtypes
import numpy as np
from jax import lax
from jax.experimental import pallas as pl
from jax.experimental.pallas import tpu as pltpu
from jax.sharding import PartitionSpec as P

STEPS = 2
LANES = 128
LONG, SHORT = 16, 4
VMEM_LIMIT = 14 * 1024 * 1024
NEAR_FLOPS = 4 * 10**9
F32 = jnp.float32
BF16 = jnp.bfloat16
RING = ("row", "col")


def call(body, ins, outs, scratch, name, flops=0):
    return pl.pallas_call(
        body,
        in_specs=[pl.BlockSpec(memory_space=pl.ANY if s is pltpu.HBM else s) for _, s in ins],
        out_specs=[pl.BlockSpec(memory_space=pl.ANY if s is pltpu.HBM else s) for *_, s in outs],
        out_shape=[
            jax.ShapeDtypeStruct(dims, kind) if s is pltpu.HBM else s(dims, kind)
            for dims, kind, s in outs
        ],
        scratch_shapes=scratch,
        compiler_params=pltpu.CompilerParams(vmem_limit_bytes=VMEM_LIMIT),
        cost_estimate=pl.CostEstimate(
            flops=int(flops) or 1000, bytes_accessed=1000, transcendentals=0
        ),
        name=name,
    )(*[pltpu.with_memory_space_constraint(a, s) for a, s in ins])


def vmem(*arrays):
    return [(a, pltpu.VMEM) for a in arrays]


def lanes(group):
    return slice(group * LANES, (group + 1) * LANES)


def spanned(group, channels, width):
    first = group * LANES // channels * channels
    last = -(-(group + 1) * LANES // channels) * channels
    return list(range(first // LANES, -(-min(last, width) // LANES)))


def span_lanes(near):
    return slice(near[0] * LANES, (near[-1] + 1) * LANES)


def split(x):
    high = x.astype(BF16)
    return high, (x - high.astype(F32)).astype(BF16)


def bases_into(outs, xs, ys, same, step, channels):
    groups = len(xs)
    width = groups * LANES
    detune = 1.0 - (step + 1.0) / (STEPS + 1.0)
    parts = [split(x) for x in xs]
    for g in range(groups):
        near = spanned(g, channels, width)
        ones = same[span_lanes(near), lanes(g)]
        totals = sum(
            jnp.dot(
                jnp.concatenate([parts[n][k] for n in near], axis=1),
                ones,
                preferred_element_type=F32,
            )
            for k in range(2)
        )
        penalty = 0.02 * (totals - (2.0 - channels))
        outs[g][...] = ys[g] + 0.5 * (-detune * xs[g] - 0.4 * penalty)


def mixed_of(fields, mixing, group, channels):
    near = spanned(group, channels, mixing.shape[0])
    return jnp.dot(
        jnp.concatenate([fields[n] for n in near], axis=1),
        mixing[span_lanes(near), lanes(group)],
        preferred_element_type=F32,
    )


def load_first(positions, groups_of):
    cells = positions.shape[0]
    n = len(groups_of)

    def body(x_ref, *refs):
        x_outs, r_outs, sent, sems = refs[:n], refs[n : 2 * n], refs[2 * n], refs[-1]
        copies = [
            pltpu.make_async_copy(x_ref.at[:, lanes(g)], x_outs[i], sems.at[i])
            for i, g in enumerate(groups_of)
        ]
        for copy in copies:
            copy.start()
        for i, copy in enumerate(copies):
            copy.wait()
            rounded = x_outs[i][...].astype(BF16)
            r_outs[i][...] = rounded
            sent[:, lanes(i)] = rounded

    outs = call(
        body,
        [(positions, pltpu.HBM)],
        [((cells, LANES), F32, pltpu.VMEM)] * n
        + [((cells, LANES), BF16, pltpu.VMEM)] * n
        + [((cells, n * LANES), BF16, pltpu.VMEM)],
        [pltpu.SemaphoreType.DMA((n,))],
        "load_first",
    )
    return outs[:n], outs[n : 2 * n], outs[2 * n]


def section(slots, per):
    return -(-(slots + per) // (2 * SHORT)) * SHORT


def make_lists(rows, cols, count, positions, groups_of, after, slots, tile, ring_index):
    cells = positions.shape[0]
    per = cells // tile
    pairs = section(slots, per)
    n = len(groups_of)

    def body(rows_hbm, cols_hbm, count_hbm, x_ref, _, list_ref, *refs):
        x_outs, r_outs = refs[:n], refs[n : 2 * n]
        rows_ref, cols_ref, count_ref, held, sems = refs[2 * n :]
        copies = [
            pltpu.make_async_copy(*ends, sems.at[k])
            for k, ends in enumerate(
                [(rows_hbm, rows_ref), (cols_hbm, cols_ref), (count_hbm, count_ref)]
                + [(x_ref.at[:, lanes(g)], x_outs[i]) for i, g in enumerate(groups_of)]
            )
        ]
        for copy in copies:
            copy.start()
        for k in range(2 * per):
            held[k] = -1
        far_third = jnp.where(lax.rem(ring_index(), 2) == 1, 2, 0)
        for copy in copies[:3]:
            copy.wait()

        def visit(slot, totals):
            near_pairs, far_pairs = totals
            row, col = rows_ref[slot], cols_ref[slot]
            third = jnp.where(col >= 2 * per, 2, jnp.where(col >= per, 1, 0))
            source = col - third * per
            far = third == far_third
            source = jnp.where(far | (third == 1), source, source + per)
            key = row + jnp.where(far, per, 0)
            place = 2 * jnp.where(far, far_pairs + pairs, near_pairs)
            entry = slot * 65536 + source * 256 + row
            other = held[key]
            full = other >= 0
            list_ref[place] = other
            list_ref[place + 1] = entry
            held[key] = jnp.where(full, -1, entry)
            one = full.astype(jnp.int32)
            far_one = jnp.where(far, one, 0)
            return near_pairs + one - far_one, far_pairs + far_one

        totals = lax.fori_loop(0, count_ref[0], visit, (jnp.int32(0), jnp.int32(0)))
        for part, zero in enumerate((2 * per, per)):
            total = totals[part]
            start = part * pairs
            for k in range(per):
                other = held[part * per + k]
                list_ref[2 * (start + total)] = other
                list_ref[2 * (start + total) + 1] = zero * 256 + k
                total = total + (other >= 0).astype(jnp.int32)
            short_turns = (total + SHORT - 1) // SHORT

            def pad(pair, carry, start=start, zero=zero):
                for e in range(2):
                    list_ref[2 * (start + pair) + e] = zero * 256 + per
                return carry

            lax.fori_loop(total, short_turns * SHORT, pad, 0)
            list_ref[4 * pairs + 2 * part] = short_turns // (LONG // SHORT)
            list_ref[4 * pairs + 2 * part + 1] = short_turns % (LONG // SHORT)
        for i, copy in enumerate(copies[3:]):
            copy.wait()
            r_outs[i][...] = x_outs[i][...].astype(BF16)

    outs = call(
        body,
        [(a, pl.ANY) for a in (rows, cols, count)] + [(positions, pltpu.HBM)] + vmem(after),
        [((4 * pairs + 4 + 2,), jnp.int32, pltpu.SMEM)]
        + [((cells, LANES), F32, pltpu.VMEM)] * n
        + [((cells, LANES), BF16, pltpu.VMEM)] * n,
        [
            pltpu.SMEM(rows.shape, jnp.int32),
            pltpu.SMEM(cols.shape, jnp.int32),
            pltpu.SMEM(count.shape, jnp.int32),
            pltpu.SMEM((2 * per,), jnp.int32),
            pltpu.SemaphoreType.DMA((3 + n,)),
        ],
        "make_lists",
    )
    return outs[0], outs[1 : 1 + n], outs[1 + n :]


def add_pairs(part, list_ref, tiles, field, window, pairs):
    def turn(first, length):
        for u in range(length):
            place = 2 * (part * pairs + first + u)
            entries = [list_ref[place + e] for e in range(2)]
            left = jnp.concatenate([tiles[n >> 16] for n in entries], axis=1)
            right = jnp.concatenate([window[(n >> 8) & 255] for n in entries], axis=0)
            field[entries[1] & 255] += jnp.dot(left, right, preferred_element_type=F32)

    def long(i, carry):
        turn(i * LONG, LONG)
        return carry

    def short(i, carry):
        turn(long_turns * LONG + i * SHORT, SHORT)
        return carry

    long_turns = list_ref[4 * pairs + 2 * part]
    lax.fori_loop(0, long_turns, long, 0)
    lax.fori_loop(0, list_ref[4 * pairs + 2 * part + 1], short, 0)


def near_fields(lists, tiles, owns, others, far_part, sent, after, flops, name):
    slots, tile, _ = tiles.shape
    cells = owns[0].shape[0]
    groups = len(owns)
    width = groups * LANES
    per = cells // tile
    pairs = section(slots, per)
    start = [] if far_part is None else [far_part]

    def body(list_ref, tiles_ref, *refs):
        own_refs, other_refs, refs = refs[:groups], refs[groups : 2 * groups], refs[2 * groups :]
        start_refs, refs = refs[: len(start)], refs[len(start) :]
        sent_refs, refs = refs[: len(sent)], refs[len(sent) + len(after) :]
        field_outs, sent_outs, (field, window) = refs[:groups], refs[groups:-2], refs[-2:]
        for out, ref in zip(sent_outs, sent_refs):
            out[...] = ref[...]
        for g in range(groups):
            window[:per, :, lanes(g)] = own_refs[g][...].reshape(per, tile, LANES)
            window[per : 2 * per, :, lanes(g)] = other_refs[g][...].reshape(per, tile, LANES)
        window[2 * per] = jnp.zeros((tile, width), BF16)
        field[:per] = jnp.zeros((per, tile, width), F32)
        for ref in start_refs:
            field[:per, :, lanes(0)] = ref[...].reshape(per, tile, LANES)
        add_pairs(0, list_ref, tiles_ref, field, window, pairs)
        for g, out in enumerate(field_outs):
            out[...] = field[:per, :, lanes(g)].reshape(cells, LANES).astype(out.dtype)

    outs = call(
        body,
        [(lists, pltpu.SMEM)] + vmem(tiles, *owns, *others, *start, *sent, *after),
        [
            ((cells, LANES), BF16 if start and g == 0 else F32, pltpu.VMEM)
            for g in range(groups)
        ]
        + [(a.shape, BF16, pltpu.VMEM) for a in sent],
        [
            pltpu.VMEM((per + 1, tile, width), F32),
            pltpu.VMEM((2 * per + 1, tile, width), BF16),
        ],
        name,
        flops,
    )
    return outs[:groups], outs[groups:]


def far_fields(lists, tiles, nears, far, extra, outs_of, work, name, flops=0):
    slots, tile, _ = tiles.shape
    cells, width = far.shape
    per = cells // tile
    pairs = section(slots, per)
    n = width // LANES
    m = len(nears)

    def body(list_ref, tiles_ref, far_ref, *refs):
        near_refs, extra_refs = refs[:m], refs[m : m + len(extra)]
        out_refs, (field, window) = refs[m + len(extra) : -2], refs[-2:]
        window[:per] = far_ref[...].reshape(per, tile, width)
        window[per] = jnp.zeros((tile, width), BF16)
        if not near_refs:
            field[:per] = jnp.zeros((per, tile, width), F32)
        for i, ref in enumerate(near_refs):
            field[:per, :, lanes(i)] = ref[...].reshape(per, tile, LANES)
        add_pairs(1, list_ref, tiles_ref, field, window, pairs)
        work([field[:per, :, lanes(i)].reshape(cells, LANES) for i in range(n)], extra_refs, out_refs)

    return call(
        body,
        [(lists, pltpu.SMEM)] + vmem(tiles, far, *nears, *extra),
        [(*out, pltpu.VMEM) for out in outs_of],
        [pltpu.VMEM((per + 1, tile, width), F32), pltpu.VMEM((per + 1, tile, width), BF16)],
        name,
        flops,
    )


def first_base(xs, momenta, same, spread, coupling, channels):
    cells, width = momenta.shape
    groups = len(xs)

    def body(*refs):
        x_refs, (y_ref, same_ref, spread_ref, coupling_ref) = refs[:groups], refs[groups : groups + 4]
        outs = refs[groups + 4 :]
        tall = jnp.dot(spread_ref[...], coupling_ref[...], preferred_element_type=F32).astype(BF16)
        wide = lax.dot_general(
            tall, spread_ref[...], (((1,), (1,)), ((), ())), preferred_element_type=F32
        )
        outs[groups][...] = (wide * same_ref[...].astype(F32)).astype(BF16)
        x = [ref[...] for ref in x_refs]
        y = [y_ref[:, lanes(g)] for g in range(groups)]
        bases_into(outs[:groups], x, y, same_ref, 0, channels)

    outs = call(
        body,
        vmem(*xs, momenta, same, spread, coupling),
        [((cells, LANES), F32, pltpu.VMEM)] * groups + [((width, width), BF16, pltpu.VMEM)],
        [],
        "first_base",
    )
    return outs[:groups], outs[groups]


def second_base(xs, ys, same, channels):
    groups = len(xs)

    def body(*refs):
        x = [ref[...] for ref in refs[:groups]]
        y = [ref[...] for ref in refs[groups : 2 * groups]]
        bases_into(refs[2 * groups + 1 :], x, y, refs[2 * groups], 1, channels)

    return call(
        body,
        vmem(*xs, *ys, same),
        [(xs[0].shape, F32, pltpu.VMEM)] * groups,
        [],
        "second_base",
    )


def assemble(xs, ys):
    groups = len(xs)
    cells = xs[0].shape[0]
    width = groups * LANES

    def body(*refs):
        outs, sems = refs[2 * groups : -1], refs[-1]
        copies = [
            pltpu.make_async_copy(
                refs[k * groups + g], outs[k].at[:, lanes(g)], sems.at[k * groups + g]
            )
            for g in range(groups)
            for k in range(2)
        ]
        for copy in copies:
            copy.start()
        for copy in copies:
            copy.wait()

    return call(
        body,
        vmem(*xs, *ys),
        [((cells, width), F32, pltpu.HBM)] * 2,
        [pltpu.SemaphoreType.DMA((2 * groups,))],
        "assemble",
    )


def local(positions, momenta, tile_values, tile_rows, tile_cols, tile_count, channel_coupling):
    cells, width = positions.shape
    slots, tile, _ = tile_values.shape
    channels = channel_coupling.shape[0]
    replicas = width // channels
    groups = width // LANES
    ring = lax.axis_size("row") * lax.axis_size("col")
    where = np.arange(width)
    same = jnp.asarray(
        (where[:, None] // channels == where[None] // channels).astype(ml_dtypes.bfloat16)
    )
    spread = jnp.asarray(
        (where[:, None] % channels == np.arange(channels)[None]).astype(ml_dtypes.bfloat16)
    )
    on_chip = [(i, i ^ 1) for i in range(ring)]
    off_chip = [(i, (i + 1) % ring if i % 2 else (i - 1) % ring) for i in range(ring)]
    wide = (cells, LANES)
    every = list(range(groups))
    first_pieces = [every[:-1], every[-1:]]
    second_pieces = [every[:1], every[1:]]

    def ring_index():
        return lax.axis_index("row") * lax.axis_size("col") + lax.axis_index("col")

    def far_swap(mine):
        return lax.ppermute(mine, RING, off_chip)

    def near_swap(mine):
        return lax.ppermute(mine, RING, on_chip)

    def ready(piece, done):
        return [
            t for t in every if t not in done and max(spanned(t, channels, width)) <= piece[-1]
        ]

    def keep(done, _, outs):
        outs[0][...] = done[0]

    def needed(todo, piece):
        return sorted({n for t in todo for n in spanned(t, channels, width)} - set(piece))

    xs, owns, sent = load_first(positions, first_pieces[0])
    fars = [far_swap(sent)]
    lists, more_x, more_own = make_lists(
        tile_rows, tile_cols, tile_count, positions, first_pieces[1], sent, slots, tile, ring_index
    )
    xs, owns = [*xs, *more_x], [*owns, *more_own]
    others = [near_swap(r) for r in owns]
    base, mixing = first_base(xs, momenta, same, spread, channel_coupling, channels)
    near, sent = near_fields(
        lists, tile_values, owns, others, None, more_own, [mixing], 0, "near_first"
    )
    fars.append(far_swap(sent[0]))

    fields, new_x, new_y, rounded, new_fars = {}, {}, {}, {}, []
    for p, piece in enumerate(first_pieces):
        todo = ready(piece, new_x)
        known = needed(todo, piece)
        going = second_pieces[p]
        assert going == todo
        last = p == len(first_pieces) - 1

        def work(done, ins, outs, piece=piece, todo=todo, known=known, last=last):
            held = {n: ins[1 + i][...] for i, n in enumerate(known)}
            done = [field.astype(BF16) for field in done]
            held.update(zip(piece, done))
            rest = ins[1 + len(known) :]
            for i, t in enumerate(todo):
                y_new = rest[2 * i][...] - 0.2 * mixed_of(held, ins[0], t, channels)
                x_new = jnp.clip(rest[2 * i + 1][...] + 0.5 * y_new, -1.0, 1.0)
                r_new = x_new.astype(BF16)
                outs[3 * i][...] = x_new
                outs[3 * i + 1][...] = y_new
                outs[3 * i + 2][...] = r_new
                outs[3 * len(todo)][:, lanes(i)] = r_new
            if not last:
                for i, field in enumerate(done):
                    outs[3 * len(todo) + 1 + i][...] = field

        results = far_fields(
            lists,
            tile_values,
            [near[n] for n in piece],
            fars[p],
            [mixing] + [fields[n] for n in known] + [a for t in todo for a in (base[t], xs[t])],
            [(wide, F32), (wide, F32), (wide, BF16)] * len(todo)
            + [((cells, len(todo) * LANES), BF16)]
            + ([] if last else [(wide, BF16)] * len(piece)),
            work,
            f"far_first_{p}",
        )
        for i, t in enumerate(todo):
            new_x[t], new_y[t], rounded[t] = results[3 * i : 3 * i + 3]
        new_fars.append(far_swap(results[3 * len(todo)]))
        fields.update(zip(piece, results[3 * len(todo) + 1 :]))

    xs, ys, owns = [[of[g] for g in every] for of in (new_x, new_y, rounded)]
    others = [near_swap(r) for r in owns]
    (part,) = far_fields(
        lists, tile_values, [], new_fars[0], [], [(wide, F32)], keep, "far_second_0", NEAR_FLOPS
    )
    near, _ = near_fields(lists, tile_values, owns, others, part, [], [], 0, "near_second")
    base = second_base(xs, ys, same, channels)
    piece = second_pieces[1]

    def last_work(done, ins, outs):
        held = {n: field.astype(BF16) for n, field in zip(piece, done)}
        held[0] = ins[1][...]
        x_refs, base_refs, rounded_refs = [ins[2 + k * groups : 2 + (k + 1) * groups] for k in range(3)]
        sums = []
        for t in every:
            value = mixed_of(held, ins[0], t, channels)
            y_new = base_refs[t][...] - 0.2 * value
            outs[t][...] = jnp.clip(x_refs[t][...] + 0.5 * y_new, -1.0, 1.0)
            outs[groups + t][...] = y_new
            sums.append(jnp.sum(rounded_refs[t][...].astype(F32) * value, axis=0, keepdims=True))
        row = jnp.broadcast_to(jnp.concatenate(sums, axis=1), (replicas, width))
        lane = lax.broadcasted_iota(jnp.int32, (replicas, width), 1)
        first = lax.broadcasted_iota(jnp.int32, (replicas, width), 0) * channels
        inside = (lane >= first) & (lane < first + channels)
        total = jnp.sum(jnp.where(inside, row, 0.0), axis=1, keepdims=True)
        place = lax.broadcasted_iota(jnp.int32, (replicas, LANES), 1)
        which = lax.broadcasted_iota(jnp.int32, (replicas, LANES), 0)
        flat = jnp.sum(jnp.where(place == which, total, 0.0), axis=0, keepdims=True)
        outs[2 * groups][...] = jnp.broadcast_to(flat, (ring, LANES))

    *results, partial = far_fields(
        lists,
        tile_values,
        near[1:],
        new_fars[1],
        [mixing, near[0], *xs, *base, *owns],
        [(wide, F32)] * (2 * groups) + [((ring, LANES), F32)],
        last_work,
        "far_second_1",
    )

    everyone = lax.all_to_all(partial, RING, 0, 0, tiled=True)
    energy = jnp.sum(everyone, axis=0)[:replicas] / jnp.sqrt(jnp.float32(cells * ring * channels))
    x_new, y_new = assemble(results[:groups], results[groups:])
    return (x_new, y_new, energy)


def solution(mesh):
    cells = P(("groups", "row", "col"), None)
    slots = P(("groups", "row", "col"))
    return jax.shard_map(
        local,
        mesh=mesh,
        in_specs=(cells, cells, P(("groups", "row", "col"), None, None), slots, slots, slots, P()),
        out_specs=(cells, cells, P("groups")),
        check_vma=False,
    )
```

```python
import jax
import jax.numpy as jnp
import ml_dtypes
import numpy as np
from jax import lax
from jax.experimental import pallas as pl
from jax.experimental.pallas import tpu as pltpu
from jax.sharding import PartitionSpec as P

STEPS = 2
LANES = 128
LONG, SHORT = 16, 4
VMEM_LIMIT = 14 * 1024 * 1024
NEAR_FLOPS = 4 * 10**9
F32 = jnp.float32
BF16 = jnp.bfloat16
RING = ("row", "col")


def call(body, ins, outs, scratch, name, flops=0, aliases=()):
    return pl.pallas_call(
        body,
        in_specs=[pl.BlockSpec(memory_space=pl.ANY if s is pltpu.HBM else s) for _, s in ins],
        out_specs=[pl.BlockSpec(memory_space=pl.ANY if s is pltpu.HBM else s) for *_, s in outs],
        out_shape=[
            jax.ShapeDtypeStruct(dims, kind) if s is pltpu.HBM else s(dims, kind)
            for dims, kind, s in outs
        ],
        scratch_shapes=scratch,
        input_output_aliases=dict(aliases),
        compiler_params=pltpu.CompilerParams(vmem_limit_bytes=VMEM_LIMIT),
        cost_estimate=pl.CostEstimate(
            flops=int(flops) or 1000, bytes_accessed=1000, transcendentals=0
        ),
        name=name,
    )(*[pltpu.with_memory_space_constraint(a, s) for a, s in ins])


def vmem(*arrays):
    return [(a, pltpu.VMEM) for a in arrays]


def lanes(group):
    return slice(group * LANES, (group + 1) * LANES)


def spanned(group, channels, width):
    first = group * LANES // channels * channels
    last = -(-(group + 1) * LANES // channels) * channels
    return list(range(first // LANES, -(-min(last, width) // LANES)))


def span_lanes(near):
    return slice(near[0] * LANES, (near[-1] + 1) * LANES)


def split(x):
    high = x.astype(BF16)
    return high, (x - high.astype(F32)).astype(BF16)


def bases_into(outs, xs, ys, same, step, channels):
    groups = len(xs)
    width = groups * LANES
    detune = 1.0 - (step + 1.0) / (STEPS + 1.0)
    parts = [split(x) for x in xs]
    for g in range(groups):
        near = spanned(g, channels, width)
        ones = same[span_lanes(near), lanes(g)]
        totals = sum(
            jnp.dot(
                jnp.concatenate([parts[n][k] for n in near], axis=1),
                ones,
                preferred_element_type=F32,
            )
            for k in range(2)
        )
        penalty = 0.02 * (totals - (2.0 - channels))
        outs[g][...] = ys[g] + 0.5 * (-detune * xs[g] - 0.4 * penalty)


def mixed_of(fields, mixing, group, channels):
    near = spanned(group, channels, mixing.shape[0])
    return jnp.dot(
        jnp.concatenate([fields[n] for n in near], axis=1),
        mixing[span_lanes(near), lanes(group)],
        preferred_element_type=F32,
    )


def load_first(positions, groups_of):
    cells = positions.shape[0]
    n = len(groups_of)

    def body(x_ref, *refs):
        x_outs, r_outs, sent, sems = refs[:n], refs[n : 2 * n], refs[2 * n], refs[-1]
        copies = [
            pltpu.make_async_copy(x_ref.at[:, lanes(g)], x_outs[i], sems.at[i])
            for i, g in enumerate(groups_of)
        ]
        for copy in copies:
            copy.start()
        for i, copy in enumerate(copies):
            copy.wait()
            rounded = x_outs[i][...].astype(BF16)
            r_outs[i][...] = rounded
            sent[:, lanes(i)] = rounded

    outs = call(
        body,
        [(positions, pltpu.HBM)],
        [((cells, LANES), F32, pltpu.VMEM)] * n
        + [((cells, LANES), BF16, pltpu.VMEM)] * n
        + [((cells, n * LANES), BF16, pltpu.VMEM)],
        [pltpu.SemaphoreType.DMA((n,))],
        "load_first",
    )
    return outs[:n], outs[n : 2 * n], outs[2 * n]


def section(slots, per):
    return -(-(slots + per) // (2 * SHORT)) * SHORT


def make_lists(rows, cols, count, positions, groups_of, after, slots, tile, ring_index):
    cells = positions.shape[0]
    per = cells // tile
    pairs = section(slots, per)
    n = len(groups_of)

    def body(rows_hbm, cols_hbm, count_hbm, x_ref, _, list_ref, *refs):
        x_outs, r_outs = refs[:n], refs[n : 2 * n]
        rows_ref, cols_ref, count_ref, held, sems = refs[2 * n :]
        copies = [
            pltpu.make_async_copy(*ends, sems.at[k])
            for k, ends in enumerate(
                [(rows_hbm, rows_ref), (cols_hbm, cols_ref), (count_hbm, count_ref)]
                + [(x_ref.at[:, lanes(g)], x_outs[i]) for i, g in enumerate(groups_of)]
            )
        ]
        for copy in copies:
            copy.start()
        for k in range(2 * per):
            held[k] = -1
        far_third = jnp.where(lax.rem(ring_index(), 2) == 1, 2, 0)
        for copy in copies[:3]:
            copy.wait()

        def visit(slot, totals):
            near_pairs, far_pairs = totals
            row, col = rows_ref[slot], cols_ref[slot]
            third = jnp.where(col >= 2 * per, 2, jnp.where(col >= per, 1, 0))
            source = col - third * per
            far = third == far_third
            source = jnp.where(far | (third == 1), source, source + per)
            key = row + jnp.where(far, per, 0)
            place = 2 * jnp.where(far, far_pairs + pairs, near_pairs)
            entry = slot * 65536 + source * 256 + row
            other = held[key]
            full = other >= 0
            list_ref[place] = other
            list_ref[place + 1] = entry
            held[key] = jnp.where(full, -1, entry)
            one = full.astype(jnp.int32)
            far_one = jnp.where(far, one, 0)
            return near_pairs + one - far_one, far_pairs + far_one

        totals = lax.fori_loop(0, count_ref[0], visit, (jnp.int32(0), jnp.int32(0)))
        for part, zero in enumerate((2 * per, per)):
            total = totals[part]
            start = part * pairs
            for k in range(per):
                other = held[part * per + k]
                list_ref[2 * (start + total)] = other
                list_ref[2 * (start + total) + 1] = zero * 256 + k
                total = total + (other >= 0).astype(jnp.int32)
            short_turns = (total + SHORT - 1) // SHORT

            def pad(pair, carry, start=start, zero=zero):
                for e in range(2):
                    list_ref[2 * (start + pair) + e] = zero * 256 + per
                return carry

            lax.fori_loop(total, short_turns * SHORT, pad, 0)
            list_ref[4 * pairs + 2 * part] = short_turns // (LONG // SHORT)
            list_ref[4 * pairs + 2 * part + 1] = short_turns % (LONG // SHORT)
        for i, copy in enumerate(copies[3:]):
            copy.wait()
            r_outs[i][...] = x_outs[i][...].astype(BF16)

    outs = call(
        body,
        [(a, pl.ANY) for a in (rows, cols, count)] + [(positions, pltpu.HBM)] + vmem(after),
        [((4 * pairs + 4 + 2,), jnp.int32, pltpu.SMEM)]
        + [((cells, LANES), F32, pltpu.VMEM)] * n
        + [((cells, LANES), BF16, pltpu.VMEM)] * n,
        [
            pltpu.SMEM(rows.shape, jnp.int32),
            pltpu.SMEM(cols.shape, jnp.int32),
            pltpu.SMEM(count.shape, jnp.int32),
            pltpu.SMEM((2 * per,), jnp.int32),
            pltpu.SemaphoreType.DMA((3 + n,)),
        ],
        "make_lists",
    )
    return outs[0], outs[1 : 1 + n], outs[1 + n :]


def add_pairs(part, list_ref, tiles, field, window, pairs):
    def turn(first, length):
        for u in range(length):
            place = 2 * (part * pairs + first + u)
            entries = [list_ref[place + e] for e in range(2)]
            left = jnp.concatenate([tiles[n >> 16] for n in entries], axis=1)
            right = jnp.concatenate([window[(n >> 8) & 255] for n in entries], axis=0)
            field[entries[1] & 255] += jnp.dot(left, right, preferred_element_type=F32)

    def long(i, carry):
        turn(i * LONG, LONG)
        return carry

    def short(i, carry):
        turn(long_turns * LONG + i * SHORT, SHORT)
        return carry

    long_turns = list_ref[4 * pairs + 2 * part]
    lax.fori_loop(0, long_turns, long, 0)
    lax.fori_loop(0, list_ref[4 * pairs + 2 * part + 1], short, 0)


def near_fields(lists, tiles, owns, others, far_part, sent, after, flops, name):
    slots, tile, _ = tiles.shape
    cells = owns[0].shape[0]
    groups = len(owns)
    width = groups * LANES
    per = cells // tile
    pairs = section(slots, per)
    start = [] if far_part is None else [far_part]

    def body(list_ref, tiles_ref, *refs):
        own_refs, other_refs, refs = refs[:groups], refs[groups : 2 * groups], refs[2 * groups :]
        start_refs, refs = refs[: len(start)], refs[len(start) :]
        sent_refs, refs = refs[: len(sent)], refs[len(sent) + len(after) :]
        field_outs, sent_outs, (field, window) = refs[:groups], refs[groups:-2], refs[-2:]
        for out, ref in zip(sent_outs, sent_refs):
            out[...] = ref[...]
        for g in range(groups):
            window[:per, :, lanes(g)] = own_refs[g][...].reshape(per, tile, LANES)
            window[per : 2 * per, :, lanes(g)] = other_refs[g][...].reshape(per, tile, LANES)
        window[2 * per] = jnp.zeros((tile, width), BF16)
        field[:per] = jnp.zeros((per, tile, width), F32)
        for ref in start_refs:
            field[:per, :, lanes(0)] = ref[...].reshape(per, tile, LANES)
        add_pairs(0, list_ref, tiles_ref, field, window, pairs)
        for g, out in enumerate(field_outs):
            out[...] = field[:per, :, lanes(g)].reshape(cells, LANES).astype(out.dtype)

    outs = call(
        body,
        [(lists, pltpu.SMEM)] + vmem(tiles, *owns, *others, *start, *sent, *after),
        [
            ((cells, LANES), BF16 if start and g == 0 else F32, pltpu.VMEM)
            for g in range(groups)
        ]
        + [(a.shape, BF16, pltpu.VMEM) for a in sent],
        [
            pltpu.VMEM((per + 1, tile, width), F32),
            pltpu.VMEM((2 * per + 1, tile, width), BF16),
        ],
        name,
        flops,
    )
    return outs[:groups], outs[groups:]


def far_fields(lists, tiles, nears, far, extra, outs_of, work, name, flops=0, through=()):
    slots, tile, _ = tiles.shape
    cells, width = far.shape
    per = cells // tile
    pairs = section(slots, per)
    n = width // LANES
    m = len(nears)

    def body(list_ref, tiles_ref, far_ref, *refs):
        near_refs, extra_refs = refs[:m], refs[m : m + len(extra)]
        through_refs = refs[m + len(extra) : m + len(extra) + len(through)]
        out_refs, (field, window) = refs[m + len(extra) + len(through) : -2], refs[-2:]
        window[:per] = far_ref[...].reshape(per, tile, width)
        window[per] = jnp.zeros((tile, width), BF16)
        if not near_refs:
            field[:per] = jnp.zeros((per, tile, width), F32)
        for i, ref in enumerate(near_refs):
            field[:per, :, lanes(i)] = ref[...].reshape(per, tile, LANES)
        add_pairs(1, list_ref, tiles_ref, field, window, pairs)
        done = [field[:per, :, lanes(i)].reshape(cells, LANES) for i in range(n)]
        work(done, [*extra_refs, *through_refs], out_refs[: len(outs_of)])

    return call(
        body,
        [(lists, pltpu.SMEM)] + vmem(tiles, far, *nears, *extra, *through),
        [(*out, pltpu.VMEM) for out in outs_of] + [(a.shape, a.dtype, pltpu.VMEM) for a in through],
        [pltpu.VMEM((per + 1, tile, width), F32), pltpu.VMEM((per + 1, tile, width), BF16)],
        name,
        flops,
        [(3 + m + len(extra) + i, len(outs_of) + i) for i in range(len(through))],
    )


def first_base(xs, momenta, same, spread, coupling, channels):
    cells, width = momenta.shape
    groups = len(xs)

    def body(*refs):
        x_refs, (y_ref, same_ref, spread_ref, coupling_ref) = refs[:groups], refs[groups : groups + 4]
        outs = refs[groups + 4 :]
        tall = jnp.dot(spread_ref[...], coupling_ref[...], preferred_element_type=F32).astype(BF16)
        wide = lax.dot_general(
            tall, spread_ref[...], (((1,), (1,)), ((), ())), preferred_element_type=F32
        )
        outs[groups][...] = (wide * same_ref[...].astype(F32)).astype(BF16)
        x = [ref[...] for ref in x_refs]
        y = [y_ref[:, lanes(g)] for g in range(groups)]
        bases_into(outs[:groups], x, y, same_ref, 0, channels)

    outs = call(
        body,
        vmem(*xs, momenta, same, spread, coupling),
        [((cells, LANES), F32, pltpu.VMEM)] * groups + [((width, width), BF16, pltpu.VMEM)],
        [],
        "first_base",
    )
    return outs[:groups], outs[groups]


def second_base(xs, ys, rounded, same, mixing, channels):
    groups = len(xs)
    cells = xs[0].shape[0]
    width = groups * LANES

    def body(*refs):
        x, y, r = [[ref[...] for ref in refs[k * groups : (k + 1) * groups]] for k in range(3)]
        same_ref, mixing_ref = refs[3 * groups : 3 * groups + 2]
        outs = refs[3 * groups + 2 :]
        bases_into(outs[:groups], x, y, same_ref, 1, channels)
        for g in range(groups):
            near = spanned(g, channels, width)
            outs[groups + g][...] = lax.dot_general(
                jnp.concatenate([r[n] for n in near], axis=1),
                mixing_ref[lanes(g), span_lanes(near)],
                (((1,), (1,)), ((), ())),
                preferred_element_type=F32,
            )

    outs = call(
        body,
        vmem(*xs, *ys, *rounded, same, mixing),
        [((cells, LANES), F32, pltpu.VMEM)] * (2 * groups),
        [],
        "second_base",
    )
    return outs[:groups], outs[groups:]


def finish(fields, xs, bases, mixing, channels):
    groups = len(xs)
    cells = xs[0].shape[0]
    width = groups * LANES

    def body(*refs):
        field_refs, x_refs, base_refs = [refs[k * groups : (k + 1) * groups] for k in range(3)]
        mixing_ref, x_out, y_out, x_buf, y_buf, sems = refs[3 * groups :]
        held = [ref[...] for ref in field_refs]
        copies = []
        for g in range(groups):
            y_new = base_refs[g][...] - 0.2 * mixed_of(held, mixing_ref, g, channels)
            y_buf[g] = y_new
            x_buf[g] = jnp.clip(x_refs[g][...] + 0.5 * y_new, -1.0, 1.0)
            for k, (buf, out) in enumerate(((y_buf, y_out), (x_buf, x_out))):
                copies.append(
                    pltpu.make_async_copy(buf.at[g], out.at[:, lanes(g)], sems.at[g, k])
                )
                copies[-1].start()
        for copy in copies:
            copy.wait()

    return call(
        body,
        vmem(*fields, *xs, *bases, mixing),
        [((cells, width), F32, pltpu.HBM)] * 2,
        [
            pltpu.VMEM((groups, cells, LANES), F32),
            pltpu.VMEM((groups, cells, LANES), F32),
            pltpu.SemaphoreType.DMA((groups, 2)),
        ],
        "finish",
    )


def local(positions, momenta, tile_values, tile_rows, tile_cols, tile_count, channel_coupling):
    cells, width = positions.shape
    slots, tile, _ = tile_values.shape
    channels = channel_coupling.shape[0]
    replicas = width // channels
    groups = width // LANES
    ring = lax.axis_size("row") * lax.axis_size("col")
    where = np.arange(width)
    same = jnp.asarray(
        (where[:, None] // channels == where[None] // channels).astype(ml_dtypes.bfloat16)
    )
    spread = jnp.asarray(
        (where[:, None] % channels == np.arange(channels)[None]).astype(ml_dtypes.bfloat16)
    )
    on_chip = [(i, i ^ 1) for i in range(ring)]
    off_chip = [(i, (i + 1) % ring if i % 2 else (i - 1) % ring) for i in range(ring)]
    wide = (cells, LANES)
    every = list(range(groups))
    first_pieces = [every[:-1], every[-1:]]
    second_pieces = [every[:1], every[1:]]

    def ring_index():
        return lax.axis_index("row") * lax.axis_size("col") + lax.axis_index("col")

    def far_swap(mine):
        return lax.ppermute(mine, RING, off_chip)

    def near_swap(mine):
        return lax.ppermute(mine, RING, on_chip)

    def ready(piece, done):
        return [
            t for t in every if t not in done and max(spanned(t, channels, width)) <= piece[-1]
        ]

    def keep(done, _, outs):
        outs[0][...] = done[0]

    def needed(todo, piece):
        return sorted({n for t in todo for n in spanned(t, channels, width)} - set(piece))

    xs, owns, sent = load_first(positions, first_pieces[0])
    fars = [far_swap(sent)]
    lists, more_x, more_own = make_lists(
        tile_rows, tile_cols, tile_count, positions, first_pieces[1], sent, slots, tile, ring_index
    )
    xs, owns = [*xs, *more_x], [*owns, *more_own]
    others = [near_swap(r) for r in owns]
    base, mixing = first_base(xs, momenta, same, spread, channel_coupling, channels)
    near, sent = near_fields(
        lists, tile_values, owns, others, None, more_own, [mixing], 0, "near_first"
    )
    fars.append(far_swap(sent[0]))

    fields, new_x, new_y, rounded, new_fars = {}, {}, {}, {}, []
    for p, piece in enumerate(first_pieces):
        todo = ready(piece, new_x)
        known = needed(todo, piece)
        going = second_pieces[p]
        assert going == todo
        last = p == len(first_pieces) - 1

        def work(done, ins, outs, piece=piece, todo=todo, known=known, last=last):
            held = {n: ins[1 + i][...] for i, n in enumerate(known)}
            done = [field.astype(BF16) for field in done]
            held.update(zip(piece, done))
            rest = ins[1 + len(known) :]
            for i, t in enumerate(todo):
                y_new = rest[2 * i][...] - 0.2 * mixed_of(held, ins[0], t, channels)
                x_new = jnp.clip(rest[2 * i + 1][...] + 0.5 * y_new, -1.0, 1.0)
                r_new = x_new.astype(BF16)
                outs[3 * i][...] = x_new
                outs[3 * i + 1][...] = y_new
                outs[3 * i + 2][...] = r_new
                outs[3 * len(todo)][:, lanes(i)] = r_new
            if not last:
                for i, field in enumerate(done):
                    outs[3 * len(todo) + 1 + i][...] = field

        results = far_fields(
            lists,
            tile_values,
            [near[n] for n in piece],
            fars[p],
            [mixing] + [fields[n] for n in known] + [a for t in todo for a in (base[t], xs[t])],
            [(wide, F32), (wide, F32), (wide, BF16)] * len(todo)
            + [((cells, len(todo) * LANES), BF16)]
            + ([] if last else [(wide, BF16)] * len(piece)),
            work,
            f"far_first_{p}",
        )
        for i, t in enumerate(todo):
            new_x[t], new_y[t], rounded[t] = results[3 * i : 3 * i + 3]
        new_fars.append(far_swap(results[3 * len(todo)]))
        fields.update(zip(piece, results[3 * len(todo) + 1 :]))

    xs, ys, owns = [[of[g] for g in every] for of in (new_x, new_y, rounded)]
    others = [near_swap(r) for r in owns]
    (part,) = far_fields(
        lists, tile_values, [], new_fars[0], [], [(wide, F32)], keep, "far_second_0", NEAR_FLOPS
    )
    near, _ = near_fields(lists, tile_values, owns, others, part, [], [], 0, "near_second")
    base, weights = second_base(xs, ys, owns, same, mixing, channels)
    piece = second_pieces[1]

    def last_work(done, ins, outs):
        held = [ins[groups][...]] + [field.astype(BF16) for field in done]
        for out, field in zip(outs, held[1:]):
            out[...] = field
        row = jnp.concatenate(
            [
                jnp.sum(field.astype(F32) * ref[...], axis=0, keepdims=True)
                for field, ref in zip(held, ins[:groups])
            ],
            axis=1,
        )
        row = jnp.broadcast_to(row, (replicas, width))
        lane = lax.broadcasted_iota(jnp.int32, (replicas, width), 1)
        first = lax.broadcasted_iota(jnp.int32, (replicas, width), 0) * channels
        inside = (lane >= first) & (lane < first + channels)
        total = jnp.sum(jnp.where(inside, row, 0.0), axis=1, keepdims=True)
        place = lax.broadcasted_iota(jnp.int32, (replicas, LANES), 1)
        which = lax.broadcasted_iota(jnp.int32, (replicas, LANES), 0)
        flat = jnp.sum(jnp.where(place == which, total, 0.0), axis=0, keepdims=True)
        outs[len(piece)][...] = jnp.broadcast_to(flat, (ring, LANES))

    results = far_fields(
        lists,
        tile_values,
        near[1:],
        new_fars[1],
        weights,
        [(wide, BF16)] * len(piece) + [((ring, LANES), F32)],
        last_work,
        "far_second_1",
        through=[near[0], *xs, *base, mixing],
    )
    fields, partial, kept = results[: len(piece)], results[len(piece)], results[len(piece) + 1 :]
    fields, kept = [kept[0], *fields], kept[1:]

    everyone = lax.all_to_all(partial, RING, 0, 0, tiled=True)
    energy = jnp.sum(everyone, axis=0)[:replicas] / jnp.sqrt(jnp.float32(cells * ring * channels))
    x_new, y_new = finish(
        fields, kept[:groups], kept[groups : 2 * groups], kept[2 * groups], channels
    )
    return (x_new, y_new, energy)


def solution(mesh):
    cells = P(("groups", "row", "col"), None)
    slots = P(("groups", "row", "col"))
    return jax.shard_map(
        local,
        mesh=mesh,
        in_specs=(cells, cells, P(("groups", "row", "col"), None, None), slots, slots, slots, P()),
        out_specs=(cells, cells, P("groups")),
        check_vma=False,
    )
```

```python
import jax
import jax.numpy as jnp
import ml_dtypes
import numpy as np
from jax import lax
from jax.experimental import pallas as pl
from jax.experimental.pallas import tpu as pltpu
from jax.sharding import PartitionSpec as P

STEPS = 2
LANES = 128
LONG, SHORT = 16, 4
VMEM_LIMIT = 14 * 1024 * 1024
NEAR_FLOPS = 4 * 10**9
F32 = jnp.float32
BF16 = jnp.bfloat16
RING = ("row", "col")


def call(body, ins, outs, scratch, name, flops=0, aliases=()):
    return pl.pallas_call(
        body,
        in_specs=[pl.BlockSpec(memory_space=pl.ANY if s is pltpu.HBM else s) for _, s in ins],
        out_specs=[pl.BlockSpec(memory_space=pl.ANY if s is pltpu.HBM else s) for *_, s in outs],
        out_shape=[
            jax.ShapeDtypeStruct(dims, kind) if s is pltpu.HBM else s(dims, kind)
            for dims, kind, s in outs
        ],
        scratch_shapes=scratch,
        input_output_aliases=dict(aliases),
        compiler_params=pltpu.CompilerParams(vmem_limit_bytes=VMEM_LIMIT),
        cost_estimate=pl.CostEstimate(
            flops=int(flops) or 1000, bytes_accessed=1000, transcendentals=0
        ),
        name=name,
    )(*[pltpu.with_memory_space_constraint(a, s) for a, s in ins])


def vmem(*arrays):
    return [(a, pltpu.VMEM) for a in arrays]


def lanes(group):
    return slice(group * LANES, (group + 1) * LANES)


def spanned(group, channels, width):
    first = group * LANES // channels * channels
    last = -(-(group + 1) * LANES // channels) * channels
    return list(range(first // LANES, -(-min(last, width) // LANES)))


def span_lanes(near):
    return slice(near[0] * LANES, (near[-1] + 1) * LANES)


def split(x):
    high = x.astype(BF16)
    return high, (x - high.astype(F32)).astype(BF16)


def bases_into(outs, xs, ys, same, step, channels):
    groups = len(xs)
    width = groups * LANES
    detune = 1.0 - (step + 1.0) / (STEPS + 1.0)
    parts = [split(x) for x in xs]
    for g in range(groups):
        near = spanned(g, channels, width)
        ones = same[span_lanes(near), lanes(g)]
        totals = sum(
            jnp.dot(
                jnp.concatenate([parts[n][k] for n in near], axis=1),
                ones,
                preferred_element_type=F32,
            )
            for k in range(2)
        )
        penalty = 0.02 * (totals - (2.0 - channels))
        outs[g][...] = ys[g] + 0.5 * (-detune * xs[g] - 0.4 * penalty)


def mixed_of(fields, mixing, group, channels):
    near = spanned(group, channels, mixing.shape[0])
    return jnp.dot(
        jnp.concatenate([fields[n] for n in near], axis=1),
        mixing[span_lanes(near), lanes(group)],
        preferred_element_type=F32,
    )


def load_first(positions, groups_of):
    cells = positions.shape[0]
    n = len(groups_of)

    def body(x_ref, *refs):
        x_outs, r_outs, sent, sems = refs[:n], refs[n : 2 * n], refs[2 * n], refs[-1]
        copies = [
            pltpu.make_async_copy(x_ref.at[:, lanes(g)], x_outs[i], sems.at[i])
            for i, g in enumerate(groups_of)
        ]
        for copy in copies:
            copy.start()
        for i, copy in enumerate(copies):
            copy.wait()
            rounded = x_outs[i][...].astype(BF16)
            r_outs[i][...] = rounded
            sent[:, lanes(i)] = rounded

    outs = call(
        body,
        [(positions, pltpu.HBM)],
        [((cells, LANES), F32, pltpu.VMEM)] * n
        + [((cells, LANES), BF16, pltpu.VMEM)] * n
        + [((cells, n * LANES), BF16, pltpu.VMEM)],
        [pltpu.SemaphoreType.DMA((n,))],
        "load_first",
    )
    return outs[:n], outs[n : 2 * n], outs[2 * n]


def section(slots, per):
    return -(-(slots + per) // (2 * SHORT)) * SHORT


def make_lists(rows, cols, count, positions, groups_of, after, slots, tile, ring_index):
    cells = positions.shape[0]
    per = cells // tile
    pairs = section(slots, per)
    n = len(groups_of)

    def body(rows_hbm, cols_hbm, count_hbm, x_ref, _, list_ref, *refs):
        x_outs, r_outs = refs[:n], refs[n : 2 * n]
        rows_ref, cols_ref, count_ref, held, sems = refs[2 * n :]
        copies = [
            pltpu.make_async_copy(*ends, sems.at[k])
            for k, ends in enumerate(
                [(rows_hbm, rows_ref), (cols_hbm, cols_ref), (count_hbm, count_ref)]
                + [(x_ref.at[:, lanes(g)], x_outs[i]) for i, g in enumerate(groups_of)]
            )
        ]
        for copy in copies:
            copy.start()
        for k in range(2 * per):
            held[k] = -1
        far_third = jnp.where(lax.rem(ring_index(), 2) == 1, 2, 0)
        for copy in copies[:3]:
            copy.wait()

        def visit(slot, totals):
            near_pairs, far_pairs = totals
            row, col = rows_ref[slot], cols_ref[slot]
            third = jnp.where(col >= 2 * per, 2, jnp.where(col >= per, 1, 0))
            source = col - third * per
            far = third == far_third
            source = jnp.where(far | (third == 1), source, source + per)
            key = row + jnp.where(far, per, 0)
            place = 2 * jnp.where(far, far_pairs + pairs, near_pairs)
            entry = slot * 65536 + source * 256 + row
            other = held[key]
            full = other >= 0
            list_ref[place] = other
            list_ref[place + 1] = entry
            held[key] = jnp.where(full, -1, entry)
            one = full.astype(jnp.int32)
            far_one = jnp.where(far, one, 0)
            return near_pairs + one - far_one, far_pairs + far_one

        totals = lax.fori_loop(0, count_ref[0], visit, (jnp.int32(0), jnp.int32(0)))
        for part, zero in enumerate((2 * per, per)):
            total = totals[part]
            start = part * pairs
            for k in range(per):
                other = held[part * per + k]
                list_ref[2 * (start + total)] = other
                list_ref[2 * (start + total) + 1] = zero * 256 + k
                total = total + (other >= 0).astype(jnp.int32)
            short_turns = (total + SHORT - 1) // SHORT

            def pad(pair, carry, start=start, zero=zero):
                for e in range(2):
                    list_ref[2 * (start + pair) + e] = zero * 256 + per
                return carry

            lax.fori_loop(total, short_turns * SHORT, pad, 0)
            list_ref[4 * pairs + 2 * part] = short_turns // (LONG // SHORT)
            list_ref[4 * pairs + 2 * part + 1] = short_turns % (LONG // SHORT)
        for i, copy in enumerate(copies[3:]):
            copy.wait()
            r_outs[i][...] = x_outs[i][...].astype(BF16)

    outs = call(
        body,
        [(a, pl.ANY) for a in (rows, cols, count)] + [(positions, pltpu.HBM)] + vmem(after),
        [((4 * pairs + 4 + 2,), jnp.int32, pltpu.SMEM)]
        + [((cells, LANES), F32, pltpu.VMEM)] * n
        + [((cells, LANES), BF16, pltpu.VMEM)] * n,
        [
            pltpu.SMEM(rows.shape, jnp.int32),
            pltpu.SMEM(cols.shape, jnp.int32),
            pltpu.SMEM(count.shape, jnp.int32),
            pltpu.SMEM((2 * per,), jnp.int32),
            pltpu.SemaphoreType.DMA((3 + n,)),
        ],
        "make_lists",
    )
    return outs[0], outs[1 : 1 + n], outs[1 + n :]


def add_pairs(part, list_ref, tiles, field, window, pairs):
    def turn(first, length):
        for u in range(length):
            place = 2 * (part * pairs + first + u)
            entries = [list_ref[place + e] for e in range(2)]
            left = jnp.concatenate([tiles[n >> 16] for n in entries], axis=1)
            right = jnp.concatenate([window[(n >> 8) & 255] for n in entries], axis=0)
            field[entries[1] & 255] += jnp.dot(left, right, preferred_element_type=F32)

    def long(i, carry):
        turn(i * LONG, LONG)
        return carry

    def short(i, carry):
        turn(long_turns * LONG + i * SHORT, SHORT)
        return carry

    long_turns = list_ref[4 * pairs + 2 * part]
    lax.fori_loop(0, long_turns, long, 0)
    lax.fori_loop(0, list_ref[4 * pairs + 2 * part + 1], short, 0)


def near_fields(lists, tiles, owns, others, far_part, sent, after, flops, name):
    slots, tile, _ = tiles.shape
    cells = owns[0].shape[0]
    groups = len(owns)
    width = groups * LANES
    per = cells // tile
    pairs = section(slots, per)
    start = [] if far_part is None else [far_part]

    def body(list_ref, tiles_ref, *refs):
        own_refs, other_refs, refs = refs[:groups], refs[groups : 2 * groups], refs[2 * groups :]
        start_refs, refs = refs[: len(start)], refs[len(start) :]
        sent_refs, refs = refs[: len(sent)], refs[len(sent) + len(after) :]
        field_outs, sent_outs, (field, window) = refs[:groups], refs[groups:-2], refs[-2:]
        for out, ref in zip(sent_outs, sent_refs):
            out[...] = ref[...]
        for g in range(groups):
            window[:per, :, lanes(g)] = own_refs[g][...].reshape(per, tile, LANES)
            window[per : 2 * per, :, lanes(g)] = other_refs[g][...].reshape(per, tile, LANES)
        window[2 * per] = jnp.zeros((tile, width), BF16)
        field[:per] = jnp.zeros((per, tile, width), F32)
        for ref in start_refs:
            field[:per, :, lanes(0)] = ref[...].reshape(per, tile, LANES)
        add_pairs(0, list_ref, tiles_ref, field, window, pairs)
        for g, out in enumerate(field_outs):
            out[...] = field[:per, :, lanes(g)].reshape(cells, LANES).astype(out.dtype)

    outs = call(
        body,
        [(lists, pltpu.SMEM)] + vmem(tiles, *owns, *others, *start, *sent, *after),
        [
            ((cells, LANES), BF16 if start and g == 0 else F32, pltpu.VMEM)
            for g in range(groups)
        ]
        + [(a.shape, BF16, pltpu.VMEM) for a in sent],
        [
            pltpu.VMEM((per + 1, tile, width), F32),
            pltpu.VMEM((2 * per + 1, tile, width), BF16),
        ],
        name,
        flops,
    )
    return outs[:groups], outs[groups:]


def far_fields(lists, tiles, nears, far, extra, outs_of, work, name, flops=0, through=()):
    slots, tile, _ = tiles.shape
    cells, width = far.shape
    per = cells // tile
    pairs = section(slots, per)
    n = width // LANES
    m = len(nears)

    def body(list_ref, tiles_ref, far_ref, *refs):
        near_refs, extra_refs = refs[:m], refs[m : m + len(extra)]
        through_refs = refs[m + len(extra) : m + len(extra) + len(through)]
        out_refs, (field, window) = refs[m + len(extra) + len(through) : -2], refs[-2:]
        window[:per] = far_ref[...].reshape(per, tile, width)
        window[per] = jnp.zeros((tile, width), BF16)
        if not near_refs:
            field[:per] = jnp.zeros((per, tile, width), F32)
        for i, ref in enumerate(near_refs):
            field[:per, :, lanes(i)] = ref[...].reshape(per, tile, LANES)
        add_pairs(1, list_ref, tiles_ref, field, window, pairs)
        done = [field[:per, :, lanes(i)].reshape(cells, LANES) for i in range(n)]
        work(done, [*extra_refs, *through_refs], out_refs[: len(outs_of)])

    return call(
        body,
        [(lists, pltpu.SMEM)] + vmem(tiles, far, *nears, *extra, *through),
        [(*out, pltpu.VMEM) for out in outs_of] + [(a.shape, a.dtype, pltpu.VMEM) for a in through],
        [pltpu.VMEM((per + 1, tile, width), F32), pltpu.VMEM((per + 1, tile, width), BF16)],
        name,
        flops,
        [(3 + m + len(extra) + i, len(outs_of) + i) for i in range(len(through))],
    )


def first_base(xs, momenta, same, spread, coupling, channels):
    cells, width = momenta.shape
    groups = len(xs)

    def body(*refs):
        x_refs, (y_ref, same_ref, spread_ref, coupling_ref) = refs[:groups], refs[groups : groups + 4]
        outs = refs[groups + 4 :]
        tall = jnp.dot(spread_ref[...], coupling_ref[...], preferred_element_type=F32).astype(BF16)
        wide = lax.dot_general(
            tall, spread_ref[...], (((1,), (1,)), ((), ())), preferred_element_type=F32
        )
        outs[groups][...] = (wide * same_ref[...].astype(F32)).astype(BF16)
        x = [ref[...] for ref in x_refs]
        y = [y_ref[:, lanes(g)] for g in range(groups)]
        bases_into(outs[:groups], x, y, same_ref, 0, channels)

    outs = call(
        body,
        vmem(*xs, momenta, same, spread, coupling),
        [((cells, LANES), F32, pltpu.VMEM)] * groups + [((width, width), BF16, pltpu.VMEM)],
        [],
        "first_base",
    )
    return outs[:groups], outs[groups]


def second_base(xs, ys, rounded, same, mixing, channels):
    groups = len(xs)
    cells = xs[0].shape[0]
    width = groups * LANES

    def body(*refs):
        x, y, r = [[ref[...] for ref in refs[k * groups : (k + 1) * groups]] for k in range(3)]
        same_ref, mixing_ref = refs[3 * groups : 3 * groups + 2]
        outs = refs[3 * groups + 2 :]
        bases_into(outs[:groups], x, y, same_ref, 1, channels)
        for g in range(groups):
            near = spanned(g, channels, width)
            outs[groups + g][...] = lax.dot_general(
                jnp.concatenate([r[n] for n in near], axis=1),
                mixing_ref[lanes(g), span_lanes(near)],
                (((1,), (1,)), ((), ())),
                preferred_element_type=F32,
            )

    outs = call(
        body,
        vmem(*xs, *ys, *rounded, same, mixing),
        [((cells, LANES), F32, pltpu.VMEM)] * (2 * groups),
        [],
        "second_base",
    )
    return outs[:groups], outs[groups:]


def finish(fields, xs, bases, mixing, channels):
    groups = len(xs)
    cells = xs[0].shape[0]
    width = groups * LANES

    def body(*refs):
        field_refs, x_refs, base_refs = [refs[k * groups : (k + 1) * groups] for k in range(3)]
        mixing_ref, x_out, y_out, x_buf, y_buf, sems = refs[3 * groups :]
        held = [ref[...] for ref in field_refs]
        copies = []
        for g in range(groups):
            y_new = base_refs[g][...] - 0.2 * mixed_of(held, mixing_ref, g, channels)
            y_buf[g] = y_new
            x_buf[g] = jnp.clip(x_refs[g][...] + 0.5 * y_new, -1.0, 1.0)
            for k, (buf, out) in enumerate(((y_buf, y_out), (x_buf, x_out))):
                copies.append(
                    pltpu.make_async_copy(buf.at[g], out.at[:, lanes(g)], sems.at[g, k])
                )
                copies[-1].start()
        for copy in copies:
            copy.wait()

    return call(
        body,
        vmem(*fields, *xs, *bases, mixing),
        [((cells, width), F32, pltpu.HBM)] * 2,
        [
            pltpu.VMEM((groups, cells, LANES), F32),
            pltpu.VMEM((groups, cells, LANES), F32),
            pltpu.SemaphoreType.DMA((groups, 2)),
        ],
        "finish",
    )


def sum_over_ring(value, ring):
    if ring & (ring - 1):
        return lax.psum(value, RING)
    size = 1
    while size < ring:
        digits = (1, 2, 3) if 4 * size <= ring else (1,)
        value = value + sum(
            lax.ppermute(value, RING, [(i, i ^ (size * d)) for i in range(ring)]) for d in digits
        )
        size *= len(digits) + 1
    return value


def local(positions, momenta, tile_values, tile_rows, tile_cols, tile_count, channel_coupling):
    cells, width = positions.shape
    slots, tile, _ = tile_values.shape
    channels = channel_coupling.shape[0]
    replicas = width // channels
    groups = width // LANES
    ring = lax.axis_size("row") * lax.axis_size("col")
    where = np.arange(width)
    same = jnp.asarray(
        (where[:, None] // channels == where[None] // channels).astype(ml_dtypes.bfloat16)
    )
    spread = jnp.asarray(
        (where[:, None] % channels == np.arange(channels)[None]).astype(ml_dtypes.bfloat16)
    )
    on_chip = [(i, i ^ 1) for i in range(ring)]
    off_chip = [(i, (i + 1) % ring if i % 2 else (i - 1) % ring) for i in range(ring)]
    wide = (cells, LANES)
    every = list(range(groups))
    first_pieces = [every[:-1], every[-1:]]
    second_pieces = [every[:1], every[1:]]

    def ring_index():
        return lax.axis_index("row") * lax.axis_size("col") + lax.axis_index("col")

    def far_swap(mine):
        return lax.ppermute(mine, RING, off_chip)

    def near_swap(mine):
        return lax.ppermute(mine, RING, on_chip)

    def ready(piece, done):
        return [
            t for t in every if t not in done and max(spanned(t, channels, width)) <= piece[-1]
        ]

    def keep(done, _, outs):
        outs[0][...] = done[0]

    def needed(todo, piece):
        return sorted({n for t in todo for n in spanned(t, channels, width)} - set(piece))

    xs, owns, sent = load_first(positions, first_pieces[0])
    fars = [far_swap(sent)]
    lists, more_x, more_own = make_lists(
        tile_rows, tile_cols, tile_count, positions, first_pieces[1], sent, slots, tile, ring_index
    )
    xs, owns = [*xs, *more_x], [*owns, *more_own]
    others = [near_swap(r) for r in owns]
    base, mixing = first_base(xs, momenta, same, spread, channel_coupling, channels)
    near, sent = near_fields(
        lists, tile_values, owns, others, None, more_own, [mixing], 0, "near_first"
    )
    fars.append(far_swap(sent[0]))

    fields, new_x, new_y, rounded, new_fars = {}, {}, {}, {}, []
    for p, piece in enumerate(first_pieces):
        todo = ready(piece, new_x)
        known = needed(todo, piece)
        going = second_pieces[p]
        assert going == todo
        last = p == len(first_pieces) - 1

        def work(done, ins, outs, piece=piece, todo=todo, known=known, last=last):
            held = {n: ins[1 + i][...] for i, n in enumerate(known)}
            done = [field.astype(BF16) for field in done]
            held.update(zip(piece, done))
            rest = ins[1 + len(known) :]
            for i, t in enumerate(todo):
                y_new = rest[2 * i][...] - 0.2 * mixed_of(held, ins[0], t, channels)
                x_new = jnp.clip(rest[2 * i + 1][...] + 0.5 * y_new, -1.0, 1.0)
                r_new = x_new.astype(BF16)
                outs[3 * i][...] = x_new
                outs[3 * i + 1][...] = y_new
                outs[3 * i + 2][...] = r_new
                outs[3 * len(todo)][:, lanes(i)] = r_new
            if not last:
                for i, field in enumerate(done):
                    outs[3 * len(todo) + 1 + i][...] = field

        results = far_fields(
            lists,
            tile_values,
            [near[n] for n in piece],
            fars[p],
            [mixing] + [fields[n] for n in known] + [a for t in todo for a in (base[t], xs[t])],
            [(wide, F32), (wide, F32), (wide, BF16)] * len(todo)
            + [((cells, len(todo) * LANES), BF16)]
            + ([] if last else [(wide, BF16)] * len(piece)),
            work,
            f"far_first_{p}",
        )
        for i, t in enumerate(todo):
            new_x[t], new_y[t], rounded[t] = results[3 * i : 3 * i + 3]
        new_fars.append(far_swap(results[3 * len(todo)]))
        fields.update(zip(piece, results[3 * len(todo) + 1 :]))

    xs, ys, owns = [[of[g] for g in every] for of in (new_x, new_y, rounded)]
    others = [near_swap(r) for r in owns]
    (part,) = far_fields(
        lists, tile_values, [], new_fars[0], [], [(wide, F32)], keep, "far_second_0", NEAR_FLOPS
    )
    near, _ = near_fields(lists, tile_values, owns, others, part, [], [], 0, "near_second")
    base, weights = second_base(xs, ys, owns, same, mixing, channels)
    piece = second_pieces[1]

    def last_work(done, ins, outs):
        held = [ins[groups][...]] + [field.astype(BF16) for field in done]
        for out, field in zip(outs, held[1:]):
            out[...] = field
        row = jnp.concatenate(
            [
                jnp.sum(field.astype(F32) * ref[...], axis=0, keepdims=True)
                for field, ref in zip(held, ins[:groups])
            ],
            axis=1,
        )
        row = jnp.broadcast_to(row, (replicas, width))
        lane = lax.broadcasted_iota(jnp.int32, (replicas, width), 1)
        first = lax.broadcasted_iota(jnp.int32, (replicas, width), 0) * channels
        inside = (lane >= first) & (lane < first + channels)
        total = jnp.sum(jnp.where(inside, row, 0.0), axis=1, keepdims=True)
        place = lax.broadcasted_iota(jnp.int32, (replicas, LANES), 1)
        which = lax.broadcasted_iota(jnp.int32, (replicas, LANES), 0)
        flat = jnp.sum(jnp.where(place == which, total, 0.0), axis=0, keepdims=True)
        outs[len(piece)][...] = jnp.broadcast_to(flat, (8, LANES))

    results = far_fields(
        lists,
        tile_values,
        near[1:],
        new_fars[1],
        weights,
        [(wide, BF16)] * len(piece) + [((8, LANES), F32)],
        last_work,
        "far_second_1",
        through=[near[0], *xs, *base, mixing],
    )
    fields, partial, kept = results[: len(piece)], results[len(piece)], results[len(piece) + 1 :]
    fields, kept = [kept[0], *fields], kept[1:]

    total = sum_over_ring(partial, ring)
    energy = total[0, :replicas] / jnp.sqrt(jnp.float32(cells * ring * channels))
    x_new, y_new = finish(
        fields, kept[:groups], kept[groups : 2 * groups], kept[2 * groups], channels
    )
    return (x_new, y_new, energy)


def solution(mesh):
    cells = P(("groups", "row", "col"), None)
    slots = P(("groups", "row", "col"))
    return jax.shard_map(
        local,
        mesh=mesh,
        in_specs=(cells, cells, P(("groups", "row", "col"), None, None), slots, slots, slots, P()),
        out_specs=(cells, cells, P("groups")),
        check_vma=False,
    )
```

```python
import jax
import jax.numpy as jnp
import ml_dtypes
import numpy as np
from jax import lax
from jax.experimental import pallas as pl
from jax.experimental.pallas import tpu as pltpu
from jax.sharding import PartitionSpec as P

STEPS = 2
LANES = 128
LONG, SHORT = 16, 4
VMEM_LIMIT = 14 * 1024 * 1024
NEAR_FLOPS = 4 * 10**9
F32 = jnp.float32
BF16 = jnp.bfloat16
RING = ("row", "col")


def call(body, ins, outs, scratch, name, flops=0, aliases=()):
    return pl.pallas_call(
        body,
        in_specs=[pl.BlockSpec(memory_space=pl.ANY if s is pltpu.HBM else s) for _, s in ins],
        out_specs=[pl.BlockSpec(memory_space=pl.ANY if s is pltpu.HBM else s) for *_, s in outs],
        out_shape=[
            jax.ShapeDtypeStruct(dims, kind) if s is pltpu.HBM else s(dims, kind)
            for dims, kind, s in outs
        ],
        scratch_shapes=scratch,
        input_output_aliases=dict(aliases),
        compiler_params=pltpu.CompilerParams(vmem_limit_bytes=VMEM_LIMIT),
        cost_estimate=pl.CostEstimate(
            flops=int(flops) or 1000, bytes_accessed=1000, transcendentals=0
        ),
        name=name,
    )(*[pltpu.with_memory_space_constraint(a, s) for a, s in ins])


def vmem(*arrays):
    return [(a, pltpu.VMEM) for a in arrays]


def lanes(group):
    return slice(group * LANES, (group + 1) * LANES)


def spanned(group, channels, width):
    first = group * LANES // channels * channels
    last = -(-(group + 1) * LANES // channels) * channels
    return list(range(first // LANES, -(-min(last, width) // LANES)))


def span_lanes(near):
    return slice(near[0] * LANES, (near[-1] + 1) * LANES)


def split(x):
    high = x.astype(BF16)
    return high, (x - high.astype(F32)).astype(BF16)


def bases_into(outs, xs, ys, same, step, channels):
    groups = len(xs)
    width = groups * LANES
    detune = 1.0 - (step + 1.0) / (STEPS + 1.0)
    parts = [split(x) for x in xs]
    for g in range(groups):
        near = spanned(g, channels, width)
        ones = same[span_lanes(near), lanes(g)]
        totals = sum(
            jnp.dot(
                jnp.concatenate([parts[n][k] for n in near], axis=1),
                ones,
                preferred_element_type=F32,
            )
            for k in range(2)
        )
        penalty = 0.02 * (totals - (2.0 - channels))
        outs[g][...] = ys[g] + 0.5 * (-detune * xs[g] - 0.4 * penalty)


def mixed_of(fields, mixing, group, channels):
    near = spanned(group, channels, mixing.shape[0])
    return jnp.dot(
        jnp.concatenate([fields[n] for n in near], axis=1),
        mixing[span_lanes(near), lanes(group)],
        preferred_element_type=F32,
    )


def load_first(positions, groups_of):
    cells = positions.shape[0]
    n = len(groups_of)

    def body(x_ref, *refs):
        x_outs, r_outs, sent, sems = refs[:n], refs[n : 2 * n], refs[2 * n], refs[-1]
        copies = [
            pltpu.make_async_copy(x_ref.at[:, lanes(g)], x_outs[i], sems.at[i])
            for i, g in enumerate(groups_of)
        ]
        for copy in copies:
            copy.start()
        for i, copy in enumerate(copies):
            copy.wait()
            rounded = x_outs[i][...].astype(BF16)
            r_outs[i][...] = rounded
            sent[:, lanes(i)] = rounded

    outs = call(
        body,
        [(positions, pltpu.HBM)],
        [((cells, LANES), F32, pltpu.VMEM)] * n
        + [((cells, LANES), BF16, pltpu.VMEM)] * n
        + [((cells, n * LANES), BF16, pltpu.VMEM)],
        [pltpu.SemaphoreType.DMA((n,))],
        "load_first",
    )
    return outs[:n], outs[n : 2 * n], outs[2 * n]


def section(slots, per):
    return -(-(slots + per) // (2 * SHORT)) * SHORT


def make_lists(rows, cols, count, positions, groups_of, after, slots, tile, ring_index):
    cells = positions.shape[0]
    per = cells // tile
    pairs = section(slots, per)
    n = len(groups_of)

    def body(rows_hbm, cols_hbm, count_hbm, x_ref, _, list_ref, *refs):
        x_outs, r_outs = refs[:n], refs[n : 2 * n]
        rows_ref, cols_ref, count_ref, held, sems = refs[2 * n :]
        copies = [
            pltpu.make_async_copy(*ends, sems.at[k])
            for k, ends in enumerate(
                [(rows_hbm, rows_ref), (cols_hbm, cols_ref), (count_hbm, count_ref)]
                + [(x_ref.at[:, lanes(g)], x_outs[i]) for i, g in enumerate(groups_of)]
            )
        ]
        for copy in copies:
            copy.start()
        for k in range(2 * per):
            held[k] = -1
        far_third = jnp.where(lax.rem(ring_index(), 2) == 1, 2, 0)
        for copy in copies[:3]:
            copy.wait()

        def visit(slot, totals):
            near_pairs, far_pairs = totals
            row, col = rows_ref[slot], cols_ref[slot]
            third = jnp.where(col >= 2 * per, 2, jnp.where(col >= per, 1, 0))
            source = col - third * per
            far = third == far_third
            source = jnp.where(far | (third == 1), source, source + per)
            key = row + jnp.where(far, per, 0)
            place = 2 * jnp.where(far, far_pairs + pairs, near_pairs)
            entry = slot * 65536 + source * 256 + row
            other = held[key]
            full = other >= 0
            list_ref[place] = other
            list_ref[place + 1] = entry
            held[key] = jnp.where(full, -1, entry)
            one = full.astype(jnp.int32)
            far_one = jnp.where(far, one, 0)
            return near_pairs + one - far_one, far_pairs + far_one

        totals = lax.fori_loop(0, count_ref[0], visit, (jnp.int32(0), jnp.int32(0)))
        for part, zero in enumerate((2 * per, per)):
            total = totals[part]
            start = part * pairs
            for k in range(per):
                other = held[part * per + k]
                list_ref[2 * (start + total)] = other
                list_ref[2 * (start + total) + 1] = zero * 256 + k
                total = total + (other >= 0).astype(jnp.int32)
            short_turns = (total + SHORT - 1) // SHORT

            def pad(pair, carry, start=start, zero=zero):
                for e in range(2):
                    list_ref[2 * (start + pair) + e] = zero * 256 + per
                return carry

            lax.fori_loop(total, short_turns * SHORT, pad, 0)
            list_ref[4 * pairs + 2 * part] = short_turns // (LONG // SHORT)
            list_ref[4 * pairs + 2 * part + 1] = short_turns % (LONG // SHORT)
        for i, copy in enumerate(copies[3:]):
            copy.wait()
            r_outs[i][...] = x_outs[i][...].astype(BF16)

    outs = call(
        body,
        [(a, pl.ANY) for a in (rows, cols, count)] + [(positions, pltpu.HBM)] + vmem(after),
        [((4 * pairs + 4 + 2,), jnp.int32, pltpu.SMEM)]
        + [((cells, LANES), F32, pltpu.VMEM)] * n
        + [((cells, LANES), BF16, pltpu.VMEM)] * n,
        [
            pltpu.SMEM(rows.shape, jnp.int32),
            pltpu.SMEM(cols.shape, jnp.int32),
            pltpu.SMEM(count.shape, jnp.int32),
            pltpu.SMEM((2 * per,), jnp.int32),
            pltpu.SemaphoreType.DMA((3 + n,)),
        ],
        "make_lists",
    )
    return outs[0], outs[1 : 1 + n], outs[1 + n :]


def add_pairs(part, list_ref, tiles, field, window, pairs):
    def turn(first, length):
        for u in range(length):
            place = 2 * (part * pairs + first + u)
            entries = [list_ref[place + e] for e in range(2)]
            left = jnp.concatenate([tiles[n >> 16] for n in entries], axis=1)
            right = jnp.concatenate([window[(n >> 8) & 255] for n in entries], axis=0)
            field[entries[1] & 255] += jnp.dot(left, right, preferred_element_type=F32)

    def long(i, carry):
        turn(i * LONG, LONG)
        return carry

    def short(i, carry):
        turn(long_turns * LONG + i * SHORT, SHORT)
        return carry

    long_turns = list_ref[4 * pairs + 2 * part]
    lax.fori_loop(0, long_turns, long, 0)
    lax.fori_loop(0, list_ref[4 * pairs + 2 * part + 1], short, 0)


def near_fields(lists, tiles, owns, others, far_part, sent, after, flops, name):
    slots, tile, _ = tiles.shape
    cells = owns[0].shape[0]
    groups = len(owns)
    width = groups * LANES
    per = cells // tile
    pairs = section(slots, per)
    start = [] if far_part is None else [far_part]

    def body(list_ref, tiles_ref, *refs):
        own_refs, other_refs, refs = refs[:groups], refs[groups : 2 * groups], refs[2 * groups :]
        start_refs, refs = refs[: len(start)], refs[len(start) :]
        sent_refs, refs = refs[: len(sent)], refs[len(sent) + len(after) :]
        field_outs, sent_outs, (field, window) = refs[:groups], refs[groups:-2], refs[-2:]
        for out, ref in zip(sent_outs, sent_refs):
            out[...] = ref[...]
        for g in range(groups):
            window[:per, :, lanes(g)] = own_refs[g][...].reshape(per, tile, LANES)
            window[per : 2 * per, :, lanes(g)] = other_refs[g][...].reshape(per, tile, LANES)
        window[2 * per] = jnp.zeros((tile, width), BF16)
        field[:per] = jnp.zeros((per, tile, width), F32)
        for ref in start_refs:
            field[:per, :, lanes(0)] = ref[...].reshape(per, tile, LANES)
        add_pairs(0, list_ref, tiles_ref, field, window, pairs)
        for g, out in enumerate(field_outs):
            out[...] = field[:per, :, lanes(g)].reshape(cells, LANES).astype(out.dtype)

    outs = call(
        body,
        [(lists, pltpu.SMEM)] + vmem(tiles, *owns, *others, *start, *sent, *after),
        [
            ((cells, LANES), BF16 if start and g == 0 else F32, pltpu.VMEM)
            for g in range(groups)
        ]
        + [(a.shape, BF16, pltpu.VMEM) for a in sent],
        [
            pltpu.VMEM((per + 1, tile, width), F32),
            pltpu.VMEM((2 * per + 1, tile, width), BF16),
        ],
        name,
        flops,
    )
    return outs[:groups], outs[groups:]


def far_fields(lists, tiles, nears, far, extra, outs_of, work, name, flops=0, through=()):
    slots, tile, _ = tiles.shape
    cells, width = far.shape
    per = cells // tile
    pairs = section(slots, per)
    n = width // LANES
    m = len(nears)

    def body(list_ref, tiles_ref, far_ref, *refs):
        near_refs, extra_refs = refs[:m], refs[m : m + len(extra)]
        through_refs = refs[m + len(extra) : m + len(extra) + len(through)]
        out_refs, (field, window) = refs[m + len(extra) + len(through) : -2], refs[-2:]
        window[:per] = far_ref[...].reshape(per, tile, width)
        window[per] = jnp.zeros((tile, width), BF16)
        if not near_refs:
            field[:per] = jnp.zeros((per, tile, width), F32)
        for i, ref in enumerate(near_refs):
            field[:per, :, lanes(i)] = ref[...].reshape(per, tile, LANES)
        add_pairs(1, list_ref, tiles_ref, field, window, pairs)
        done = [field[:per, :, lanes(i)].reshape(cells, LANES) for i in range(n)]
        work(done, [*extra_refs, *through_refs], out_refs[: len(outs_of)])

    return call(
        body,
        [(lists, pltpu.SMEM)] + vmem(tiles, far, *nears, *extra, *through),
        [(*out, pltpu.VMEM) for out in outs_of] + [(a.shape, a.dtype, pltpu.VMEM) for a in through],
        [pltpu.VMEM((per + 1, tile, width), F32), pltpu.VMEM((per + 1, tile, width), BF16)],
        name,
        flops,
        [(3 + m + len(extra) + i, len(outs_of) + i) for i in range(len(through))],
    )


def first_base(xs, momenta, same, spread, coupling, channels):
    cells, width = momenta.shape
    groups = len(xs)

    def body(*refs):
        x_refs, (y_ref, same_ref, spread_ref, coupling_ref) = refs[:groups], refs[groups : groups + 4]
        outs = refs[groups + 4 :]
        tall = jnp.dot(spread_ref[...], coupling_ref[...], preferred_element_type=F32).astype(BF16)
        wide = lax.dot_general(
            tall, spread_ref[...], (((1,), (1,)), ((), ())), preferred_element_type=F32
        )
        outs[groups][...] = (wide * same_ref[...].astype(F32)).astype(BF16)
        x = [ref[...] for ref in x_refs]
        y = [y_ref[:, lanes(g)] for g in range(groups)]
        bases_into(outs[:groups], x, y, same_ref, 0, channels)

    outs = call(
        body,
        vmem(*xs, momenta, same, spread, coupling),
        [((cells, LANES), F32, pltpu.VMEM)] * groups + [((width, width), BF16, pltpu.VMEM)],
        [],
        "first_base",
    )
    return outs[:groups], outs[groups]


def second_base(xs, ys, rounded, same, mixing, channels):
    groups = len(xs)
    cells = xs[0].shape[0]
    width = groups * LANES

    def body(*refs):
        x, y, r = [[ref[...] for ref in refs[k * groups : (k + 1) * groups]] for k in range(3)]
        same_ref, mixing_ref = refs[3 * groups : 3 * groups + 2]
        outs = refs[3 * groups + 2 :]
        bases_into(outs[:groups], x, y, same_ref, 1, channels)
        for g in range(groups):
            near = spanned(g, channels, width)
            outs[groups + g][...] = lax.dot_general(
                jnp.concatenate([r[n] for n in near], axis=1),
                mixing_ref[lanes(g), span_lanes(near)],
                (((1,), (1,)), ((), ())),
                preferred_element_type=F32,
            )

    outs = call(
        body,
        vmem(*xs, *ys, *rounded, same, mixing),
        [((cells, LANES), F32, pltpu.VMEM)] * (2 * groups),
        [],
        "second_base",
    )
    return outs[:groups], outs[groups:]


def finish(todo, fields, xs, bases, mixing, channels, outputs, name):
    width = mixing.shape[0]
    cells = xs[0].shape[0]
    near = sorted({n for t in todo for n in spanned(t, channels, width)})
    m, n = len(near), len(todo)

    def body(*refs):
        field_refs, x_refs, base_refs = refs[:m], refs[m : m + n], refs[m + n : m + 2 * n]
        mixing_ref = refs[m + 2 * n]
        x_out, y_out, token, x_buf, y_buf, sems = refs[-6:]
        held = {g: ref[...] for g, ref in zip(near, field_refs)}
        copies = []
        for i, t in enumerate(todo):
            y_new = base_refs[i][...] - 0.2 * mixed_of(held, mixing_ref, t, channels)
            y_buf[i] = y_new
            x_buf[i] = jnp.clip(x_refs[i][...] + 0.5 * y_new, -1.0, 1.0)
            for k, (buf, out) in enumerate(((y_buf, y_out), (x_buf, x_out))):
                copies.append(
                    pltpu.make_async_copy(buf.at[i], out.at[:, lanes(t)], sems.at[i, k])
                )
                copies[-1].start()
        token[...] = jnp.zeros_like(token)
        for copy in copies:
            copy.wait()

    ins = vmem(*[fields[g] for g in near], *[xs[t] for t in todo], *[bases[t] for t in todo], mixing)
    first = len(ins)
    return call(
        body,
        ins + [(a, pltpu.HBM) for a in outputs],
        [((cells, width), F32, pltpu.HBM)] * 2 + [((8, LANES), F32, pltpu.VMEM)],
        [
            pltpu.VMEM((n, cells, LANES), F32),
            pltpu.VMEM((n, cells, LANES), F32),
            pltpu.SemaphoreType.DMA((n, 2)),
        ],
        name,
        0,
        [(first + i, i) for i in range(len(outputs))],
    )


def add_up(arrays, token):
    def body(*refs):
        refs[-1][...] = sum(ref[...] for ref in refs[:-2])

    return call(
        body,
        vmem(*arrays, token),
        [(arrays[0].shape, F32, pltpu.VMEM)],
        [],
        "add_up",
    )[0]


def sum_over_ring(value, ring, token):
    if ring & (ring - 1):
        return lax.psum(value, RING)
    size = 1
    while size < ring:
        digits = (1, 2, 3) if 4 * size <= ring else (1,)
        parts = [value] + [
            lax.ppermute(value, RING, [(i, i ^ (size * d)) for i in range(ring)]) for d in digits
        ]
        value = add_up(parts, token) if size == 1 else sum(parts)
        size *= len(digits) + 1
    return value


def local(positions, momenta, tile_values, tile_rows, tile_cols, tile_count, channel_coupling):
    cells, width = positions.shape
    slots, tile, _ = tile_values.shape
    channels = channel_coupling.shape[0]
    replicas = width // channels
    groups = width // LANES
    ring = lax.axis_size("row") * lax.axis_size("col")
    where = np.arange(width)
    same = jnp.asarray(
        (where[:, None] // channels == where[None] // channels).astype(ml_dtypes.bfloat16)
    )
    spread = jnp.asarray(
        (where[:, None] % channels == np.arange(channels)[None]).astype(ml_dtypes.bfloat16)
    )
    on_chip = [(i, i ^ 1) for i in range(ring)]
    off_chip = [(i, (i + 1) % ring if i % 2 else (i - 1) % ring) for i in range(ring)]
    wide = (cells, LANES)
    every = list(range(groups))
    first_pieces = [every[:-1], every[-1:]]
    second_pieces = [every[:1], every[1:]]

    def ring_index():
        return lax.axis_index("row") * lax.axis_size("col") + lax.axis_index("col")

    def far_swap(mine):
        return lax.ppermute(mine, RING, off_chip)

    def near_swap(mine):
        return lax.ppermute(mine, RING, on_chip)

    def ready(piece, done):
        return [
            t for t in every if t not in done and max(spanned(t, channels, width)) <= piece[-1]
        ]

    def keep(done, _, outs):
        outs[0][...] = done[0]

    def needed(todo, piece):
        return sorted({n for t in todo for n in spanned(t, channels, width)} - set(piece))

    xs, owns, sent = load_first(positions, first_pieces[0])
    fars = [far_swap(sent)]
    lists, more_x, more_own = make_lists(
        tile_rows, tile_cols, tile_count, positions, first_pieces[1], sent, slots, tile, ring_index
    )
    xs, owns = [*xs, *more_x], [*owns, *more_own]
    others = [near_swap(r) for r in owns]
    base, mixing = first_base(xs, momenta, same, spread, channel_coupling, channels)
    near, sent = near_fields(
        lists, tile_values, owns, others, None, more_own, [mixing], 0, "near_first"
    )
    fars.append(far_swap(sent[0]))

    fields, new_x, new_y, rounded, new_fars = {}, {}, {}, {}, []
    for p, piece in enumerate(first_pieces):
        todo = ready(piece, new_x)
        known = needed(todo, piece)
        going = second_pieces[p]
        assert going == todo
        last = p == len(first_pieces) - 1

        def work(done, ins, outs, piece=piece, todo=todo, known=known, last=last):
            held = {n: ins[1 + i][...] for i, n in enumerate(known)}
            done = [field.astype(BF16) for field in done]
            held.update(zip(piece, done))
            rest = ins[1 + len(known) :]
            for i, t in enumerate(todo):
                y_new = rest[2 * i][...] - 0.2 * mixed_of(held, ins[0], t, channels)
                x_new = jnp.clip(rest[2 * i + 1][...] + 0.5 * y_new, -1.0, 1.0)
                r_new = x_new.astype(BF16)
                outs[3 * i][...] = x_new
                outs[3 * i + 1][...] = y_new
                outs[3 * i + 2][...] = r_new
                outs[3 * len(todo)][:, lanes(i)] = r_new
            if not last:
                for i, field in enumerate(done):
                    outs[3 * len(todo) + 1 + i][...] = field

        results = far_fields(
            lists,
            tile_values,
            [near[n] for n in piece],
            fars[p],
            [mixing] + [fields[n] for n in known] + [a for t in todo for a in (base[t], xs[t])],
            [(wide, F32), (wide, F32), (wide, BF16)] * len(todo)
            + [((cells, len(todo) * LANES), BF16)]
            + ([] if last else [(wide, BF16)] * len(piece)),
            work,
            f"far_first_{p}",
        )
        for i, t in enumerate(todo):
            new_x[t], new_y[t], rounded[t] = results[3 * i : 3 * i + 3]
        new_fars.append(far_swap(results[3 * len(todo)]))
        fields.update(zip(piece, results[3 * len(todo) + 1 :]))

    xs, ys, owns = [[of[g] for g in every] for of in (new_x, new_y, rounded)]
    others = [near_swap(r) for r in owns]
    (part,) = far_fields(
        lists, tile_values, [], new_fars[0], [], [(wide, F32)], keep, "far_second_0", NEAR_FLOPS
    )
    near, _ = near_fields(lists, tile_values, owns, others, part, [], [], 0, "near_second")
    base, weights = second_base(xs, ys, owns, same, mixing, channels)
    piece = second_pieces[1]

    def last_work(done, ins, outs):
        held = [ins[groups][...]] + [field.astype(BF16) for field in done]
        for out, field in zip(outs, held[1:]):
            out[...] = field
        row = jnp.concatenate(
            [
                jnp.sum(field.astype(F32) * ref[...], axis=0, keepdims=True)
                for field, ref in zip(held, ins[:groups])
            ],
            axis=1,
        )
        row = jnp.broadcast_to(row, (replicas, width))
        lane = lax.broadcasted_iota(jnp.int32, (replicas, width), 1)
        first = lax.broadcasted_iota(jnp.int32, (replicas, width), 0) * channels
        inside = (lane >= first) & (lane < first + channels)
        total = jnp.sum(jnp.where(inside, row, 0.0), axis=1, keepdims=True)
        place = lax.broadcasted_iota(jnp.int32, (replicas, LANES), 1)
        which = lax.broadcasted_iota(jnp.int32, (replicas, LANES), 0)
        flat = jnp.sum(jnp.where(place == which, total, 0.0), axis=0, keepdims=True)
        outs[len(piece)][...] = jnp.broadcast_to(flat, (8, LANES))

    results = far_fields(
        lists,
        tile_values,
        near[1:],
        new_fars[1],
        weights,
        [(wide, BF16)] * len(piece) + [((8, LANES), F32)],
        last_work,
        "far_second_1",
        through=[near[0], *xs, *base, mixing],
    )
    fields, partial, kept = results[: len(piece)], results[len(piece)], results[len(piece) + 1 :]
    fields, kept = [kept[0], *fields], kept[1:]

    outputs = []
    for part, todo in enumerate((every[:-1], every[-1:])):
        *outputs, token = finish(
            todo,
            fields,
            kept[:groups],
            kept[groups : 2 * groups],
            kept[2 * groups],
            channels,
            outputs,
            f"finish_{part}",
        )
        if part == 0:
            total = sum_over_ring(partial, ring, token)
    energy = total[0, :replicas] / jnp.sqrt(jnp.float32(cells * ring * channels))
    x_new, y_new = outputs
    return (x_new, y_new, energy)


def solution(mesh):
    cells = P(("groups", "row", "col"), None)
    slots = P(("groups", "row", "col"))
    return jax.shard_map(
        local,
        mesh=mesh,
        in_specs=(cells, cells, P(("groups", "row", "col"), None, None), slots, slots, slots, P()),
        out_specs=(cells, cells, P("groups")),
        check_vma=False,
    )
```

```python
import jax
import jax.numpy as jnp
import ml_dtypes
import numpy as np
from jax import lax
from jax.experimental import pallas as pl
from jax.experimental.pallas import tpu as pltpu
from jax.sharding import PartitionSpec as P

STEPS = 2
LANES = 128
LONG, SHORT = 16, 4
VMEM_LIMIT = 14 * 1024 * 1024
NEAR_FLOPS = 4 * 10**9
F32 = jnp.float32
BF16 = jnp.bfloat16
RING = ("row", "col")


def call(body, ins, outs, scratch, name, flops=0, aliases=()):
    return pl.pallas_call(
        body,
        in_specs=[pl.BlockSpec(memory_space=pl.ANY if s is pltpu.HBM else s) for _, s in ins],
        out_specs=[pl.BlockSpec(memory_space=pl.ANY if s is pltpu.HBM else s) for *_, s in outs],
        out_shape=[
            jax.ShapeDtypeStruct(dims, kind) if s is pltpu.HBM else s(dims, kind)
            for dims, kind, s in outs
        ],
        scratch_shapes=scratch,
        input_output_aliases=dict(aliases),
        compiler_params=pltpu.CompilerParams(vmem_limit_bytes=VMEM_LIMIT),
        cost_estimate=pl.CostEstimate(
            flops=int(flops) or 1000, bytes_accessed=1000, transcendentals=0
        ),
        name=name,
    )(*[pltpu.with_memory_space_constraint(a, s) for a, s in ins])


def vmem(*arrays):
    return [(a, pltpu.VMEM) for a in arrays]


def lanes(group):
    return slice(group * LANES, (group + 1) * LANES)


def spanned(group, channels, width):
    first = group * LANES // channels * channels
    last = -(-(group + 1) * LANES // channels) * channels
    return list(range(first // LANES, -(-min(last, width) // LANES)))


def span_lanes(near):
    return slice(near[0] * LANES, (near[-1] + 1) * LANES)


def split(x):
    high = x.astype(BF16)
    return high, (x - high.astype(F32)).astype(BF16)


def bases_into(outs, xs, ys, same, step, channels):
    groups = len(xs)
    width = groups * LANES
    detune = 1.0 - (step + 1.0) / (STEPS + 1.0)
    parts = [split(x) for x in xs]
    for g in range(groups):
        near = spanned(g, channels, width)
        ones = same[span_lanes(near), lanes(g)]
        totals = sum(
            jnp.dot(
                jnp.concatenate([parts[n][k] for n in near], axis=1),
                ones,
                preferred_element_type=F32,
            )
            for k in range(2)
        )
        penalty = 0.02 * (totals - (2.0 - channels))
        outs[g][...] = ys[g] + 0.5 * (-detune * xs[g] - 0.4 * penalty)


def mixed_of(fields, mixing, group, channels):
    near = spanned(group, channels, mixing.shape[0])
    return jnp.dot(
        jnp.concatenate([fields[n] for n in near], axis=1),
        mixing[span_lanes(near), lanes(group)],
        preferred_element_type=F32,
    )


def load_first(positions, groups_of):
    cells = positions.shape[0]
    n = len(groups_of)

    def body(x_ref, *refs):
        x_outs, r_outs, sent, sems = refs[:n], refs[n : 2 * n], refs[2 * n], refs[-1]
        copies = [
            pltpu.make_async_copy(x_ref.at[:, lanes(g)], x_outs[i], sems.at[i])
            for i, g in enumerate(groups_of)
        ]
        for copy in copies:
            copy.start()
        for i, copy in enumerate(copies):
            copy.wait()
            rounded = x_outs[i][...].astype(BF16)
            r_outs[i][...] = rounded
            sent[:, lanes(i)] = rounded

    outs = call(
        body,
        [(positions, pltpu.HBM)],
        [((cells, LANES), F32, pltpu.VMEM)] * n
        + [((cells, LANES), BF16, pltpu.VMEM)] * n
        + [((cells, n * LANES), BF16, pltpu.VMEM)],
        [pltpu.SemaphoreType.DMA((n,))],
        "load_first",
    )
    return outs[:n], outs[n : 2 * n], outs[2 * n]


def section(slots, per):
    return -(-(slots + per) // (2 * SHORT)) * SHORT


def make_lists(rows, cols, count, positions, groups_of, after, slots, tile, ring_index):
    cells = positions.shape[0]
    per = cells // tile
    pairs = section(slots, per)
    n = len(groups_of)

    def body(rows_hbm, cols_hbm, count_hbm, x_ref, _, list_ref, *refs):
        x_outs, r_outs = refs[:n], refs[n : 2 * n]
        rows_ref, cols_ref, count_ref, held, sems = refs[2 * n :]
        copies = [
            pltpu.make_async_copy(*ends, sems.at[k])
            for k, ends in enumerate(
                [(rows_hbm, rows_ref), (cols_hbm, cols_ref), (count_hbm, count_ref)]
                + [(x_ref.at[:, lanes(g)], x_outs[i]) for i, g in enumerate(groups_of)]
            )
        ]
        for copy in copies:
            copy.start()
        for k in range(2 * per):
            held[k] = -1
        far_third = jnp.where(lax.rem(ring_index(), 2) == 1, 2, 0)
        for copy in copies[:3]:
            copy.wait()

        def visit(slot, totals):
            near_pairs, far_pairs = totals
            row, col = rows_ref[slot], cols_ref[slot]
            third = jnp.where(col >= 2 * per, 2, jnp.where(col >= per, 1, 0))
            source = col - third * per
            far = third == far_third
            source = jnp.where(far | (third == 1), source, source + per)
            key = row + jnp.where(far, per, 0)
            place = 2 * jnp.where(far, far_pairs + pairs, near_pairs)
            entry = slot * 65536 + source * 256 + row
            other = held[key]
            full = other >= 0
            list_ref[place] = other
            list_ref[place + 1] = entry
            held[key] = jnp.where(full, -1, entry)
            one = full.astype(jnp.int32)
            far_one = jnp.where(far, one, 0)
            return near_pairs + one - far_one, far_pairs + far_one

        totals = lax.fori_loop(0, count_ref[0], visit, (jnp.int32(0), jnp.int32(0)))
        for part, zero in enumerate((2 * per, per)):
            total = totals[part]
            start = part * pairs
            for k in range(per):
                other = held[part * per + k]
                list_ref[2 * (start + total)] = other
                list_ref[2 * (start + total) + 1] = zero * 256 + k
                total = total + (other >= 0).astype(jnp.int32)
            short_turns = (total + SHORT - 1) // SHORT

            def pad(pair, carry, start=start, zero=zero):
                for e in range(2):
                    list_ref[2 * (start + pair) + e] = zero * 256 + per
                return carry

            lax.fori_loop(total, short_turns * SHORT, pad, 0)
            list_ref[4 * pairs + 2 * part] = short_turns // (LONG // SHORT)
            list_ref[4 * pairs + 2 * part + 1] = short_turns % (LONG // SHORT)
        for i, copy in enumerate(copies[3:]):
            copy.wait()
            r_outs[i][...] = x_outs[i][...].astype(BF16)

    outs = call(
        body,
        [(a, pl.ANY) for a in (rows, cols, count)] + [(positions, pltpu.HBM)] + vmem(after),
        [((4 * pairs + 4 + 2,), jnp.int32, pltpu.SMEM)]
        + [((cells, LANES), F32, pltpu.VMEM)] * n
        + [((cells, LANES), BF16, pltpu.VMEM)] * n,
        [
            pltpu.SMEM(rows.shape, jnp.int32),
            pltpu.SMEM(cols.shape, jnp.int32),
            pltpu.SMEM(count.shape, jnp.int32),
            pltpu.SMEM((2 * per,), jnp.int32),
            pltpu.SemaphoreType.DMA((3 + n,)),
        ],
        "make_lists",
    )
    return outs[0], outs[1 : 1 + n], outs[1 + n :]


def add_pairs(part, list_ref, tiles, field, window, pairs):
    def turn(first, length):
        for u in range(length):
            place = 2 * (part * pairs + first + u)
            entries = [list_ref[place + e] for e in range(2)]
            left = jnp.concatenate([tiles[n >> 16] for n in entries], axis=1)
            right = jnp.concatenate([window[(n >> 8) & 255] for n in entries], axis=0)
            field[entries[1] & 255] += jnp.dot(left, right, preferred_element_type=F32)

    def long(i, carry):
        turn(i * LONG, LONG)
        return carry

    def short(i, carry):
        turn(long_turns * LONG + i * SHORT, SHORT)
        return carry

    long_turns = list_ref[4 * pairs + 2 * part]
    lax.fori_loop(0, long_turns, long, 0)
    lax.fori_loop(0, list_ref[4 * pairs + 2 * part + 1], short, 0)


def near_fields(lists, tiles, owns, others, far_part, sent, after, flops, name):
    slots, tile, _ = tiles.shape
    cells = owns[0].shape[0]
    groups = len(owns)
    width = groups * LANES
    per = cells // tile
    pairs = section(slots, per)
    start = [] if far_part is None else [far_part]

    def body(list_ref, tiles_ref, *refs):
        own_refs, other_refs, refs = refs[:groups], refs[groups : 2 * groups], refs[2 * groups :]
        start_refs, refs = refs[: len(start)], refs[len(start) :]
        sent_refs, refs = refs[: len(sent)], refs[len(sent) + len(after) :]
        field_outs, sent_outs, (field, window) = refs[:groups], refs[groups:-2], refs[-2:]
        for out, ref in zip(sent_outs, sent_refs):
            out[...] = ref[...]
        for g in range(groups):
            window[:per, :, lanes(g)] = own_refs[g][...].reshape(per, tile, LANES)
            window[per : 2 * per, :, lanes(g)] = other_refs[g][...].reshape(per, tile, LANES)
        window[2 * per] = jnp.zeros((tile, width), BF16)
        field[:per] = jnp.zeros((per, tile, width), F32)
        for ref in start_refs:
            field[:per, :, lanes(0)] = ref[...].reshape(per, tile, LANES)
        add_pairs(0, list_ref, tiles_ref, field, window, pairs)
        for g, out in enumerate(field_outs):
            out[...] = field[:per, :, lanes(g)].reshape(cells, LANES).astype(out.dtype)

    outs = call(
        body,
        [(lists, pltpu.SMEM)] + vmem(tiles, *owns, *others, *start, *sent, *after),
        [
            ((cells, LANES), BF16 if start and g == 0 else F32, pltpu.VMEM)
            for g in range(groups)
        ]
        + [(a.shape, BF16, pltpu.VMEM) for a in sent],
        [
            pltpu.VMEM((per + 1, tile, width), F32),
            pltpu.VMEM((2 * per + 1, tile, width), BF16),
        ],
        name,
        flops,
    )
    return outs[:groups], outs[groups:]


def far_fields(lists, tiles, nears, far, extra, outs_of, work, name, flops=0, through=()):
    slots, tile, _ = tiles.shape
    cells, width = far.shape
    per = cells // tile
    pairs = section(slots, per)
    n = width // LANES
    m = len(nears)

    def body(list_ref, tiles_ref, far_ref, *refs):
        near_refs, extra_refs = refs[:m], refs[m : m + len(extra)]
        through_refs = refs[m + len(extra) : m + len(extra) + len(through)]
        out_refs, (field, window) = refs[m + len(extra) + len(through) : -2], refs[-2:]
        window[:per] = far_ref[...].reshape(per, tile, width)
        window[per] = jnp.zeros((tile, width), BF16)
        if not near_refs:
            field[:per] = jnp.zeros((per, tile, width), F32)
        for i, ref in enumerate(near_refs):
            field[:per, :, lanes(i)] = ref[...].reshape(per, tile, LANES)
        add_pairs(1, list_ref, tiles_ref, field, window, pairs)
        done = [field[:per, :, lanes(i)].reshape(cells, LANES) for i in range(n)]
        work(done, [*extra_refs, *through_refs], out_refs[: len(outs_of)])

    return call(
        body,
        [(lists, pltpu.SMEM)] + vmem(tiles, far, *nears, *extra, *through),
        [(*out, pltpu.VMEM) for out in outs_of] + [(a.shape, a.dtype, pltpu.VMEM) for a in through],
        [pltpu.VMEM((per + 1, tile, width), F32), pltpu.VMEM((per + 1, tile, width), BF16)],
        name,
        flops,
        [(3 + m + len(extra) + i, len(outs_of) + i) for i in range(len(through))],
    )


def first_base(xs, momenta, same, spread, coupling, channels):
    cells, width = momenta.shape
    groups = len(xs)

    def body(*refs):
        x_refs, (y_ref, same_ref, spread_ref, coupling_ref) = refs[:groups], refs[groups : groups + 4]
        outs = refs[groups + 4 :]
        tall = jnp.dot(spread_ref[...], coupling_ref[...], preferred_element_type=F32).astype(BF16)
        wide = lax.dot_general(
            tall, spread_ref[...], (((1,), (1,)), ((), ())), preferred_element_type=F32
        )
        outs[groups][...] = (wide * same_ref[...].astype(F32)).astype(BF16)
        x = [ref[...] for ref in x_refs]
        y = [y_ref[:, lanes(g)] for g in range(groups)]
        bases_into(outs[:groups], x, y, same_ref, 0, channels)

    outs = call(
        body,
        vmem(*xs, momenta, same, spread, coupling),
        [((cells, LANES), F32, pltpu.VMEM)] * groups + [((width, width), BF16, pltpu.VMEM)],
        [],
        "first_base",
    )
    return outs[:groups], outs[groups]


def second_base(xs, ys, rounded, same, mixing, channels):
    groups = len(xs)
    cells = xs[0].shape[0]
    width = groups * LANES

    def body(*refs):
        x, y, r = [[ref[...] for ref in refs[k * groups : (k + 1) * groups]] for k in range(3)]
        same_ref, mixing_ref = refs[3 * groups : 3 * groups + 2]
        outs = refs[3 * groups + 2 :]
        bases_into(outs[:groups], x, y, same_ref, 1, channels)
        for g in range(groups):
            near = spanned(g, channels, width)
            outs[groups + g][...] = lax.dot_general(
                jnp.concatenate([r[n] for n in near], axis=1),
                mixing_ref[lanes(g), span_lanes(near)],
                (((1,), (1,)), ((), ())),
                preferred_element_type=F32,
            )

    outs = call(
        body,
        vmem(*xs, *ys, *rounded, same, mixing),
        [((cells, LANES), F32, pltpu.VMEM)] * (2 * groups),
        [],
        "second_base",
    )
    return outs[:groups], outs[groups:]


def finish(fields, xs, bases, mixing, channels):
    groups = len(xs)
    cells = xs[0].shape[0]
    width = groups * LANES

    def body(*refs):
        field_refs, x_refs, base_refs = [refs[k * groups : (k + 1) * groups] for k in range(3)]
        mixing_ref, x_out, y_out, token, x_buf, y_buf, sems = refs[3 * groups :]
        held = [ref[...] for ref in field_refs]
        copies = []
        for g in range(groups):
            y_new = base_refs[g][...] - 0.2 * mixed_of(held, mixing_ref, g, channels)
            y_buf[g] = y_new
            x_buf[g] = jnp.clip(x_refs[g][...] + 0.5 * y_new, -1.0, 1.0)
            for k, (buf, out) in enumerate(((y_buf, y_out), (x_buf, x_out))):
                copies.append(
                    pltpu.make_async_copy(buf.at[g], out.at[:, lanes(g)], sems.at[g, k])
                )
                copies[-1].start()
        token[...] = jnp.zeros_like(token)
        for copy in copies:
            copy.wait()

    return call(
        body,
        vmem(*fields, *xs, *bases, mixing),
        [((cells, width), F32, pltpu.HBM)] * 2 + [((8, LANES), F32, pltpu.VMEM)],
        [
            pltpu.VMEM((groups, cells, LANES), F32),
            pltpu.VMEM((groups, cells, LANES), F32),
            pltpu.SemaphoreType.DMA((groups, 2)),
        ],
        "finish",
    )


def add_up(arrays, token):
    def body(*refs):
        refs[-1][...] = sum(ref[...] for ref in refs[:-2])

    return call(
        body,
        vmem(*arrays, token),
        [(arrays[0].shape, F32, pltpu.VMEM)],
        [],
        "add_up",
    )[0]


def sum_over_ring(value, ring, token):
    if ring & (ring - 1):
        return lax.psum(value, RING)
    size = 1
    while size < ring:
        digits = (1, 2, 3) if 4 * size <= ring else (1,)
        parts = [value] + [
            lax.ppermute(value, RING, [(i, i ^ (size * d)) for i in range(ring)]) for d in digits
        ]
        value = add_up(parts, token) if size == 1 else sum(parts)
        size *= len(digits) + 1
    return value


def local(positions, momenta, tile_values, tile_rows, tile_cols, tile_count, channel_coupling):
    cells, width = positions.shape
    slots, tile, _ = tile_values.shape
    channels = channel_coupling.shape[0]
    replicas = width // channels
    groups = width // LANES
    ring = lax.axis_size("row") * lax.axis_size("col")
    where = np.arange(width)
    same = jnp.asarray(
        (where[:, None] // channels == where[None] // channels).astype(ml_dtypes.bfloat16)
    )
    spread = jnp.asarray(
        (where[:, None] % channels == np.arange(channels)[None]).astype(ml_dtypes.bfloat16)
    )
    on_chip = [(i, i ^ 1) for i in range(ring)]
    off_chip = [(i, (i + 1) % ring if i % 2 else (i - 1) % ring) for i in range(ring)]
    wide = (cells, LANES)
    every = list(range(groups))
    first_pieces = [every[:-1], every[-1:]]
    second_pieces = [every[:1], every[1:]]

    def ring_index():
        return lax.axis_index("row") * lax.axis_size("col") + lax.axis_index("col")

    def far_swap(mine):
        return lax.ppermute(mine, RING, off_chip)

    def near_swap(mine):
        return lax.ppermute(mine, RING, on_chip)

    def ready(piece, done):
        return [
            t for t in every if t not in done and max(spanned(t, channels, width)) <= piece[-1]
        ]

    def keep(done, _, outs):
        outs[0][...] = done[0]

    def needed(todo, piece):
        return sorted({n for t in todo for n in spanned(t, channels, width)} - set(piece))

    xs, owns, sent = load_first(positions, first_pieces[0])
    fars = [far_swap(sent)]
    lists, more_x, more_own = make_lists(
        tile_rows, tile_cols, tile_count, positions, first_pieces[1], sent, slots, tile, ring_index
    )
    xs, owns = [*xs, *more_x], [*owns, *more_own]
    others = [near_swap(r) for r in owns]
    base, mixing = first_base(xs, momenta, same, spread, channel_coupling, channels)
    near, sent = near_fields(
        lists, tile_values, owns, others, None, more_own, [mixing], 0, "near_first"
    )
    fars.append(far_swap(sent[0]))

    fields, new_x, new_y, rounded, new_fars = {}, {}, {}, {}, []
    for p, piece in enumerate(first_pieces):
        todo = ready(piece, new_x)
        known = needed(todo, piece)
        going = second_pieces[p]
        assert going == todo
        last = p == len(first_pieces) - 1

        def work(done, ins, outs, piece=piece, todo=todo, known=known, last=last):
            held = {n: ins[1 + i][...] for i, n in enumerate(known)}
            done = [field.astype(BF16) for field in done]
            held.update(zip(piece, done))
            rest = ins[1 + len(known) :]
            for i, t in enumerate(todo):
                y_new = rest[2 * i][...] - 0.2 * mixed_of(held, ins[0], t, channels)
                x_new = jnp.clip(rest[2 * i + 1][...] + 0.5 * y_new, -1.0, 1.0)
                r_new = x_new.astype(BF16)
                outs[3 * i][...] = x_new
                outs[3 * i + 1][...] = y_new
                outs[3 * i + 2][...] = r_new
                outs[3 * len(todo)][:, lanes(i)] = r_new
            if not last:
                for i, field in enumerate(done):
                    outs[3 * len(todo) + 1 + i][...] = field

        results = far_fields(
            lists,
            tile_values,
            [near[n] for n in piece],
            fars[p],
            [mixing] + [fields[n] for n in known] + [a for t in todo for a in (base[t], xs[t])],
            [(wide, F32), (wide, F32), (wide, BF16)] * len(todo)
            + [((cells, len(todo) * LANES), BF16)]
            + ([] if last else [(wide, BF16)] * len(piece)),
            work,
            f"far_first_{p}",
        )
        for i, t in enumerate(todo):
            new_x[t], new_y[t], rounded[t] = results[3 * i : 3 * i + 3]
        new_fars.append(far_swap(results[3 * len(todo)]))
        fields.update(zip(piece, results[3 * len(todo) + 1 :]))

    xs, ys, owns = [[of[g] for g in every] for of in (new_x, new_y, rounded)]
    others = [near_swap(r) for r in owns]
    (part,) = far_fields(
        lists, tile_values, [], new_fars[0], [], [(wide, F32)], keep, "far_second_0", NEAR_FLOPS
    )
    near, _ = near_fields(lists, tile_values, owns, others, part, [], [], 0, "near_second")
    base, weights = second_base(xs, ys, owns, same, mixing, channels)
    piece = second_pieces[1]

    def last_work(done, ins, outs):
        held = [ins[groups][...]] + [field.astype(BF16) for field in done]
        for out, field in zip(outs, held[1:]):
            out[...] = field
        row = jnp.concatenate(
            [
                jnp.sum(field.astype(F32) * ref[...], axis=0, keepdims=True)
                for field, ref in zip(held, ins[:groups])
            ],
            axis=1,
        )
        row = jnp.broadcast_to(row, (replicas, width))
        lane = lax.broadcasted_iota(jnp.int32, (replicas, width), 1)
        first = lax.broadcasted_iota(jnp.int32, (replicas, width), 0) * channels
        inside = (lane >= first) & (lane < first + channels)
        total = jnp.sum(jnp.where(inside, row, 0.0), axis=1, keepdims=True)
        place = lax.broadcasted_iota(jnp.int32, (replicas, LANES), 1)
        which = lax.broadcasted_iota(jnp.int32, (replicas, LANES), 0)
        flat = jnp.sum(jnp.where(place == which, total, 0.0), axis=0, keepdims=True)
        outs[len(piece)][...] = jnp.broadcast_to(flat, (8, LANES))

    results = far_fields(
        lists,
        tile_values,
        near[1:],
        new_fars[1],
        weights,
        [(wide, BF16)] * len(piece) + [((8, LANES), F32)],
        last_work,
        "far_second_1",
        through=[near[0], *xs, *base, mixing],
    )
    fields, partial, kept = results[: len(piece)], results[len(piece)], results[len(piece) + 1 :]
    fields, kept = [kept[0], *fields], kept[1:]

    x_new, y_new, token = finish(
        fields, kept[:groups], kept[groups : 2 * groups], kept[2 * groups], channels
    )
    total = sum_over_ring(partial, ring, token)
    energy = total[0, :replicas] / jnp.sqrt(jnp.float32(cells * ring * channels))
    return (x_new, y_new, energy)


def solution(mesh):
    cells = P(("groups", "row", "col"), None)
    slots = P(("groups", "row", "col"))
    return jax.shard_map(
        local,
        mesh=mesh,
        in_specs=(cells, cells, P(("groups", "row", "col"), None, None), slots, slots, slots, P()),
        out_specs=(cells, cells, P("groups")),
        check_vma=False,
    )
```

```python
import jax
import jax.numpy as jnp
import ml_dtypes
import numpy as np
from jax import lax
from jax.experimental import pallas as pl
from jax.experimental.pallas import tpu as pltpu
from jax.sharding import PartitionSpec as P

STEPS = 2
LANES = 128
LONG, SHORT = 16, 4
VMEM_LIMIT = 14 * 1024 * 1024
NEAR_FLOPS = 4 * 10**9
F32 = jnp.float32
BF16 = jnp.bfloat16
RING = ("row", "col")


def call(body, ins, outs, scratch, name, flops=0, aliases=()):
    return pl.pallas_call(
        body,
        in_specs=[pl.BlockSpec(memory_space=pl.ANY if s is pltpu.HBM else s) for _, s in ins],
        out_specs=[pl.BlockSpec(memory_space=pl.ANY if s is pltpu.HBM else s) for *_, s in outs],
        out_shape=[
            jax.ShapeDtypeStruct(dims, kind) if s is pltpu.HBM else s(dims, kind)
            for dims, kind, s in outs
        ],
        scratch_shapes=scratch,
        input_output_aliases=dict(aliases),
        compiler_params=pltpu.CompilerParams(vmem_limit_bytes=VMEM_LIMIT),
        cost_estimate=pl.CostEstimate(
            flops=int(flops) or 1000, bytes_accessed=1000, transcendentals=0
        ),
        name=name,
    )(*[pltpu.with_memory_space_constraint(a, s) for a, s in ins])


def vmem(*arrays):
    return [(a, pltpu.VMEM) for a in arrays]


def lanes(group):
    return slice(group * LANES, (group + 1) * LANES)


def spanned(group, channels, width):
    first = group * LANES // channels * channels
    last = -(-(group + 1) * LANES // channels) * channels
    return list(range(first // LANES, -(-min(last, width) // LANES)))


def span_lanes(near):
    return slice(near[0] * LANES, (near[-1] + 1) * LANES)


def split(x):
    high = x.astype(BF16)
    return high, (x - high.astype(F32)).astype(BF16)


def bases_into(outs, xs, ys, same, step, channels):
    groups = len(xs)
    width = groups * LANES
    detune = 1.0 - (step + 1.0) / (STEPS + 1.0)
    parts = [split(x) for x in xs]
    for g in range(groups):
        near = spanned(g, channels, width)
        ones = same[span_lanes(near), lanes(g)]
        totals = sum(
            jnp.dot(
                jnp.concatenate([parts[n][k] for n in near], axis=1),
                ones,
                preferred_element_type=F32,
            )
            for k in range(2)
        )
        penalty = 0.02 * (totals - (2.0 - channels))
        outs[g][...] = ys[g] + 0.5 * (-detune * xs[g] - 0.4 * penalty)


def mixed_of(fields, mixing, group, channels):
    near = spanned(group, channels, mixing.shape[0])
    return jnp.dot(
        jnp.concatenate([fields[n] for n in near], axis=1),
        mixing[span_lanes(near), lanes(group)],
        preferred_element_type=F32,
    )


def load_first(positions, groups_of):
    cells = positions.shape[0]
    n = len(groups_of)

    def body(x_ref, *refs):
        x_outs, r_outs, sent, sems = refs[:n], refs[n : 2 * n], refs[2 * n], refs[-1]
        copies = [
            pltpu.make_async_copy(x_ref.at[:, lanes(g)], x_outs[i], sems.at[i])
            for i, g in enumerate(groups_of)
        ]
        for copy in copies:
            copy.start()
        for i, copy in enumerate(copies):
            copy.wait()
            rounded = x_outs[i][...].astype(BF16)
            r_outs[i][...] = rounded
            sent[:, lanes(i)] = rounded

    outs = call(
        body,
        [(positions, pltpu.HBM)],
        [((cells, LANES), F32, pltpu.VMEM)] * n
        + [((cells, LANES), BF16, pltpu.VMEM)] * n
        + [((cells, n * LANES), BF16, pltpu.VMEM)],
        [pltpu.SemaphoreType.DMA((n,))],
        "load_first",
    )
    return outs[:n], outs[n : 2 * n], outs[2 * n]


def section(slots, per):
    return -(-(slots + per) // (2 * SHORT)) * SHORT


def make_lists(rows, cols, count, positions, groups_of, after, slots, tile, ring_index):
    cells = positions.shape[0]
    per = cells // tile
    pairs = section(slots, per)
    n = len(groups_of)

    def body(rows_hbm, cols_hbm, count_hbm, x_ref, _, list_ref, *refs):
        x_outs, r_outs = refs[:n], refs[n : 2 * n]
        rows_ref, cols_ref, count_ref, held, sems = refs[2 * n :]
        copies = [
            pltpu.make_async_copy(*ends, sems.at[k])
            for k, ends in enumerate(
                [(rows_hbm, rows_ref), (cols_hbm, cols_ref), (count_hbm, count_ref)]
                + [(x_ref.at[:, lanes(g)], x_outs[i]) for i, g in enumerate(groups_of)]
            )
        ]
        for copy in copies:
            copy.start()
        for k in range(2 * per):
            held[k] = -1
        far_third = jnp.where(lax.rem(ring_index(), 2) == 1, 2, 0)
        for copy in copies[:3]:
            copy.wait()

        def visit(slot, totals):
            near_pairs, far_pairs = totals
            row, col = rows_ref[slot], cols_ref[slot]
            third = jnp.where(col >= 2 * per, 2, jnp.where(col >= per, 1, 0))
            source = col - third * per
            far = third == far_third
            source = jnp.where(far | (third == 1), source, source + per)
            key = row + jnp.where(far, per, 0)
            place = 2 * jnp.where(far, far_pairs + pairs, near_pairs)
            entry = slot * 65536 + source * 256 + row
            other = held[key]
            full = other >= 0
            list_ref[place] = other
            list_ref[place + 1] = entry
            held[key] = jnp.where(full, -1, entry)
            one = full.astype(jnp.int32)
            far_one = jnp.where(far, one, 0)
            return near_pairs + one - far_one, far_pairs + far_one

        totals = lax.fori_loop(0, count_ref[0], visit, (jnp.int32(0), jnp.int32(0)))
        for part, zero in enumerate((2 * per, per)):
            total = totals[part]
            start = part * pairs
            for k in range(per):
                other = held[part * per + k]
                list_ref[2 * (start + total)] = other
                list_ref[2 * (start + total) + 1] = zero * 256 + k
                total = total + (other >= 0).astype(jnp.int32)
            short_turns = (total + SHORT - 1) // SHORT

            def pad(pair, carry, start=start, zero=zero):
                for e in range(2):
                    list_ref[2 * (start + pair) + e] = zero * 256 + per
                return carry

            lax.fori_loop(total, short_turns * SHORT, pad, 0)
            list_ref[4 * pairs + 2 * part] = short_turns // (LONG // SHORT)
            list_ref[4 * pairs + 2 * part + 1] = short_turns % (LONG // SHORT)
        for i, copy in enumerate(copies[3:]):
            copy.wait()
            r_outs[i][...] = x_outs[i][...].astype(BF16)

    outs = call(
        body,
        [(a, pl.ANY) for a in (rows, cols, count)] + [(positions, pltpu.HBM)] + vmem(after),
        [((4 * pairs + 4 + 2,), jnp.int32, pltpu.SMEM)]
        + [((cells, LANES), F32, pltpu.VMEM)] * n
        + [((cells, LANES), BF16, pltpu.VMEM)] * n,
        [
            pltpu.SMEM(rows.shape, jnp.int32),
            pltpu.SMEM(cols.shape, jnp.int32),
            pltpu.SMEM(count.shape, jnp.int32),
            pltpu.SMEM((2 * per,), jnp.int32),
            pltpu.SemaphoreType.DMA((3 + n,)),
        ],
        "make_lists",
    )
    return outs[0], outs[1 : 1 + n], outs[1 + n :]


def add_pairs(part, list_ref, tiles, field, window, pairs):
    def turn(first, length):
        for u in range(length):
            place = 2 * (part * pairs + first + u)
            entries = [list_ref[place + e] for e in range(2)]
            left = jnp.concatenate([tiles[n >> 16] for n in entries], axis=1)
            right = jnp.concatenate([window[(n >> 8) & 255] for n in entries], axis=0)
            field[entries[1] & 255] += jnp.dot(left, right, preferred_element_type=F32)

    def long(i, carry):
        turn(i * LONG, LONG)
        return carry

    def short(i, carry):
        turn(long_turns * LONG + i * SHORT, SHORT)
        return carry

    long_turns = list_ref[4 * pairs + 2 * part]
    lax.fori_loop(0, long_turns, long, 0)
    lax.fori_loop(0, list_ref[4 * pairs + 2 * part + 1], short, 0)


def near_fields(lists, tiles, owns, others, far_part, sent, after, flops, name):
    slots, tile, _ = tiles.shape
    cells = owns[0].shape[0]
    groups = len(owns)
    width = groups * LANES
    per = cells // tile
    pairs = section(slots, per)
    start = [] if far_part is None else [far_part]

    def body(list_ref, tiles_ref, *refs):
        own_refs, other_refs, refs = refs[:groups], refs[groups : 2 * groups], refs[2 * groups :]
        start_refs, refs = refs[: len(start)], refs[len(start) :]
        sent_refs, refs = refs[: len(sent)], refs[len(sent) + len(after) :]
        field_outs, sent_outs, (field, window) = refs[:groups], refs[groups:-2], refs[-2:]
        for out, ref in zip(sent_outs, sent_refs):
            out[...] = ref[...]
        for g in range(groups):
            window[:per, :, lanes(g)] = own_refs[g][...].reshape(per, tile, LANES)
            window[per : 2 * per, :, lanes(g)] = other_refs[g][...].reshape(per, tile, LANES)
        window[2 * per] = jnp.zeros((tile, width), BF16)
        field[:per] = jnp.zeros((per, tile, width), F32)
        for ref in start_refs:
            field[:per, :, lanes(0)] = ref[...].reshape(per, tile, LANES)
        add_pairs(0, list_ref, tiles_ref, field, window, pairs)
        for g, out in enumerate(field_outs):
            out[...] = field[:per, :, lanes(g)].reshape(cells, LANES).astype(out.dtype)

    outs = call(
        body,
        [(lists, pltpu.SMEM)] + vmem(tiles, *owns, *others, *start, *sent, *after),
        [
            ((cells, LANES), BF16 if start and g == 0 else F32, pltpu.VMEM)
            for g in range(groups)
        ]
        + [(a.shape, BF16, pltpu.VMEM) for a in sent],
        [
            pltpu.VMEM((per + 1, tile, width), F32),
            pltpu.VMEM((2 * per + 1, tile, width), BF16),
        ],
        name,
        flops,
    )
    return outs[:groups], outs[groups:]


def far_fields(lists, tiles, nears, far, extra, outs_of, work, name, flops=0, through=()):
    slots, tile, _ = tiles.shape
    cells, width = far.shape
    per = cells // tile
    pairs = section(slots, per)
    n = width // LANES
    m = len(nears)

    def body(list_ref, tiles_ref, far_ref, *refs):
        near_refs, extra_refs = refs[:m], refs[m : m + len(extra)]
        through_refs = refs[m + len(extra) : m + len(extra) + len(through)]
        out_refs, (field, window) = refs[m + len(extra) + len(through) : -2], refs[-2:]
        window[:per] = far_ref[...].reshape(per, tile, width)
        window[per] = jnp.zeros((tile, width), BF16)
        if not near_refs:
            field[:per] = jnp.zeros((per, tile, width), F32)
        for i, ref in enumerate(near_refs):
            field[:per, :, lanes(i)] = ref[...].reshape(per, tile, LANES)
        add_pairs(1, list_ref, tiles_ref, field, window, pairs)
        done = [field[:per, :, lanes(i)].reshape(cells, LANES) for i in range(n)]
        work(done, [*extra_refs, *through_refs], out_refs[: len(outs_of)])

    return call(
        body,
        [(lists, pltpu.SMEM)] + vmem(tiles, far, *nears, *extra, *through),
        [(*out, pltpu.VMEM) for out in outs_of] + [(a.shape, a.dtype, pltpu.VMEM) for a in through],
        [pltpu.VMEM((per + 1, tile, width), F32), pltpu.VMEM((per + 1, tile, width), BF16)],
        name,
        flops,
        [(3 + m + len(extra) + i, len(outs_of) + i) for i in range(len(through))],
    )


def first_base(xs, momenta, same, spread, coupling, channels):
    cells, width = momenta.shape
    groups = len(xs)

    def body(*refs):
        x_refs, (y_ref, same_ref, spread_ref, coupling_ref) = refs[:groups], refs[groups : groups + 4]
        outs = refs[groups + 4 :]
        tall = jnp.dot(spread_ref[...], coupling_ref[...], preferred_element_type=F32).astype(BF16)
        wide = lax.dot_general(
            tall, spread_ref[...], (((1,), (1,)), ((), ())), preferred_element_type=F32
        )
        outs[groups][...] = (wide * same_ref[...].astype(F32)).astype(BF16)
        x = [ref[...] for ref in x_refs]
        y = [y_ref[:, lanes(g)] for g in range(groups)]
        bases_into(outs[:groups], x, y, same_ref, 0, channels)

    outs = call(
        body,
        vmem(*xs, momenta, same, spread, coupling),
        [((cells, LANES), F32, pltpu.VMEM)] * groups + [((width, width), BF16, pltpu.VMEM)],
        [],
        "first_base",
    )
    return outs[:groups], outs[groups]


def second_base(xs, ys, rounded, same, mixing, channels):
    groups = len(xs)
    cells = xs[0].shape[0]
    width = groups * LANES

    def body(*refs):
        x, y, r = [[ref[...] for ref in refs[k * groups : (k + 1) * groups]] for k in range(3)]
        same_ref, mixing_ref = refs[3 * groups : 3 * groups + 2]
        outs = refs[3 * groups + 2 :]
        bases_into(outs[:groups], x, y, same_ref, 1, channels)
        for g in range(groups):
            near = spanned(g, channels, width)
            outs[groups + g][...] = lax.dot_general(
                jnp.concatenate([r[n] for n in near], axis=1),
                mixing_ref[lanes(g), span_lanes(near)],
                (((1,), (1,)), ((), ())),
                preferred_element_type=F32,
            )

    outs = call(
        body,
        vmem(*xs, *ys, *rounded, same, mixing),
        [((cells, LANES), F32, pltpu.VMEM)] * (2 * groups),
        [],
        "second_base",
    )
    return outs[:groups], outs[groups:]


def finish(fields, xs, bases, mixing, channels):
    groups = len(xs)
    cells = xs[0].shape[0]
    width = groups * LANES

    def body(*refs):
        field_refs, x_refs, base_refs = [refs[k * groups : (k + 1) * groups] for k in range(3)]
        mixing_ref, x_out, y_out, x_buf, y_buf, sems = refs[3 * groups :]
        held = [ref[...] for ref in field_refs]
        copies = []
        for g in range(groups):
            y_new = base_refs[g][...] - 0.2 * mixed_of(held, mixing_ref, g, channels)
            y_buf[g] = y_new
            x_buf[g] = jnp.clip(x_refs[g][...] + 0.5 * y_new, -1.0, 1.0)
            for k, (buf, out) in enumerate(((y_buf, y_out), (x_buf, x_out))):
                copies.append(
                    pltpu.make_async_copy(buf.at[g], out.at[:, lanes(g)], sems.at[g, k])
                )
                copies[-1].start()
        for copy in copies:
            copy.wait()

    return call(
        body,
        vmem(*fields, *xs, *bases, mixing),
        [((cells, width), F32, pltpu.HBM)] * 2,
        [
            pltpu.VMEM((groups, cells, LANES), F32),
            pltpu.VMEM((groups, cells, LANES), F32),
            pltpu.SemaphoreType.DMA((groups, 2)),
        ],
        "finish",
    )


def sum_over_ring(value, ring):
    if ring & (ring - 1):
        return lax.psum(value, RING)
    rounds, size = [], 1
    while size < ring:
        digits = (1, 2, 3) if 4 * size <= ring else (1,)
        rounds.append([size * d for d in digits])
        size *= len(digits) + 1
    for bits in reversed(rounds):
        value = value + sum(
            lax.ppermute(value, RING, [(i, i ^ bit) for i in range(ring)]) for bit in bits
        )
    return value


def local(positions, momenta, tile_values, tile_rows, tile_cols, tile_count, channel_coupling):
    cells, width = positions.shape
    slots, tile, _ = tile_values.shape
    channels = channel_coupling.shape[0]
    replicas = width // channels
    groups = width // LANES
    ring = lax.axis_size("row") * lax.axis_size("col")
    where = np.arange(width)
    same = jnp.asarray(
        (where[:, None] // channels == where[None] // channels).astype(ml_dtypes.bfloat16)
    )
    spread = jnp.asarray(
        (where[:, None] % channels == np.arange(channels)[None]).astype(ml_dtypes.bfloat16)
    )
    on_chip = [(i, i ^ 1) for i in range(ring)]
    off_chip = [(i, (i + 1) % ring if i % 2 else (i - 1) % ring) for i in range(ring)]
    wide = (cells, LANES)
    every = list(range(groups))
    first_pieces = [every[:-1], every[-1:]]
    second_pieces = [every[:1], every[1:]]

    def ring_index():
        return lax.axis_index("row") * lax.axis_size("col") + lax.axis_index("col")

    def far_swap(mine):
        return lax.ppermute(mine, RING, off_chip)

    def near_swap(mine):
        return lax.ppermute(mine, RING, on_chip)

    def ready(piece, done):
        return [
            t for t in every if t not in done and max(spanned(t, channels, width)) <= piece[-1]
        ]

    def keep(done, _, outs):
        outs[0][...] = done[0]

    def needed(todo, piece):
        return sorted({n for t in todo for n in spanned(t, channels, width)} - set(piece))

    xs, owns, sent = load_first(positions, first_pieces[0])
    fars = [far_swap(sent)]
    lists, more_x, more_own = make_lists(
        tile_rows, tile_cols, tile_count, positions, first_pieces[1], sent, slots, tile, ring_index
    )
    xs, owns = [*xs, *more_x], [*owns, *more_own]
    others = [near_swap(r) for r in owns]
    base, mixing = first_base(xs, momenta, same, spread, channel_coupling, channels)
    near, sent = near_fields(
        lists, tile_values, owns, others, None, more_own, [mixing], 0, "near_first"
    )
    fars.append(far_swap(sent[0]))

    fields, new_x, new_y, rounded, new_fars = {}, {}, {}, {}, []
    for p, piece in enumerate(first_pieces):
        todo = ready(piece, new_x)
        known = needed(todo, piece)
        going = second_pieces[p]
        assert going == todo
        last = p == len(first_pieces) - 1

        def work(done, ins, outs, piece=piece, todo=todo, known=known, last=last):
            held = {n: ins[1 + i][...] for i, n in enumerate(known)}
            done = [field.astype(BF16) for field in done]
            held.update(zip(piece, done))
            rest = ins[1 + len(known) :]
            for i, t in enumerate(todo):
                y_new = rest[2 * i][...] - 0.2 * mixed_of(held, ins[0], t, channels)
                x_new = jnp.clip(rest[2 * i + 1][...] + 0.5 * y_new, -1.0, 1.0)
                r_new = x_new.astype(BF16)
                outs[3 * i][...] = x_new
                outs[3 * i + 1][...] = y_new
                outs[3 * i + 2][...] = r_new
                outs[3 * len(todo)][:, lanes(i)] = r_new
            if not last:
                for i, field in enumerate(done):
                    outs[3 * len(todo) + 1 + i][...] = field

        results = far_fields(
            lists,
            tile_values,
            [near[n] for n in piece],
            fars[p],
            [mixing] + [fields[n] for n in known] + [a for t in todo for a in (base[t], xs[t])],
            [(wide, F32), (wide, F32), (wide, BF16)] * len(todo)
            + [((cells, len(todo) * LANES), BF16)]
            + ([] if last else [(wide, BF16)] * len(piece)),
            work,
            f"far_first_{p}",
        )
        for i, t in enumerate(todo):
            new_x[t], new_y[t], rounded[t] = results[3 * i : 3 * i + 3]
        new_fars.append(far_swap(results[3 * len(todo)]))
        fields.update(zip(piece, results[3 * len(todo) + 1 :]))

    xs, ys, owns = [[of[g] for g in every] for of in (new_x, new_y, rounded)]
    others = [near_swap(r) for r in owns]
    (part,) = far_fields(
        lists, tile_values, [], new_fars[0], [], [(wide, F32)], keep, "far_second_0", NEAR_FLOPS
    )
    near, _ = near_fields(lists, tile_values, owns, others, part, [], [], 0, "near_second")
    base, weights = second_base(xs, ys, owns, same, mixing, channels)
    piece = second_pieces[1]

    def last_work(done, ins, outs):
        held = [ins[groups][...]] + [field.astype(BF16) for field in done]
        for out, field in zip(outs, held[1:]):
            out[...] = field
        row = jnp.concatenate(
            [
                jnp.sum(field.astype(F32) * ref[...], axis=0, keepdims=True)
                for field, ref in zip(held, ins[:groups])
            ],
            axis=1,
        )
        row = jnp.broadcast_to(row, (replicas, width))
        lane = lax.broadcasted_iota(jnp.int32, (replicas, width), 1)
        first = lax.broadcasted_iota(jnp.int32, (replicas, width), 0) * channels
        inside = (lane >= first) & (lane < first + channels)
        total = jnp.sum(jnp.where(inside, row, 0.0), axis=1, keepdims=True)
        place = lax.broadcasted_iota(jnp.int32, (replicas, LANES), 1)
        which = lax.broadcasted_iota(jnp.int32, (replicas, LANES), 0)
        flat = jnp.sum(jnp.where(place == which, total, 0.0), axis=0, keepdims=True)
        outs[len(piece)][...] = jnp.broadcast_to(flat, (8, LANES))

    results = far_fields(
        lists,
        tile_values,
        near[1:],
        new_fars[1],
        weights,
        [(wide, BF16)] * len(piece) + [((8, LANES), F32)],
        last_work,
        "far_second_1",
        through=[near[0], *xs, *base, mixing],
    )
    fields, partial, kept = results[: len(piece)], results[len(piece)], results[len(piece) + 1 :]
    fields, kept = [kept[0], *fields], kept[1:]

    total = sum_over_ring(partial, ring)
    energy = total[0, :replicas] / jnp.sqrt(jnp.float32(cells * ring * channels))
    x_new, y_new = finish(
        fields, kept[:groups], kept[groups : 2 * groups], kept[2 * groups], channels
    )
    return (x_new, y_new, energy)


def solution(mesh):
    cells = P(("groups", "row", "col"), None)
    slots = P(("groups", "row", "col"))
    return jax.shard_map(
        local,
        mesh=mesh,
        in_specs=(cells, cells, P(("groups", "row", "col"), None, None), slots, slots, slots, P()),
        out_specs=(cells, cells, P("groups")),
        check_vma=False,
    )
```

```python
import jax
import jax.numpy as jnp
import ml_dtypes
import numpy as np
from jax import lax
from jax.experimental import pallas as pl
from jax.experimental.pallas import tpu as pltpu
from jax.sharding import PartitionSpec as P

STEPS = 2
LANES = 128
LONG, SHORT = 16, 4
VMEM_LIMIT = 14 * 1024 * 1024
NEAR_FLOPS = 4 * 10**9
F32 = jnp.float32
BF16 = jnp.bfloat16
RING = ("row", "col")


def call(body, ins, outs, scratch, name, flops=0, aliases=()):
    return pl.pallas_call(
        body,
        in_specs=[pl.BlockSpec(memory_space=pl.ANY if s is pltpu.HBM else s) for _, s in ins],
        out_specs=[pl.BlockSpec(memory_space=pl.ANY if s is pltpu.HBM else s) for *_, s in outs],
        out_shape=[
            jax.ShapeDtypeStruct(dims, kind) if s is pltpu.HBM else s(dims, kind)
            for dims, kind, s in outs
        ],
        scratch_shapes=scratch,
        input_output_aliases=dict(aliases),
        compiler_params=pltpu.CompilerParams(vmem_limit_bytes=VMEM_LIMIT),
        cost_estimate=pl.CostEstimate(
            flops=int(flops) or 1000, bytes_accessed=1000, transcendentals=0
        ),
        name=name,
    )(*[pltpu.with_memory_space_constraint(a, s) for a, s in ins])


def vmem(*arrays):
    return [(a, pltpu.VMEM) for a in arrays]


def lanes(group):
    return slice(group * LANES, (group + 1) * LANES)


def spanned(group, channels, width):
    first = group * LANES // channels * channels
    last = -(-(group + 1) * LANES // channels) * channels
    return list(range(first // LANES, -(-min(last, width) // LANES)))


def span_lanes(near):
    return slice(near[0] * LANES, (near[-1] + 1) * LANES)


def split(x):
    high = x.astype(BF16)
    return high, (x - high.astype(F32)).astype(BF16)


def bases_into(outs, xs, ys, same, step, channels):
    groups = len(xs)
    width = groups * LANES
    detune = 1.0 - (step + 1.0) / (STEPS + 1.0)
    parts = [split(x) for x in xs]
    for g in range(groups):
        near = spanned(g, channels, width)
        ones = same[span_lanes(near), lanes(g)]
        totals = sum(
            jnp.dot(
                jnp.concatenate([parts[n][k] for n in near], axis=1),
                ones,
                preferred_element_type=F32,
            )
            for k in range(2)
        )
        penalty = 0.02 * (totals - (2.0 - channels))
        outs[g][...] = ys[g] + 0.5 * (-detune * xs[g] - 0.4 * penalty)


def mixed_of(fields, mixing, group, channels):
    near = spanned(group, channels, mixing.shape[0])
    return jnp.dot(
        jnp.concatenate([fields[n] for n in near], axis=1),
        mixing[span_lanes(near), lanes(group)],
        preferred_element_type=F32,
    )


def load_first(positions, groups_of):
    cells = positions.shape[0]
    n = len(groups_of)

    def body(x_ref, *refs):
        x_outs, r_outs, sent, sems = refs[:n], refs[n : 2 * n], refs[2 * n], refs[-1]
        copies = [
            pltpu.make_async_copy(x_ref.at[:, lanes(g)], x_outs[i], sems.at[i])
            for i, g in enumerate(groups_of)
        ]
        for copy in copies:
            copy.start()
        for i, copy in enumerate(copies):
            copy.wait()
            rounded = x_outs[i][...].astype(BF16)
            r_outs[i][...] = rounded
            sent[:, lanes(i)] = rounded

    outs = call(
        body,
        [(positions, pltpu.HBM)],
        [((cells, LANES), F32, pltpu.VMEM)] * n
        + [((cells, LANES), BF16, pltpu.VMEM)] * n
        + [((cells, n * LANES), BF16, pltpu.VMEM)],
        [pltpu.SemaphoreType.DMA((n,))],
        "load_first",
    )
    return outs[:n], outs[n : 2 * n], outs[2 * n]


def section(slots, per):
    return -(-(slots + per) // (2 * SHORT)) * SHORT


def make_lists(rows, cols, count, positions, groups_of, after, slots, tile, ring_index):
    cells = positions.shape[0]
    per = cells // tile
    pairs = section(slots, per)
    n = len(groups_of)

    def body(rows_hbm, cols_hbm, count_hbm, x_ref, _, list_ref, *refs):
        x_outs, r_outs = refs[:n], refs[n : 2 * n]
        rows_ref, cols_ref, count_ref, held, sems = refs[2 * n :]
        copies = [
            pltpu.make_async_copy(*ends, sems.at[k])
            for k, ends in enumerate(
                [(rows_hbm, rows_ref), (cols_hbm, cols_ref), (count_hbm, count_ref)]
                + [(x_ref.at[:, lanes(g)], x_outs[i]) for i, g in enumerate(groups_of)]
            )
        ]
        for copy in copies:
            copy.start()
        for k in range(2 * per):
            held[k] = -1
        far_third = jnp.where(lax.rem(ring_index(), 2) == 1, 2, 0)
        for copy in copies[:3]:
            copy.wait()

        def visit(slot, totals):
            near_pairs, far_pairs = totals
            row, col = rows_ref[slot], cols_ref[slot]
            third = jnp.where(col >= 2 * per, 2, jnp.where(col >= per, 1, 0))
            source = col - third * per
            far = third == far_third
            source = jnp.where(far | (third == 1), source, source + per)
            key = row + jnp.where(far, per, 0)
            place = 2 * jnp.where(far, far_pairs + pairs, near_pairs)
            entry = slot * 65536 + source * 256 + row
            other = held[key]
            full = other >= 0
            list_ref[place] = other
            list_ref[place + 1] = entry
            held[key] = jnp.where(full, -1, entry)
            one = full.astype(jnp.int32)
            far_one = jnp.where(far, one, 0)
            return near_pairs + one - far_one, far_pairs + far_one

        totals = lax.fori_loop(0, count_ref[0], visit, (jnp.int32(0), jnp.int32(0)))
        for part, zero in enumerate((2 * per, per)):
            total = totals[part]
            start = part * pairs
            for k in range(per):
                other = held[part * per + k]
                list_ref[2 * (start + total)] = other
                list_ref[2 * (start + total) + 1] = zero * 256 + k
                total = total + (other >= 0).astype(jnp.int32)
            short_turns = (total + SHORT - 1) // SHORT

            def pad(pair, carry, start=start, zero=zero):
                for e in range(2):
                    list_ref[2 * (start + pair) + e] = zero * 256 + per
                return carry

            lax.fori_loop(total, short_turns * SHORT, pad, 0)
            list_ref[4 * pairs + 2 * part] = short_turns // (LONG // SHORT)
            list_ref[4 * pairs + 2 * part + 1] = short_turns % (LONG // SHORT)
        for i, copy in enumerate(copies[3:]):
            copy.wait()
            r_outs[i][...] = x_outs[i][...].astype(BF16)

    outs = call(
        body,
        [(a, pl.ANY) for a in (rows, cols, count)] + [(positions, pltpu.HBM)] + vmem(after),
        [((4 * pairs + 4 + 2,), jnp.int32, pltpu.SMEM)]
        + [((cells, LANES), F32, pltpu.VMEM)] * n
        + [((cells, LANES), BF16, pltpu.VMEM)] * n,
        [
            pltpu.SMEM(rows.shape, jnp.int32),
            pltpu.SMEM(cols.shape, jnp.int32),
            pltpu.SMEM(count.shape, jnp.int32),
            pltpu.SMEM((2 * per,), jnp.int32),
            pltpu.SemaphoreType.DMA((3 + n,)),
        ],
        "make_lists",
    )
    return outs[0], outs[1 : 1 + n], outs[1 + n :]


def add_pairs(part, list_ref, tiles, field, window, pairs):
    def turn(first, length):
        for u in range(length):
            place = 2 * (part * pairs + first + u)
            entries = [list_ref[place + e] for e in range(2)]
            left = jnp.concatenate([tiles[n >> 16] for n in entries], axis=1)
            right = jnp.concatenate([window[(n >> 8) & 255] for n in entries], axis=0)
            field[entries[1] & 255] += jnp.dot(left, right, preferred_element_type=F32)

    def long(i, carry):
        turn(i * LONG, LONG)
        return carry

    def short(i, carry):
        turn(long_turns * LONG + i * SHORT, SHORT)
        return carry

    long_turns = list_ref[4 * pairs + 2 * part]
    lax.fori_loop(0, long_turns, long, 0)
    lax.fori_loop(0, list_ref[4 * pairs + 2 * part + 1], short, 0)


def near_fields(lists, tiles, owns, others, far_part, sent, after, flops, name):
    slots, tile, _ = tiles.shape
    cells = owns[0].shape[0]
    groups = len(owns)
    width = groups * LANES
    per = cells // tile
    pairs = section(slots, per)
    start = [] if far_part is None else [far_part]

    def body(list_ref, tiles_ref, *refs):
        own_refs, other_refs, refs = refs[:groups], refs[groups : 2 * groups], refs[2 * groups :]
        start_refs, refs = refs[: len(start)], refs[len(start) :]
        sent_refs, refs = refs[: len(sent)], refs[len(sent) + len(after) :]
        field_outs, sent_outs, (field, window) = refs[:groups], refs[groups:-2], refs[-2:]
        for out, ref in zip(sent_outs, sent_refs):
            out[...] = ref[...]
        for g in range(groups):
            window[:per, :, lanes(g)] = own_refs[g][...].reshape(per, tile, LANES)
            window[per : 2 * per, :, lanes(g)] = other_refs[g][...].reshape(per, tile, LANES)
        window[2 * per] = jnp.zeros((tile, width), BF16)
        field[:per] = jnp.zeros((per, tile, width), F32)
        for ref in start_refs:
            field[:per, :, lanes(0)] = ref[...].reshape(per, tile, LANES)
        add_pairs(0, list_ref, tiles_ref, field, window, pairs)
        for g, out in enumerate(field_outs):
            out[...] = field[:per, :, lanes(g)].reshape(cells, LANES).astype(out.dtype)

    outs = call(
        body,
        [(lists, pltpu.SMEM)] + vmem(tiles, *owns, *others, *start, *sent, *after),
        [
            ((cells, LANES), BF16 if start and g == 0 else F32, pltpu.VMEM)
            for g in range(groups)
        ]
        + [(a.shape, BF16, pltpu.VMEM) for a in sent],
        [
            pltpu.VMEM((per + 1, tile, width), F32),
            pltpu.VMEM((2 * per + 1, tile, width), BF16),
        ],
        name,
        flops,
    )
    return outs[:groups], outs[groups:]


def far_fields(lists, tiles, nears, far, extra, outs_of, work, name, flops=0, through=()):
    slots, tile, _ = tiles.shape
    cells, width = far.shape
    per = cells // tile
    pairs = section(slots, per)
    n = width // LANES
    m = len(nears)

    def body(list_ref, tiles_ref, far_ref, *refs):
        near_refs, extra_refs = refs[:m], refs[m : m + len(extra)]
        through_refs = refs[m + len(extra) : m + len(extra) + len(through)]
        out_refs, (field, window) = refs[m + len(extra) + len(through) : -2], refs[-2:]
        window[:per] = far_ref[...].reshape(per, tile, width)
        window[per] = jnp.zeros((tile, width), BF16)
        if not near_refs:
            field[:per] = jnp.zeros((per, tile, width), F32)
        for i, ref in enumerate(near_refs):
            field[:per, :, lanes(i)] = ref[...].reshape(per, tile, LANES)
        add_pairs(1, list_ref, tiles_ref, field, window, pairs)
        done = [field[:per, :, lanes(i)].reshape(cells, LANES) for i in range(n)]
        work(done, [*extra_refs, *through_refs], out_refs[: len(outs_of)])

    return call(
        body,
        [(lists, pltpu.SMEM)] + vmem(tiles, far, *nears, *extra, *through),
        [(*out, pltpu.VMEM) for out in outs_of] + [(a.shape, a.dtype, pltpu.VMEM) for a in through],
        [pltpu.VMEM((per + 1, tile, width), F32), pltpu.VMEM((per + 1, tile, width), BF16)],
        name,
        flops,
        [(3 + m + len(extra) + i, len(outs_of) + i) for i in range(len(through))],
    )


def first_base(xs, momenta, same, spread, coupling, channels):
    cells, width = momenta.shape
    groups = len(xs)

    def body(*refs):
        x_refs, (y_ref, same_ref, spread_ref, coupling_ref) = refs[:groups], refs[groups : groups + 4]
        outs = refs[groups + 4 :]
        tall = jnp.dot(spread_ref[...], coupling_ref[...], preferred_element_type=F32).astype(BF16)
        wide = lax.dot_general(
            tall, spread_ref[...], (((1,), (1,)), ((), ())), preferred_element_type=F32
        )
        outs[groups][...] = (wide * same_ref[...].astype(F32)).astype(BF16)
        x = [ref[...] for ref in x_refs]
        y = [y_ref[:, lanes(g)] for g in range(groups)]
        bases_into(outs[:groups], x, y, same_ref, 0, channels)

    outs = call(
        body,
        vmem(*xs, momenta, same, spread, coupling),
        [((cells, LANES), F32, pltpu.VMEM)] * groups + [((width, width), BF16, pltpu.VMEM)],
        [],
        "first_base",
    )
    return outs[:groups], outs[groups]


def second_base(xs, ys, rounded, same, mixing, channels):
    groups = len(xs)
    cells = xs[0].shape[0]
    width = groups * LANES

    def body(*refs):
        x, y, r = [[ref[...] for ref in refs[k * groups : (k + 1) * groups]] for k in range(3)]
        same_ref, mixing_ref = refs[3 * groups : 3 * groups + 2]
        outs = refs[3 * groups + 2 :]
        bases_into(outs[:groups], x, y, same_ref, 1, channels)
        for g in range(groups):
            near = spanned(g, channels, width)
            outs[groups + g][...] = lax.dot_general(
                jnp.concatenate([r[n] for n in near], axis=1),
                mixing_ref[lanes(g), span_lanes(near)],
                (((1,), (1,)), ((), ())),
                preferred_element_type=F32,
            )

    outs = call(
        body,
        vmem(*xs, *ys, *rounded, same, mixing),
        [((cells, LANES), F32, pltpu.VMEM)] * (2 * groups),
        [],
        "second_base",
    )
    return outs[:groups], outs[groups:]


def finish(fields, xs, bases, mixing, channels):
    groups = len(xs)
    cells = xs[0].shape[0]
    width = groups * LANES

    def body(*refs):
        field_refs, x_refs, base_refs = [refs[k * groups : (k + 1) * groups] for k in range(3)]
        mixing_ref, x_out, y_out, token, x_buf, y_buf, sems = refs[3 * groups :]
        held = [ref[...] for ref in field_refs]
        copies = []
        for g in range(groups):
            y_new = base_refs[g][...] - 0.2 * mixed_of(held, mixing_ref, g, channels)
            y_buf[g] = y_new
            x_buf[g] = jnp.clip(x_refs[g][...] + 0.5 * y_new, -1.0, 1.0)
            for k, (buf, out) in enumerate(((y_buf, y_out), (x_buf, x_out))):
                copies.append(
                    pltpu.make_async_copy(buf.at[g], out.at[:, lanes(g)], sems.at[g, k])
                )
                copies[-1].start()
        token[...] = jnp.zeros_like(token)
        for copy in copies:
            copy.wait()

    return call(
        body,
        vmem(*fields, *xs, *bases, mixing),
        [((cells, width), F32, pltpu.HBM)] * 2 + [((8, LANES), F32, pltpu.VMEM)],
        [
            pltpu.VMEM((groups, cells, LANES), F32),
            pltpu.VMEM((groups, cells, LANES), F32),
            pltpu.SemaphoreType.DMA((groups, 2)),
        ],
        "finish",
    )


def add_up(arrays, token):
    def body(*refs):
        refs[-1][...] = sum(ref[...] for ref in refs[:-2])

    return call(
        body,
        vmem(*arrays, token),
        [(arrays[0].shape, F32, pltpu.VMEM)],
        [],
        "add_up",
    )[0]


def sum_over_ring(value, ring, token):
    if ring & (ring - 1):
        return lax.psum(value, RING)
    rounds, size = [], 1
    while size < ring:
        digits = (1, 2, 3) if 4 * size <= ring else (1,)
        rounds.append([size * d for d in digits])
        size *= len(digits) + 1
    for i, bits in enumerate(reversed(rounds)):
        parts = [value] + [
            lax.ppermute(value, RING, [(j, j ^ bit) for j in range(ring)]) for bit in bits
        ]
        value = add_up(parts, token) if i == 0 else sum(parts)
    return value


def local(positions, momenta, tile_values, tile_rows, tile_cols, tile_count, channel_coupling):
    cells, width = positions.shape
    slots, tile, _ = tile_values.shape
    channels = channel_coupling.shape[0]
    replicas = width // channels
    groups = width // LANES
    ring = lax.axis_size("row") * lax.axis_size("col")
    where = np.arange(width)
    same = jnp.asarray(
        (where[:, None] // channels == where[None] // channels).astype(ml_dtypes.bfloat16)
    )
    spread = jnp.asarray(
        (where[:, None] % channels == np.arange(channels)[None]).astype(ml_dtypes.bfloat16)
    )
    on_chip = [(i, i ^ 1) for i in range(ring)]
    off_chip = [(i, (i + 1) % ring if i % 2 else (i - 1) % ring) for i in range(ring)]
    wide = (cells, LANES)
    every = list(range(groups))
    first_pieces = [every[:-1], every[-1:]]
    second_pieces = [every[:1], every[1:]]

    def ring_index():
        return lax.axis_index("row") * lax.axis_size("col") + lax.axis_index("col")

    def far_swap(mine):
        return lax.ppermute(mine, RING, off_chip)

    def near_swap(mine):
        return lax.ppermute(mine, RING, on_chip)

    def ready(piece, done):
        return [
            t for t in every if t not in done and max(spanned(t, channels, width)) <= piece[-1]
        ]

    def keep(done, _, outs):
        outs[0][...] = done[0]

    def needed(todo, piece):
        return sorted({n for t in todo for n in spanned(t, channels, width)} - set(piece))

    xs, owns, sent = load_first(positions, first_pieces[0])
    fars = [far_swap(sent)]
    lists, more_x, more_own = make_lists(
        tile_rows, tile_cols, tile_count, positions, first_pieces[1], sent, slots, tile, ring_index
    )
    xs, owns = [*xs, *more_x], [*owns, *more_own]
    others = [near_swap(r) for r in owns]
    base, mixing = first_base(xs, momenta, same, spread, channel_coupling, channels)
    near, sent = near_fields(
        lists, tile_values, owns, others, None, more_own, [mixing], 0, "near_first"
    )
    fars.append(far_swap(sent[0]))

    fields, new_x, new_y, rounded, new_fars = {}, {}, {}, {}, []
    for p, piece in enumerate(first_pieces):
        todo = ready(piece, new_x)
        known = needed(todo, piece)
        going = second_pieces[p]
        assert going == todo
        last = p == len(first_pieces) - 1

        def work(done, ins, outs, piece=piece, todo=todo, known=known, last=last):
            held = {n: ins[1 + i][...] for i, n in enumerate(known)}
            done = [field.astype(BF16) for field in done]
            held.update(zip(piece, done))
            rest = ins[1 + len(known) :]
            for i, t in enumerate(todo):
                y_new = rest[2 * i][...] - 0.2 * mixed_of(held, ins[0], t, channels)
                x_new = jnp.clip(rest[2 * i + 1][...] + 0.5 * y_new, -1.0, 1.0)
                r_new = x_new.astype(BF16)
                outs[3 * i][...] = x_new
                outs[3 * i + 1][...] = y_new
                outs[3 * i + 2][...] = r_new
                outs[3 * len(todo)][:, lanes(i)] = r_new
            if not last:
                for i, field in enumerate(done):
                    outs[3 * len(todo) + 1 + i][...] = field

        results = far_fields(
            lists,
            tile_values,
            [near[n] for n in piece],
            fars[p],
            [mixing] + [fields[n] for n in known] + [a for t in todo for a in (base[t], xs[t])],
            [(wide, F32), (wide, F32), (wide, BF16)] * len(todo)
            + [((cells, len(todo) * LANES), BF16)]
            + ([] if last else [(wide, BF16)] * len(piece)),
            work,
            f"far_first_{p}",
        )
        for i, t in enumerate(todo):
            new_x[t], new_y[t], rounded[t] = results[3 * i : 3 * i + 3]
        new_fars.append(far_swap(results[3 * len(todo)]))
        fields.update(zip(piece, results[3 * len(todo) + 1 :]))

    xs, ys, owns = [[of[g] for g in every] for of in (new_x, new_y, rounded)]
    others = [near_swap(r) for r in owns]
    (part,) = far_fields(
        lists, tile_values, [], new_fars[0], [], [(wide, F32)], keep, "far_second_0", NEAR_FLOPS
    )
    near, _ = near_fields(lists, tile_values, owns, others, part, [], [], 0, "near_second")
    base, weights = second_base(xs, ys, owns, same, mixing, channels)
    piece = second_pieces[1]

    def last_work(done, ins, outs):
        held = [ins[groups][...]] + [field.astype(BF16) for field in done]
        for out, field in zip(outs, held[1:]):
            out[...] = field
        row = jnp.concatenate(
            [
                jnp.sum(field.astype(F32) * ref[...], axis=0, keepdims=True)
                for field, ref in zip(held, ins[:groups])
            ],
            axis=1,
        )
        row = jnp.broadcast_to(row, (replicas, width))
        lane = lax.broadcasted_iota(jnp.int32, (replicas, width), 1)
        first = lax.broadcasted_iota(jnp.int32, (replicas, width), 0) * channels
        inside = (lane >= first) & (lane < first + channels)
        total = jnp.sum(jnp.where(inside, row, 0.0), axis=1, keepdims=True)
        place = lax.broadcasted_iota(jnp.int32, (replicas, LANES), 1)
        which = lax.broadcasted_iota(jnp.int32, (replicas, LANES), 0)
        flat = jnp.sum(jnp.where(place == which, total, 0.0), axis=0, keepdims=True)
        outs[len(piece)][...] = jnp.broadcast_to(flat, (8, LANES))

    results = far_fields(
        lists,
        tile_values,
        near[1:],
        new_fars[1],
        weights,
        [(wide, BF16)] * len(piece) + [((8, LANES), F32)],
        last_work,
        "far_second_1",
        through=[near[0], *xs, *base, mixing],
    )
    fields, partial, kept = results[: len(piece)], results[len(piece)], results[len(piece) + 1 :]
    fields, kept = [kept[0], *fields], kept[1:]

    x_new, y_new, token = finish(
        fields, kept[:groups], kept[groups : 2 * groups], kept[2 * groups], channels
    )
    total = sum_over_ring(partial, ring, token)
    energy = total[0, :replicas] / jnp.sqrt(jnp.float32(cells * ring * channels))
    return (x_new, y_new, energy)


def solution(mesh):
    cells = P(("groups", "row", "col"), None)
    slots = P(("groups", "row", "col"))
    return jax.shard_map(
        local,
        mesh=mesh,
        in_specs=(cells, cells, P(("groups", "row", "col"), None, None), slots, slots, slots, P()),
        out_specs=(cells, cells, P("groups")),
        check_vma=False,
    )
```

```python
import jax
import jax.numpy as jnp
import ml_dtypes
import numpy as np
from jax import lax
from jax.experimental import pallas as pl
from jax.experimental.pallas import tpu as pltpu
from jax.sharding import PartitionSpec as P

STEPS = 2
LANES = 128
LONG, SHORT = 16, 4
VMEM_LIMIT = 14 * 1024 * 1024
NEAR_FLOPS = 4 * 10**9
F32 = jnp.float32
BF16 = jnp.bfloat16
RING = ("row", "col")


def call(body, ins, outs, scratch, name, flops=0, aliases=()):
    return pl.pallas_call(
        body,
        in_specs=[pl.BlockSpec(memory_space=pl.ANY if s is pltpu.HBM else s) for _, s in ins],
        out_specs=[pl.BlockSpec(memory_space=pl.ANY if s is pltpu.HBM else s) for *_, s in outs],
        out_shape=[
            jax.ShapeDtypeStruct(dims, kind) if s is pltpu.HBM else s(dims, kind)
            for dims, kind, s in outs
        ],
        scratch_shapes=scratch,
        input_output_aliases=dict(aliases),
        compiler_params=pltpu.CompilerParams(vmem_limit_bytes=VMEM_LIMIT),
        cost_estimate=pl.CostEstimate(
            flops=int(flops) or 1000, bytes_accessed=1000, transcendentals=0
        ),
        name=name,
    )(*[pltpu.with_memory_space_constraint(a, s) for a, s in ins])


def vmem(*arrays):
    return [(a, pltpu.VMEM) for a in arrays]


def lanes(group):
    return slice(group * LANES, (group + 1) * LANES)


def spanned(group, channels, width):
    first = group * LANES // channels * channels
    last = -(-(group + 1) * LANES // channels) * channels
    return list(range(first // LANES, -(-min(last, width) // LANES)))


def span_lanes(near):
    return slice(near[0] * LANES, (near[-1] + 1) * LANES)


def split(x):
    high = x.astype(BF16)
    return high, (x - high.astype(F32)).astype(BF16)


def bases_into(outs, xs, ys, same, step, channels):
    groups = len(xs)
    width = groups * LANES
    detune = 1.0 - (step + 1.0) / (STEPS + 1.0)
    parts = [split(x) for x in xs]
    for g in range(groups):
        near = spanned(g, channels, width)
        ones = same[span_lanes(near), lanes(g)]
        totals = sum(
            jnp.dot(
                jnp.concatenate([parts[n][k] for n in near], axis=1),
                ones,
                preferred_element_type=F32,
            )
            for k in range(2)
        )
        penalty = 0.02 * (totals - (2.0 - channels))
        outs[g][...] = ys[g] + 0.5 * (-detune * xs[g] - 0.4 * penalty)


def mixed_of(fields, mixing, group, channels):
    near = spanned(group, channels, mixing.shape[0])
    return jnp.dot(
        jnp.concatenate([fields[n] for n in near], axis=1),
        mixing[span_lanes(near), lanes(group)],
        preferred_element_type=F32,
    )


def load_first(positions, groups_of):
    cells = positions.shape[0]
    n = len(groups_of)

    def body(x_ref, *refs):
        x_outs, r_outs, sent, sems = refs[:n], refs[n : 2 * n], refs[2 * n], refs[-1]
        copies = [
            pltpu.make_async_copy(x_ref.at[:, lanes(g)], x_outs[i], sems.at[i])
            for i, g in enumerate(groups_of)
        ]
        for copy in copies:
            copy.start()
        for i, copy in enumerate(copies):
            copy.wait()
            rounded = x_outs[i][...].astype(BF16)
            r_outs[i][...] = rounded
            sent[:, lanes(i)] = rounded

    outs = call(
        body,
        [(positions, pltpu.HBM)],
        [((cells, LANES), F32, pltpu.VMEM)] * n
        + [((cells, LANES), BF16, pltpu.VMEM)] * n
        + [((cells, n * LANES), BF16, pltpu.VMEM)],
        [pltpu.SemaphoreType.DMA((n,))],
        "load_first",
    )
    return outs[:n], outs[n : 2 * n], outs[2 * n]


def section(slots, per):
    return -(-(slots + per) // (2 * SHORT)) * SHORT


def make_lists(rows, cols, count, positions, groups_of, after, slots, tile, ring_index):
    cells = positions.shape[0]
    per = cells // tile
    pairs = section(slots, per)
    n = len(groups_of)

    def body(rows_hbm, cols_hbm, count_hbm, x_ref, _, list_ref, *refs):
        x_outs, r_outs = refs[:n], refs[n : 2 * n]
        rows_ref, cols_ref, count_ref, held, sems = refs[2 * n :]
        copies = [
            pltpu.make_async_copy(*ends, sems.at[k])
            for k, ends in enumerate(
                [(rows_hbm, rows_ref), (cols_hbm, cols_ref), (count_hbm, count_ref)]
                + [(x_ref.at[:, lanes(g)], x_outs[i]) for i, g in enumerate(groups_of)]
            )
        ]
        for copy in copies:
            copy.start()
        for k in range(2 * per):
            held[k] = -1
        far_third = jnp.where(lax.rem(ring_index(), 2) == 1, 2, 0)
        for copy in copies[:3]:
            copy.wait()

        def visit(slot, totals):
            near_pairs, far_pairs = totals
            row, col = rows_ref[slot], cols_ref[slot]
            third = jnp.where(col >= 2 * per, 2, jnp.where(col >= per, 1, 0))
            source = col - third * per
            far = third == far_third
            source = jnp.where(far | (third == 1), source, source + per)
            key = row + jnp.where(far, per, 0)
            place = 2 * jnp.where(far, far_pairs + pairs, near_pairs)
            entry = slot * 65536 + source * 256 + row
            other = held[key]
            full = other >= 0
            list_ref[place] = other
            list_ref[place + 1] = entry
            held[key] = jnp.where(full, -1, entry)
            one = full.astype(jnp.int32)
            far_one = jnp.where(far, one, 0)
            return near_pairs + one - far_one, far_pairs + far_one

        totals = lax.fori_loop(0, count_ref[0], visit, (jnp.int32(0), jnp.int32(0)))
        for part, zero in enumerate((2 * per, per)):
            total = totals[part]
            start = part * pairs
            for k in range(per):
                other = held[part * per + k]
                list_ref[2 * (start + total)] = other
                list_ref[2 * (start + total) + 1] = zero * 256 + k
                total = total + (other >= 0).astype(jnp.int32)
            short_turns = (total + SHORT - 1) // SHORT

            def pad(pair, carry, start=start, zero=zero):
                for e in range(2):
                    list_ref[2 * (start + pair) + e] = zero * 256 + per
                return carry

            lax.fori_loop(total, short_turns * SHORT, pad, 0)
            list_ref[4 * pairs + 2 * part] = short_turns // (LONG // SHORT)
            list_ref[4 * pairs + 2 * part + 1] = short_turns % (LONG // SHORT)
        for i, copy in enumerate(copies[3:]):
            copy.wait()
            r_outs[i][...] = x_outs[i][...].astype(BF16)

    outs = call(
        body,
        [(a, pl.ANY) for a in (rows, cols, count)] + [(positions, pltpu.HBM)] + vmem(after),
        [((4 * pairs + 4 + 2,), jnp.int32, pltpu.SMEM)]
        + [((cells, LANES), F32, pltpu.VMEM)] * n
        + [((cells, LANES), BF16, pltpu.VMEM)] * n,
        [
            pltpu.SMEM(rows.shape, jnp.int32),
            pltpu.SMEM(cols.shape, jnp.int32),
            pltpu.SMEM(count.shape, jnp.int32),
            pltpu.SMEM((2 * per,), jnp.int32),
            pltpu.SemaphoreType.DMA((3 + n,)),
        ],
        "make_lists",
    )
    return outs[0], outs[1 : 1 + n], outs[1 + n :]


def add_pairs(part, list_ref, tiles, field, window, pairs):
    def turn(first, length):
        for u in range(length):
            place = 2 * (part * pairs + first + u)
            entries = [list_ref[place + e] for e in range(2)]
            left = jnp.concatenate([tiles[n >> 16] for n in entries], axis=1)
            right = jnp.concatenate([window[(n >> 8) & 255] for n in entries], axis=0)
            field[entries[1] & 255] += jnp.dot(left, right, preferred_element_type=F32)

    def long(i, carry):
        turn(i * LONG, LONG)
        return carry

    def short(i, carry):
        turn(long_turns * LONG + i * SHORT, SHORT)
        return carry

    long_turns = list_ref[4 * pairs + 2 * part]
    lax.fori_loop(0, long_turns, long, 0)
    lax.fori_loop(0, list_ref[4 * pairs + 2 * part + 1], short, 0)


def near_fields(lists, tiles, owns, others, far_part, sent, after, flops, name):
    slots, tile, _ = tiles.shape
    cells = owns[0].shape[0]
    groups = len(owns)
    width = groups * LANES
    per = cells // tile
    pairs = section(slots, per)
    start = [] if far_part is None else [far_part]

    def body(list_ref, tiles_ref, *refs):
        own_refs, other_refs, refs = refs[:groups], refs[groups : 2 * groups], refs[2 * groups :]
        start_refs, refs = refs[: len(start)], refs[len(start) :]
        sent_refs, refs = refs[: len(sent)], refs[len(sent) + len(after) :]
        field_outs, sent_outs, (field, window) = refs[:groups], refs[groups:-2], refs[-2:]
        for out, ref in zip(sent_outs, sent_refs):
            out[...] = ref[...]
        for g in range(groups):
            window[:per, :, lanes(g)] = own_refs[g][...].reshape(per, tile, LANES)
            window[per : 2 * per, :, lanes(g)] = other_refs[g][...].reshape(per, tile, LANES)
        window[2 * per] = jnp.zeros((tile, width), BF16)
        field[:per] = jnp.zeros((per, tile, width), F32)
        for ref in start_refs:
            field[:per, :, lanes(0)] = ref[...].reshape(per, tile, LANES)
        add_pairs(0, list_ref, tiles_ref, field, window, pairs)
        for g, out in enumerate(field_outs):
            out[...] = field[:per, :, lanes(g)].reshape(cells, LANES).astype(out.dtype)

    outs = call(
        body,
        [(lists, pltpu.SMEM)] + vmem(tiles, *owns, *others, *start, *sent, *after),
        [
            ((cells, LANES), BF16 if start and g == 0 else F32, pltpu.VMEM)
            for g in range(groups)
        ]
        + [(a.shape, BF16, pltpu.VMEM) for a in sent],
        [
            pltpu.VMEM((per + 1, tile, width), F32),
            pltpu.VMEM((2 * per + 1, tile, width), BF16),
        ],
        name,
        flops,
    )
    return outs[:groups], outs[groups:]


def far_fields(lists, tiles, nears, far, extra, outs_of, work, name, flops=0, through=()):
    slots, tile, _ = tiles.shape
    cells, width = far.shape
    per = cells // tile
    pairs = section(slots, per)
    n = width // LANES
    m = len(nears)

    def body(list_ref, tiles_ref, far_ref, *refs):
        near_refs, extra_refs = refs[:m], refs[m : m + len(extra)]
        through_refs = refs[m + len(extra) : m + len(extra) + len(through)]
        out_refs, (field, window) = refs[m + len(extra) + len(through) : -2], refs[-2:]
        window[:per] = far_ref[...].reshape(per, tile, width)
        window[per] = jnp.zeros((tile, width), BF16)
        if not near_refs:
            field[:per] = jnp.zeros((per, tile, width), F32)
        for i, ref in enumerate(near_refs):
            field[:per, :, lanes(i)] = ref[...].reshape(per, tile, LANES)
        add_pairs(1, list_ref, tiles_ref, field, window, pairs)
        done = [field[:per, :, lanes(i)].reshape(cells, LANES) for i in range(n)]
        work(done, [*extra_refs, *through_refs], out_refs[: len(outs_of)])

    return call(
        body,
        [(lists, pltpu.SMEM)] + vmem(tiles, far, *nears, *extra, *through),
        [(*out, pltpu.VMEM) for out in outs_of] + [(a.shape, a.dtype, pltpu.VMEM) for a in through],
        [pltpu.VMEM((per + 1, tile, width), F32), pltpu.VMEM((per + 1, tile, width), BF16)],
        name,
        flops,
        [(3 + m + len(extra) + i, len(outs_of) + i) for i in range(len(through))],
    )


def first_base(xs, momenta, same, spread, coupling, channels):
    cells, width = momenta.shape
    groups = len(xs)

    def body(*refs):
        x_refs, (y_ref, same_ref, spread_ref, coupling_ref) = refs[:groups], refs[groups : groups + 4]
        outs = refs[groups + 4 :]
        tall = jnp.dot(spread_ref[...], coupling_ref[...], preferred_element_type=F32).astype(BF16)
        wide = lax.dot_general(
            tall, spread_ref[...], (((1,), (1,)), ((), ())), preferred_element_type=F32
        )
        outs[groups][...] = (wide * same_ref[...].astype(F32)).astype(BF16)
        x = [ref[...] for ref in x_refs]
        y = [y_ref[:, lanes(g)] for g in range(groups)]
        bases_into(outs[:groups], x, y, same_ref, 0, channels)

    outs = call(
        body,
        vmem(*xs, momenta, same, spread, coupling),
        [((cells, LANES), F32, pltpu.VMEM)] * groups + [((width, width), BF16, pltpu.VMEM)],
        [],
        "first_base",
    )
    return outs[:groups], outs[groups]


def second_base(xs, ys, rounded, same, mixing, channels):
    groups = len(xs)
    cells = xs[0].shape[0]
    width = groups * LANES

    def body(*refs):
        x, y, r = [[ref[...] for ref in refs[k * groups : (k + 1) * groups]] for k in range(3)]
        same_ref, mixing_ref = refs[3 * groups : 3 * groups + 2]
        outs = refs[3 * groups + 2 :]
        bases_into(outs[:groups], x, y, same_ref, 1, channels)
        for g in range(groups):
            near = spanned(g, channels, width)
            outs[groups + g][...] = lax.dot_general(
                jnp.concatenate([r[n] for n in near], axis=1),
                mixing_ref[lanes(g), span_lanes(near)],
                (((1,), (1,)), ((), ())),
                preferred_element_type=F32,
            )

    outs = call(
        body,
        vmem(*xs, *ys, *rounded, same, mixing),
        [((cells, LANES), F32, pltpu.VMEM)] * (2 * groups),
        [],
        "second_base",
    )
    return outs[:groups], outs[groups:]


def finish(here, fields, xs, bases, mixing, channels, outputs, name):
    groups = len(xs)
    cells = xs[0].shape[0]
    width = groups * LANES

    def body(*refs):
        field_refs, x_refs, base_refs = [refs[k * groups : (k + 1) * groups] for k in range(3)]
        mixing_ref = refs[3 * groups]
        x_out, y_out, token, x_buf, y_buf, sems = refs[-6:]
        token[...] = jnp.zeros_like(token)

        @pl.when(here())
        def _():
            held = [ref[...] for ref in field_refs]
            copies = []
            for g in range(groups):
                y_new = base_refs[g][...] - 0.2 * mixed_of(held, mixing_ref, g, channels)
                y_buf[g] = y_new
                x_buf[g] = jnp.clip(x_refs[g][...] + 0.5 * y_new, -1.0, 1.0)
                for k, (buf, out) in enumerate(((y_buf, y_out), (x_buf, x_out))):
                    copies.append(
                        pltpu.make_async_copy(buf.at[g], out.at[:, lanes(g)], sems.at[g, k])
                    )
                    copies[-1].start()
            for copy in copies:
                copy.wait()

    ins = vmem(*fields, *xs, *bases, mixing)
    return call(
        body,
        ins + [(a, pltpu.HBM) for a in outputs],
        [((cells, width), F32, pltpu.HBM)] * 2 + [((8, LANES), F32, pltpu.VMEM)],
        [
            pltpu.VMEM((groups, cells, LANES), F32),
            pltpu.VMEM((groups, cells, LANES), F32),
            pltpu.SemaphoreType.DMA((groups, 2)),
        ],
        name,
        0,
        [(len(ins) + i, i) for i in range(len(outputs))],
    )


def add_up(arrays, token):
    def body(*refs):
        refs[-1][...] = sum(ref[...] for ref in refs[:-2])

    return call(
        body,
        vmem(*arrays, token),
        [(arrays[0].shape, F32, pltpu.VMEM)],
        [],
        "add_up",
    )[0]


def sum_over_ring(value, ring, token):
    if ring & (ring - 1):
        return lax.psum(value, RING)
    rounds, size = [], 1
    while size < ring:
        digits = (1, 2, 3) if 4 * size <= ring else (1,)
        rounds.append([size * d for d in digits])
        size *= len(digits) + 1
    for i, bits in enumerate(reversed(rounds)):
        parts = [value] + [
            lax.ppermute(value, RING, [(j, j ^ bit) for j in range(ring)]) for bit in bits
        ]
        value = add_up(parts, token) if i == 0 else sum(parts)
    return value


def local(positions, momenta, tile_values, tile_rows, tile_cols, tile_count, channel_coupling):
    cells, width = positions.shape
    slots, tile, _ = tile_values.shape
    channels = channel_coupling.shape[0]
    replicas = width // channels
    groups = width // LANES
    ring = lax.axis_size("row") * lax.axis_size("col")
    where = np.arange(width)
    same = jnp.asarray(
        (where[:, None] // channels == where[None] // channels).astype(ml_dtypes.bfloat16)
    )
    spread = jnp.asarray(
        (where[:, None] % channels == np.arange(channels)[None]).astype(ml_dtypes.bfloat16)
    )
    on_chip = [(i, i ^ 1) for i in range(ring)]
    off_chip = [(i, (i + 1) % ring if i % 2 else (i - 1) % ring) for i in range(ring)]
    wide = (cells, LANES)
    every = list(range(groups))
    first_pieces = [every[:-1], every[-1:]]
    second_pieces = [every[:1], every[1:]]

    def ring_index():
        return lax.axis_index("row") * lax.axis_size("col") + lax.axis_index("col")

    def far_swap(mine):
        return lax.ppermute(mine, RING, off_chip)

    def near_swap(mine):
        return lax.ppermute(mine, RING, on_chip)

    def ready(piece, done):
        return [
            t for t in every if t not in done and max(spanned(t, channels, width)) <= piece[-1]
        ]

    def keep(done, _, outs):
        outs[0][...] = done[0]

    def needed(todo, piece):
        return sorted({n for t in todo for n in spanned(t, channels, width)} - set(piece))

    xs, owns, sent = load_first(positions, first_pieces[0])
    fars = [far_swap(sent)]
    lists, more_x, more_own = make_lists(
        tile_rows, tile_cols, tile_count, positions, first_pieces[1], sent, slots, tile, ring_index
    )
    xs, owns = [*xs, *more_x], [*owns, *more_own]
    others = [near_swap(r) for r in owns]
    base, mixing = first_base(xs, momenta, same, spread, channel_coupling, channels)
    near, sent = near_fields(
        lists, tile_values, owns, others, None, more_own, [mixing], 0, "near_first"
    )
    fars.append(far_swap(sent[0]))

    fields, new_x, new_y, rounded, new_fars = {}, {}, {}, {}, []
    for p, piece in enumerate(first_pieces):
        todo = ready(piece, new_x)
        known = needed(todo, piece)
        going = second_pieces[p]
        assert going == todo
        last = p == len(first_pieces) - 1

        def work(done, ins, outs, piece=piece, todo=todo, known=known, last=last):
            held = {n: ins[1 + i][...] for i, n in enumerate(known)}
            done = [field.astype(BF16) for field in done]
            held.update(zip(piece, done))
            rest = ins[1 + len(known) :]
            for i, t in enumerate(todo):
                y_new = rest[2 * i][...] - 0.2 * mixed_of(held, ins[0], t, channels)
                x_new = jnp.clip(rest[2 * i + 1][...] + 0.5 * y_new, -1.0, 1.0)
                r_new = x_new.astype(BF16)
                outs[3 * i][...] = x_new
                outs[3 * i + 1][...] = y_new
                outs[3 * i + 2][...] = r_new
                outs[3 * len(todo)][:, lanes(i)] = r_new
            if not last:
                for i, field in enumerate(done):
                    outs[3 * len(todo) + 1 + i][...] = field

        results = far_fields(
            lists,
            tile_values,
            [near[n] for n in piece],
            fars[p],
            [mixing] + [fields[n] for n in known] + [a for t in todo for a in (base[t], xs[t])],
            [(wide, F32), (wide, F32), (wide, BF16)] * len(todo)
            + [((cells, len(todo) * LANES), BF16)]
            + ([] if last else [(wide, BF16)] * len(piece)),
            work,
            f"far_first_{p}",
        )
        for i, t in enumerate(todo):
            new_x[t], new_y[t], rounded[t] = results[3 * i : 3 * i + 3]
        new_fars.append(far_swap(results[3 * len(todo)]))
        fields.update(zip(piece, results[3 * len(todo) + 1 :]))

    xs, ys, owns = [[of[g] for g in every] for of in (new_x, new_y, rounded)]
    others = [near_swap(r) for r in owns]
    (part,) = far_fields(
        lists, tile_values, [], new_fars[0], [], [(wide, F32)], keep, "far_second_0", NEAR_FLOPS
    )
    near, _ = near_fields(lists, tile_values, owns, others, part, [], [], 0, "near_second")
    base, weights = second_base(xs, ys, owns, same, mixing, channels)
    piece = second_pieces[1]

    def last_work(done, ins, outs):
        held = [ins[groups][...]] + [field.astype(BF16) for field in done]
        for out, field in zip(outs, held[1:]):
            out[...] = field
        row = jnp.concatenate(
            [
                jnp.sum(field.astype(F32) * ref[...], axis=0, keepdims=True)
                for field, ref in zip(held, ins[:groups])
            ],
            axis=1,
        )
        row = jnp.broadcast_to(row, (replicas, width))
        lane = lax.broadcasted_iota(jnp.int32, (replicas, width), 1)
        first = lax.broadcasted_iota(jnp.int32, (replicas, width), 0) * channels
        inside = (lane >= first) & (lane < first + channels)
        total = jnp.sum(jnp.where(inside, row, 0.0), axis=1, keepdims=True)
        place = lax.broadcasted_iota(jnp.int32, (replicas, LANES), 1)
        which = lax.broadcasted_iota(jnp.int32, (replicas, LANES), 0)
        flat = jnp.sum(jnp.where(place == which, total, 0.0), axis=0, keepdims=True)
        outs[len(piece)][...] = jnp.broadcast_to(flat, (8, LANES))

    results = far_fields(
        lists,
        tile_values,
        near[1:],
        new_fars[1],
        weights,
        [(wide, BF16)] * len(piece) + [((8, LANES), F32)],
        last_work,
        "far_second_1",
        through=[near[0], *xs, *base, mixing],
    )
    fields, partial, kept = results[: len(piece)], results[len(piece)], results[len(piece) + 1 :]
    fields, kept = [kept[0], *fields], kept[1:]

    def early():
        return ((ring_index() + 1) // 2) % 2 == 0

    def late():
        return ((ring_index() + 1) // 2) % 2 == 1

    rest = (fields, kept[:groups], kept[groups : 2 * groups], kept[2 * groups], channels)
    *outputs, token = finish(early, *rest, [], "finish_early")
    total = sum_over_ring(partial, ring, token)
    energy = total[0, :replicas] / jnp.sqrt(jnp.float32(cells * ring * channels))
    x_new, y_new, _ = finish(late, *rest, outputs, "finish_late")
    return (x_new, y_new, energy)


def solution(mesh):
    cells = P(("groups", "row", "col"), None)
    slots = P(("groups", "row", "col"))
    return jax.shard_map(
        local,
        mesh=mesh,
        in_specs=(cells, cells, P(("groups", "row", "col"), None, None), slots, slots, slots, P()),
        out_specs=(cells, cells, P("groups")),
        check_vma=False,
    )
```

```python
import jax
import jax.numpy as jnp
import ml_dtypes
import numpy as np
from jax import lax
from jax.experimental import pallas as pl
from jax.experimental.pallas import tpu as pltpu
from jax.sharding import PartitionSpec as P

STEPS = 2
LANES = 128
LONG, SHORT = 16, 4
VMEM_LIMIT = 14 * 1024 * 1024
NEAR_FLOPS = 4 * 10**9
F32 = jnp.float32
BF16 = jnp.bfloat16
RING = ("row", "col")


def call(body, ins, outs, scratch, name, flops=0, aliases=()):
    return pl.pallas_call(
        body,
        in_specs=[pl.BlockSpec(memory_space=pl.ANY if s is pltpu.HBM else s) for _, s in ins],
        out_specs=[pl.BlockSpec(memory_space=pl.ANY if s is pltpu.HBM else s) for *_, s in outs],
        out_shape=[
            jax.ShapeDtypeStruct(dims, kind) if s is pltpu.HBM else s(dims, kind)
            for dims, kind, s in outs
        ],
        scratch_shapes=scratch,
        input_output_aliases=dict(aliases),
        compiler_params=pltpu.CompilerParams(vmem_limit_bytes=VMEM_LIMIT),
        cost_estimate=pl.CostEstimate(
            flops=int(flops) or 1000, bytes_accessed=1000, transcendentals=0
        ),
        name=name,
    )(*[pltpu.with_memory_space_constraint(a, s) for a, s in ins])


def vmem(*arrays):
    return [(a, pltpu.VMEM) for a in arrays]


def lanes(group):
    return slice(group * LANES, (group + 1) * LANES)


def spanned(group, channels, width):
    first = group * LANES // channels * channels
    last = -(-(group + 1) * LANES // channels) * channels
    return list(range(first // LANES, -(-min(last, width) // LANES)))


def span_lanes(near):
    return slice(near[0] * LANES, (near[-1] + 1) * LANES)


def split(x):
    high = x.astype(BF16)
    return high, (x - high.astype(F32)).astype(BF16)


def bases_into(outs, xs, ys, same, step, channels):
    groups = len(xs)
    width = groups * LANES
    detune = 1.0 - (step + 1.0) / (STEPS + 1.0)
    parts = [split(x) for x in xs]
    for g in range(groups):
        near = spanned(g, channels, width)
        ones = same[span_lanes(near), lanes(g)]
        totals = sum(
            jnp.dot(
                jnp.concatenate([parts[n][k] for n in near], axis=1),
                ones,
                preferred_element_type=F32,
            )
            for k in range(2)
        )
        penalty = 0.02 * (totals - (2.0 - channels))
        outs[g][...] = ys[g] + 0.5 * (-detune * xs[g] - 0.4 * penalty)


def mixed_of(fields, mixing, group, channels):
    near = spanned(group, channels, mixing.shape[0])
    return jnp.dot(
        jnp.concatenate([fields[n] for n in near], axis=1),
        mixing[span_lanes(near), lanes(group)],
        preferred_element_type=F32,
    )


def load_first(positions, groups_of):
    cells = positions.shape[0]
    n = len(groups_of)

    def body(x_ref, *refs):
        x_outs, r_outs, sent, sems = refs[:n], refs[n : 2 * n], refs[2 * n], refs[-1]
        copies = [
            pltpu.make_async_copy(x_ref.at[:, lanes(g)], x_outs[i], sems.at[i])
            for i, g in enumerate(groups_of)
        ]
        for copy in copies:
            copy.start()
        for i, copy in enumerate(copies):
            copy.wait()
            rounded = x_outs[i][...].astype(BF16)
            r_outs[i][...] = rounded
            sent[:, lanes(i)] = rounded

    outs = call(
        body,
        [(positions, pltpu.HBM)],
        [((cells, LANES), F32, pltpu.VMEM)] * n
        + [((cells, LANES), BF16, pltpu.VMEM)] * n
        + [((cells, n * LANES), BF16, pltpu.VMEM)],
        [pltpu.SemaphoreType.DMA((n,))],
        "load_first",
    )
    return outs[:n], outs[n : 2 * n], outs[2 * n]


def section(slots, per):
    return -(-(slots + per) // (2 * SHORT)) * SHORT


def make_lists(rows, cols, count, positions, groups_of, after, slots, tile, ring_index):
    cells = positions.shape[0]
    per = cells // tile
    pairs = section(slots, per)
    n = len(groups_of)

    def body(rows_hbm, cols_hbm, count_hbm, x_ref, _, list_ref, *refs):
        x_outs, r_outs = refs[:n], refs[n : 2 * n]
        rows_ref, cols_ref, count_ref, held, sems = refs[2 * n :]
        copies = [
            pltpu.make_async_copy(*ends, sems.at[k])
            for k, ends in enumerate(
                [(rows_hbm, rows_ref), (cols_hbm, cols_ref), (count_hbm, count_ref)]
                + [(x_ref.at[:, lanes(g)], x_outs[i]) for i, g in enumerate(groups_of)]
            )
        ]
        for copy in copies:
            copy.start()
        for k in range(2 * per):
            held[k] = -1
        far_third = jnp.where(lax.rem(ring_index(), 2) == 1, 2, 0)
        for copy in copies[:3]:
            copy.wait()

        def visit(slot, totals):
            near_pairs, far_pairs = totals
            row, col = rows_ref[slot], cols_ref[slot]
            third = jnp.where(col >= 2 * per, 2, jnp.where(col >= per, 1, 0))
            source = col - third * per
            far = third == far_third
            source = jnp.where(far | (third == 1), source, source + per)
            key = row + jnp.where(far, per, 0)
            place = 2 * jnp.where(far, far_pairs + pairs, near_pairs)
            entry = slot * 65536 + source * 256 + row
            other = held[key]
            full = other >= 0
            list_ref[place] = other
            list_ref[place + 1] = entry
            held[key] = jnp.where(full, -1, entry)
            one = full.astype(jnp.int32)
            far_one = jnp.where(far, one, 0)
            return near_pairs + one - far_one, far_pairs + far_one

        totals = lax.fori_loop(0, count_ref[0], visit, (jnp.int32(0), jnp.int32(0)))
        for part, zero in enumerate((2 * per, per)):
            total = totals[part]
            start = part * pairs
            for k in range(per):
                other = held[part * per + k]
                list_ref[2 * (start + total)] = other
                list_ref[2 * (start + total) + 1] = zero * 256 + k
                total = total + (other >= 0).astype(jnp.int32)
            short_turns = (total + SHORT - 1) // SHORT

            def pad(pair, carry, start=start, zero=zero):
                for e in range(2):
                    list_ref[2 * (start + pair) + e] = zero * 256 + per
                return carry

            lax.fori_loop(total, short_turns * SHORT, pad, 0)
            list_ref[4 * pairs + 2 * part] = short_turns // (LONG // SHORT)
            list_ref[4 * pairs + 2 * part + 1] = short_turns % (LONG // SHORT)
        for i, copy in enumerate(copies[3:]):
            copy.wait()
            r_outs[i][...] = x_outs[i][...].astype(BF16)

    outs = call(
        body,
        [(a, pl.ANY) for a in (rows, cols, count)] + [(positions, pltpu.HBM)] + vmem(after),
        [((4 * pairs + 4 + 2,), jnp.int32, pltpu.SMEM)]
        + [((cells, LANES), F32, pltpu.VMEM)] * n
        + [((cells, LANES), BF16, pltpu.VMEM)] * n,
        [
            pltpu.SMEM(rows.shape, jnp.int32),
            pltpu.SMEM(cols.shape, jnp.int32),
            pltpu.SMEM(count.shape, jnp.int32),
            pltpu.SMEM((2 * per,), jnp.int32),
            pltpu.SemaphoreType.DMA((3 + n,)),
        ],
        "make_lists",
    )
    return outs[0], outs[1 : 1 + n], outs[1 + n :]


def add_pairs(part, list_ref, tiles, field, window, pairs):
    def turn(first, length):
        for u in range(length):
            place = 2 * (part * pairs + first + u)
            entries = [list_ref[place + e] for e in range(2)]
            left = jnp.concatenate([tiles[n >> 16] for n in entries], axis=1)
            right = jnp.concatenate([window[(n >> 8) & 255] for n in entries], axis=0)
            field[entries[1] & 255] += jnp.dot(left, right, preferred_element_type=F32)

    def long(i, carry):
        turn(i * LONG, LONG)
        return carry

    def short(i, carry):
        turn(long_turns * LONG + i * SHORT, SHORT)
        return carry

    long_turns = list_ref[4 * pairs + 2 * part]
    lax.fori_loop(0, long_turns, long, 0)
    lax.fori_loop(0, list_ref[4 * pairs + 2 * part + 1], short, 0)


def near_fields(lists, tiles, owns, others, far_part, sent, after, flops, name):
    slots, tile, _ = tiles.shape
    cells = owns[0].shape[0]
    groups = len(owns)
    width = groups * LANES
    per = cells // tile
    pairs = section(slots, per)
    start = [] if far_part is None else [far_part]

    def body(list_ref, tiles_ref, *refs):
        own_refs, other_refs, refs = refs[:groups], refs[groups : 2 * groups], refs[2 * groups :]
        start_refs, refs = refs[: len(start)], refs[len(start) :]
        sent_refs, refs = refs[: len(sent)], refs[len(sent) + len(after) :]
        field_outs, sent_outs, (field, window) = refs[:groups], refs[groups:-2], refs[-2:]
        for out, ref in zip(sent_outs, sent_refs):
            out[...] = ref[...]
        for g in range(groups):
            window[:per, :, lanes(g)] = own_refs[g][...].reshape(per, tile, LANES)
            window[per : 2 * per, :, lanes(g)] = other_refs[g][...].reshape(per, tile, LANES)
        window[2 * per] = jnp.zeros((tile, width), BF16)
        field[:per] = jnp.zeros((per, tile, width), F32)
        for ref in start_refs:
            field[:per, :, lanes(0)] = ref[...].reshape(per, tile, LANES)
        add_pairs(0, list_ref, tiles_ref, field, window, pairs)
        for g, out in enumerate(field_outs):
            out[...] = field[:per, :, lanes(g)].reshape(cells, LANES).astype(out.dtype)

    outs = call(
        body,
        [(lists, pltpu.SMEM)] + vmem(tiles, *owns, *others, *start, *sent, *after),
        [
            ((cells, LANES), BF16 if start and g == 0 else F32, pltpu.VMEM)
            for g in range(groups)
        ]
        + [(a.shape, BF16, pltpu.VMEM) for a in sent],
        [
            pltpu.VMEM((per + 1, tile, width), F32),
            pltpu.VMEM((2 * per + 1, tile, width), BF16),
        ],
        name,
        flops,
    )
    return outs[:groups], outs[groups:]


def far_fields(lists, tiles, nears, far, extra, outs_of, work, name, flops=0, through=()):
    slots, tile, _ = tiles.shape
    cells, width = far.shape
    per = cells // tile
    pairs = section(slots, per)
    n = width // LANES
    m = len(nears)

    def body(list_ref, tiles_ref, far_ref, *refs):
        near_refs, extra_refs = refs[:m], refs[m : m + len(extra)]
        through_refs = refs[m + len(extra) : m + len(extra) + len(through)]
        out_refs, (field, window) = refs[m + len(extra) + len(through) : -2], refs[-2:]
        window[:per] = far_ref[...].reshape(per, tile, width)
        window[per] = jnp.zeros((tile, width), BF16)
        if not near_refs:
            field[:per] = jnp.zeros((per, tile, width), F32)
        for i, ref in enumerate(near_refs):
            field[:per, :, lanes(i)] = ref[...].reshape(per, tile, LANES)
        add_pairs(1, list_ref, tiles_ref, field, window, pairs)
        done = [field[:per, :, lanes(i)].reshape(cells, LANES) for i in range(n)]
        work(done, [*extra_refs, *through_refs], out_refs[: len(outs_of)])

    return call(
        body,
        [(lists, pltpu.SMEM)] + vmem(tiles, far, *nears, *extra, *through),
        [(*out, pltpu.VMEM) for out in outs_of] + [(a.shape, a.dtype, pltpu.VMEM) for a in through],
        [pltpu.VMEM((per + 1, tile, width), F32), pltpu.VMEM((per + 1, tile, width), BF16)],
        name,
        flops,
        [(3 + m + len(extra) + i, len(outs_of) + i) for i in range(len(through))],
    )


def first_base(xs, momenta, same, spread, coupling, channels):
    cells, width = momenta.shape
    groups = len(xs)

    def body(*refs):
        x_refs, (y_ref, same_ref, spread_ref, coupling_ref) = refs[:groups], refs[groups : groups + 4]
        outs = refs[groups + 4 :]
        tall = jnp.dot(spread_ref[...], coupling_ref[...], preferred_element_type=F32).astype(BF16)
        wide = lax.dot_general(
            tall, spread_ref[...], (((1,), (1,)), ((), ())), preferred_element_type=F32
        )
        outs[groups][...] = (wide * same_ref[...].astype(F32)).astype(BF16)
        x = [ref[...] for ref in x_refs]
        y = [y_ref[:, lanes(g)] for g in range(groups)]
        bases_into(outs[:groups], x, y, same_ref, 0, channels)

    outs = call(
        body,
        vmem(*xs, momenta, same, spread, coupling),
        [((cells, LANES), F32, pltpu.VMEM)] * groups + [((width, width), BF16, pltpu.VMEM)],
        [],
        "first_base",
    )
    return outs[:groups], outs[groups]


def updated(field_mixed, base, x):
    y_new = base - 0.2 * field_mixed
    return jnp.clip(x + 0.5 * y_new, -1.0, 1.0), y_new


def second_base(xs, ys, later, fields, first_base, first_x, rounded, same, mixing, channels):
    groups = len(rounded)
    cells = rounded[0].shape[0]
    width = groups * LANES
    done, m = len(xs), len(later)

    def body(*refs):
        refs = list(refs)

        def take(n):
            taken = refs[:n]
            del refs[:n]
            return taken

        x = [ref[...] for ref in take(done)]
        y = [ref[...] for ref in take(done)]
        held = [ref[...] for ref in take(groups)]
        base_refs, x_refs = take(m), take(m)
        r = [ref[...] for ref in take(groups)]
        same_ref, mixing_ref = take(2)
        for i, t in enumerate(later):
            x_new, y_new = updated(
                mixed_of(held, mixing_ref, t, channels), base_refs[i][...], x_refs[i][...]
            )
            x.append(x_new)
            y.append(y_new)
            refs[2 * groups + i][...] = x_new
        bases_into(refs[:groups], x, y, same_ref, 1, channels)
        for g in range(groups):
            near = spanned(g, channels, width)
            refs[groups + g][...] = lax.dot_general(
                jnp.concatenate([r[n] for n in near], axis=1),
                mixing_ref[lanes(g), span_lanes(near)],
                (((1,), (1,)), ((), ())),
                preferred_element_type=F32,
            )

    outs = call(
        body,
        vmem(*xs, *ys, *fields, *first_base, *first_x, *rounded, same, mixing),
        [((cells, LANES), F32, pltpu.VMEM)] * (2 * groups + m),
        [],
        "second_base",
    )
    return outs[:groups], outs[groups : 2 * groups], outs[2 * groups :]


def finish(fields, xs, bases, mixing, channels):
    groups = len(xs)
    cells = xs[0].shape[0]
    width = groups * LANES

    def body(*refs):
        field_refs, x_refs, base_refs = [refs[k * groups : (k + 1) * groups] for k in range(3)]
        mixing_ref, x_out, y_out, token, x_buf, y_buf, sems = refs[3 * groups :]
        held = [ref[...] for ref in field_refs]
        copies = []
        for g in range(groups):
            y_new = base_refs[g][...] - 0.2 * mixed_of(held, mixing_ref, g, channels)
            y_buf[g] = y_new
            x_buf[g] = jnp.clip(x_refs[g][...] + 0.5 * y_new, -1.0, 1.0)
            for k, (buf, out) in enumerate(((y_buf, y_out), (x_buf, x_out))):
                copies.append(
                    pltpu.make_async_copy(buf.at[g], out.at[:, lanes(g)], sems.at[g, k])
                )
                copies[-1].start()
        token[...] = jnp.zeros_like(token)
        for copy in copies:
            copy.wait()

    return call(
        body,
        vmem(*fields, *xs, *bases, mixing),
        [((cells, width), F32, pltpu.HBM)] * 2 + [((8, LANES), F32, pltpu.VMEM)],
        [
            pltpu.VMEM((groups, cells, LANES), F32),
            pltpu.VMEM((groups, cells, LANES), F32),
            pltpu.SemaphoreType.DMA((groups, 2)),
        ],
        "finish",
    )


def add_up(arrays, token):
    def body(*refs):
        refs[-1][...] = sum(ref[...] for ref in refs[:-2])

    return call(
        body,
        vmem(*arrays, token),
        [(arrays[0].shape, F32, pltpu.VMEM)],
        [],
        "add_up",
    )[0]


def sum_over_ring(value, ring, token):
    if ring & (ring - 1):
        return lax.psum(value, RING)
    rounds, size = [], 1
    while size < ring:
        digits = (1, 2, 3) if 4 * size <= ring else (1,)
        rounds.append([size * d for d in digits])
        size *= len(digits) + 1
    for i, bits in enumerate(reversed(rounds)):
        parts = [value] + [
            lax.ppermute(value, RING, [(j, j ^ bit) for j in range(ring)]) for bit in bits
        ]
        value = add_up(parts, token) if i == 0 else sum(parts)
    return value


def local(positions, momenta, tile_values, tile_rows, tile_cols, tile_count, channel_coupling):
    cells, width = positions.shape
    slots, tile, _ = tile_values.shape
    channels = channel_coupling.shape[0]
    replicas = width // channels
    groups = width // LANES
    ring = lax.axis_size("row") * lax.axis_size("col")
    where = np.arange(width)
    same = jnp.asarray(
        (where[:, None] // channels == where[None] // channels).astype(ml_dtypes.bfloat16)
    )
    spread = jnp.asarray(
        (where[:, None] % channels == np.arange(channels)[None]).astype(ml_dtypes.bfloat16)
    )
    on_chip = [(i, i ^ 1) for i in range(ring)]
    off_chip = [(i, (i + 1) % ring if i % 2 else (i - 1) % ring) for i in range(ring)]
    wide = (cells, LANES)
    every = list(range(groups))
    first_pieces = [every[:-1], every[-1:]]
    second_pieces = [every[:1], every[1:]]

    def ring_index():
        return lax.axis_index("row") * lax.axis_size("col") + lax.axis_index("col")

    def far_swap(mine):
        return lax.ppermute(mine, RING, off_chip)

    def near_swap(mine):
        return lax.ppermute(mine, RING, on_chip)

    def ready(piece, done):
        return [
            t for t in every if t not in done and max(spanned(t, channels, width)) <= piece[-1]
        ]

    def keep(done, _, outs):
        outs[0][...] = done[0]

    def needed(todo, piece):
        return sorted({n for t in todo for n in spanned(t, channels, width)} - set(piece))

    xs, owns, sent = load_first(positions, first_pieces[0])
    fars = [far_swap(sent)]
    lists, more_x, more_own = make_lists(
        tile_rows, tile_cols, tile_count, positions, first_pieces[1], sent, slots, tile, ring_index
    )
    xs, owns = [*xs, *more_x], [*owns, *more_own]
    others = [near_swap(r) for r in owns]
    base, mixing = first_base(xs, momenta, same, spread, channel_coupling, channels)
    near, sent = near_fields(
        lists, tile_values, owns, others, None, more_own, [mixing], 0, "near_first"
    )
    fars.append(far_swap(sent[0]))

    fields, new_x, new_y, rounded, new_fars = {}, [], [], {}, []
    for p, piece in enumerate(first_pieces):
        last = p == len(first_pieces) - 1
        todo = ready(piece, rounded)
        known = needed(todo, piece)
        assert second_pieces[p] == todo

        def work(done, ins, outs, piece=piece, todo=todo, known=known, last=last):
            held = {n: ins[1 + i][...] for i, n in enumerate(known)}
            done = [field.astype(BF16) for field in done]
            held.update(zip(piece, done))
            rest = ins[1 + len(known) :]
            for i, t in enumerate(todo):
                x_new, y_new = updated(
                    mixed_of(held, ins[0], t, channels), rest[2 * i][...], rest[2 * i + 1][...]
                )
                r_new = x_new.astype(BF16)
                outs[0][:, lanes(i)] = r_new
                outs[1 + i][...] = r_new
                if not last:
                    outs[1 + len(todo) + len(piece) + 2 * i][...] = x_new
                    outs[2 + len(todo) + len(piece) + 2 * i][...] = y_new
            for i, field in enumerate(done):
                outs[1 + len(todo) + i][...] = field

        results = far_fields(
            lists,
            tile_values,
            [near[n] for n in piece],
            fars[p],
            [mixing] + [fields[n] for n in known] + [a for t in todo for a in (base[t], xs[t])],
            [((cells, len(todo) * LANES), BF16)]
            + [(wide, BF16)] * (len(todo) + len(piece))
            + ([] if last else [(wide, F32)] * (2 * len(todo))),
            work,
            f"far_first_{p}",
        )
        new_fars.append(far_swap(results[0]))
        rounded.update(zip(todo, results[1:]))
        fields.update(zip(piece, results[1 + len(todo) :]))
        new_x += results[1 + len(todo) + len(piece) :: 2]
        new_y += results[2 + len(todo) + len(piece) :: 2]

    owns = [rounded[g] for g in every]
    others = [near_swap(r) for r in owns]
    (part,) = far_fields(
        lists, tile_values, [], new_fars[0], [], [(wide, F32)], keep, "far_second_0", NEAR_FLOPS
    )
    near, _ = near_fields(lists, tile_values, owns, others, part, [], [], 0, "near_second")
    later = second_pieces[1]
    base, weights, more_x = second_base(
        new_x,
        new_y,
        later,
        [fields[g] for g in every],
        [base[t] for t in later],
        [xs[t] for t in later],
        owns,
        same,
        mixing,
        channels,
    )
    xs = [*new_x, *more_x]
    piece = second_pieces[1]

    def last_work(done, ins, outs):
        held = [ins[groups][...]] + [field.astype(BF16) for field in done]
        for out, field in zip(outs, held[1:]):
            out[...] = field
        row = jnp.concatenate(
            [
                jnp.sum(field.astype(F32) * ref[...], axis=0, keepdims=True)
                for field, ref in zip(held, ins[:groups])
            ],
            axis=1,
        )
        row = jnp.broadcast_to(row, (replicas, width))
        lane = lax.broadcasted_iota(jnp.int32, (replicas, width), 1)
        first = lax.broadcasted_iota(jnp.int32, (replicas, width), 0) * channels
        inside = (lane >= first) & (lane < first + channels)
        total = jnp.sum(jnp.where(inside, row, 0.0), axis=1, keepdims=True)
        place = lax.broadcasted_iota(jnp.int32, (replicas, LANES), 1)
        which = lax.broadcasted_iota(jnp.int32, (replicas, LANES), 0)
        flat = jnp.sum(jnp.where(place == which, total, 0.0), axis=0, keepdims=True)
        outs[len(piece)][...] = jnp.broadcast_to(flat, (8, LANES))

    results = far_fields(
        lists,
        tile_values,
        near[1:],
        new_fars[1],
        weights,
        [(wide, BF16)] * len(piece) + [((8, LANES), F32)],
        last_work,
        "far_second_1",
        through=[near[0], *xs, *base, mixing],
    )
    fields, partial, kept = results[: len(piece)], results[len(piece)], results[len(piece) + 1 :]
    fields, kept = [kept[0], *fields], kept[1:]

    x_new, y_new, token = finish(
        fields, kept[:groups], kept[groups : 2 * groups], kept[2 * groups], channels
    )
    total = sum_over_ring(partial, ring, token)
    energy = total[0, :replicas] / jnp.sqrt(jnp.float32(cells * ring * channels))
    return (x_new, y_new, energy)


def solution(mesh):
    cells = P(("groups", "row", "col"), None)
    slots = P(("groups", "row", "col"))
    return jax.shard_map(
        local,
        mesh=mesh,
        in_specs=(cells, cells, P(("groups", "row", "col"), None, None), slots, slots, slots, P()),
        out_specs=(cells, cells, P("groups")),
        check_vma=False,
    )
```

```python
import jax
import jax.numpy as jnp
import ml_dtypes
import numpy as np
from jax import lax
from jax.experimental import pallas as pl
from jax.experimental.pallas import tpu as pltpu
from jax.sharding import PartitionSpec as P

STEPS = 2
LANES = 128
LONG, SHORT = 24, 4
VMEM_LIMIT = 14 * 1024 * 1024
NEAR_FLOPS = 4 * 10**9
F32 = jnp.float32
BF16 = jnp.bfloat16
RING = ("row", "col")


def call(body, ins, outs, scratch, name, flops=0, aliases=()):
    return pl.pallas_call(
        body,
        in_specs=[pl.BlockSpec(memory_space=pl.ANY if s is pltpu.HBM else s) for _, s in ins],
        out_specs=[pl.BlockSpec(memory_space=pl.ANY if s is pltpu.HBM else s) for *_, s in outs],
        out_shape=[
            jax.ShapeDtypeStruct(dims, kind) if s is pltpu.HBM else s(dims, kind)
            for dims, kind, s in outs
        ],
        scratch_shapes=scratch,
        input_output_aliases=dict(aliases),
        compiler_params=pltpu.CompilerParams(vmem_limit_bytes=VMEM_LIMIT),
        cost_estimate=pl.CostEstimate(
            flops=int(flops) or 1000, bytes_accessed=1000, transcendentals=0
        ),
        name=name,
    )(*[pltpu.with_memory_space_constraint(a, s) for a, s in ins])


def vmem(*arrays):
    return [(a, pltpu.VMEM) for a in arrays]


def lanes(group):
    return slice(group * LANES, (group + 1) * LANES)


def spanned(group, channels, width):
    first = group * LANES // channels * channels
    last = -(-(group + 1) * LANES // channels) * channels
    return list(range(first // LANES, -(-min(last, width) // LANES)))


def span_lanes(near):
    return slice(near[0] * LANES, (near[-1] + 1) * LANES)


def split(x):
    high = x.astype(BF16)
    return high, (x - high.astype(F32)).astype(BF16)


def bases_into(outs, xs, ys, same, step, channels):
    groups = len(xs)
    width = groups * LANES
    detune = 1.0 - (step + 1.0) / (STEPS + 1.0)
    parts = [split(x) for x in xs]
    for g in range(groups):
        near = spanned(g, channels, width)
        ones = same[span_lanes(near), lanes(g)]
        totals = sum(
            jnp.dot(
                jnp.concatenate([parts[n][k] for n in near], axis=1),
                ones,
                preferred_element_type=F32,
            )
            for k in range(2)
        )
        penalty = 0.02 * (totals - (2.0 - channels))
        outs[g][...] = ys[g] + 0.5 * (-detune * xs[g] - 0.4 * penalty)


def mixed_of(fields, mixing, group, channels):
    near = spanned(group, channels, mixing.shape[0])
    return jnp.dot(
        jnp.concatenate([fields[n] for n in near], axis=1),
        mixing[span_lanes(near), lanes(group)],
        preferred_element_type=F32,
    )


def load_first(positions, groups_of):
    cells = positions.shape[0]
    n = len(groups_of)

    def body(x_ref, *refs):
        x_outs, r_outs, sent, sems = refs[:n], refs[n : 2 * n], refs[2 * n], refs[-1]
        copies = [
            pltpu.make_async_copy(x_ref.at[:, lanes(g)], x_outs[i], sems.at[i])
            for i, g in enumerate(groups_of)
        ]
        for copy in copies:
            copy.start()
        for i, copy in enumerate(copies):
            copy.wait()
            rounded = x_outs[i][...].astype(BF16)
            r_outs[i][...] = rounded
            sent[:, lanes(i)] = rounded

    outs = call(
        body,
        [(positions, pltpu.HBM)],
        [((cells, LANES), F32, pltpu.VMEM)] * n
        + [((cells, LANES), BF16, pltpu.VMEM)] * n
        + [((cells, n * LANES), BF16, pltpu.VMEM)],
        [pltpu.SemaphoreType.DMA((n,))],
        "load_first",
    )
    return outs[:n], outs[n : 2 * n], outs[2 * n]


def section(slots, per):
    return -(-(slots + per) // (2 * LONG)) * LONG


def make_lists(rows, cols, count, positions, groups_of, after, slots, tile, ring_index):
    cells = positions.shape[0]
    per = cells // tile
    pairs = section(slots, per)
    n = len(groups_of)

    def body(rows_hbm, cols_hbm, count_hbm, x_ref, _, list_ref, *refs):
        x_outs, r_outs = refs[:n], refs[n : 2 * n]
        rows_ref, cols_ref, count_ref, held, sems = refs[2 * n :]
        copies = [
            pltpu.make_async_copy(*ends, sems.at[k])
            for k, ends in enumerate(
                [(rows_hbm, rows_ref), (cols_hbm, cols_ref), (count_hbm, count_ref)]
                + [(x_ref.at[:, lanes(g)], x_outs[i]) for i, g in enumerate(groups_of)]
            )
        ]
        for copy in copies:
            copy.start()
        for k in range(2 * per):
            held[k] = -1
        far_third = jnp.where(lax.rem(ring_index(), 2) == 1, 2, 0)
        for copy in copies[:3]:
            copy.wait()

        def visit(slot, totals):
            near_pairs, far_pairs = totals
            row, col = rows_ref[slot], cols_ref[slot]
            third = jnp.where(col >= 2 * per, 2, jnp.where(col >= per, 1, 0))
            source = col - third * per
            far = third == far_third
            source = jnp.where(far | (third == 1), source, source + per)
            key = row + jnp.where(far, per, 0)
            place = 2 * jnp.where(far, far_pairs + pairs, near_pairs)
            entry = slot * 65536 + source * 256 + row
            other = held[key]
            full = other >= 0
            list_ref[place] = other
            list_ref[place + 1] = entry
            held[key] = jnp.where(full, -1, entry)
            one = full.astype(jnp.int32)
            far_one = jnp.where(far, one, 0)
            return near_pairs + one - far_one, far_pairs + far_one

        totals = lax.fori_loop(0, count_ref[0], visit, (jnp.int32(0), jnp.int32(0)))
        for part, zero in enumerate((2 * per, per)):
            total = totals[part]
            start = part * pairs
            for k in range(per):
                other = held[part * per + k]
                list_ref[2 * (start + total)] = other
                list_ref[2 * (start + total) + 1] = zero * 256 + k
                total = total + (other >= 0).astype(jnp.int32)
            rest = total % LONG
            padded = rest > 2 * SHORT
            long_turns = total // LONG + padded.astype(jnp.int32)
            short_turns = jnp.where(padded, 0, (rest + SHORT - 1) // SHORT)

            def pad(pair, carry, start=start, zero=zero):
                for e in range(2):
                    list_ref[2 * (start + pair) + e] = zero * 256 + per
                return carry

            lax.fori_loop(total, long_turns * LONG + short_turns * SHORT, pad, 0)
            list_ref[4 * pairs + 2 * part] = long_turns
            list_ref[4 * pairs + 2 * part + 1] = short_turns
        for i, copy in enumerate(copies[3:]):
            copy.wait()
            r_outs[i][...] = x_outs[i][...].astype(BF16)

    outs = call(
        body,
        [(a, pl.ANY) for a in (rows, cols, count)] + [(positions, pltpu.HBM)] + vmem(after),
        [((4 * pairs + 4 + 2,), jnp.int32, pltpu.SMEM)]
        + [((cells, LANES), F32, pltpu.VMEM)] * n
        + [((cells, LANES), BF16, pltpu.VMEM)] * n,
        [
            pltpu.SMEM(rows.shape, jnp.int32),
            pltpu.SMEM(cols.shape, jnp.int32),
            pltpu.SMEM(count.shape, jnp.int32),
            pltpu.SMEM((2 * per,), jnp.int32),
            pltpu.SemaphoreType.DMA((3 + n,)),
        ],
        "make_lists",
    )
    return outs[0], outs[1 : 1 + n], outs[1 + n :]


def add_pairs(part, list_ref, tiles, field, window, pairs):
    def turn(first, length):
        for u in range(length):
            place = 2 * (part * pairs + first + u)
            entries = [list_ref[place + e] for e in range(2)]
            left = jnp.concatenate([tiles[n >> 16] for n in entries], axis=1)
            right = jnp.concatenate([window[(n >> 8) & 255] for n in entries], axis=0)
            field[entries[1] & 255] += jnp.dot(left, right, preferred_element_type=F32)

    def long(i, carry):
        turn(i * LONG, LONG)
        return carry

    def short(i, carry):
        turn(long_turns * LONG + i * SHORT, SHORT)
        return carry

    long_turns = list_ref[4 * pairs + 2 * part]
    lax.fori_loop(0, long_turns, long, 0)
    lax.fori_loop(0, list_ref[4 * pairs + 2 * part + 1], short, 0)


def near_fields(lists, tiles, owns, others, far_part, sent, after, flops, name):
    slots, tile, _ = tiles.shape
    cells = owns[0].shape[0]
    groups = len(owns)
    width = groups * LANES
    per = cells // tile
    pairs = section(slots, per)
    start = [] if far_part is None else [far_part]

    def body(list_ref, tiles_ref, *refs):
        own_refs, other_refs, refs = refs[:groups], refs[groups : 2 * groups], refs[2 * groups :]
        start_refs, refs = refs[: len(start)], refs[len(start) :]
        sent_refs, refs = refs[: len(sent)], refs[len(sent) + len(after) :]
        field_outs, sent_outs, (field, window) = refs[:groups], refs[groups:-2], refs[-2:]
        for out, ref in zip(sent_outs, sent_refs):
            out[...] = ref[...]
        for g in range(groups):
            window[:per, :, lanes(g)] = own_refs[g][...].reshape(per, tile, LANES)
            window[per : 2 * per, :, lanes(g)] = other_refs[g][...].reshape(per, tile, LANES)
        window[2 * per] = jnp.zeros((tile, width), BF16)
        field[:per] = jnp.zeros((per, tile, width), F32)
        for ref in start_refs:
            field[:per, :, lanes(0)] = ref[...].reshape(per, tile, LANES)
        add_pairs(0, list_ref, tiles_ref, field, window, pairs)
        for g, out in enumerate(field_outs):
            out[...] = field[:per, :, lanes(g)].reshape(cells, LANES).astype(out.dtype)

    outs = call(
        body,
        [(lists, pltpu.SMEM)] + vmem(tiles, *owns, *others, *start, *sent, *after),
        [
            ((cells, LANES), BF16 if start and g == 0 else F32, pltpu.VMEM)
            for g in range(groups)
        ]
        + [(a.shape, BF16, pltpu.VMEM) for a in sent],
        [
            pltpu.VMEM((per + 1, tile, width), F32),
            pltpu.VMEM((2 * per + 1, tile, width), BF16),
        ],
        name,
        flops,
    )
    return outs[:groups], outs[groups:]


def far_fields(lists, tiles, nears, far, extra, outs_of, work, name, flops=0, through=()):
    slots, tile, _ = tiles.shape
    cells, width = far.shape
    per = cells // tile
    pairs = section(slots, per)
    n = width // LANES
    m = len(nears)

    def body(list_ref, tiles_ref, far_ref, *refs):
        near_refs, extra_refs = refs[:m], refs[m : m + len(extra)]
        through_refs = refs[m + len(extra) : m + len(extra) + len(through)]
        out_refs, (field, window) = refs[m + len(extra) + len(through) : -2], refs[-2:]
        window[:per] = far_ref[...].reshape(per, tile, width)
        window[per] = jnp.zeros((tile, width), BF16)
        if not near_refs:
            field[:per] = jnp.zeros((per, tile, width), F32)
        for i, ref in enumerate(near_refs):
            field[:per, :, lanes(i)] = ref[...].reshape(per, tile, LANES)
        add_pairs(1, list_ref, tiles_ref, field, window, pairs)
        done = [field[:per, :, lanes(i)].reshape(cells, LANES) for i in range(n)]
        work(done, [*extra_refs, *through_refs], out_refs[: len(outs_of)])

    return call(
        body,
        [(lists, pltpu.SMEM)] + vmem(tiles, far, *nears, *extra, *through),
        [(*out, pltpu.VMEM) for out in outs_of] + [(a.shape, a.dtype, pltpu.VMEM) for a in through],
        [pltpu.VMEM((per + 1, tile, width), F32), pltpu.VMEM((per + 1, tile, width), BF16)],
        name,
        flops,
        [(3 + m + len(extra) + i, len(outs_of) + i) for i in range(len(through))],
    )


def first_base(xs, momenta, same, spread, coupling, channels):
    cells, width = momenta.shape
    groups = len(xs)

    def body(*refs):
        x_refs, (y_ref, same_ref, spread_ref, coupling_ref) = refs[:groups], refs[groups : groups + 4]
        outs = refs[groups + 4 :]
        tall = jnp.dot(spread_ref[...], coupling_ref[...], preferred_element_type=F32).astype(BF16)
        wide = lax.dot_general(
            tall, spread_ref[...], (((1,), (1,)), ((), ())), preferred_element_type=F32
        )
        outs[groups][...] = (wide * same_ref[...].astype(F32)).astype(BF16)
        x = [ref[...] for ref in x_refs]
        y = [y_ref[:, lanes(g)] for g in range(groups)]
        bases_into(outs[:groups], x, y, same_ref, 0, channels)

    outs = call(
        body,
        vmem(*xs, momenta, same, spread, coupling),
        [((cells, LANES), F32, pltpu.VMEM)] * groups + [((width, width), BF16, pltpu.VMEM)],
        [],
        "first_base",
    )
    return outs[:groups], outs[groups]


def updated(field_mixed, base, x):
    y_new = base - 0.2 * field_mixed
    return jnp.clip(x + 0.5 * y_new, -1.0, 1.0), y_new


def second_base(xs, ys, later, fields, first_base, first_x, rounded, same, mixing, channels):
    groups = len(rounded)
    cells = rounded[0].shape[0]
    width = groups * LANES
    done, m = len(xs), len(later)

    def body(*refs):
        refs = list(refs)

        def take(n):
            taken = refs[:n]
            del refs[:n]
            return taken

        x = [ref[...] for ref in take(done)]
        y = [ref[...] for ref in take(done)]
        held = [ref[...] for ref in take(groups)]
        base_refs, x_refs = take(m), take(m)
        r = [ref[...] for ref in take(groups)]
        same_ref, mixing_ref = take(2)
        for i, t in enumerate(later):
            x_new, y_new = updated(
                mixed_of(held, mixing_ref, t, channels), base_refs[i][...], x_refs[i][...]
            )
            x.append(x_new)
            y.append(y_new)
            refs[2 * groups + i][...] = x_new
        bases_into(refs[:groups], x, y, same_ref, 1, channels)
        for g in range(groups):
            near = spanned(g, channels, width)
            refs[groups + g][...] = lax.dot_general(
                jnp.concatenate([r[n] for n in near], axis=1),
                mixing_ref[lanes(g), span_lanes(near)],
                (((1,), (1,)), ((), ())),
                preferred_element_type=F32,
            )

    outs = call(
        body,
        vmem(*xs, *ys, *fields, *first_base, *first_x, *rounded, same, mixing),
        [((cells, LANES), F32, pltpu.VMEM)] * (2 * groups + m),
        [],
        "second_base",
    )
    return outs[:groups], outs[groups : 2 * groups], outs[2 * groups :]


def finish(fields, xs, bases, mixing, channels):
    groups = len(xs)
    cells = xs[0].shape[0]
    width = groups * LANES

    def body(*refs):
        field_refs, x_refs, base_refs = [refs[k * groups : (k + 1) * groups] for k in range(3)]
        mixing_ref, x_out, y_out, token, x_buf, y_buf, sems = refs[3 * groups :]
        held = [ref[...] for ref in field_refs]
        copies = []
        for g in range(groups):
            y_new = base_refs[g][...] - 0.2 * mixed_of(held, mixing_ref, g, channels)
            y_buf[g] = y_new
            x_buf[g] = jnp.clip(x_refs[g][...] + 0.5 * y_new, -1.0, 1.0)
            for k, (buf, out) in enumerate(((y_buf, y_out), (x_buf, x_out))):
                copies.append(
                    pltpu.make_async_copy(buf.at[g], out.at[:, lanes(g)], sems.at[g, k])
                )
                copies[-1].start()
        token[...] = jnp.zeros_like(token)
        for copy in copies:
            copy.wait()

    return call(
        body,
        vmem(*fields, *xs, *bases, mixing),
        [((cells, width), F32, pltpu.HBM)] * 2 + [((8, LANES), F32, pltpu.VMEM)],
        [
            pltpu.VMEM((groups, cells, LANES), F32),
            pltpu.VMEM((groups, cells, LANES), F32),
            pltpu.SemaphoreType.DMA((groups, 2)),
        ],
        "finish",
    )


def add_up(arrays, token):
    def body(*refs):
        refs[-1][...] = sum(ref[...] for ref in refs[:-2])

    return call(
        body,
        vmem(*arrays, token),
        [(arrays[0].shape, F32, pltpu.VMEM)],
        [],
        "add_up",
    )[0]


def sum_over_ring(value, ring, token):
    if ring & (ring - 1):
        return lax.psum(value, RING)
    rounds, size = [], 1
    while size < ring:
        digits = (1, 2, 3) if 4 * size <= ring else (1,)
        rounds.append([size * d for d in digits])
        size *= len(digits) + 1
    for i, bits in enumerate(reversed(rounds)):
        parts = [value] + [
            lax.ppermute(value, RING, [(j, j ^ bit) for j in range(ring)]) for bit in bits
        ]
        value = add_up(parts, token) if i == 0 else sum(parts)
    return value


def local(positions, momenta, tile_values, tile_rows, tile_cols, tile_count, channel_coupling):
    cells, width = positions.shape
    slots, tile, _ = tile_values.shape
    channels = channel_coupling.shape[0]
    replicas = width // channels
    groups = width // LANES
    ring = lax.axis_size("row") * lax.axis_size("col")
    where = np.arange(width)
    same = jnp.asarray(
        (where[:, None] // channels == where[None] // channels).astype(ml_dtypes.bfloat16)
    )
    spread = jnp.asarray(
        (where[:, None] % channels == np.arange(channels)[None]).astype(ml_dtypes.bfloat16)
    )
    on_chip = [(i, i ^ 1) for i in range(ring)]
    off_chip = [(i, (i + 1) % ring if i % 2 else (i - 1) % ring) for i in range(ring)]
    wide = (cells, LANES)
    every = list(range(groups))
    first_pieces = [every[:-1], every[-1:]]
    second_pieces = [every[:1], every[1:]]

    def ring_index():
        return lax.axis_index("row") * lax.axis_size("col") + lax.axis_index("col")

    def far_swap(mine):
        return lax.ppermute(mine, RING, off_chip)

    def near_swap(mine):
        return lax.ppermute(mine, RING, on_chip)

    def ready(piece, done):
        return [
            t for t in every if t not in done and max(spanned(t, channels, width)) <= piece[-1]
        ]

    def keep(done, _, outs):
        outs[0][...] = done[0]

    def needed(todo, piece):
        return sorted({n for t in todo for n in spanned(t, channels, width)} - set(piece))

    xs, owns, sent = load_first(positions, first_pieces[0])
    fars = [far_swap(sent)]
    lists, more_x, more_own = make_lists(
        tile_rows, tile_cols, tile_count, positions, first_pieces[1], sent, slots, tile, ring_index
    )
    xs, owns = [*xs, *more_x], [*owns, *more_own]
    others = [near_swap(r) for r in owns]
    base, mixing = first_base(xs, momenta, same, spread, channel_coupling, channels)
    near, sent = near_fields(
        lists, tile_values, owns, others, None, more_own, [mixing], 0, "near_first"
    )
    fars.append(far_swap(sent[0]))

    fields, new_x, new_y, rounded, new_fars = {}, [], [], {}, []
    for p, piece in enumerate(first_pieces):
        last = p == len(first_pieces) - 1
        todo = ready(piece, rounded)
        known = needed(todo, piece)
        assert second_pieces[p] == todo

        def work(done, ins, outs, piece=piece, todo=todo, known=known, last=last):
            held = {n: ins[1 + i][...] for i, n in enumerate(known)}
            done = [field.astype(BF16) for field in done]
            held.update(zip(piece, done))
            rest = ins[1 + len(known) :]
            for i, t in enumerate(todo):
                x_new, y_new = updated(
                    mixed_of(held, ins[0], t, channels), rest[2 * i][...], rest[2 * i + 1][...]
                )
                r_new = x_new.astype(BF16)
                outs[0][:, lanes(i)] = r_new
                outs[1 + i][...] = r_new
                if not last:
                    outs[1 + len(todo) + len(piece) + 2 * i][...] = x_new
                    outs[2 + len(todo) + len(piece) + 2 * i][...] = y_new
            for i, field in enumerate(done):
                outs[1 + len(todo) + i][...] = field

        results = far_fields(
            lists,
            tile_values,
            [near[n] for n in piece],
            fars[p],
            [mixing] + [fields[n] for n in known] + [a for t in todo for a in (base[t], xs[t])],
            [((cells, len(todo) * LANES), BF16)]
            + [(wide, BF16)] * (len(todo) + len(piece))
            + ([] if last else [(wide, F32)] * (2 * len(todo))),
            work,
            f"far_first_{p}",
        )
        new_fars.append(far_swap(results[0]))
        rounded.update(zip(todo, results[1:]))
        fields.update(zip(piece, results[1 + len(todo) :]))
        new_x += results[1 + len(todo) + len(piece) :: 2]
        new_y += results[2 + len(todo) + len(piece) :: 2]

    owns = [rounded[g] for g in every]
    others = [near_swap(r) for r in owns]
    (part,) = far_fields(
        lists, tile_values, [], new_fars[0], [], [(wide, F32)], keep, "far_second_0", NEAR_FLOPS
    )
    near, _ = near_fields(lists, tile_values, owns, others, part, [], [], 0, "near_second")
    later = second_pieces[1]
    base, weights, more_x = second_base(
        new_x,
        new_y,
        later,
        [fields[g] for g in every],
        [base[t] for t in later],
        [xs[t] for t in later],
        owns,
        same,
        mixing,
        channels,
    )
    xs = [*new_x, *more_x]
    piece = second_pieces[1]

    def last_work(done, ins, outs):
        held = [ins[groups][...]] + [field.astype(BF16) for field in done]
        for out, field in zip(outs, held[1:]):
            out[...] = field
        row = jnp.concatenate(
            [
                jnp.sum(field.astype(F32) * ref[...], axis=0, keepdims=True)
                for field, ref in zip(held, ins[:groups])
            ],
            axis=1,
        )
        row = jnp.broadcast_to(row, (replicas, width))
        lane = lax.broadcasted_iota(jnp.int32, (replicas, width), 1)
        first = lax.broadcasted_iota(jnp.int32, (replicas, width), 0) * channels
        inside = (lane >= first) & (lane < first + channels)
        total = jnp.sum(jnp.where(inside, row, 0.0), axis=1, keepdims=True)
        place = lax.broadcasted_iota(jnp.int32, (replicas, LANES), 1)
        which = lax.broadcasted_iota(jnp.int32, (replicas, LANES), 0)
        flat = jnp.sum(jnp.where(place == which, total, 0.0), axis=0, keepdims=True)
        outs[len(piece)][...] = jnp.broadcast_to(flat, (8, LANES))

    results = far_fields(
        lists,
        tile_values,
        near[1:],
        new_fars[1],
        weights,
        [(wide, BF16)] * len(piece) + [((8, LANES), F32)],
        last_work,
        "far_second_1",
        through=[near[0], *xs, *base, mixing],
    )
    fields, partial, kept = results[: len(piece)], results[len(piece)], results[len(piece) + 1 :]
    fields, kept = [kept[0], *fields], kept[1:]

    x_new, y_new, token = finish(
        fields, kept[:groups], kept[groups : 2 * groups], kept[2 * groups], channels
    )
    total = sum_over_ring(partial, ring, token)
    energy = total[0, :replicas] / jnp.sqrt(jnp.float32(cells * ring * channels))
    return (x_new, y_new, energy)


def solution(mesh):
    cells = P(("groups", "row", "col"), None)
    slots = P(("groups", "row", "col"))
    return jax.shard_map(
        local,
        mesh=mesh,
        in_specs=(cells, cells, P(("groups", "row", "col"), None, None), slots, slots, slots, P()),
        out_specs=(cells, cells, P("groups")),
        check_vma=False,
    )
```

```python
import jax
import jax.numpy as jnp
import ml_dtypes
import numpy as np
from jax import lax
from jax.experimental import pallas as pl
from jax.experimental.pallas import tpu as pltpu
from jax.sharding import PartitionSpec as P

STEPS = 2
LANES = 128
LONG, SHORT = 16, 4
VMEM_LIMIT = 14 * 1024 * 1024
NEAR_FLOPS = 4 * 10**9
F32 = jnp.float32
BF16 = jnp.bfloat16
RING = ("row", "col")


def call(body, ins, outs, scratch, name, flops=0, aliases=()):
    return pl.pallas_call(
        body,
        in_specs=[pl.BlockSpec(memory_space=pl.ANY if s is pltpu.HBM else s) for _, s in ins],
        out_specs=[pl.BlockSpec(memory_space=pl.ANY if s is pltpu.HBM else s) for *_, s in outs],
        out_shape=[
            jax.ShapeDtypeStruct(dims, kind) if s is pltpu.HBM else s(dims, kind)
            for dims, kind, s in outs
        ],
        scratch_shapes=scratch,
        input_output_aliases=dict(aliases),
        compiler_params=pltpu.CompilerParams(vmem_limit_bytes=VMEM_LIMIT),
        cost_estimate=pl.CostEstimate(
            flops=int(flops) or 1000, bytes_accessed=1000, transcendentals=0
        ),
        name=name,
    )(*[pltpu.with_memory_space_constraint(a, s) for a, s in ins])


def vmem(*arrays):
    return [(a, pltpu.VMEM) for a in arrays]


def lanes(group):
    return slice(group * LANES, (group + 1) * LANES)


def spanned(group, channels, width):
    first = group * LANES // channels * channels
    last = -(-(group + 1) * LANES // channels) * channels
    return list(range(first // LANES, -(-min(last, width) // LANES)))


def span_lanes(near):
    return slice(near[0] * LANES, (near[-1] + 1) * LANES)


def split(x):
    high = x.astype(BF16)
    return high, (x - high.astype(F32)).astype(BF16)


def bases_into(outs, xs, ys, same, step, channels):
    groups = len(xs)
    width = groups * LANES
    detune = 1.0 - (step + 1.0) / (STEPS + 1.0)
    parts = [split(x) for x in xs]
    for g in range(groups):
        near = spanned(g, channels, width)
        ones = same[span_lanes(near), lanes(g)]
        totals = sum(
            jnp.dot(
                jnp.concatenate([parts[n][k] for n in near], axis=1),
                ones,
                preferred_element_type=F32,
            )
            for k in range(2)
        )
        penalty = 0.02 * (totals - (2.0 - channels))
        outs[g][...] = ys[g] + 0.5 * (-detune * xs[g] - 0.4 * penalty)


def mixed_of(fields, mixing, group, channels):
    near = spanned(group, channels, mixing.shape[0])
    return jnp.dot(
        jnp.concatenate([fields[n] for n in near], axis=1),
        mixing[span_lanes(near), lanes(group)],
        preferred_element_type=F32,
    )


def load_first(positions, groups_of):
    cells = positions.shape[0]
    n = len(groups_of)

    def body(x_ref, *refs):
        x_outs, r_outs, sent, sems = refs[:n], refs[n : 2 * n], refs[2 * n], refs[-1]
        copies = [
            pltpu.make_async_copy(x_ref.at[:, lanes(g)], x_outs[i], sems.at[i])
            for i, g in enumerate(groups_of)
        ]
        for copy in copies:
            copy.start()
        for i, copy in enumerate(copies):
            copy.wait()
            rounded = x_outs[i][...].astype(BF16)
            r_outs[i][...] = rounded
            sent[:, lanes(i)] = rounded

    outs = call(
        body,
        [(positions, pltpu.HBM)],
        [((cells, LANES), F32, pltpu.VMEM)] * n
        + [((cells, LANES), BF16, pltpu.VMEM)] * n
        + [((cells, n * LANES), BF16, pltpu.VMEM)],
        [pltpu.SemaphoreType.DMA((n,))],
        "load_first",
    )
    return outs[:n], outs[n : 2 * n], outs[2 * n]


def section(slots, per):
    return -(-(slots + per) // (2 * SHORT)) * SHORT


def make_lists(rows, cols, count, positions, groups_of, after, slots, tile, ring_index):
    cells = positions.shape[0]
    per = cells // tile
    pairs = section(slots, per)
    n = len(groups_of)

    def body(rows_hbm, cols_hbm, count_hbm, x_ref, _, list_ref, *refs):
        x_outs, r_outs = refs[:n], refs[n : 2 * n]
        rows_ref, cols_ref, count_ref, held, sems = refs[2 * n :]
        copies = [
            pltpu.make_async_copy(*ends, sems.at[k])
            for k, ends in enumerate(
                [(rows_hbm, rows_ref), (cols_hbm, cols_ref), (count_hbm, count_ref)]
                + [(x_ref.at[:, lanes(g)], x_outs[i]) for i, g in enumerate(groups_of)]
            )
        ]
        for copy in copies:
            copy.start()
        for k in range(2 * per):
            held[k] = -1
        far_third = jnp.where(lax.rem(ring_index(), 2) == 1, 2, 0)
        for copy in copies[:3]:
            copy.wait()

        def visit(slot, totals):
            near_pairs, far_pairs = totals
            row, col = rows_ref[slot], cols_ref[slot]
            third = jnp.where(col >= 2 * per, 2, jnp.where(col >= per, 1, 0))
            source = col - third * per
            far = third == far_third
            source = jnp.where(far | (third == 1), source, source + per)
            key = row + jnp.where(far, per, 0)
            place = 2 * jnp.where(far, far_pairs + pairs, near_pairs)
            entry = slot * 65536 + source * 256 + row
            other = held[key]
            full = other >= 0
            list_ref[place] = other
            list_ref[place + 1] = entry
            held[key] = jnp.where(full, -1, entry)
            one = full.astype(jnp.int32)
            far_one = jnp.where(far, one, 0)
            return near_pairs + one - far_one, far_pairs + far_one

        totals = lax.fori_loop(0, count_ref[0], visit, (jnp.int32(0), jnp.int32(0)))
        for part, zero in enumerate((2 * per, per)):
            total = totals[part]
            start = part * pairs
            for k in range(per):
                other = held[part * per + k]
                list_ref[2 * (start + total)] = other
                list_ref[2 * (start + total) + 1] = zero * 256 + k
                total = total + (other >= 0).astype(jnp.int32)
            short_turns = (total + SHORT - 1) // SHORT

            def pad(pair, carry, start=start, zero=zero):
                for e in range(2):
                    list_ref[2 * (start + pair) + e] = zero * 256 + per
                return carry

            lax.fori_loop(total, short_turns * SHORT, pad, 0)
            list_ref[4 * pairs + 2 * part] = short_turns // (LONG // SHORT)
            list_ref[4 * pairs + 2 * part + 1] = short_turns % (LONG // SHORT)
        for i, copy in enumerate(copies[3:]):
            copy.wait()
            r_outs[i][...] = x_outs[i][...].astype(BF16)

    outs = call(
        body,
        [(a, pl.ANY) for a in (rows, cols, count)] + [(positions, pltpu.HBM)] + vmem(after),
        [((4 * pairs + 4 + 2,), jnp.int32, pltpu.SMEM)]
        + [((cells, LANES), F32, pltpu.VMEM)] * n
        + [((cells, LANES), BF16, pltpu.VMEM)] * n,
        [
            pltpu.SMEM(rows.shape, jnp.int32),
            pltpu.SMEM(cols.shape, jnp.int32),
            pltpu.SMEM(count.shape, jnp.int32),
            pltpu.SMEM((2 * per,), jnp.int32),
            pltpu.SemaphoreType.DMA((3 + n,)),
        ],
        "make_lists",
    )
    return outs[0], outs[1 : 1 + n], outs[1 + n :]


def add_pairs(part, list_ref, tiles, field, window, pairs):
    def turn(first, length):
        for u in range(length):
            place = 2 * (part * pairs + first + u)
            entries = [list_ref[place + e] for e in range(2)]
            left = jnp.concatenate([tiles[n >> 16] for n in entries], axis=1)
            right = jnp.concatenate([window[(n >> 8) & 255] for n in entries], axis=0)
            field[entries[1] & 255] += jnp.dot(left, right, preferred_element_type=F32)

    def long(i, carry):
        turn(i * LONG, LONG)
        return carry

    def short(i, carry):
        turn(long_turns * LONG + i * SHORT, SHORT)
        return carry

    long_turns = list_ref[4 * pairs + 2 * part]
    lax.fori_loop(0, long_turns, long, 0)
    lax.fori_loop(0, list_ref[4 * pairs + 2 * part + 1], short, 0)


def weighted(field, weight):
    return jnp.sum(field.astype(F32) * weight[...], axis=0, keepdims=True)


def near_fields(lists, tiles, owns, others, far_part, weight, sent, after, name):
    slots, tile, _ = tiles.shape
    cells = owns[0].shape[0]
    groups = len(owns)
    width = groups * LANES
    per = cells // tile
    pairs = section(slots, per)
    start = [] if far_part is None else [far_part, weight]

    def body(list_ref, tiles_ref, *refs):
        own_refs, other_refs, refs = refs[:groups], refs[groups : 2 * groups], refs[2 * groups :]
        start_refs, refs = refs[: len(start)], refs[len(start) :]
        sent_refs, refs = refs[: len(sent)], refs[len(sent) + len(after) :]
        field_outs, sent_outs, (field, window) = refs[:groups], refs[groups:-2], refs[-2:]
        for out, ref in zip(sent_outs, sent_refs):
            out[...] = ref[...]
        for g in range(groups):
            window[:per, :, lanes(g)] = own_refs[g][...].reshape(per, tile, LANES)
            window[per : 2 * per, :, lanes(g)] = other_refs[g][...].reshape(per, tile, LANES)
        window[2 * per] = jnp.zeros((tile, width), BF16)
        field[:per] = jnp.zeros((per, tile, width), F32)
        if start:
            field[:per, :, lanes(0)] = start_refs[0][...].reshape(per, tile, LANES)
        add_pairs(0, list_ref, tiles_ref, field, window, pairs)
        for g, out in enumerate(field_outs):
            out[...] = field[:per, :, lanes(g)].reshape(cells, LANES).astype(out.dtype)
        if start:
            sent_outs[len(sent)][...] = weighted(field_outs[0][...], start_refs[1])

    outs = call(
        body,
        [(lists, pltpu.SMEM)] + vmem(tiles, *owns, *others, *start, *sent, *after),
        [
            ((cells, LANES), BF16 if start and g == 0 else F32, pltpu.VMEM)
            for g in range(groups)
        ]
        + [(a.shape, BF16, pltpu.VMEM) for a in sent]
        + ([((1, LANES), F32, pltpu.VMEM)] if start else []),
        [
            pltpu.VMEM((per + 1, tile, width), F32),
            pltpu.VMEM((2 * per + 1, tile, width), BF16),
        ],
        name,
    )
    return outs[:groups], outs[groups:]


def far_fields(lists, tiles, nears, far, extra, outs_of, work, name, flops=0, through=()):
    slots, tile, _ = tiles.shape
    cells, width = far.shape
    per = cells // tile
    pairs = section(slots, per)
    n = width // LANES
    m = len(nears)

    def body(list_ref, tiles_ref, far_ref, *refs):
        near_refs, extra_refs = refs[:m], refs[m : m + len(extra)]
        through_refs = refs[m + len(extra) : m + len(extra) + len(through)]
        out_refs, (field, window) = refs[m + len(extra) + len(through) : -2], refs[-2:]
        window[:per] = far_ref[...].reshape(per, tile, width)
        window[per] = jnp.zeros((tile, width), BF16)
        if not near_refs:
            field[:per] = jnp.zeros((per, tile, width), F32)
        for i, ref in enumerate(near_refs):
            field[:per, :, lanes(i)] = ref[...].reshape(per, tile, LANES)
        add_pairs(1, list_ref, tiles_ref, field, window, pairs)
        done = [field[:per, :, lanes(i)].reshape(cells, LANES) for i in range(n)]
        work(done, [*extra_refs, *through_refs], out_refs[: len(outs_of)])

    return call(
        body,
        [(lists, pltpu.SMEM)] + vmem(tiles, far, *nears, *extra, *through),
        [(*out, pltpu.VMEM) for out in outs_of] + [(a.shape, a.dtype, pltpu.VMEM) for a in through],
        [pltpu.VMEM((per + 1, tile, width), F32), pltpu.VMEM((per + 1, tile, width), BF16)],
        name,
        flops,
        [(3 + m + len(extra) + i, len(outs_of) + i) for i in range(len(through))],
    )


def first_base(xs, momenta, same, spread, coupling, channels):
    cells, width = momenta.shape
    groups = len(xs)

    def body(*refs):
        x_refs, (y_ref, same_ref, spread_ref, coupling_ref) = refs[:groups], refs[groups : groups + 4]
        outs = refs[groups + 4 :]
        tall = jnp.dot(spread_ref[...], coupling_ref[...], preferred_element_type=F32).astype(BF16)
        wide = lax.dot_general(
            tall, spread_ref[...], (((1,), (1,)), ((), ())), preferred_element_type=F32
        )
        outs[groups][...] = (wide * same_ref[...].astype(F32)).astype(BF16)
        x = [ref[...] for ref in x_refs]
        y = [y_ref[:, lanes(g)] for g in range(groups)]
        bases_into(outs[:groups], x, y, same_ref, 0, channels)

    outs = call(
        body,
        vmem(*xs, momenta, same, spread, coupling),
        [((cells, LANES), F32, pltpu.VMEM)] * groups + [((width, width), BF16, pltpu.VMEM)],
        [],
        "first_base",
    )
    return outs[:groups], outs[groups]


def updated(field_mixed, base, x):
    y_new = base - 0.2 * field_mixed
    return jnp.clip(x + 0.5 * y_new, -1.0, 1.0), y_new


def second_base(xs, ys, later, fields, first_base, first_x, rounded, same, mixing, channels):
    groups = len(rounded)
    cells = rounded[0].shape[0]
    width = groups * LANES
    done, m = len(xs), len(later)

    def body(*refs):
        refs = list(refs)

        def take(n):
            taken = refs[:n]
            del refs[:n]
            return taken

        x = [ref[...] for ref in take(done)]
        y = [ref[...] for ref in take(done)]
        held = [ref[...] for ref in take(groups)]
        base_refs, x_refs = take(m), take(m)
        r = [ref[...] for ref in take(groups)]
        same_ref, mixing_ref = take(2)
        for i, t in enumerate(later):
            x_new, y_new = updated(
                mixed_of(held, mixing_ref, t, channels), base_refs[i][...], x_refs[i][...]
            )
            x.append(x_new)
            y.append(y_new)
            refs[2 * groups + i][...] = x_new
        bases_into(refs[:groups], x, y, same_ref, 1, channels)
        for g in range(groups):
            near = spanned(g, channels, width)
            refs[groups + g][...] = lax.dot_general(
                jnp.concatenate([r[n] for n in near], axis=1),
                mixing_ref[lanes(g), span_lanes(near)],
                (((1,), (1,)), ((), ())),
                preferred_element_type=F32,
            )

    outs = call(
        body,
        vmem(*xs, *ys, *fields, *first_base, *first_x, *rounded, same, mixing),
        [((cells, LANES), F32, pltpu.VMEM)] * (2 * groups + m),
        [],
        "second_base",
    )
    return outs[:groups], outs[groups : 2 * groups], outs[2 * groups :]


def finish(fields, xs, bases, mixing, channels):
    groups = len(xs)
    cells = xs[0].shape[0]
    width = groups * LANES
    blocks = 4 if cells % 64 == 0 else 1
    size = cells // blocks

    def body(*refs):
        field_refs, x_refs, base_refs = [refs[k * groups : (k + 1) * groups] for k in range(3)]
        mixing_ref, x_out, y_out, token, x_buf, y_buf, sems = refs[3 * groups :]
        copies = []
        for b in range(blocks):
            rows = slice(b * size, (b + 1) * size)
            held = [ref[rows, :] for ref in field_refs]
            for g in range(groups):
                x_new, y_new = updated(
                    mixed_of(held, mixing_ref, g, channels), base_refs[g][rows, :], x_refs[g][rows, :]
                )
                x_buf[rows, lanes(g)] = x_new
                y_buf[rows, lanes(g)] = y_new
            for k, (buf, out) in enumerate(((y_buf, y_out), (x_buf, x_out))):
                copies.append(pltpu.make_async_copy(buf.at[rows], out.at[rows], sems.at[b, k]))
                copies[-1].start()
        token[...] = jnp.zeros_like(token)
        for copy in copies:
            copy.wait()

    return call(
        body,
        vmem(*fields, *xs, *bases, mixing),
        [((cells, width), F32, pltpu.HBM)] * 2 + [((8, LANES), F32, pltpu.VMEM)],
        [
            pltpu.VMEM((cells, width), F32),
            pltpu.VMEM((cells, width), F32),
            pltpu.SemaphoreType.DMA((blocks, 2)),
        ],
        "finish",
    )


def add_up(arrays, token):
    def body(*refs):
        refs[-1][...] = sum(ref[...] for ref in refs[:-2])

    return call(
        body,
        vmem(*arrays, token),
        [(arrays[0].shape, F32, pltpu.VMEM)],
        [],
        "add_up",
    )[0]


def sum_over_ring(value, ring, token):
    if ring & (ring - 1):
        return lax.psum(value, RING)
    rounds, size = [], 1
    while size < ring:
        digits = (1, 2, 3) if 4 * size <= ring else (1,)
        rounds.append([size * d for d in digits])
        size *= len(digits) + 1
    for i, bits in enumerate(reversed(rounds)):
        parts = [value] + [
            lax.ppermute(value, RING, [(j, j ^ bit) for j in range(ring)]) for bit in bits
        ]
        value = add_up(parts, token) if i == 0 else sum(parts)
    return value


def local(positions, momenta, tile_values, tile_rows, tile_cols, tile_count, channel_coupling):
    cells, width = positions.shape
    slots, tile, _ = tile_values.shape
    channels = channel_coupling.shape[0]
    replicas = width // channels
    groups = width // LANES
    ring = lax.axis_size("row") * lax.axis_size("col")
    where = np.arange(width)
    same = jnp.asarray(
        (where[:, None] // channels == where[None] // channels).astype(ml_dtypes.bfloat16)
    )
    spread = jnp.asarray(
        (where[:, None] % channels == np.arange(channels)[None]).astype(ml_dtypes.bfloat16)
    )
    on_chip = [(i, i ^ 1) for i in range(ring)]
    off_chip = [(i, (i + 1) % ring if i % 2 else (i - 1) % ring) for i in range(ring)]
    wide = (cells, LANES)
    every = list(range(groups))
    first_pieces = [every[:-1], every[-1:]]
    second_pieces = [every[:1], every[1:]]

    def ring_index():
        return lax.axis_index("row") * lax.axis_size("col") + lax.axis_index("col")

    def far_swap(mine):
        return lax.ppermute(mine, RING, off_chip)

    def near_swap(mine):
        return lax.ppermute(mine, RING, on_chip)

    def ready(piece, done):
        return [
            t for t in every if t not in done and max(spanned(t, channels, width)) <= piece[-1]
        ]

    def keep(done, _, outs):
        outs[0][...] = done[0]

    def needed(todo, piece):
        return sorted({n for t in todo for n in spanned(t, channels, width)} - set(piece))

    xs, owns, sent = load_first(positions, first_pieces[0])
    fars = [far_swap(sent)]
    lists, more_x, more_own = make_lists(
        tile_rows, tile_cols, tile_count, positions, first_pieces[1], sent, slots, tile, ring_index
    )
    xs, owns = [*xs, *more_x], [*owns, *more_own]
    others = [near_swap(r) for r in owns]
    base, mixing = first_base(xs, momenta, same, spread, channel_coupling, channels)
    near, sent = near_fields(
        lists, tile_values, owns, others, None, None, more_own, [mixing], "near_first"
    )
    fars.append(far_swap(sent[0]))

    fields, new_x, new_y, rounded, new_fars = {}, [], [], {}, []
    for p, piece in enumerate(first_pieces):
        last = p == len(first_pieces) - 1
        todo = ready(piece, rounded)
        known = needed(todo, piece)
        assert second_pieces[p] == todo

        def work(done, ins, outs, piece=piece, todo=todo, known=known, last=last):
            held = {n: ins[1 + i][...] for i, n in enumerate(known)}
            done = [field.astype(BF16) for field in done]
            held.update(zip(piece, done))
            rest = ins[1 + len(known) :]
            for i, t in enumerate(todo):
                x_new, y_new = updated(
                    mixed_of(held, ins[0], t, channels), rest[2 * i][...], rest[2 * i + 1][...]
                )
                r_new = x_new.astype(BF16)
                outs[0][:, lanes(i)] = r_new
                outs[1 + i][...] = r_new
                if not last:
                    outs[1 + len(todo) + len(piece) + 2 * i][...] = x_new
                    outs[2 + len(todo) + len(piece) + 2 * i][...] = y_new
            for i, field in enumerate(done):
                outs[1 + len(todo) + i][...] = field

        results = far_fields(
            lists,
            tile_values,
            [near[n] for n in piece],
            fars[p],
            [mixing] + [fields[n] for n in known] + [a for t in todo for a in (base[t], xs[t])],
            [((cells, len(todo) * LANES), BF16)]
            + [(wide, BF16)] * (len(todo) + len(piece))
            + ([] if last else [(wide, F32)] * (2 * len(todo))),
            work,
            f"far_first_{p}",
        )
        new_fars.append(far_swap(results[0]))
        rounded.update(zip(todo, results[1:]))
        fields.update(zip(piece, results[1 + len(todo) :]))
        new_x += results[1 + len(todo) + len(piece) :: 2]
        new_y += results[2 + len(todo) + len(piece) :: 2]

    owns = [rounded[g] for g in every]
    others = [near_swap(r) for r in owns]
    (part,) = far_fields(
        lists, tile_values, [], new_fars[0], [], [(wide, F32)], keep, "far_second_0", NEAR_FLOPS
    )
    later = second_pieces[1]
    base, weights, more_x = second_base(
        new_x,
        new_y,
        later,
        [fields[g] for g in every],
        [base[t] for t in later],
        [xs[t] for t in later],
        owns,
        same,
        mixing,
        channels,
    )
    xs = [*new_x, *more_x]
    near, (share,) = near_fields(
        lists, tile_values, owns, others, part, weights[0], [], [], "near_second"
    )
    piece = second_pieces[1]

    def last_work(done, ins, outs):
        held = [field.astype(BF16) for field in done]
        for out, field in zip(outs, held):
            out[...] = field
        row = jnp.concatenate(
            [ins[0][...]] + [weighted(field, ref) for field, ref in zip(held, ins[1:])], axis=1
        )
        row = jnp.broadcast_to(row, (replicas, width))
        lane = lax.broadcasted_iota(jnp.int32, (replicas, width), 1)
        first = lax.broadcasted_iota(jnp.int32, (replicas, width), 0) * channels
        inside = (lane >= first) & (lane < first + channels)
        total = jnp.sum(jnp.where(inside, row, 0.0), axis=1, keepdims=True)
        place = lax.broadcasted_iota(jnp.int32, (replicas, LANES), 1)
        which = lax.broadcasted_iota(jnp.int32, (replicas, LANES), 0)
        flat = jnp.sum(jnp.where(place == which, total, 0.0), axis=0, keepdims=True)
        outs[len(piece)][...] = jnp.broadcast_to(flat, (8, LANES))

    results = far_fields(
        lists,
        tile_values,
        near[1:],
        new_fars[1],
        [share, *weights[1:]],
        [(wide, BF16)] * len(piece) + [((8, LANES), F32)],
        last_work,
        "far_second_1",
        through=[near[0], *xs, *base, mixing],
    )
    fields, partial, kept = results[: len(piece)], results[len(piece)], results[len(piece) + 1 :]
    fields, kept = [kept[0], *fields], kept[1:]

    x_new, y_new, token = finish(
        fields, kept[:groups], kept[groups : 2 * groups], kept[2 * groups], channels
    )
    total = sum_over_ring(partial, ring, token)
    energy = total[0, :replicas] / jnp.sqrt(jnp.float32(cells * ring * channels))
    return (x_new, y_new, energy)


def solution(mesh):
    cells = P(("groups", "row", "col"), None)
    slots = P(("groups", "row", "col"))
    return jax.shard_map(
        local,
        mesh=mesh,
        in_specs=(cells, cells, P(("groups", "row", "col"), None, None), slots, slots, slots, P()),
        out_specs=(cells, cells, P("groups")),
        check_vma=False,
    )
```

```python
import jax
import jax.numpy as jnp
import ml_dtypes
import numpy as np
from jax import lax
from jax.experimental import pallas as pl
from jax.experimental.pallas import tpu as pltpu
from jax.sharding import PartitionSpec as P

STEPS = 2
LANES = 128
LONG, SHORT = 16, 4
VMEM_LIMIT = 14 * 1024 * 1024
NEAR_FLOPS = 4 * 10**9
F32 = jnp.float32
BF16 = jnp.bfloat16
RING = ("row", "col")


def call(body, ins, outs, scratch, name, flops=0, aliases=()):
    return pl.pallas_call(
        body,
        in_specs=[pl.BlockSpec(memory_space=pl.ANY if s is pltpu.HBM else s) for _, s in ins],
        out_specs=[pl.BlockSpec(memory_space=pl.ANY if s is pltpu.HBM else s) for *_, s in outs],
        out_shape=[
            jax.ShapeDtypeStruct(dims, kind) if s is pltpu.HBM else s(dims, kind)
            for dims, kind, s in outs
        ],
        scratch_shapes=scratch,
        input_output_aliases=dict(aliases),
        compiler_params=pltpu.CompilerParams(vmem_limit_bytes=VMEM_LIMIT),
        cost_estimate=pl.CostEstimate(
            flops=int(flops) or 1000, bytes_accessed=1000, transcendentals=0
        ),
        name=name,
    )(*[pltpu.with_memory_space_constraint(a, s) for a, s in ins])


def vmem(*arrays):
    return [(a, pltpu.VMEM) for a in arrays]


def lanes(group):
    return slice(group * LANES, (group + 1) * LANES)


def spanned(group, channels, width):
    first = group * LANES // channels * channels
    last = -(-(group + 1) * LANES // channels) * channels
    return list(range(first // LANES, -(-min(last, width) // LANES)))


def span_lanes(near):
    return slice(near[0] * LANES, (near[-1] + 1) * LANES)


def split(x):
    high = x.astype(BF16)
    return high, (x - high.astype(F32)).astype(BF16)


def bases_into(outs, xs, ys, same, step, channels):
    groups = len(xs)
    width = groups * LANES
    detune = 1.0 - (step + 1.0) / (STEPS + 1.0)
    parts = [split(x) for x in xs]
    for g in range(groups):
        near = spanned(g, channels, width)
        ones = same[span_lanes(near), lanes(g)]
        totals = sum(
            jnp.dot(
                jnp.concatenate([parts[n][k] for n in near], axis=1),
                ones,
                preferred_element_type=F32,
            )
            for k in range(2)
        )
        penalty = 0.02 * (totals - (2.0 - channels))
        outs[g][...] = ys[g] + 0.5 * (-detune * xs[g] - 0.4 * penalty)


def mixed_of(fields, mixing, group, channels):
    near = spanned(group, channels, mixing.shape[0])
    return jnp.dot(
        jnp.concatenate([fields[n] for n in near], axis=1),
        mixing[span_lanes(near), lanes(group)],
        preferred_element_type=F32,
    )


def load_first(positions, groups_of):
    cells = positions.shape[0]
    n = len(groups_of)

    def body(x_ref, *refs):
        x_outs, r_outs, sent, sems = refs[:n], refs[n : 2 * n], refs[2 * n], refs[-1]
        copies = [
            pltpu.make_async_copy(x_ref.at[:, lanes(g)], x_outs[i], sems.at[i])
            for i, g in enumerate(groups_of)
        ]
        for copy in copies:
            copy.start()
        for i, copy in enumerate(copies):
            copy.wait()
            rounded = x_outs[i][...].astype(BF16)
            r_outs[i][...] = rounded
            sent[:, lanes(i)] = rounded

    outs = call(
        body,
        [(positions, pltpu.HBM)],
        [((cells, LANES), F32, pltpu.VMEM)] * n
        + [((cells, LANES), BF16, pltpu.VMEM)] * n
        + [((cells, n * LANES), BF16, pltpu.VMEM)],
        [pltpu.SemaphoreType.DMA((n,))],
        "load_first",
    )
    return outs[:n], outs[n : 2 * n], outs[2 * n]


def section(slots, per):
    return -(-(slots + per) // (2 * SHORT)) * SHORT


def make_lists(rows, cols, count, positions, groups_of, after, slots, tile, ring_index):
    cells = positions.shape[0]
    per = cells // tile
    pairs = section(slots, per)
    n = len(groups_of)

    def body(rows_hbm, cols_hbm, count_hbm, x_ref, _, list_ref, *refs):
        x_outs, r_outs = refs[:n], refs[n : 2 * n]
        rows_ref, cols_ref, count_ref, held, sems = refs[2 * n :]
        copies = [
            pltpu.make_async_copy(*ends, sems.at[k])
            for k, ends in enumerate(
                [(rows_hbm, rows_ref), (cols_hbm, cols_ref), (count_hbm, count_ref)]
                + [(x_ref.at[:, lanes(g)], x_outs[i]) for i, g in enumerate(groups_of)]
            )
        ]
        for copy in copies:
            copy.start()
        for k in range(2 * per):
            held[k] = -1
        far_third = jnp.where(lax.rem(ring_index(), 2) == 1, 2, 0)
        for copy in copies[:3]:
            copy.wait()

        def visit(slot, totals):
            near_pairs, far_pairs = totals
            row, col = rows_ref[slot], cols_ref[slot]
            third = jnp.where(col >= 2 * per, 2, jnp.where(col >= per, 1, 0))
            source = col - third * per
            far = third == far_third
            source = jnp.where(far | (third == 1), source, source + per)
            key = row + jnp.where(far, per, 0)
            place = 2 * jnp.where(far, far_pairs + pairs, near_pairs)
            entry = slot * 65536 + source * 256 + row
            other = held[key]
            full = other >= 0
            list_ref[place] = other
            list_ref[place + 1] = entry
            held[key] = jnp.where(full, -1, entry)
            one = full.astype(jnp.int32)
            far_one = jnp.where(far, one, 0)
            return near_pairs + one - far_one, far_pairs + far_one

        totals = lax.fori_loop(0, count_ref[0], visit, (jnp.int32(0), jnp.int32(0)))
        for part, zero in enumerate((2 * per, per)):
            total = totals[part]
            start = part * pairs
            for k in range(per):
                other = held[part * per + k]
                list_ref[2 * (start + total)] = other
                list_ref[2 * (start + total) + 1] = zero * 256 + k
                total = total + (other >= 0).astype(jnp.int32)
            short_turns = (total + SHORT - 1) // SHORT

            def pad(pair, carry, start=start, zero=zero):
                for e in range(2):
                    list_ref[2 * (start + pair) + e] = zero * 256 + per
                return carry

            lax.fori_loop(total, short_turns * SHORT, pad, 0)
            list_ref[4 * pairs + 2 * part] = short_turns // (LONG // SHORT)
            list_ref[4 * pairs + 2 * part + 1] = short_turns % (LONG // SHORT)
        for i, copy in enumerate(copies[3:]):
            copy.wait()
            r_outs[i][...] = x_outs[i][...].astype(BF16)

    outs = call(
        body,
        [(a, pl.ANY) for a in (rows, cols, count)] + [(positions, pltpu.HBM)] + vmem(after),
        [((4 * pairs + 4 + 2,), jnp.int32, pltpu.SMEM)]
        + [((cells, LANES), F32, pltpu.VMEM)] * n
        + [((cells, LANES), BF16, pltpu.VMEM)] * n,
        [
            pltpu.SMEM(rows.shape, jnp.int32),
            pltpu.SMEM(cols.shape, jnp.int32),
            pltpu.SMEM(count.shape, jnp.int32),
            pltpu.SMEM((2 * per,), jnp.int32),
            pltpu.SemaphoreType.DMA((3 + n,)),
        ],
        "make_lists",
    )
    return outs[0], outs[1 : 1 + n], outs[1 + n :]


def add_pairs(part, list_ref, tiles, field, window, pairs):
    def turn(first, length):
        for u in range(length):
            place = 2 * (part * pairs + first + u)
            entries = [list_ref[place + e] for e in range(2)]
            left = jnp.concatenate([tiles[n >> 16] for n in entries], axis=1)
            right = jnp.concatenate([window[(n >> 8) & 255] for n in entries], axis=0)
            field[entries[1] & 255] += jnp.dot(left, right, preferred_element_type=F32)

    def long(i, carry):
        turn(i * LONG, LONG)
        return carry

    def short(i, carry):
        turn(long_turns * LONG + i * SHORT, SHORT)
        return carry

    long_turns = list_ref[4 * pairs + 2 * part]
    lax.fori_loop(0, long_turns, long, 0)
    lax.fori_loop(0, list_ref[4 * pairs + 2 * part + 1], short, 0)


def near_fields(lists, tiles, owns, others, far_part, sent, after, flops, name):
    slots, tile, _ = tiles.shape
    cells = owns[0].shape[0]
    groups = len(owns)
    width = groups * LANES
    per = cells // tile
    pairs = section(slots, per)
    start = [] if far_part is None else [far_part]

    def body(list_ref, tiles_ref, *refs):
        own_refs, other_refs, refs = refs[:groups], refs[groups : 2 * groups], refs[2 * groups :]
        start_refs, refs = refs[: len(start)], refs[len(start) :]
        sent_refs, refs = refs[: len(sent)], refs[len(sent) + len(after) :]
        field_outs, sent_outs, (field, window) = refs[:groups], refs[groups:-2], refs[-2:]
        for out, ref in zip(sent_outs, sent_refs):
            out[...] = ref[...]
        for g in range(groups):
            window[:per, :, lanes(g)] = own_refs[g][...].reshape(per, tile, LANES)
            window[per : 2 * per, :, lanes(g)] = other_refs[g][...].reshape(per, tile, LANES)
        window[2 * per] = jnp.zeros((tile, width), BF16)
        field[:per] = jnp.zeros((per, tile, width), F32)
        for ref in start_refs:
            field[:per, :, lanes(0)] = ref[...].reshape(per, tile, LANES)
        add_pairs(0, list_ref, tiles_ref, field, window, pairs)
        for g, out in enumerate(field_outs):
            out[...] = field[:per, :, lanes(g)].reshape(cells, LANES).astype(out.dtype)

    outs = call(
        body,
        [(lists, pltpu.SMEM)] + vmem(tiles, *owns, *others, *start, *sent, *after),
        [
            ((cells, LANES), BF16 if start and g == 0 else F32, pltpu.VMEM)
            for g in range(groups)
        ]
        + [(a.shape, BF16, pltpu.VMEM) for a in sent],
        [
            pltpu.VMEM((per + 1, tile, width), F32),
            pltpu.VMEM((2 * per + 1, tile, width), BF16),
        ],
        name,
        flops,
    )
    return outs[:groups], outs[groups:]


def far_fields(lists, tiles, nears, far, extra, outs_of, work, name, flops=0, through=()):
    slots, tile, _ = tiles.shape
    cells, width = far.shape
    per = cells // tile
    pairs = section(slots, per)
    n = width // LANES
    m = len(nears)

    def body(list_ref, tiles_ref, far_ref, *refs):
        near_refs, extra_refs = refs[:m], refs[m : m + len(extra)]
        through_refs = refs[m + len(extra) : m + len(extra) + len(through)]
        out_refs, (field, window) = refs[m + len(extra) + len(through) : -2], refs[-2:]
        window[:per] = far_ref[...].reshape(per, tile, width)
        window[per] = jnp.zeros((tile, width), BF16)
        if not near_refs:
            field[:per] = jnp.zeros((per, tile, width), F32)
        for i, ref in enumerate(near_refs):
            field[:per, :, lanes(i)] = ref[...].reshape(per, tile, LANES)
        add_pairs(1, list_ref, tiles_ref, field, window, pairs)
        done = [field[:per, :, lanes(i)].reshape(cells, LANES) for i in range(n)]
        work(done, [*extra_refs, *through_refs], out_refs[: len(outs_of)])

    return call(
        body,
        [(lists, pltpu.SMEM)] + vmem(tiles, far, *nears, *extra, *through),
        [(*out, pltpu.VMEM) for out in outs_of] + [(a.shape, a.dtype, pltpu.VMEM) for a in through],
        [pltpu.VMEM((per + 1, tile, width), F32), pltpu.VMEM((per + 1, tile, width), BF16)],
        name,
        flops,
        [(3 + m + len(extra) + i, len(outs_of) + i) for i in range(len(through))],
    )


def first_base(xs, momenta, same, spread, coupling, channels):
    cells, width = momenta.shape
    groups = len(xs)

    def body(*refs):
        x_refs, (y_ref, same_ref, spread_ref, coupling_ref) = refs[:groups], refs[groups : groups + 4]
        outs = refs[groups + 4 :]
        tall = jnp.dot(spread_ref[...], coupling_ref[...], preferred_element_type=F32).astype(BF16)
        wide = lax.dot_general(
            tall, spread_ref[...], (((1,), (1,)), ((), ())), preferred_element_type=F32
        )
        outs[groups][...] = (wide * same_ref[...].astype(F32)).astype(BF16)
        x = [ref[...] for ref in x_refs]
        y = [y_ref[:, lanes(g)] for g in range(groups)]
        bases_into(outs[:groups], x, y, same_ref, 0, channels)

    outs = call(
        body,
        vmem(*xs, momenta, same, spread, coupling),
        [((cells, LANES), F32, pltpu.VMEM)] * groups + [((width, width), BF16, pltpu.VMEM)],
        [],
        "first_base",
    )
    return outs[:groups], outs[groups]


def updated(field_mixed, base, x):
    y_new = base - 0.2 * field_mixed
    return jnp.clip(x + 0.5 * y_new, -1.0, 1.0), y_new


def second_base(xs, ys, later, fields, first_base, first_x, rounded, same, mixing, channels):
    groups = len(rounded)
    cells = rounded[0].shape[0]
    width = groups * LANES
    done, m = len(xs), len(later)

    def body(*refs):
        refs = list(refs)

        def take(n):
            taken = refs[:n]
            del refs[:n]
            return taken

        x = [ref[...] for ref in take(done)]
        y = [ref[...] for ref in take(done)]
        held = [ref[...] for ref in take(groups)]
        base_refs, x_refs = take(m), take(m)
        r = [ref[...] for ref in take(groups)]
        same_ref, mixing_ref = take(2)
        for i, t in enumerate(later):
            x_new, y_new = updated(
                mixed_of(held, mixing_ref, t, channels), base_refs[i][...], x_refs[i][...]
            )
            x.append(x_new)
            y.append(y_new)
            refs[2 * groups + i][...] = x_new
        bases_into(refs[:groups], x, y, same_ref, 1, channels)
        for g in range(groups):
            near = spanned(g, channels, width)
            refs[groups + g][...] = lax.dot_general(
                jnp.concatenate([r[n] for n in near], axis=1),
                mixing_ref[lanes(g), span_lanes(near)],
                (((1,), (1,)), ((), ())),
                preferred_element_type=F32,
            )

    outs = call(
        body,
        vmem(*xs, *ys, *fields, *first_base, *first_x, *rounded, same, mixing),
        [((cells, LANES), F32, pltpu.VMEM)] * (2 * groups + m),
        [],
        "second_base",
    )
    return outs[:groups], outs[groups : 2 * groups], outs[2 * groups :]


def finish(fields, xs, bases, mixing, channels):
    groups = len(xs)
    cells = xs[0].shape[0]
    width = groups * LANES

    def body(*refs):
        field_refs, x_refs, base_refs = [refs[k * groups : (k + 1) * groups] for k in range(3)]
        mixing_ref, x_out, y_out, token, x_buf, y_buf, sems = refs[3 * groups :]
        held = [ref[...] for ref in field_refs]
        copies = []
        for g in range(groups):
            y_new = base_refs[g][...] - 0.2 * mixed_of(held, mixing_ref, g, channels)
            y_buf[g] = y_new
            x_buf[g] = jnp.clip(x_refs[g][...] + 0.5 * y_new, -1.0, 1.0)
            for k, (buf, out) in enumerate(((y_buf, y_out), (x_buf, x_out))):
                copies.append(
                    pltpu.make_async_copy(buf.at[g], out.at[:, lanes(g)], sems.at[g, k])
                )
                copies[-1].start()
        token[...] = jnp.zeros_like(token)
        for copy in copies:
            copy.wait()

    return call(
        body,
        vmem(*fields, *xs, *bases, mixing),
        [((cells, width), F32, pltpu.HBM)] * 2 + [((8, LANES), F32, pltpu.VMEM)],
        [
            pltpu.VMEM((groups, cells, LANES), F32),
            pltpu.VMEM((groups, cells, LANES), F32),
            pltpu.SemaphoreType.DMA((groups, 2)),
        ],
        "finish",
    )


def copies_of(rows):
    return [((rows * n, LANES), F32) for n in (1, 2, 3)]


def spread_out(outs, value):
    for out in outs:
        out[...] = jnp.concatenate([value] * (out.shape[0] // value.shape[0]), axis=0)


def add_up(arrays, token, name):
    rows = arrays[0].shape[0]

    def body(*refs):
        total = refs[0][...]
        for ref in refs[1 : len(arrays)]:
            total = total + ref[:rows, :]
        spread_out(refs[len(arrays) + len(token) :], total)

    return call(
        body,
        vmem(*arrays, *token),
        [(*size, pltpu.VMEM) for size in copies_of(rows)],
        [],
        name,
    )


def sum_over_ring(values, ring, token):
    if ring & (ring - 1):
        return lax.psum(values[0], RING)
    rounds, size = [], 1
    while size < ring:
        digits = (1, 2, 3) if 4 * size <= ring else (1,)
        rounds.append([size * d for d in digits])
        size *= len(digits) + 1
    for i, bits in enumerate(reversed(rounds)):
        received = [
            lax.ppermute(value, RING, [(j, j ^ bit) for j in range(ring)])
            for value, bit in zip(values, bits)
        ]
        values = add_up([values[0], *received], [token] if i == 0 else [], f"add_up_{i}")
    return values[0]


def local(positions, momenta, tile_values, tile_rows, tile_cols, tile_count, channel_coupling):
    cells, width = positions.shape
    slots, tile, _ = tile_values.shape
    channels = channel_coupling.shape[0]
    replicas = width // channels
    groups = width // LANES
    ring = lax.axis_size("row") * lax.axis_size("col")
    where = np.arange(width)
    same = jnp.asarray(
        (where[:, None] // channels == where[None] // channels).astype(ml_dtypes.bfloat16)
    )
    spread = jnp.asarray(
        (where[:, None] % channels == np.arange(channels)[None]).astype(ml_dtypes.bfloat16)
    )
    on_chip = [(i, i ^ 1) for i in range(ring)]
    off_chip = [(i, (i + 1) % ring if i % 2 else (i - 1) % ring) for i in range(ring)]
    wide = (cells, LANES)
    every = list(range(groups))
    first_pieces = [every[:-1], every[-1:]]
    second_pieces = [every[:1], every[1:]]

    def ring_index():
        return lax.axis_index("row") * lax.axis_size("col") + lax.axis_index("col")

    def far_swap(mine):
        return lax.ppermute(mine, RING, off_chip)

    def near_swap(mine):
        return lax.ppermute(mine, RING, on_chip)

    def ready(piece, done):
        return [
            t for t in every if t not in done and max(spanned(t, channels, width)) <= piece[-1]
        ]

    def keep(done, _, outs):
        outs[0][...] = done[0]

    def needed(todo, piece):
        return sorted({n for t in todo for n in spanned(t, channels, width)} - set(piece))

    xs, owns, sent = load_first(positions, first_pieces[0])
    fars = [far_swap(sent)]
    lists, more_x, more_own = make_lists(
        tile_rows, tile_cols, tile_count, positions, first_pieces[1], sent, slots, tile, ring_index
    )
    xs, owns = [*xs, *more_x], [*owns, *more_own]
    others = [near_swap(r) for r in owns]
    base, mixing = first_base(xs, momenta, same, spread, channel_coupling, channels)
    near, sent = near_fields(
        lists, tile_values, owns, others, None, more_own, [mixing], 0, "near_first"
    )
    fars.append(far_swap(sent[0]))

    fields, new_x, new_y, rounded, new_fars = {}, [], [], {}, []
    for p, piece in enumerate(first_pieces):
        last = p == len(first_pieces) - 1
        todo = ready(piece, rounded)
        known = needed(todo, piece)
        assert second_pieces[p] == todo

        def work(done, ins, outs, piece=piece, todo=todo, known=known, last=last):
            held = {n: ins[1 + i][...] for i, n in enumerate(known)}
            done = [field.astype(BF16) for field in done]
            held.update(zip(piece, done))
            rest = ins[1 + len(known) :]
            for i, t in enumerate(todo):
                x_new, y_new = updated(
                    mixed_of(held, ins[0], t, channels), rest[2 * i][...], rest[2 * i + 1][...]
                )
                r_new = x_new.astype(BF16)
                outs[0][:, lanes(i)] = r_new
                outs[1 + i][...] = r_new
                if not last:
                    outs[1 + len(todo) + len(piece) + 2 * i][...] = x_new
                    outs[2 + len(todo) + len(piece) + 2 * i][...] = y_new
            for i, field in enumerate(done):
                outs[1 + len(todo) + i][...] = field

        results = far_fields(
            lists,
            tile_values,
            [near[n] for n in piece],
            fars[p],
            [mixing] + [fields[n] for n in known] + [a for t in todo for a in (base[t], xs[t])],
            [((cells, len(todo) * LANES), BF16)]
            + [(wide, BF16)] * (len(todo) + len(piece))
            + ([] if last else [(wide, F32)] * (2 * len(todo))),
            work,
            f"far_first_{p}",
        )
        new_fars.append(far_swap(results[0]))
        rounded.update(zip(todo, results[1:]))
        fields.update(zip(piece, results[1 + len(todo) :]))
        new_x += results[1 + len(todo) + len(piece) :: 2]
        new_y += results[2 + len(todo) + len(piece) :: 2]

    owns = [rounded[g] for g in every]
    others = [near_swap(r) for r in owns]
    (part,) = far_fields(
        lists, tile_values, [], new_fars[0], [], [(wide, F32)], keep, "far_second_0", NEAR_FLOPS
    )
    near, _ = near_fields(lists, tile_values, owns, others, part, [], [], 0, "near_second")
    later = second_pieces[1]
    base, weights, more_x = second_base(
        new_x,
        new_y,
        later,
        [fields[g] for g in every],
        [base[t] for t in later],
        [xs[t] for t in later],
        owns,
        same,
        mixing,
        channels,
    )
    xs = [*new_x, *more_x]
    piece = second_pieces[1]

    def last_work(done, ins, outs):
        held = [ins[groups][...]] + [field.astype(BF16) for field in done]
        for out, field in zip(outs, held[1:]):
            out[...] = field
        row = jnp.concatenate(
            [
                jnp.sum(field.astype(F32) * ref[...], axis=0, keepdims=True)
                for field, ref in zip(held, ins[:groups])
            ],
            axis=1,
        )
        row = jnp.broadcast_to(row, (replicas, width))
        lane = lax.broadcasted_iota(jnp.int32, (replicas, width), 1)
        first = lax.broadcasted_iota(jnp.int32, (replicas, width), 0) * channels
        inside = (lane >= first) & (lane < first + channels)
        total = jnp.sum(jnp.where(inside, row, 0.0), axis=1, keepdims=True)
        place = lax.broadcasted_iota(jnp.int32, (replicas, LANES), 1)
        which = lax.broadcasted_iota(jnp.int32, (replicas, LANES), 0)
        flat = jnp.sum(jnp.where(place == which, total, 0.0), axis=0, keepdims=True)
        spread_out(outs[len(piece) :], jnp.broadcast_to(flat, (8, LANES)))

    results = far_fields(
        lists,
        tile_values,
        near[1:],
        new_fars[1],
        weights,
        [(wide, BF16)] * len(piece) + copies_of(8),
        last_work,
        "far_second_1",
        through=[near[0], *xs, *base, mixing],
    )
    sent = len(piece) + len(copies_of(8))
    fields, partials, kept = results[: len(piece)], results[len(piece) : sent], results[sent:]
    fields, kept = [kept[0], *fields], kept[1:]

    x_new, y_new, token = finish(
        fields, kept[:groups], kept[groups : 2 * groups], kept[2 * groups], channels
    )
    total = sum_over_ring(partials, ring, token)
    energy = total[0, :replicas] / jnp.sqrt(jnp.float32(cells * ring * channels))
    return (x_new, y_new, energy)


def solution(mesh):
    cells = P(("groups", "row", "col"), None)
    slots = P(("groups", "row", "col"))
    return jax.shard_map(
        local,
        mesh=mesh,
        in_specs=(cells, cells, P(("groups", "row", "col"), None, None), slots, slots, slots, P()),
        out_specs=(cells, cells, P("groups")),
        check_vma=False,
    )
```

```python
import jax
import jax.numpy as jnp
import ml_dtypes
import numpy as np
from jax import lax
from jax.experimental import pallas as pl
from jax.experimental.pallas import tpu as pltpu
from jax.sharding import PartitionSpec as P

STEPS = 2
LANES = 128
LONG, SHORT = 16, 4
VMEM_LIMIT = 14 * 1024 * 1024
NEAR_FLOPS = 4 * 10**9
F32 = jnp.float32
BF16 = jnp.bfloat16
RING = ("row", "col")


def call(body, ins, outs, scratch, name, flops=0, aliases=()):
    return pl.pallas_call(
        body,
        in_specs=[pl.BlockSpec(memory_space=pl.ANY if s is pltpu.HBM else s) for _, s in ins],
        out_specs=[pl.BlockSpec(memory_space=pl.ANY if s is pltpu.HBM else s) for *_, s in outs],
        out_shape=[
            jax.ShapeDtypeStruct(dims, kind) if s is pltpu.HBM else s(dims, kind)
            for dims, kind, s in outs
        ],
        scratch_shapes=scratch,
        input_output_aliases=dict(aliases),
        compiler_params=pltpu.CompilerParams(vmem_limit_bytes=VMEM_LIMIT),
        cost_estimate=pl.CostEstimate(
            flops=int(flops) or 1000, bytes_accessed=1000, transcendentals=0
        ),
        name=name,
    )(*[pltpu.with_memory_space_constraint(a, s) for a, s in ins])


def vmem(*arrays):
    return [(a, pltpu.VMEM) for a in arrays]


def lanes(group):
    return slice(group * LANES, (group + 1) * LANES)


def spanned(group, channels, width):
    first = group * LANES // channels * channels
    last = -(-(group + 1) * LANES // channels) * channels
    return list(range(first // LANES, -(-min(last, width) // LANES)))


def span_lanes(near):
    return slice(near[0] * LANES, (near[-1] + 1) * LANES)


def split(x):
    high = x.astype(BF16)
    return high, (x - high.astype(F32)).astype(BF16)


def bases_into(outs, xs, ys, same, step, channels):
    groups = len(xs)
    width = groups * LANES
    detune = 1.0 - (step + 1.0) / (STEPS + 1.0)
    parts = [split(x) for x in xs]
    for g in range(groups):
        near = spanned(g, channels, width)
        ones = same[span_lanes(near), lanes(g)]
        totals = sum(
            jnp.dot(
                jnp.concatenate([parts[n][k] for n in near], axis=1),
                ones,
                preferred_element_type=F32,
            )
            for k in range(2)
        )
        penalty = 0.02 * (totals - (2.0 - channels))
        outs[g][...] = ys[g] + 0.5 * (-detune * xs[g] - 0.4 * penalty)


def mixed_of(fields, mixing, group, channels):
    near = spanned(group, channels, mixing.shape[0])
    return jnp.dot(
        jnp.concatenate([fields[n] for n in near], axis=1),
        mixing[span_lanes(near), lanes(group)],
        preferred_element_type=F32,
    )


def load_first(positions, groups_of):
    cells = positions.shape[0]
    n = len(groups_of)

    def body(x_ref, *refs):
        x_outs, r_outs, sent, sems = refs[:n], refs[n : 2 * n], refs[2 * n], refs[-1]
        copies = [
            pltpu.make_async_copy(x_ref.at[:, lanes(g)], x_outs[i], sems.at[i])
            for i, g in enumerate(groups_of)
        ]
        for copy in copies:
            copy.start()
        for i, copy in enumerate(copies):
            copy.wait()
            rounded = x_outs[i][...].astype(BF16)
            r_outs[i][...] = rounded
            sent[:, lanes(i)] = rounded

    outs = call(
        body,
        [(positions, pltpu.HBM)],
        [((cells, LANES), F32, pltpu.VMEM)] * n
        + [((cells, LANES), BF16, pltpu.VMEM)] * n
        + [((cells, n * LANES), BF16, pltpu.VMEM)],
        [pltpu.SemaphoreType.DMA((n,))],
        "load_first",
    )
    return outs[:n], outs[n : 2 * n], outs[2 * n]


def section(slots, per):
    return -(-(slots + per) // (2 * SHORT)) * SHORT


def make_lists(rows, cols, count, positions, groups_of, after, slots, tile, ring_index):
    cells = positions.shape[0]
    per = cells // tile
    pairs = section(slots, per)
    n = len(groups_of)

    def body(rows_hbm, cols_hbm, count_hbm, x_ref, _, list_ref, *refs):
        x_outs, r_outs = refs[:n], refs[n : 2 * n]
        rows_ref, cols_ref, count_ref, held, sems = refs[2 * n :]
        copies = [
            pltpu.make_async_copy(*ends, sems.at[k])
            for k, ends in enumerate(
                [(rows_hbm, rows_ref), (cols_hbm, cols_ref), (count_hbm, count_ref)]
                + [(x_ref.at[:, lanes(g)], x_outs[i]) for i, g in enumerate(groups_of)]
            )
        ]
        for copy in copies:
            copy.start()
        for k in range(2 * per):
            held[k] = -1
        far_third = jnp.where(lax.rem(ring_index(), 2) == 1, 2, 0)
        for copy in copies[:3]:
            copy.wait()

        def visit(slot, totals):
            near_pairs, far_pairs = totals
            row, col = rows_ref[slot], cols_ref[slot]
            third = jnp.where(col >= 2 * per, 2, jnp.where(col >= per, 1, 0))
            source = col - third * per
            far = third == far_third
            source = jnp.where(far | (third == 1), source, source + per)
            key = row + jnp.where(far, per, 0)
            place = 2 * jnp.where(far, far_pairs + pairs, near_pairs)
            entry = slot * 65536 + source * 256 + row
            other = held[key]
            full = other >= 0
            list_ref[place] = other
            list_ref[place + 1] = entry
            held[key] = jnp.where(full, -1, entry)
            one = full.astype(jnp.int32)
            far_one = jnp.where(far, one, 0)
            return near_pairs + one - far_one, far_pairs + far_one

        totals = lax.fori_loop(0, count_ref[0], visit, (jnp.int32(0), jnp.int32(0)))
        for part, zero in enumerate((2 * per, per)):
            total = totals[part]
            start = part * pairs
            for k in range(per):
                other = held[part * per + k]
                list_ref[2 * (start + total)] = other
                list_ref[2 * (start + total) + 1] = zero * 256 + k
                total = total + (other >= 0).astype(jnp.int32)
            short_turns = (total + SHORT - 1) // SHORT

            def pad(pair, carry, start=start, zero=zero):
                for e in range(2):
                    list_ref[2 * (start + pair) + e] = zero * 256 + per
                return carry

            lax.fori_loop(total, short_turns * SHORT, pad, 0)
            list_ref[4 * pairs + 2 * part] = short_turns // (LONG // SHORT)
            list_ref[4 * pairs + 2 * part + 1] = short_turns % (LONG // SHORT)
        for i, copy in enumerate(copies[3:]):
            copy.wait()
            r_outs[i][...] = x_outs[i][...].astype(BF16)

    outs = call(
        body,
        [(a, pl.ANY) for a in (rows, cols, count)] + [(positions, pltpu.HBM)] + vmem(after),
        [((4 * pairs + 4 + 2,), jnp.int32, pltpu.SMEM)]
        + [((cells, LANES), F32, pltpu.VMEM)] * n
        + [((cells, LANES), BF16, pltpu.VMEM)] * n,
        [
            pltpu.SMEM(rows.shape, jnp.int32),
            pltpu.SMEM(cols.shape, jnp.int32),
            pltpu.SMEM(count.shape, jnp.int32),
            pltpu.SMEM((2 * per,), jnp.int32),
            pltpu.SemaphoreType.DMA((3 + n,)),
        ],
        "make_lists",
    )
    return outs[0], outs[1 : 1 + n], outs[1 + n :]


def add_pairs(part, list_ref, tiles, field, window, pairs):
    def turn(first, length):
        for u in range(length):
            place = 2 * (part * pairs + first + u)
            entries = [list_ref[place + e] for e in range(2)]
            left = jnp.concatenate([tiles[n >> 16] for n in entries], axis=1)
            right = jnp.concatenate([window[(n >> 8) & 255] for n in entries], axis=0)
            field[entries[1] & 255] += jnp.dot(left, right, preferred_element_type=F32)

    def long(i, carry):
        turn(i * LONG, LONG)
        return carry

    def short(i, carry):
        turn(long_turns * LONG + i * SHORT, SHORT)
        return carry

    long_turns = list_ref[4 * pairs + 2 * part]
    lax.fori_loop(0, long_turns, long, 0)
    lax.fori_loop(0, list_ref[4 * pairs + 2 * part + 1], short, 0)


def near_fields(lists, tiles, owns, others, far_part, sent, after, flops, name):
    slots, tile, _ = tiles.shape
    cells = owns[0].shape[0]
    groups = len(owns)
    width = groups * LANES
    per = cells // tile
    pairs = section(slots, per)
    start = [] if far_part is None else [far_part]

    def body(list_ref, tiles_ref, *refs):
        own_refs, other_refs, refs = refs[:groups], refs[groups : 2 * groups], refs[2 * groups :]
        start_refs, refs = refs[: len(start)], refs[len(start) :]
        sent_refs, refs = refs[: len(sent)], refs[len(sent) + len(after) :]
        field_outs, sent_outs, (field, window) = refs[:groups], refs[groups:-2], refs[-2:]
        for out, ref in zip(sent_outs, sent_refs):
            out[...] = ref[...]
        for g in range(groups):
            window[:per, :, lanes(g)] = own_refs[g][...].reshape(per, tile, LANES)
            window[per : 2 * per, :, lanes(g)] = other_refs[g][...].reshape(per, tile, LANES)
        window[2 * per] = jnp.zeros((tile, width), BF16)
        field[:per] = jnp.zeros((per, tile, width), F32)
        for ref in start_refs:
            field[:per, :, lanes(0)] = ref[...].reshape(per, tile, LANES)
        add_pairs(0, list_ref, tiles_ref, field, window, pairs)
        for g, out in enumerate(field_outs):
            out[...] = field[:per, :, lanes(g)].reshape(cells, LANES).astype(out.dtype)

    outs = call(
        body,
        [(lists, pltpu.SMEM)] + vmem(tiles, *owns, *others, *start, *sent, *after),
        [
            ((cells, LANES), BF16 if start and g == 0 else F32, pltpu.VMEM)
            for g in range(groups)
        ]
        + [(a.shape, BF16, pltpu.VMEM) for a in sent],
        [
            pltpu.VMEM((per + 1, tile, width), F32),
            pltpu.VMEM((2 * per + 1, tile, width), BF16),
        ],
        name,
        flops,
    )
    return outs[:groups], outs[groups:]


def far_fields(lists, tiles, nears, far, extra, outs_of, work, name, flops=0, through=()):
    slots, tile, _ = tiles.shape
    cells, width = far.shape
    per = cells // tile
    pairs = section(slots, per)
    n = width // LANES
    m = len(nears)

    def body(list_ref, tiles_ref, far_ref, *refs):
        near_refs, extra_refs = refs[:m], refs[m : m + len(extra)]
        through_refs = refs[m + len(extra) : m + len(extra) + len(through)]
        out_refs, (field, window) = refs[m + len(extra) + len(through) : -2], refs[-2:]
        window[:per] = far_ref[...].reshape(per, tile, width)
        window[per] = jnp.zeros((tile, width), BF16)
        if not near_refs:
            field[:per] = jnp.zeros((per, tile, width), F32)
        for i, ref in enumerate(near_refs):
            field[:per, :, lanes(i)] = ref[...].reshape(per, tile, LANES)
        add_pairs(1, list_ref, tiles_ref, field, window, pairs)
        done = [field[:per, :, lanes(i)].reshape(cells, LANES) for i in range(n)]
        work(done, [*extra_refs, *through_refs], out_refs[: len(outs_of)])

    return call(
        body,
        [(lists, pltpu.SMEM)] + vmem(tiles, far, *nears, *extra, *through),
        [(*out, pltpu.VMEM) for out in outs_of] + [(a.shape, a.dtype, pltpu.VMEM) for a in through],
        [pltpu.VMEM((per + 1, tile, width), F32), pltpu.VMEM((per + 1, tile, width), BF16)],
        name,
        flops,
        [(3 + m + len(extra) + i, len(outs_of) + i) for i in range(len(through))],
    )


def first_base(xs, momenta, same, spread, coupling, channels):
    cells, width = momenta.shape
    groups = len(xs)

    def body(*refs):
        x_refs, (y_ref, same_ref, spread_ref, coupling_ref) = refs[:groups], refs[groups : groups + 4]
        outs = refs[groups + 4 :]
        tall = jnp.dot(spread_ref[...], coupling_ref[...], preferred_element_type=F32).astype(BF16)
        wide = lax.dot_general(
            tall, spread_ref[...], (((1,), (1,)), ((), ())), preferred_element_type=F32
        )
        outs[groups][...] = (wide * same_ref[...].astype(F32)).astype(BF16)
        x = [ref[...] for ref in x_refs]
        y = [y_ref[:, lanes(g)] for g in range(groups)]
        bases_into(outs[:groups], x, y, same_ref, 0, channels)

    outs = call(
        body,
        vmem(*xs, momenta, same, spread, coupling),
        [((cells, LANES), F32, pltpu.VMEM)] * groups + [((width, width), BF16, pltpu.VMEM)],
        [],
        "first_base",
    )
    return outs[:groups], outs[groups]


def updated(field_mixed, base, x):
    y_new = base - 0.2 * field_mixed
    return jnp.clip(x + 0.5 * y_new, -1.0, 1.0), y_new


def second_base(xs, ys, later, fields, first_base, first_x, rounded, same, mixing, channels):
    groups = len(rounded)
    cells = rounded[0].shape[0]
    width = groups * LANES
    done, m = len(xs), len(later)

    def body(*refs):
        refs = list(refs)

        def take(n):
            taken = refs[:n]
            del refs[:n]
            return taken

        x = [ref[...] for ref in take(done)]
        y = [ref[...] for ref in take(done)]
        held = [ref[...] for ref in take(groups)]
        base_refs, x_refs = take(m), take(m)
        r = [ref[...] for ref in take(groups)]
        same_ref, mixing_ref = take(2)
        for i, t in enumerate(later):
            x_new, y_new = updated(
                mixed_of(held, mixing_ref, t, channels), base_refs[i][...], x_refs[i][...]
            )
            x.append(x_new)
            y.append(y_new)
            refs[2 * groups + i][...] = x_new
        bases_into(refs[:groups], x, y, same_ref, 1, channels)
        for g in range(groups):
            near = spanned(g, channels, width)
            refs[groups + g][...] = lax.dot_general(
                jnp.concatenate([r[n] for n in near], axis=1),
                mixing_ref[lanes(g), span_lanes(near)],
                (((1,), (1,)), ((), ())),
                preferred_element_type=F32,
            )

    outs = call(
        body,
        vmem(*xs, *ys, *fields, *first_base, *first_x, *rounded, same, mixing),
        [((cells, LANES), F32, pltpu.VMEM)] * (2 * groups + m),
        [],
        "second_base",
    )
    return outs[:groups], outs[groups : 2 * groups], outs[2 * groups :]


def finish(fields, xs, bases, mixing, channels):
    groups = len(xs)
    cells = xs[0].shape[0]
    width = groups * LANES

    def body(*refs):
        field_refs, x_refs, base_refs = [refs[k * groups : (k + 1) * groups] for k in range(3)]
        mixing_ref, x_out, y_out, token, x_buf, y_buf, sems = refs[3 * groups :]
        held = [ref[...] for ref in field_refs]
        copies = []
        for g in range(groups):
            y_new = base_refs[g][...] - 0.2 * mixed_of(held, mixing_ref, g, channels)
            y_buf[g] = y_new
            x_buf[g] = jnp.clip(x_refs[g][...] + 0.5 * y_new, -1.0, 1.0)
            for k, (buf, out) in enumerate(((y_buf, y_out), (x_buf, x_out))):
                copies.append(
                    pltpu.make_async_copy(buf.at[g], out.at[:, lanes(g)], sems.at[g, k])
                )
                copies[-1].start()
        token[...] = jnp.zeros_like(token)
        for copy in copies:
            copy.wait()

    return call(
        body,
        vmem(*fields, *xs, *bases, mixing),
        [((cells, width), F32, pltpu.HBM)] * 2 + [((8, LANES), F32, pltpu.VMEM)],
        [
            pltpu.VMEM((groups, cells, LANES), F32),
            pltpu.VMEM((groups, cells, LANES), F32),
            pltpu.SemaphoreType.DMA((groups, 2)),
        ],
        "finish",
    )


def copies_of(rows):
    return [((rows * n, LANES), F32) for n in (1, 2, 3)]


def spread_out(outs, value):
    for out in outs:
        out[...] = jnp.concatenate([value] * (out.shape[0] // value.shape[0]), axis=0)


def add_up(arrays, token, name):
    rows = arrays[0].shape[0]

    def body(*refs):
        total = refs[0][...]
        for ref in refs[1 : len(arrays)]:
            total = total + ref[:rows, :]
        spread_out(refs[len(arrays) + len(token) :], total)

    return call(
        body,
        vmem(*arrays, *token),
        [(*size, pltpu.VMEM) for size in copies_of(rows)],
        [],
        name,
    )


def sum_over_ring(values, ring, token):
    if ring & (ring - 1):
        return lax.psum(values[0], RING)
    rounds, size = [], 1
    while size < ring:
        digits = (1, 2, 3) if 4 * size <= ring else (1,)
        rounds.append([size * d for d in digits])
        size *= len(digits) + 1
    for i, bits in enumerate(reversed(rounds)):
        received = [
            lax.ppermute(value, RING, [(j, j ^ bit) for j in range(ring)])
            for value, bit in zip(values, bits)
        ]
        if i == len(rounds) - 1:
            rows = values[0].shape[0]
            return values[0] + sum(part[:rows] for part in received)
        values = add_up([values[0], *received], [token] if i == 0 else [], f"add_up_{i}")
    return values[0]


def local(positions, momenta, tile_values, tile_rows, tile_cols, tile_count, channel_coupling):
    cells, width = positions.shape
    slots, tile, _ = tile_values.shape
    channels = channel_coupling.shape[0]
    replicas = width // channels
    groups = width // LANES
    ring = lax.axis_size("row") * lax.axis_size("col")
    where = np.arange(width)
    same = jnp.asarray(
        (where[:, None] // channels == where[None] // channels).astype(ml_dtypes.bfloat16)
    )
    spread = jnp.asarray(
        (where[:, None] % channels == np.arange(channels)[None]).astype(ml_dtypes.bfloat16)
    )
    on_chip = [(i, i ^ 1) for i in range(ring)]
    off_chip = [(i, (i + 1) % ring if i % 2 else (i - 1) % ring) for i in range(ring)]
    wide = (cells, LANES)
    every = list(range(groups))
    first_pieces = [every[:-1], every[-1:]]
    second_pieces = [every[:1], every[1:]]

    def ring_index():
        return lax.axis_index("row") * lax.axis_size("col") + lax.axis_index("col")

    def far_swap(mine):
        return lax.ppermute(mine, RING, off_chip)

    def near_swap(mine):
        return lax.ppermute(mine, RING, on_chip)

    def ready(piece, done):
        return [
            t for t in every if t not in done and max(spanned(t, channels, width)) <= piece[-1]
        ]

    def keep(done, _, outs):
        outs[0][...] = done[0]

    def needed(todo, piece):
        return sorted({n for t in todo for n in spanned(t, channels, width)} - set(piece))

    xs, owns, sent = load_first(positions, first_pieces[0])
    fars = [far_swap(sent)]
    lists, more_x, more_own = make_lists(
        tile_rows, tile_cols, tile_count, positions, first_pieces[1], sent, slots, tile, ring_index
    )
    xs, owns = [*xs, *more_x], [*owns, *more_own]
    others = [near_swap(r) for r in owns]
    base, mixing = first_base(xs, momenta, same, spread, channel_coupling, channels)
    near, sent = near_fields(
        lists, tile_values, owns, others, None, more_own, [mixing], 0, "near_first"
    )
    fars.append(far_swap(sent[0]))

    fields, new_x, new_y, rounded, new_fars = {}, [], [], {}, []
    for p, piece in enumerate(first_pieces):
        last = p == len(first_pieces) - 1
        todo = ready(piece, rounded)
        known = needed(todo, piece)
        assert second_pieces[p] == todo

        def work(done, ins, outs, piece=piece, todo=todo, known=known, last=last):
            held = {n: ins[1 + i][...] for i, n in enumerate(known)}
            done = [field.astype(BF16) for field in done]
            held.update(zip(piece, done))
            rest = ins[1 + len(known) :]
            for i, t in enumerate(todo):
                x_new, y_new = updated(
                    mixed_of(held, ins[0], t, channels), rest[2 * i][...], rest[2 * i + 1][...]
                )
                r_new = x_new.astype(BF16)
                outs[0][:, lanes(i)] = r_new
                outs[1 + i][...] = r_new
                if not last:
                    outs[1 + len(todo) + len(piece) + 2 * i][...] = x_new
                    outs[2 + len(todo) + len(piece) + 2 * i][...] = y_new
            for i, field in enumerate(done):
                outs[1 + len(todo) + i][...] = field

        results = far_fields(
            lists,
            tile_values,
            [near[n] for n in piece],
            fars[p],
            [mixing] + [fields[n] for n in known] + [a for t in todo for a in (base[t], xs[t])],
            [((cells, len(todo) * LANES), BF16)]
            + [(wide, BF16)] * (len(todo) + len(piece))
            + ([] if last else [(wide, F32)] * (2 * len(todo))),
            work,
            f"far_first_{p}",
        )
        new_fars.append(far_swap(results[0]))
        rounded.update(zip(todo, results[1:]))
        fields.update(zip(piece, results[1 + len(todo) :]))
        new_x += results[1 + len(todo) + len(piece) :: 2]
        new_y += results[2 + len(todo) + len(piece) :: 2]

    owns = [rounded[g] for g in every]
    others = [near_swap(r) for r in owns]
    (part,) = far_fields(
        lists, tile_values, [], new_fars[0], [], [(wide, F32)], keep, "far_second_0", NEAR_FLOPS
    )
    near, _ = near_fields(lists, tile_values, owns, others, part, [], [], 0, "near_second")
    later = second_pieces[1]
    base, weights, more_x = second_base(
        new_x,
        new_y,
        later,
        [fields[g] for g in every],
        [base[t] for t in later],
        [xs[t] for t in later],
        owns,
        same,
        mixing,
        channels,
    )
    xs = [*new_x, *more_x]
    piece = second_pieces[1]

    def last_work(done, ins, outs):
        held = [ins[groups][...]] + [field.astype(BF16) for field in done]
        for out, field in zip(outs, held[1:]):
            out[...] = field
        row = jnp.concatenate(
            [
                jnp.sum(field.astype(F32) * ref[...], axis=0, keepdims=True)
                for field, ref in zip(held, ins[:groups])
            ],
            axis=1,
        )
        row = jnp.broadcast_to(row, (replicas, width))
        lane = lax.broadcasted_iota(jnp.int32, (replicas, width), 1)
        first = lax.broadcasted_iota(jnp.int32, (replicas, width), 0) * channels
        inside = (lane >= first) & (lane < first + channels)
        total = jnp.sum(jnp.where(inside, row, 0.0), axis=1, keepdims=True)
        place = lax.broadcasted_iota(jnp.int32, (replicas, LANES), 1)
        which = lax.broadcasted_iota(jnp.int32, (replicas, LANES), 0)
        flat = jnp.sum(jnp.where(place == which, total, 0.0), axis=0, keepdims=True)
        spread_out(outs[len(piece) :], jnp.broadcast_to(flat, (8, LANES)))

    results = far_fields(
        lists,
        tile_values,
        near[1:],
        new_fars[1],
        weights,
        [(wide, BF16)] * len(piece) + copies_of(8),
        last_work,
        "far_second_1",
        through=[near[0], *xs, *base, mixing],
    )
    sent = len(piece) + len(copies_of(8))
    fields, partials, kept = results[: len(piece)], results[len(piece) : sent], results[sent:]
    fields, kept = [kept[0], *fields], kept[1:]

    x_new, y_new, token = finish(
        fields, kept[:groups], kept[groups : 2 * groups], kept[2 * groups], channels
    )
    total = sum_over_ring(partials, ring, token)
    energy = total[0, :replicas] / jnp.sqrt(jnp.float32(cells * ring * channels))
    return (x_new, y_new, energy)


def solution(mesh):
    cells = P(("groups", "row", "col"), None)
    slots = P(("groups", "row", "col"))
    return jax.shard_map(
        local,
        mesh=mesh,
        in_specs=(cells, cells, P(("groups", "row", "col"), None, None), slots, slots, slots, P()),
        out_specs=(cells, cells, P("groups")),
        check_vma=False,
    )
```

```python
import jax
import jax.numpy as jnp
import ml_dtypes
import numpy as np
from jax import lax
from jax.experimental import pallas as pl
from jax.experimental.pallas import tpu as pltpu
from jax.sharding import PartitionSpec as P

STEPS = 2
LANES = 128
LONG, SHORT = 16, 4
VMEM_LIMIT = 14 * 1024 * 1024
NEAR_FLOPS = 4 * 10**9
F32 = jnp.float32
BF16 = jnp.bfloat16
RING = ("row", "col")


def call(body, ins, outs, scratch, name, flops=0, aliases=()):
    return pl.pallas_call(
        body,
        in_specs=[pl.BlockSpec(memory_space=pl.ANY if s is pltpu.HBM else s) for _, s in ins],
        out_specs=[pl.BlockSpec(memory_space=pl.ANY if s is pltpu.HBM else s) for *_, s in outs],
        out_shape=[
            jax.ShapeDtypeStruct(dims, kind) if s is pltpu.HBM else s(dims, kind)
            for dims, kind, s in outs
        ],
        scratch_shapes=scratch,
        input_output_aliases=dict(aliases),
        compiler_params=pltpu.CompilerParams(vmem_limit_bytes=VMEM_LIMIT),
        cost_estimate=pl.CostEstimate(
            flops=int(flops) or 1000, bytes_accessed=1000, transcendentals=0
        ),
        name=name,
    )(*[pltpu.with_memory_space_constraint(a, s) for a, s in ins])


def vmem(*arrays):
    return [(a, pltpu.VMEM) for a in arrays]


def lanes(group):
    return slice(group * LANES, (group + 1) * LANES)


def spanned(group, channels, width):
    first = group * LANES // channels * channels
    last = -(-(group + 1) * LANES // channels) * channels
    return list(range(first // LANES, -(-min(last, width) // LANES)))


def span_lanes(near):
    return slice(near[0] * LANES, (near[-1] + 1) * LANES)


def split(x):
    high = x.astype(BF16)
    return high, (x - high.astype(F32)).astype(BF16)


def bases_into(outs, xs, ys, same, step, channels):
    groups = len(xs)
    width = groups * LANES
    detune = 1.0 - (step + 1.0) / (STEPS + 1.0)
    parts = [split(x) for x in xs]
    for g in range(groups):
        near = spanned(g, channels, width)
        ones = same[span_lanes(near), lanes(g)]
        totals = sum(
            jnp.dot(
                jnp.concatenate([parts[n][k] for n in near], axis=1),
                ones,
                preferred_element_type=F32,
            )
            for k in range(2)
        )
        penalty = 0.02 * (totals - (2.0 - channels))
        outs[g][...] = ys[g] + 0.5 * (-detune * xs[g] - 0.4 * penalty)


def mixed_of(fields, mixing, group, channels):
    near = spanned(group, channels, mixing.shape[0])
    return jnp.dot(
        jnp.concatenate([fields[n] for n in near], axis=1),
        mixing[span_lanes(near), lanes(group)],
        preferred_element_type=F32,
    )


def load_first(positions, groups_of):
    cells = positions.shape[0]
    n = len(groups_of)

    def body(x_ref, *refs):
        x_outs, r_outs, sent, sems = refs[:n], refs[n : 2 * n], refs[2 * n], refs[-1]
        copies = [
            pltpu.make_async_copy(x_ref.at[:, lanes(g)], x_outs[i], sems.at[i])
            for i, g in enumerate(groups_of)
        ]
        for copy in copies:
            copy.start()
        for i, copy in enumerate(copies):
            copy.wait()
            rounded = x_outs[i][...].astype(BF16)
            r_outs[i][...] = rounded
            sent[:, lanes(i)] = rounded

    outs = call(
        body,
        [(positions, pltpu.HBM)],
        [((cells, LANES), F32, pltpu.VMEM)] * n
        + [((cells, LANES), BF16, pltpu.VMEM)] * n
        + [((cells, n * LANES), BF16, pltpu.VMEM)],
        [pltpu.SemaphoreType.DMA((n,))],
        "load_first",
    )
    return outs[:n], outs[n : 2 * n], outs[2 * n]


def section(slots, per):
    return -(-(slots + per) // (2 * SHORT)) * SHORT


def make_lists(rows, cols, count, positions, groups_of, after, slots, tile, ring_index):
    cells = positions.shape[0]
    per = cells // tile
    pairs = section(slots, per)
    n = len(groups_of)

    def body(rows_hbm, cols_hbm, count_hbm, x_ref, _, list_ref, *refs):
        x_outs, r_outs = refs[:n], refs[n : 2 * n]
        rows_ref, cols_ref, count_ref, held, sems = refs[2 * n :]
        copies = [
            pltpu.make_async_copy(*ends, sems.at[k])
            for k, ends in enumerate(
                [(rows_hbm, rows_ref), (cols_hbm, cols_ref), (count_hbm, count_ref)]
                + [(x_ref.at[:, lanes(g)], x_outs[i]) for i, g in enumerate(groups_of)]
            )
        ]
        for copy in copies:
            copy.start()
        for k in range(2 * per):
            held[k] = -1
        far_third = jnp.where(lax.rem(ring_index(), 2) == 1, 2, 0)
        for copy in copies[:3]:
            copy.wait()

        def visit(slot, totals):
            near_pairs, far_pairs = totals
            row, col = rows_ref[slot], cols_ref[slot]
            third = jnp.where(col >= 2 * per, 2, jnp.where(col >= per, 1, 0))
            source = col - third * per
            far = third == far_third
            source = jnp.where(far | (third == 1), source, source + per)
            key = row + jnp.where(far, per, 0)
            place = 2 * jnp.where(far, far_pairs + pairs, near_pairs)
            entry = slot * 65536 + source * 256 + row
            other = held[key]
            full = other >= 0
            list_ref[place] = other
            list_ref[place + 1] = entry
            held[key] = jnp.where(full, -1, entry)
            one = full.astype(jnp.int32)
            far_one = jnp.where(far, one, 0)
            return near_pairs + one - far_one, far_pairs + far_one

        totals = lax.fori_loop(0, count_ref[0], visit, (jnp.int32(0), jnp.int32(0)))
        for part, zero in enumerate((2 * per, per)):
            total = totals[part]
            start = part * pairs
            for k in range(per):
                other = held[part * per + k]
                list_ref[2 * (start + total)] = other
                list_ref[2 * (start + total) + 1] = zero * 256 + k
                total = total + (other >= 0).astype(jnp.int32)
            short_turns = (total + SHORT - 1) // SHORT

            def pad(pair, carry, start=start, zero=zero):
                for e in range(2):
                    list_ref[2 * (start + pair) + e] = zero * 256 + per
                return carry

            lax.fori_loop(total, short_turns * SHORT, pad, 0)
            list_ref[4 * pairs + 2 * part] = short_turns // (LONG // SHORT)
            list_ref[4 * pairs + 2 * part + 1] = short_turns % (LONG // SHORT)
        for i, copy in enumerate(copies[3:]):
            copy.wait()
            r_outs[i][...] = x_outs[i][...].astype(BF16)

    outs = call(
        body,
        [(a, pl.ANY) for a in (rows, cols, count)] + [(positions, pltpu.HBM)] + vmem(after),
        [((4 * pairs + 4 + 2,), jnp.int32, pltpu.SMEM)]
        + [((cells, LANES), F32, pltpu.VMEM)] * n
        + [((cells, LANES), BF16, pltpu.VMEM)] * n,
        [
            pltpu.SMEM(rows.shape, jnp.int32),
            pltpu.SMEM(cols.shape, jnp.int32),
            pltpu.SMEM(count.shape, jnp.int32),
            pltpu.SMEM((2 * per,), jnp.int32),
            pltpu.SemaphoreType.DMA((3 + n,)),
        ],
        "make_lists",
    )
    return outs[0], outs[1 : 1 + n], outs[1 + n :]


def add_pairs(part, list_ref, tiles, field, window, pairs):
    def turn(first, length):
        for u in range(length):
            place = 2 * (part * pairs + first + u)
            entries = [list_ref[place + e] for e in range(2)]
            left = jnp.concatenate([tiles[n >> 16] for n in entries], axis=1)
            right = jnp.concatenate([window[(n >> 8) & 255] for n in entries], axis=0)
            field[entries[1] & 255] += jnp.dot(left, right, preferred_element_type=F32)

    def long(i, carry):
        turn(i * LONG, LONG)
        return carry

    def short(i, carry):
        turn(long_turns * LONG + i * SHORT, SHORT)
        return carry

    long_turns = list_ref[4 * pairs + 2 * part]
    lax.fori_loop(0, long_turns, long, 0)
    lax.fori_loop(0, list_ref[4 * pairs + 2 * part + 1], short, 0)


def near_fields(lists, tiles, owns, others, far_part, sent, after, flops, name):
    slots, tile, _ = tiles.shape
    cells = owns[0].shape[0]
    groups = len(owns)
    width = groups * LANES
    per = cells // tile
    pairs = section(slots, per)
    start = [] if far_part is None else [far_part]

    def body(list_ref, tiles_ref, *refs):
        own_refs, other_refs, refs = refs[:groups], refs[groups : 2 * groups], refs[2 * groups :]
        start_refs, refs = refs[: len(start)], refs[len(start) :]
        sent_refs, refs = refs[: len(sent)], refs[len(sent) + len(after) :]
        field_outs, sent_outs, (field, window) = refs[:groups], refs[groups:-2], refs[-2:]
        for out, ref in zip(sent_outs, sent_refs):
            out[...] = ref[...]
        for g in range(groups):
            window[:per, :, lanes(g)] = own_refs[g][...].reshape(per, tile, LANES)
            window[per : 2 * per, :, lanes(g)] = other_refs[g][...].reshape(per, tile, LANES)
        window[2 * per] = jnp.zeros((tile, width), BF16)
        field[:per] = jnp.zeros((per, tile, width), F32)
        for ref in start_refs:
            field[:per, :, lanes(0)] = ref[...].reshape(per, tile, LANES)
        add_pairs(0, list_ref, tiles_ref, field, window, pairs)
        for g, out in enumerate(field_outs):
            out[...] = field[:per, :, lanes(g)].reshape(cells, LANES).astype(out.dtype)

    outs = call(
        body,
        [(lists, pltpu.SMEM)] + vmem(tiles, *owns, *others, *start, *sent, *after),
        [
            ((cells, LANES), BF16 if start and g == 0 else F32, pltpu.VMEM)
            for g in range(groups)
        ]
        + [(a.shape, BF16, pltpu.VMEM) for a in sent],
        [
            pltpu.VMEM((per + 1, tile, width), F32),
            pltpu.VMEM((2 * per + 1, tile, width), BF16),
        ],
        name,
        flops,
    )
    return outs[:groups], outs[groups:]


def far_fields(lists, tiles, nears, far, extra, outs_of, work, name, flops=0, through=()):
    slots, tile, _ = tiles.shape
    cells, width = far.shape
    per = cells // tile
    pairs = section(slots, per)
    n = width // LANES
    m = len(nears)

    def body(list_ref, tiles_ref, far_ref, *refs):
        near_refs, extra_refs = refs[:m], refs[m : m + len(extra)]
        through_refs = refs[m + len(extra) : m + len(extra) + len(through)]
        out_refs, (field, window) = refs[m + len(extra) + len(through) : -2], refs[-2:]
        window[:per] = far_ref[...].reshape(per, tile, width)
        window[per] = jnp.zeros((tile, width), BF16)
        if not near_refs:
            field[:per] = jnp.zeros((per, tile, width), F32)
        for i, ref in enumerate(near_refs):
            field[:per, :, lanes(i)] = ref[...].reshape(per, tile, LANES)
        add_pairs(1, list_ref, tiles_ref, field, window, pairs)
        done = [field[:per, :, lanes(i)].reshape(cells, LANES) for i in range(n)]
        work(done, [*extra_refs, *through_refs], out_refs[: len(outs_of)])

    return call(
        body,
        [(lists, pltpu.SMEM)] + vmem(tiles, far, *nears, *extra, *through),
        [(*out, pltpu.VMEM) for out in outs_of] + [(a.shape, a.dtype, pltpu.VMEM) for a in through],
        [pltpu.VMEM((per + 1, tile, width), F32), pltpu.VMEM((per + 1, tile, width), BF16)],
        name,
        flops,
        [(3 + m + len(extra) + i, len(outs_of) + i) for i in range(len(through))],
    )


def first_base(xs, momenta, same, spread, coupling, channels):
    cells, width = momenta.shape
    groups = len(xs)

    def body(*refs):
        x_refs, (y_ref, same_ref, spread_ref, coupling_ref) = refs[:groups], refs[groups : groups + 4]
        outs = refs[groups + 4 :]
        tall = jnp.dot(spread_ref[...], coupling_ref[...], preferred_element_type=F32).astype(BF16)
        wide = lax.dot_general(
            tall, spread_ref[...], (((1,), (1,)), ((), ())), preferred_element_type=F32
        )
        outs[groups][...] = (wide * same_ref[...].astype(F32)).astype(BF16)
        x = [ref[...] for ref in x_refs]
        y = [y_ref[:, lanes(g)] for g in range(groups)]
        bases_into(outs[:groups], x, y, same_ref, 0, channels)

    outs = call(
        body,
        vmem(*xs, momenta, same, spread, coupling),
        [((cells, LANES), F32, pltpu.VMEM)] * groups + [((width, width), BF16, pltpu.VMEM)],
        [],
        "first_base",
    )
    return outs[:groups], outs[groups]


def updated(field_mixed, base, x):
    y_new = base - 0.2 * field_mixed
    return jnp.clip(x + 0.5 * y_new, -1.0, 1.0), y_new


def second_base(xs, ys, later, fields, first_base, first_x, rounded, same, mixing, channels):
    groups = len(rounded)
    cells = rounded[0].shape[0]
    width = groups * LANES
    done, m = len(xs), len(later)

    def body(*refs):
        refs = list(refs)

        def take(n):
            taken = refs[:n]
            del refs[:n]
            return taken

        x = [ref[...] for ref in take(done)]
        y = [ref[...] for ref in take(done)]
        held = [ref[...] for ref in take(groups)]
        base_refs, x_refs = take(m), take(m)
        r = [ref[...] for ref in take(groups)]
        same_ref, mixing_ref = take(2)
        for i, t in enumerate(later):
            x_new, y_new = updated(
                mixed_of(held, mixing_ref, t, channels), base_refs[i][...], x_refs[i][...]
            )
            x.append(x_new)
            y.append(y_new)
            refs[2 * groups + i][...] = x_new
        bases_into(refs[:groups], x, y, same_ref, 1, channels)
        for g in range(groups):
            near = spanned(g, channels, width)
            refs[groups + g][...] = lax.dot_general(
                jnp.concatenate([r[n] for n in near], axis=1),
                mixing_ref[lanes(g), span_lanes(near)],
                (((1,), (1,)), ((), ())),
                preferred_element_type=F32,
            )

    outs = call(
        body,
        vmem(*xs, *ys, *fields, *first_base, *first_x, *rounded, same, mixing),
        [((cells, LANES), F32, pltpu.VMEM)] * (2 * groups + m),
        [],
        "second_base",
    )
    return outs[:groups], outs[groups : 2 * groups], outs[2 * groups :]


def finish(here, fields, xs, bases, mixing, channels, outputs, name):
    groups = len(xs)
    cells = xs[0].shape[0]
    width = groups * LANES

    def body(*refs):
        field_refs, x_refs, base_refs = [refs[k * groups : (k + 1) * groups] for k in range(3)]
        mixing_ref = refs[3 * groups]
        x_buf, y_buf, sems = refs[-3:]
        x_out, y_out = refs[-5:-3] if outputs else refs[-6:-4]
        if not outputs:
            refs[-4][...] = jnp.zeros_like(refs[-4])

        @pl.when(here())
        def _():
            held = [ref[...] for ref in field_refs]
            copies = []
            for g in range(groups):
                x_buf[g], y_buf[g] = updated(
                    mixed_of(held, mixing_ref, g, channels), base_refs[g][...], x_refs[g][...]
                )
                for k, (buf, out) in enumerate(((y_buf, y_out), (x_buf, x_out))):
                    copies.append(
                        pltpu.make_async_copy(buf.at[g], out.at[:, lanes(g)], sems.at[g, k])
                    )
                    copies[-1].start()
            for copy in copies:
                copy.wait()

    ins = vmem(*fields, *xs, *bases, mixing)
    return call(
        body,
        ins + [(a, pltpu.HBM) for a in outputs],
        [((cells, width), F32, pltpu.HBM)] * 2
        + ([] if outputs else [((8, LANES), F32, pltpu.VMEM)]),
        [
            pltpu.VMEM((groups, cells, LANES), F32),
            pltpu.VMEM((groups, cells, LANES), F32),
            pltpu.SemaphoreType.DMA((groups, 2)),
        ],
        name,
        0,
        [(len(ins) + i, i) for i in range(len(outputs))],
    )


def copies_of(rows):
    return [((rows * n, LANES), F32) for n in (1, 2, 3)]


def spread_out(outs, value):
    for out in outs:
        out[...] = jnp.concatenate([value] * (out.shape[0] // value.shape[0]), axis=0)


def add_up(arrays, token, name):
    rows = arrays[0].shape[0]

    def body(*refs):
        total = refs[0][...]
        for ref in refs[1 : len(arrays)]:
            total = total + ref[:rows, :]
        spread_out(refs[len(arrays) + len(token) :], total)

    return call(
        body,
        vmem(*arrays, *token),
        [(*size, pltpu.VMEM) for size in copies_of(rows)],
        [],
        name,
    )


def sum_over_ring(values, ring, token):
    if ring & (ring - 1):
        return lax.psum(values[0], RING)
    rounds, size = [], 1
    while size < ring:
        digits = (1, 2, 3) if 4 * size <= ring else (1,)
        rounds.append([size * d for d in digits])
        size *= len(digits) + 1
    for i, bits in enumerate(reversed(rounds)):
        received = [
            lax.ppermute(value, RING, [(j, j ^ bit) for j in range(ring)])
            for value, bit in zip(values, bits)
        ]
        if i == len(rounds) - 1:
            rows = values[0].shape[0]
            return values[0] + sum(part[:rows] for part in received)
        values = add_up([values[0], *received], [token] if i == 0 else [], f"add_up_{i}")
    return values[0]


def local(positions, momenta, tile_values, tile_rows, tile_cols, tile_count, channel_coupling):
    cells, width = positions.shape
    slots, tile, _ = tile_values.shape
    channels = channel_coupling.shape[0]
    replicas = width // channels
    groups = width // LANES
    ring = lax.axis_size("row") * lax.axis_size("col")
    where = np.arange(width)
    same = jnp.asarray(
        (where[:, None] // channels == where[None] // channels).astype(ml_dtypes.bfloat16)
    )
    spread = jnp.asarray(
        (where[:, None] % channels == np.arange(channels)[None]).astype(ml_dtypes.bfloat16)
    )
    on_chip = [(i, i ^ 1) for i in range(ring)]
    off_chip = [(i, (i + 1) % ring if i % 2 else (i - 1) % ring) for i in range(ring)]
    wide = (cells, LANES)
    every = list(range(groups))
    first_pieces = [every[:-1], every[-1:]]
    second_pieces = [every[:1], every[1:]]

    def ring_index():
        return lax.axis_index("row") * lax.axis_size("col") + lax.axis_index("col")

    def far_swap(mine):
        return lax.ppermute(mine, RING, off_chip)

    def near_swap(mine):
        return lax.ppermute(mine, RING, on_chip)

    def ready(piece, done):
        return [
            t for t in every if t not in done and max(spanned(t, channels, width)) <= piece[-1]
        ]

    def keep(done, _, outs):
        outs[0][...] = done[0]

    def needed(todo, piece):
        return sorted({n for t in todo for n in spanned(t, channels, width)} - set(piece))

    xs, owns, sent = load_first(positions, first_pieces[0])
    fars = [far_swap(sent)]
    lists, more_x, more_own = make_lists(
        tile_rows, tile_cols, tile_count, positions, first_pieces[1], sent, slots, tile, ring_index
    )
    xs, owns = [*xs, *more_x], [*owns, *more_own]
    others = [near_swap(r) for r in owns]
    base, mixing = first_base(xs, momenta, same, spread, channel_coupling, channels)
    near, sent = near_fields(
        lists, tile_values, owns, others, None, more_own, [mixing], 0, "near_first"
    )
    fars.append(far_swap(sent[0]))

    fields, new_x, new_y, rounded, new_fars = {}, [], [], {}, []
    for p, piece in enumerate(first_pieces):
        last = p == len(first_pieces) - 1
        todo = ready(piece, rounded)
        known = needed(todo, piece)
        assert second_pieces[p] == todo

        def work(done, ins, outs, piece=piece, todo=todo, known=known, last=last):
            held = {n: ins[1 + i][...] for i, n in enumerate(known)}
            done = [field.astype(BF16) for field in done]
            held.update(zip(piece, done))
            rest = ins[1 + len(known) :]
            for i, t in enumerate(todo):
                x_new, y_new = updated(
                    mixed_of(held, ins[0], t, channels), rest[2 * i][...], rest[2 * i + 1][...]
                )
                r_new = x_new.astype(BF16)
                outs[0][:, lanes(i)] = r_new
                outs[1 + i][...] = r_new
                if not last:
                    outs[1 + len(todo) + len(piece) + 2 * i][...] = x_new
                    outs[2 + len(todo) + len(piece) + 2 * i][...] = y_new
            for i, field in enumerate(done):
                outs[1 + len(todo) + i][...] = field

        results = far_fields(
            lists,
            tile_values,
            [near[n] for n in piece],
            fars[p],
            [mixing] + [fields[n] for n in known] + [a for t in todo for a in (base[t], xs[t])],
            [((cells, len(todo) * LANES), BF16)]
            + [(wide, BF16)] * (len(todo) + len(piece))
            + ([] if last else [(wide, F32)] * (2 * len(todo))),
            work,
            f"far_first_{p}",
        )
        new_fars.append(far_swap(results[0]))
        rounded.update(zip(todo, results[1:]))
        fields.update(zip(piece, results[1 + len(todo) :]))
        new_x += results[1 + len(todo) + len(piece) :: 2]
        new_y += results[2 + len(todo) + len(piece) :: 2]

    owns = [rounded[g] for g in every]
    others = [near_swap(r) for r in owns]
    (part,) = far_fields(
        lists, tile_values, [], new_fars[0], [], [(wide, F32)], keep, "far_second_0", NEAR_FLOPS
    )
    near, _ = near_fields(lists, tile_values, owns, others, part, [], [], 0, "near_second")
    later = second_pieces[1]
    base, weights, more_x = second_base(
        new_x,
        new_y,
        later,
        [fields[g] for g in every],
        [base[t] for t in later],
        [xs[t] for t in later],
        owns,
        same,
        mixing,
        channels,
    )
    xs = [*new_x, *more_x]
    piece = second_pieces[1]

    def last_work(done, ins, outs):
        held = [ins[groups][...]] + [field.astype(BF16) for field in done]
        for out, field in zip(outs, held[1:]):
            out[...] = field
        row = jnp.concatenate(
            [
                jnp.sum(field.astype(F32) * ref[...], axis=0, keepdims=True)
                for field, ref in zip(held, ins[:groups])
            ],
            axis=1,
        )
        row = jnp.broadcast_to(row, (replicas, width))
        lane = lax.broadcasted_iota(jnp.int32, (replicas, width), 1)
        first = lax.broadcasted_iota(jnp.int32, (replicas, width), 0) * channels
        inside = (lane >= first) & (lane < first + channels)
        total = jnp.sum(jnp.where(inside, row, 0.0), axis=1, keepdims=True)
        place = lax.broadcasted_iota(jnp.int32, (replicas, LANES), 1)
        which = lax.broadcasted_iota(jnp.int32, (replicas, LANES), 0)
        flat = jnp.sum(jnp.where(place == which, total, 0.0), axis=0, keepdims=True)
        spread_out(outs[len(piece) :], jnp.broadcast_to(flat, (8, LANES)))

    results = far_fields(
        lists,
        tile_values,
        near[1:],
        new_fars[1],
        weights,
        [(wide, BF16)] * len(piece) + copies_of(8),
        last_work,
        "far_second_1",
        through=[near[0], *xs, *base, mixing],
    )
    sent = len(piece) + len(copies_of(8))
    fields, partials, kept = results[: len(piece)], results[len(piece) : sent], results[sent:]
    fields, kept = [kept[0], *fields], kept[1:]

    def early():
        return ((ring_index() + 1) // 2) % 2 == 0

    def late():
        return ((ring_index() + 1) // 2) % 2 == 1

    rest = (fields, kept[:groups], kept[groups : 2 * groups], kept[2 * groups], channels)
    *outputs, token = finish(early, *rest, [], "finish_early")
    total = sum_over_ring(partials, ring, token)
    energy = total[0, :replicas] / jnp.sqrt(jnp.float32(cells * ring * channels))
    x_new, y_new = finish(late, *rest, outputs, "finish_late")
    return (x_new, y_new, energy)


def solution(mesh):
    cells = P(("groups", "row", "col"), None)
    slots = P(("groups", "row", "col"))
    return jax.shard_map(
        local,
        mesh=mesh,
        in_specs=(cells, cells, P(("groups", "row", "col"), None, None), slots, slots, slots, P()),
        out_specs=(cells, cells, P("groups")),
        check_vma=False,
    )
```

```python
import jax
import jax.numpy as jnp
import ml_dtypes
import numpy as np
from jax import lax
from jax.experimental import pallas as pl
from jax.experimental.pallas import tpu as pltpu
from jax.sharding import PartitionSpec as P

STEPS = 2
LANES = 128
LONG, SHORT = 20, 4
VMEM_LIMIT = 14 * 1024 * 1024
NEAR_FLOPS = 4 * 10**9
F32 = jnp.float32
BF16 = jnp.bfloat16
RING = ("row", "col")


def call(body, ins, outs, scratch, name, flops=0, aliases=()):
    return pl.pallas_call(
        body,
        in_specs=[pl.BlockSpec(memory_space=pl.ANY if s is pltpu.HBM else s) for _, s in ins],
        out_specs=[pl.BlockSpec(memory_space=pl.ANY if s is pltpu.HBM else s) for *_, s in outs],
        out_shape=[
            jax.ShapeDtypeStruct(dims, kind) if s is pltpu.HBM else s(dims, kind)
            for dims, kind, s in outs
        ],
        scratch_shapes=scratch,
        input_output_aliases=dict(aliases),
        compiler_params=pltpu.CompilerParams(vmem_limit_bytes=VMEM_LIMIT),
        cost_estimate=pl.CostEstimate(
            flops=int(flops) or 1000, bytes_accessed=1000, transcendentals=0
        ),
        name=name,
    )(*[pltpu.with_memory_space_constraint(a, s) for a, s in ins])


def vmem(*arrays):
    return [(a, pltpu.VMEM) for a in arrays]


def lanes(group):
    return slice(group * LANES, (group + 1) * LANES)


def spanned(group, channels, width):
    first = group * LANES // channels * channels
    last = -(-(group + 1) * LANES // channels) * channels
    return list(range(first // LANES, -(-min(last, width) // LANES)))


def span_lanes(near):
    return slice(near[0] * LANES, (near[-1] + 1) * LANES)


def split(x):
    high = x.astype(BF16)
    return high, (x - high.astype(F32)).astype(BF16)


def bases_into(outs, xs, ys, same, step, channels):
    groups = len(xs)
    width = groups * LANES
    detune = 1.0 - (step + 1.0) / (STEPS + 1.0)
    parts = [split(x) for x in xs]
    for g in range(groups):
        near = spanned(g, channels, width)
        ones = same[span_lanes(near), lanes(g)]
        totals = sum(
            jnp.dot(
                jnp.concatenate([parts[n][k] for n in near], axis=1),
                ones,
                preferred_element_type=F32,
            )
            for k in range(2)
        )
        penalty = 0.02 * (totals - (2.0 - channels))
        outs[g][...] = ys[g] + 0.5 * (-detune * xs[g] - 0.4 * penalty)


def mixed_of(fields, mixing, group, channels):
    near = spanned(group, channels, mixing.shape[0])
    return jnp.dot(
        jnp.concatenate([fields[n] for n in near], axis=1),
        mixing[span_lanes(near), lanes(group)],
        preferred_element_type=F32,
    )


def load_first(positions, groups_of):
    cells = positions.shape[0]
    n = len(groups_of)

    def body(x_ref, *refs):
        x_outs, r_outs, sent, sems = refs[:n], refs[n : 2 * n], refs[2 * n], refs[-1]
        copies = [
            pltpu.make_async_copy(x_ref.at[:, lanes(g)], x_outs[i], sems.at[i])
            for i, g in enumerate(groups_of)
        ]
        for copy in copies:
            copy.start()
        for i, copy in enumerate(copies):
            copy.wait()
            rounded = x_outs[i][...].astype(BF16)
            r_outs[i][...] = rounded
            sent[:, lanes(i)] = rounded

    outs = call(
        body,
        [(positions, pltpu.HBM)],
        [((cells, LANES), F32, pltpu.VMEM)] * n
        + [((cells, LANES), BF16, pltpu.VMEM)] * n
        + [((cells, n * LANES), BF16, pltpu.VMEM)],
        [pltpu.SemaphoreType.DMA((n,))],
        "load_first",
    )
    return outs[:n], outs[n : 2 * n], outs[2 * n]


def section(slots, per):
    return -(-(slots + per) // (2 * LONG)) * LONG


def make_lists(rows, cols, count, positions, groups_of, after, slots, tile, ring_index):
    cells = positions.shape[0]
    per = cells // tile
    pairs = section(slots, per)
    n = len(groups_of)

    def body(rows_hbm, cols_hbm, count_hbm, x_ref, _, list_ref, *refs):
        x_outs, r_outs = refs[:n], refs[n : 2 * n]
        rows_ref, cols_ref, count_ref, held, sems = refs[2 * n :]
        copies = [
            pltpu.make_async_copy(*ends, sems.at[k])
            for k, ends in enumerate(
                [(rows_hbm, rows_ref), (cols_hbm, cols_ref), (count_hbm, count_ref)]
                + [(x_ref.at[:, lanes(g)], x_outs[i]) for i, g in enumerate(groups_of)]
            )
        ]
        for copy in copies:
            copy.start()
        for k in range(2 * per):
            held[k] = -1
        far_third = jnp.where(lax.rem(ring_index(), 2) == 1, 2, 0)
        for copy in copies[:3]:
            copy.wait()

        def visit(slot, totals):
            near_pairs, far_pairs = totals
            row, col = rows_ref[slot], cols_ref[slot]
            third = jnp.where(col >= 2 * per, 2, jnp.where(col >= per, 1, 0))
            source = col - third * per
            far = third == far_third
            source = jnp.where(far | (third == 1), source, source + per)
            key = row + jnp.where(far, per, 0)
            place = 2 * jnp.where(far, far_pairs + pairs, near_pairs)
            entry = slot * 65536 + source * 256 + row
            other = held[key]
            full = other >= 0
            list_ref[place] = other
            list_ref[place + 1] = entry
            held[key] = jnp.where(full, -1, entry)
            one = full.astype(jnp.int32)
            far_one = jnp.where(far, one, 0)
            return near_pairs + one - far_one, far_pairs + far_one

        totals = lax.fori_loop(0, count_ref[0], visit, (jnp.int32(0), jnp.int32(0)))
        for part, zero in enumerate((2 * per, per)):
            total = totals[part]
            start = part * pairs
            for k in range(per):
                other = held[part * per + k]
                list_ref[2 * (start + total)] = other
                list_ref[2 * (start + total) + 1] = zero * 256 + k
                total = total + (other >= 0).astype(jnp.int32)
            rest = total % LONG
            padded = rest > 2 * SHORT
            long_turns = total // LONG + padded.astype(jnp.int32)
            short_turns = jnp.where(padded, 0, (rest + SHORT - 1) // SHORT)

            def pad(pair, carry, start=start, zero=zero):
                for e in range(2):
                    list_ref[2 * (start + pair) + e] = zero * 256 + per
                return carry

            lax.fori_loop(total, long_turns * LONG + short_turns * SHORT, pad, 0)
            list_ref[4 * pairs + 2 * part] = long_turns
            list_ref[4 * pairs + 2 * part + 1] = short_turns
        for i, copy in enumerate(copies[3:]):
            copy.wait()
            r_outs[i][...] = x_outs[i][...].astype(BF16)

    outs = call(
        body,
        [(a, pl.ANY) for a in (rows, cols, count)] + [(positions, pltpu.HBM)] + vmem(after),
        [((4 * pairs + 4 + 2,), jnp.int32, pltpu.SMEM)]
        + [((cells, LANES), F32, pltpu.VMEM)] * n
        + [((cells, LANES), BF16, pltpu.VMEM)] * n,
        [
            pltpu.SMEM(rows.shape, jnp.int32),
            pltpu.SMEM(cols.shape, jnp.int32),
            pltpu.SMEM(count.shape, jnp.int32),
            pltpu.SMEM((2 * per,), jnp.int32),
            pltpu.SemaphoreType.DMA((3 + n,)),
        ],
        "make_lists",
    )
    return outs[0], outs[1 : 1 + n], outs[1 + n :]


def add_pairs(part, list_ref, tiles, field, window, pairs):
    def turn(first, length):
        for u in range(length):
            place = 2 * (part * pairs + first + u)
            entries = [list_ref[place + e] for e in range(2)]
            left = jnp.concatenate([tiles[n >> 16] for n in entries], axis=1)
            right = jnp.concatenate([window[(n >> 8) & 255] for n in entries], axis=0)
            field[entries[1] & 255] += jnp.dot(left, right, preferred_element_type=F32)

    def long(i, carry):
        turn(i * LONG, LONG)
        return carry

    def short(i, carry):
        turn(long_turns * LONG + i * SHORT, SHORT)
        return carry

    long_turns = list_ref[4 * pairs + 2 * part]
    lax.fori_loop(0, long_turns, long, 0)
    lax.fori_loop(0, list_ref[4 * pairs + 2 * part + 1], short, 0)


def near_fields(lists, tiles, owns, others, far_part, sent, after, flops, name):
    slots, tile, _ = tiles.shape
    cells = owns[0].shape[0]
    groups = len(owns)
    width = groups * LANES
    per = cells // tile
    pairs = section(slots, per)
    start = [] if far_part is None else [far_part]

    def body(list_ref, tiles_ref, *refs):
        own_refs, other_refs, refs = refs[:groups], refs[groups : 2 * groups], refs[2 * groups :]
        start_refs, refs = refs[: len(start)], refs[len(start) :]
        sent_refs, refs = refs[: len(sent)], refs[len(sent) + len(after) :]
        field_outs, sent_outs, (field, window) = refs[:groups], refs[groups:-2], refs[-2:]
        for out, ref in zip(sent_outs, sent_refs):
            out[...] = ref[...]
        for g in range(groups):
            window[:per, :, lanes(g)] = own_refs[g][...].reshape(per, tile, LANES)
            window[per : 2 * per, :, lanes(g)] = other_refs[g][...].reshape(per, tile, LANES)
        window[2 * per] = jnp.zeros((tile, width), BF16)
        field[:per] = jnp.zeros((per, tile, width), F32)
        for ref in start_refs:
            field[:per, :, lanes(0)] = ref[...].reshape(per, tile, LANES)
        add_pairs(0, list_ref, tiles_ref, field, window, pairs)
        for g, out in enumerate(field_outs):
            out[...] = field[:per, :, lanes(g)].reshape(cells, LANES).astype(out.dtype)

    outs = call(
        body,
        [(lists, pltpu.SMEM)] + vmem(tiles, *owns, *others, *start, *sent, *after),
        [
            ((cells, LANES), BF16 if start and g == 0 else F32, pltpu.VMEM)
            for g in range(groups)
        ]
        + [(a.shape, BF16, pltpu.VMEM) for a in sent],
        [
            pltpu.VMEM((per + 1, tile, width), F32),
            pltpu.VMEM((2 * per + 1, tile, width), BF16),
        ],
        name,
        flops,
    )
    return outs[:groups], outs[groups:]


def far_fields(lists, tiles, nears, far, extra, outs_of, work, name, flops=0, through=()):
    slots, tile, _ = tiles.shape
    cells, width = far.shape
    per = cells // tile
    pairs = section(slots, per)
    n = width // LANES
    m = len(nears)

    def body(list_ref, tiles_ref, far_ref, *refs):
        near_refs, extra_refs = refs[:m], refs[m : m + len(extra)]
        through_refs = refs[m + len(extra) : m + len(extra) + len(through)]
        out_refs, (field, window) = refs[m + len(extra) + len(through) : -2], refs[-2:]
        window[:per] = far_ref[...].reshape(per, tile, width)
        window[per] = jnp.zeros((tile, width), BF16)
        if not near_refs:
            field[:per] = jnp.zeros((per, tile, width), F32)
        for i, ref in enumerate(near_refs):
            field[:per, :, lanes(i)] = ref[...].reshape(per, tile, LANES)
        add_pairs(1, list_ref, tiles_ref, field, window, pairs)
        done = [field[:per, :, lanes(i)].reshape(cells, LANES) for i in range(n)]
        work(done, [*extra_refs, *through_refs], out_refs[: len(outs_of)])

    return call(
        body,
        [(lists, pltpu.SMEM)] + vmem(tiles, far, *nears, *extra, *through),
        [(*out, pltpu.VMEM) for out in outs_of] + [(a.shape, a.dtype, pltpu.VMEM) for a in through],
        [pltpu.VMEM((per + 1, tile, width), F32), pltpu.VMEM((per + 1, tile, width), BF16)],
        name,
        flops,
        [(3 + m + len(extra) + i, len(outs_of) + i) for i in range(len(through))],
    )


def first_base(xs, momenta, same, spread, coupling, channels):
    cells, width = momenta.shape
    groups = len(xs)

    def body(*refs):
        x_refs, (y_ref, same_ref, spread_ref, coupling_ref) = refs[:groups], refs[groups : groups + 4]
        outs = refs[groups + 4 :]
        tall = jnp.dot(spread_ref[...], coupling_ref[...], preferred_element_type=F32).astype(BF16)
        wide = lax.dot_general(
            tall, spread_ref[...], (((1,), (1,)), ((), ())), preferred_element_type=F32
        )
        outs[groups][...] = (wide * same_ref[...].astype(F32)).astype(BF16)
        x = [ref[...] for ref in x_refs]
        y = [y_ref[:, lanes(g)] for g in range(groups)]
        bases_into(outs[:groups], x, y, same_ref, 0, channels)

    outs = call(
        body,
        vmem(*xs, momenta, same, spread, coupling),
        [((cells, LANES), F32, pltpu.VMEM)] * groups + [((width, width), BF16, pltpu.VMEM)],
        [],
        "first_base",
    )
    return outs[:groups], outs[groups]


def updated(field_mixed, base, x):
    y_new = base - 0.2 * field_mixed
    return jnp.clip(x + 0.5 * y_new, -1.0, 1.0), y_new


def second_base(xs, ys, later, fields, first_base, first_x, rounded, same, mixing, channels):
    groups = len(rounded)
    cells = rounded[0].shape[0]
    width = groups * LANES
    done, m = len(xs), len(later)

    def body(*refs):
        refs = list(refs)

        def take(n):
            taken = refs[:n]
            del refs[:n]
            return taken

        x = [ref[...] for ref in take(done)]
        y = [ref[...] for ref in take(done)]
        held = [ref[...] for ref in take(groups)]
        base_refs, x_refs = take(m), take(m)
        r = [ref[...] for ref in take(groups)]
        same_ref, mixing_ref = take(2)
        for i, t in enumerate(later):
            x_new, y_new = updated(
                mixed_of(held, mixing_ref, t, channels), base_refs[i][...], x_refs[i][...]
            )
            x.append(x_new)
            y.append(y_new)
            refs[2 * groups + i][...] = x_new
        bases_into(refs[:groups], x, y, same_ref, 1, channels)
        for g in range(groups):
            near = spanned(g, channels, width)
            refs[groups + g][...] = lax.dot_general(
                jnp.concatenate([r[n] for n in near], axis=1),
                mixing_ref[lanes(g), span_lanes(near)],
                (((1,), (1,)), ((), ())),
                preferred_element_type=F32,
            )

    outs = call(
        body,
        vmem(*xs, *ys, *fields, *first_base, *first_x, *rounded, same, mixing),
        [((cells, LANES), F32, pltpu.VMEM)] * (2 * groups + m),
        [],
        "second_base",
    )
    return outs[:groups], outs[groups : 2 * groups], outs[2 * groups :]


def finish(fields, xs, bases, mixing, channels):
    groups = len(xs)
    cells = xs[0].shape[0]
    width = groups * LANES

    def body(*refs):
        field_refs, x_refs, base_refs = [refs[k * groups : (k + 1) * groups] for k in range(3)]
        mixing_ref, x_out, y_out, token, x_buf, y_buf, sems = refs[3 * groups :]
        held = [ref[...] for ref in field_refs]
        copies = []
        for g in range(groups):
            y_new = base_refs[g][...] - 0.2 * mixed_of(held, mixing_ref, g, channels)
            y_buf[g] = y_new
            x_buf[g] = jnp.clip(x_refs[g][...] + 0.5 * y_new, -1.0, 1.0)
            for k, (buf, out) in enumerate(((y_buf, y_out), (x_buf, x_out))):
                copies.append(
                    pltpu.make_async_copy(buf.at[g], out.at[:, lanes(g)], sems.at[g, k])
                )
                copies[-1].start()
        token[...] = jnp.zeros_like(token)
        for copy in copies:
            copy.wait()

    return call(
        body,
        vmem(*fields, *xs, *bases, mixing),
        [((cells, width), F32, pltpu.HBM)] * 2 + [((8, LANES), F32, pltpu.VMEM)],
        [
            pltpu.VMEM((groups, cells, LANES), F32),
            pltpu.VMEM((groups, cells, LANES), F32),
            pltpu.SemaphoreType.DMA((groups, 2)),
        ],
        "finish",
    )


def copies_of(rows):
    return [((rows * n, LANES), F32) for n in (1, 2, 3)]


def spread_out(outs, value):
    for out in outs:
        out[...] = jnp.concatenate([value] * (out.shape[0] // value.shape[0]), axis=0)


def add_up(arrays, token, name):
    rows = arrays[0].shape[0]

    def body(*refs):
        total = refs[0][...]
        for ref in refs[1 : len(arrays)]:
            total = total + ref[:rows, :]
        spread_out(refs[len(arrays) + len(token) :], total)

    return call(
        body,
        vmem(*arrays, *token),
        [(*size, pltpu.VMEM) for size in copies_of(rows)],
        [],
        name,
    )


def sum_over_ring(values, ring, token):
    if ring & (ring - 1):
        return lax.psum(values[0], RING)
    rounds, size = [], 1
    while size < ring:
        digits = (1, 2, 3) if 4 * size <= ring else (1,)
        rounds.append([size * d for d in digits])
        size *= len(digits) + 1
    for i, bits in enumerate(reversed(rounds)):
        received = [
            lax.ppermute(value, RING, [(j, j ^ bit) for j in range(ring)])
            for value, bit in zip(values, bits)
        ]
        if i == len(rounds) - 1:
            rows = values[0].shape[0]
            return values[0] + sum(part[:rows] for part in received)
        values = add_up([values[0], *received], [token] if i == 0 else [], f"add_up_{i}")
    return values[0]


def local(positions, momenta, tile_values, tile_rows, tile_cols, tile_count, channel_coupling):
    cells, width = positions.shape
    slots, tile, _ = tile_values.shape
    channels = channel_coupling.shape[0]
    replicas = width // channels
    groups = width // LANES
    ring = lax.axis_size("row") * lax.axis_size("col")
    where = np.arange(width)
    same = jnp.asarray(
        (where[:, None] // channels == where[None] // channels).astype(ml_dtypes.bfloat16)
    )
    spread = jnp.asarray(
        (where[:, None] % channels == np.arange(channels)[None]).astype(ml_dtypes.bfloat16)
    )
    on_chip = [(i, i ^ 1) for i in range(ring)]
    off_chip = [(i, (i + 1) % ring if i % 2 else (i - 1) % ring) for i in range(ring)]
    wide = (cells, LANES)
    every = list(range(groups))
    first_pieces = [every[:-1], every[-1:]]
    second_pieces = [every[:1], every[1:]]

    def ring_index():
        return lax.axis_index("row") * lax.axis_size("col") + lax.axis_index("col")

    def far_swap(mine):
        return lax.ppermute(mine, RING, off_chip)

    def near_swap(mine):
        return lax.ppermute(mine, RING, on_chip)

    def ready(piece, done):
        return [
            t for t in every if t not in done and max(spanned(t, channels, width)) <= piece[-1]
        ]

    def keep(done, _, outs):
        outs[0][...] = done[0]

    def needed(todo, piece):
        return sorted({n for t in todo for n in spanned(t, channels, width)} - set(piece))

    xs, owns, sent = load_first(positions, first_pieces[0])
    fars = [far_swap(sent)]
    lists, more_x, more_own = make_lists(
        tile_rows, tile_cols, tile_count, positions, first_pieces[1], sent, slots, tile, ring_index
    )
    xs, owns = [*xs, *more_x], [*owns, *more_own]
    others = [near_swap(r) for r in owns]
    base, mixing = first_base(xs, momenta, same, spread, channel_coupling, channels)
    near, sent = near_fields(
        lists, tile_values, owns, others, None, more_own, [mixing], 0, "near_first"
    )
    fars.append(far_swap(sent[0]))

    fields, new_x, new_y, rounded, new_fars = {}, [], [], {}, []
    for p, piece in enumerate(first_pieces):
        last = p == len(first_pieces) - 1
        todo = ready(piece, rounded)
        known = needed(todo, piece)
        assert second_pieces[p] == todo

        def work(done, ins, outs, piece=piece, todo=todo, known=known, last=last):
            held = {n: ins[1 + i][...] for i, n in enumerate(known)}
            done = [field.astype(BF16) for field in done]
            held.update(zip(piece, done))
            rest = ins[1 + len(known) :]
            for i, t in enumerate(todo):
                x_new, y_new = updated(
                    mixed_of(held, ins[0], t, channels), rest[2 * i][...], rest[2 * i + 1][...]
                )
                r_new = x_new.astype(BF16)
                outs[0][:, lanes(i)] = r_new
                outs[1 + i][...] = r_new
                if not last:
                    outs[1 + len(todo) + len(piece) + 2 * i][...] = x_new
                    outs[2 + len(todo) + len(piece) + 2 * i][...] = y_new
            for i, field in enumerate(done):
                outs[1 + len(todo) + i][...] = field

        results = far_fields(
            lists,
            tile_values,
            [near[n] for n in piece],
            fars[p],
            [mixing] + [fields[n] for n in known] + [a for t in todo for a in (base[t], xs[t])],
            [((cells, len(todo) * LANES), BF16)]
            + [(wide, BF16)] * (len(todo) + len(piece))
            + ([] if last else [(wide, F32)] * (2 * len(todo))),
            work,
            f"far_first_{p}",
        )
        new_fars.append(far_swap(results[0]))
        rounded.update(zip(todo, results[1:]))
        fields.update(zip(piece, results[1 + len(todo) :]))
        new_x += results[1 + len(todo) + len(piece) :: 2]
        new_y += results[2 + len(todo) + len(piece) :: 2]

    owns = [rounded[g] for g in every]
    others = [near_swap(r) for r in owns]
    (part,) = far_fields(
        lists, tile_values, [], new_fars[0], [], [(wide, F32)], keep, "far_second_0", NEAR_FLOPS
    )
    near, _ = near_fields(lists, tile_values, owns, others, part, [], [], 0, "near_second")
    later = second_pieces[1]
    base, weights, more_x = second_base(
        new_x,
        new_y,
        later,
        [fields[g] for g in every],
        [base[t] for t in later],
        [xs[t] for t in later],
        owns,
        same,
        mixing,
        channels,
    )
    xs = [*new_x, *more_x]
    piece = second_pieces[1]

    def last_work(done, ins, outs):
        held = [ins[groups][...]] + [field.astype(BF16) for field in done]
        for out, field in zip(outs, held[1:]):
            out[...] = field
        row = jnp.concatenate(
            [
                jnp.sum(field.astype(F32) * ref[...], axis=0, keepdims=True)
                for field, ref in zip(held, ins[:groups])
            ],
            axis=1,
        )
        row = jnp.broadcast_to(row, (replicas, width))
        lane = lax.broadcasted_iota(jnp.int32, (replicas, width), 1)
        first = lax.broadcasted_iota(jnp.int32, (replicas, width), 0) * channels
        inside = (lane >= first) & (lane < first + channels)
        total = jnp.sum(jnp.where(inside, row, 0.0), axis=1, keepdims=True)
        place = lax.broadcasted_iota(jnp.int32, (replicas, LANES), 1)
        which = lax.broadcasted_iota(jnp.int32, (replicas, LANES), 0)
        flat = jnp.sum(jnp.where(place == which, total, 0.0), axis=0, keepdims=True)
        spread_out(outs[len(piece) :], jnp.broadcast_to(flat, (8, LANES)))

    results = far_fields(
        lists,
        tile_values,
        near[1:],
        new_fars[1],
        weights,
        [(wide, BF16)] * len(piece) + copies_of(8),
        last_work,
        "far_second_1",
        through=[near[0], *xs, *base, mixing],
    )
    sent = len(piece) + len(copies_of(8))
    fields, partials, kept = results[: len(piece)], results[len(piece) : sent], results[sent:]
    fields, kept = [kept[0], *fields], kept[1:]

    x_new, y_new, token = finish(
        fields, kept[:groups], kept[groups : 2 * groups], kept[2 * groups], channels
    )
    total = sum_over_ring(partials, ring, token)
    energy = total[0, :replicas] / jnp.sqrt(jnp.float32(cells * ring * channels))
    return (x_new, y_new, energy)


def solution(mesh):
    cells = P(("groups", "row", "col"), None)
    slots = P(("groups", "row", "col"))
    return jax.shard_map(
        local,
        mesh=mesh,
        in_specs=(cells, cells, P(("groups", "row", "col"), None, None), slots, slots, slots, P()),
        out_specs=(cells, cells, P("groups")),
        check_vma=False,
    )
```

```python
import jax
import jax.numpy as jnp
import ml_dtypes
import numpy as np
from jax import lax
from jax.experimental import pallas as pl
from jax.experimental.pallas import tpu as pltpu
from jax.sharding import PartitionSpec as P

STEPS = 2
LANES = 128
LONG, SHORT = 20, 4
VMEM_LIMIT = 14 * 1024 * 1024
NEAR_FLOPS = 4 * 10**9
F32 = jnp.float32
BF16 = jnp.bfloat16
RING = ("row", "col")


def call(body, ins, outs, scratch, name, flops=0, aliases=()):
    return pl.pallas_call(
        body,
        in_specs=[pl.BlockSpec(memory_space=pl.ANY if s is pltpu.HBM else s) for _, s in ins],
        out_specs=[pl.BlockSpec(memory_space=pl.ANY if s is pltpu.HBM else s) for *_, s in outs],
        out_shape=[
            jax.ShapeDtypeStruct(dims, kind) if s is pltpu.HBM else s(dims, kind)
            for dims, kind, s in outs
        ],
        scratch_shapes=scratch,
        input_output_aliases=dict(aliases),
        compiler_params=pltpu.CompilerParams(vmem_limit_bytes=VMEM_LIMIT),
        cost_estimate=pl.CostEstimate(
            flops=int(flops) or 1000, bytes_accessed=1000, transcendentals=0
        ),
        name=name,
    )(*[pltpu.with_memory_space_constraint(a, s) for a, s in ins])


def vmem(*arrays):
    return [(a, pltpu.VMEM) for a in arrays]


def lanes(group):
    return slice(group * LANES, (group + 1) * LANES)


def spanned(group, channels, width):
    first = group * LANES // channels * channels
    last = -(-(group + 1) * LANES // channels) * channels
    return list(range(first // LANES, -(-min(last, width) // LANES)))


def span_lanes(near):
    return slice(near[0] * LANES, (near[-1] + 1) * LANES)


def split(x):
    high = x.astype(BF16)
    return high, (x - high.astype(F32)).astype(BF16)


def bases_into(outs, xs, ys, same, step, channels):
    groups = len(xs)
    width = groups * LANES
    detune = 1.0 - (step + 1.0) / (STEPS + 1.0)
    parts = [split(x) for x in xs]
    for g in range(groups):
        near = spanned(g, channels, width)
        ones = same[span_lanes(near), lanes(g)]
        totals = sum(
            jnp.dot(
                jnp.concatenate([parts[n][k] for n in near], axis=1),
                ones,
                preferred_element_type=F32,
            )
            for k in range(2)
        )
        penalty = 0.02 * (totals - (2.0 - channels))
        outs[g][...] = ys[g] + 0.5 * (-detune * xs[g] - 0.4 * penalty)


def mixed_of(fields, mixing, group, channels):
    near = spanned(group, channels, mixing.shape[0])
    return jnp.dot(
        jnp.concatenate([fields[n] for n in near], axis=1),
        mixing[span_lanes(near), lanes(group)],
        preferred_element_type=F32,
    )


def load_first(positions, groups_of):
    cells = positions.shape[0]
    n = len(groups_of)

    def body(x_ref, *refs):
        x_outs, sent, sems = refs[:n], refs[n], refs[-1]
        copies = [
            pltpu.make_async_copy(x_ref.at[:, lanes(g)], x_outs[i], sems.at[i])
            for i, g in enumerate(groups_of)
        ]
        for copy in copies:
            copy.start()
        for i, copy in enumerate(copies):
            copy.wait()
            sent[:, lanes(i)] = x_outs[i][...].astype(BF16)

    outs = call(
        body,
        [(positions, pltpu.HBM)],
        [((cells, LANES), F32, pltpu.VMEM)] * n + [((cells, n * LANES), BF16, pltpu.VMEM)],
        [pltpu.SemaphoreType.DMA((n,))],
        "load_first",
    )
    return outs[:n], outs[n]


def section(slots, per):
    return -(-(slots + per) // (2 * LONG)) * LONG


def make_lists(rows, cols, count, positions, groups_of, sent, slots, tile, ring_index):
    cells = positions.shape[0]
    per = cells // tile
    pairs = section(slots, per)
    n, early = len(groups_of), sent.shape[1] // LANES

    def body(rows_hbm, cols_hbm, count_hbm, x_ref, sent_ref, list_ref, *refs):
        x_outs, r_outs, cut_outs = refs[:n], refs[n : 2 * n], refs[2 * n : 2 * n + early]
        rows_ref, cols_ref, count_ref, held, sems = refs[2 * n + early :]
        copies = [
            pltpu.make_async_copy(*ends, sems.at[k])
            for k, ends in enumerate(
                [(rows_hbm, rows_ref), (cols_hbm, cols_ref), (count_hbm, count_ref)]
                + [(x_ref.at[:, lanes(g)], x_outs[i]) for i, g in enumerate(groups_of)]
            )
        ]
        for copy in copies:
            copy.start()
        for i, out in enumerate(cut_outs):
            out[...] = sent_ref[:, lanes(i)]
        for k in range(2 * per):
            held[k] = -1
        far_third = jnp.where(lax.rem(ring_index(), 2) == 1, 2, 0)
        for copy in copies[:3]:
            copy.wait()

        def visit(slot, totals):
            near_pairs, far_pairs = totals
            row, col = rows_ref[slot], cols_ref[slot]
            third = jnp.where(col >= 2 * per, 2, jnp.where(col >= per, 1, 0))
            source = col - third * per
            far = third == far_third
            source = jnp.where(far | (third == 1), source, source + per)
            key = row + jnp.where(far, per, 0)
            place = 2 * jnp.where(far, far_pairs + pairs, near_pairs)
            entry = slot * 65536 + source * 256 + row
            other = held[key]
            full = other >= 0
            list_ref[place] = other
            list_ref[place + 1] = entry
            held[key] = jnp.where(full, -1, entry)
            one = full.astype(jnp.int32)
            far_one = jnp.where(far, one, 0)
            return near_pairs + one - far_one, far_pairs + far_one

        totals = lax.fori_loop(0, count_ref[0], visit, (jnp.int32(0), jnp.int32(0)))
        for part, zero in enumerate((2 * per, per)):
            total = totals[part]
            start = part * pairs
            for k in range(per):
                other = held[part * per + k]
                list_ref[2 * (start + total)] = other
                list_ref[2 * (start + total) + 1] = zero * 256 + k
                total = total + (other >= 0).astype(jnp.int32)
            rest = total % LONG
            padded = rest > 2 * SHORT
            long_turns = total // LONG + padded.astype(jnp.int32)
            short_turns = jnp.where(padded, 0, (rest + SHORT - 1) // SHORT)

            def pad(pair, carry, start=start, zero=zero):
                for e in range(2):
                    list_ref[2 * (start + pair) + e] = zero * 256 + per
                return carry

            lax.fori_loop(total, long_turns * LONG + short_turns * SHORT, pad, 0)
            list_ref[4 * pairs + 2 * part] = long_turns
            list_ref[4 * pairs + 2 * part + 1] = short_turns
        for i, copy in enumerate(copies[3:]):
            copy.wait()
            r_outs[i][...] = x_outs[i][...].astype(BF16)

    outs = call(
        body,
        [(a, pl.ANY) for a in (rows, cols, count)] + [(positions, pltpu.HBM)] + vmem(sent),
        [((4 * pairs + 4 + 2,), jnp.int32, pltpu.SMEM)]
        + [((cells, LANES), F32, pltpu.VMEM)] * n
        + [((cells, LANES), BF16, pltpu.VMEM)] * (n + early),
        [
            pltpu.SMEM(rows.shape, jnp.int32),
            pltpu.SMEM(cols.shape, jnp.int32),
            pltpu.SMEM(count.shape, jnp.int32),
            pltpu.SMEM((2 * per,), jnp.int32),
            pltpu.SemaphoreType.DMA((3 + n,)),
        ],
        "make_lists",
    )
    return outs[0], outs[1 : 1 + n], outs[1 + n : 1 + 2 * n], outs[1 + 2 * n :]


def add_pairs(part, list_ref, tiles, field, window, pairs):
    def turn(first, length):
        for u in range(length):
            place = 2 * (part * pairs + first + u)
            entries = [list_ref[place + e] for e in range(2)]
            left = jnp.concatenate([tiles[n >> 16] for n in entries], axis=1)
            right = jnp.concatenate([window[(n >> 8) & 255] for n in entries], axis=0)
            field[entries[1] & 255] += jnp.dot(left, right, preferred_element_type=F32)

    def long(i, carry):
        turn(i * LONG, LONG)
        return carry

    def short(i, carry):
        turn(long_turns * LONG + i * SHORT, SHORT)
        return carry

    long_turns = list_ref[4 * pairs + 2 * part]
    lax.fori_loop(0, long_turns, long, 0)
    lax.fori_loop(0, list_ref[4 * pairs + 2 * part + 1], short, 0)


def near_fields(lists, tiles, owns, others, far_part, sent, after, flops, name):
    slots, tile, _ = tiles.shape
    cells = owns[0].shape[0]
    groups = len(owns)
    width = groups * LANES
    per = cells // tile
    pairs = section(slots, per)
    start = [] if far_part is None else [far_part]

    def body(list_ref, tiles_ref, *refs):
        own_refs, other_refs, refs = refs[:groups], refs[groups : 2 * groups], refs[2 * groups :]
        start_refs, refs = refs[: len(start)], refs[len(start) :]
        sent_refs, refs = refs[: len(sent)], refs[len(sent) + len(after) :]
        field_outs, sent_outs, (field, window) = refs[:groups], refs[groups:-2], refs[-2:]
        for out, ref in zip(sent_outs, sent_refs):
            out[...] = ref[...]
        for g in range(groups):
            window[:per, :, lanes(g)] = own_refs[g][...].reshape(per, tile, LANES)
            window[per : 2 * per, :, lanes(g)] = other_refs[g][...].reshape(per, tile, LANES)
        window[2 * per] = jnp.zeros((tile, width), BF16)
        field[:per] = jnp.zeros((per, tile, width), F32)
        for ref in start_refs:
            field[:per, :, lanes(0)] = ref[...].reshape(per, tile, LANES)
        add_pairs(0, list_ref, tiles_ref, field, window, pairs)
        for g, out in enumerate(field_outs):
            out[...] = field[:per, :, lanes(g)].reshape(cells, LANES).astype(out.dtype)

    outs = call(
        body,
        [(lists, pltpu.SMEM)] + vmem(tiles, *owns, *others, *start, *sent, *after),
        [
            ((cells, LANES), BF16 if start and g == 0 else F32, pltpu.VMEM)
            for g in range(groups)
        ]
        + [(a.shape, BF16, pltpu.VMEM) for a in sent],
        [
            pltpu.VMEM((per + 1, tile, width), F32),
            pltpu.VMEM((2 * per + 1, tile, width), BF16),
        ],
        name,
        flops,
    )
    return outs[:groups], outs[groups:]


def far_fields(lists, tiles, nears, far, extra, outs_of, work, name, flops=0, through=()):
    slots, tile, _ = tiles.shape
    cells, width = far.shape
    per = cells // tile
    pairs = section(slots, per)
    n = width // LANES
    m = len(nears)

    def body(list_ref, tiles_ref, far_ref, *refs):
        near_refs, extra_refs = refs[:m], refs[m : m + len(extra)]
        through_refs = refs[m + len(extra) : m + len(extra) + len(through)]
        out_refs, (field, window) = refs[m + len(extra) + len(through) : -2], refs[-2:]
        window[:per] = far_ref[...].reshape(per, tile, width)
        window[per] = jnp.zeros((tile, width), BF16)
        if not near_refs:
            field[:per] = jnp.zeros((per, tile, width), F32)
        for i, ref in enumerate(near_refs):
            field[:per, :, lanes(i)] = ref[...].reshape(per, tile, LANES)
        add_pairs(1, list_ref, tiles_ref, field, window, pairs)
        done = [field[:per, :, lanes(i)].reshape(cells, LANES) for i in range(n)]
        work(done, [*extra_refs, *through_refs], out_refs[: len(outs_of)])

    return call(
        body,
        [(lists, pltpu.SMEM)] + vmem(tiles, far, *nears, *extra, *through),
        [(*out, pltpu.VMEM) for out in outs_of] + [(a.shape, a.dtype, pltpu.VMEM) for a in through],
        [pltpu.VMEM((per + 1, tile, width), F32), pltpu.VMEM((per + 1, tile, width), BF16)],
        name,
        flops,
        [(3 + m + len(extra) + i, len(outs_of) + i) for i in range(len(through))],
    )


def first_base(xs, momenta, same, spread, coupling, channels):
    cells, width = momenta.shape
    groups = len(xs)

    def body(*refs):
        x_refs, (y_ref, same_ref, spread_ref, coupling_ref) = refs[:groups], refs[groups : groups + 4]
        outs = refs[groups + 4 :]
        tall = jnp.dot(spread_ref[...], coupling_ref[...], preferred_element_type=F32).astype(BF16)
        wide = lax.dot_general(
            tall, spread_ref[...], (((1,), (1,)), ((), ())), preferred_element_type=F32
        )
        outs[groups][...] = (wide * same_ref[...].astype(F32)).astype(BF16)
        x = [ref[...] for ref in x_refs]
        y = [y_ref[:, lanes(g)] for g in range(groups)]
        bases_into(outs[:groups], x, y, same_ref, 0, channels)

    outs = call(
        body,
        vmem(*xs, momenta, same, spread, coupling),
        [((cells, LANES), F32, pltpu.VMEM)] * groups + [((width, width), BF16, pltpu.VMEM)],
        [],
        "first_base",
    )
    return outs[:groups], outs[groups]


def updated(field_mixed, base, x):
    y_new = base - 0.2 * field_mixed
    return jnp.clip(x + 0.5 * y_new, -1.0, 1.0), y_new


def second_base(xs, ys, later, fields, first_base, first_x, rounded, same, mixing, channels):
    groups = len(rounded)
    cells = rounded[0].shape[0]
    width = groups * LANES
    done, m = len(xs), len(later)

    def body(*refs):
        refs = list(refs)

        def take(n):
            taken = refs[:n]
            del refs[:n]
            return taken

        x = [ref[...] for ref in take(done)]
        y = [ref[...] for ref in take(done)]
        held = [ref[...] for ref in take(groups)]
        base_refs, x_refs = take(m), take(m)
        r = [ref[...] for ref in take(groups)]
        same_ref, mixing_ref = take(2)
        for i, t in enumerate(later):
            x_new, y_new = updated(
                mixed_of(held, mixing_ref, t, channels), base_refs[i][...], x_refs[i][...]
            )
            x.append(x_new)
            y.append(y_new)
            refs[2 * groups + i][...] = x_new
        bases_into(refs[:groups], x, y, same_ref, 1, channels)
        for g in range(groups):
            near = spanned(g, channels, width)
            refs[groups + g][...] = lax.dot_general(
                jnp.concatenate([r[n] for n in near], axis=1),
                mixing_ref[lanes(g), span_lanes(near)],
                (((1,), (1,)), ((), ())),
                preferred_element_type=F32,
            )

    outs = call(
        body,
        vmem(*xs, *ys, *fields, *first_base, *first_x, *rounded, same, mixing),
        [((cells, LANES), F32, pltpu.VMEM)] * (2 * groups + m),
        [],
        "second_base",
    )
    return outs[:groups], outs[groups : 2 * groups], outs[2 * groups :]


def finish(fields, xs, bases, mixing, channels):
    groups = len(xs)
    cells = xs[0].shape[0]
    width = groups * LANES

    def body(*refs):
        field_refs, x_refs, base_refs = [refs[k * groups : (k + 1) * groups] for k in range(3)]
        mixing_ref, x_out, y_out, token, x_buf, y_buf, sems = refs[3 * groups :]
        held = [ref[...] for ref in field_refs]
        copies = []
        for g in range(groups):
            y_new = base_refs[g][...] - 0.2 * mixed_of(held, mixing_ref, g, channels)
            y_buf[g] = y_new
            x_buf[g] = jnp.clip(x_refs[g][...] + 0.5 * y_new, -1.0, 1.0)
            for k, (buf, out) in enumerate(((y_buf, y_out), (x_buf, x_out))):
                copies.append(
                    pltpu.make_async_copy(buf.at[g], out.at[:, lanes(g)], sems.at[g, k])
                )
                copies[-1].start()
        token[...] = jnp.zeros_like(token)
        for copy in copies:
            copy.wait()

    return call(
        body,
        vmem(*fields, *xs, *bases, mixing),
        [((cells, width), F32, pltpu.HBM)] * 2 + [((8, LANES), F32, pltpu.VMEM)],
        [
            pltpu.VMEM((groups, cells, LANES), F32),
            pltpu.VMEM((groups, cells, LANES), F32),
            pltpu.SemaphoreType.DMA((groups, 2)),
        ],
        "finish",
    )


def copies_of(rows):
    return [((rows * n, LANES), F32) for n in (1, 2, 3)]


def spread_out(outs, value):
    for out in outs:
        out[...] = jnp.concatenate([value] * (out.shape[0] // value.shape[0]), axis=0)


def add_up(arrays, token, name):
    rows = arrays[0].shape[0]

    def body(*refs):
        total = refs[0][...]
        for ref in refs[1 : len(arrays)]:
            total = total + ref[:rows, :]
        spread_out(refs[len(arrays) + len(token) :], total)

    return call(
        body,
        vmem(*arrays, *token),
        [(*size, pltpu.VMEM) for size in copies_of(rows)],
        [],
        name,
    )


def sum_over_ring(values, ring, token):
    if ring & (ring - 1):
        return lax.psum(values[0], RING)
    rounds, size = [], 1
    while size < ring:
        digits = (1, 2, 3) if 4 * size <= ring else (1,)
        rounds.append([size * d for d in digits])
        size *= len(digits) + 1
    for i, bits in enumerate(reversed(rounds)):
        received = [
            lax.ppermute(value, RING, [(j, j ^ bit) for j in range(ring)])
            for value, bit in zip(values, bits)
        ]
        if i == len(rounds) - 1:
            rows = values[0].shape[0]
            return values[0] + sum(part[:rows] for part in received)
        values = add_up([values[0], *received], [token] if i == 0 else [], f"add_up_{i}")
    return values[0]


def local(positions, momenta, tile_values, tile_rows, tile_cols, tile_count, channel_coupling):
    cells, width = positions.shape
    slots, tile, _ = tile_values.shape
    channels = channel_coupling.shape[0]
    replicas = width // channels
    groups = width // LANES
    ring = lax.axis_size("row") * lax.axis_size("col")
    where = np.arange(width)
    same = jnp.asarray(
        (where[:, None] // channels == where[None] // channels).astype(ml_dtypes.bfloat16)
    )
    spread = jnp.asarray(
        (where[:, None] % channels == np.arange(channels)[None]).astype(ml_dtypes.bfloat16)
    )
    on_chip = [(i, i ^ 1) for i in range(ring)]
    off_chip = [(i, (i + 1) % ring if i % 2 else (i - 1) % ring) for i in range(ring)]
    wide = (cells, LANES)
    every = list(range(groups))
    first_pieces = [every[:-1], every[-1:]]
    second_pieces = [every[:1], every[1:]]

    def ring_index():
        return lax.axis_index("row") * lax.axis_size("col") + lax.axis_index("col")

    def far_swap(mine):
        return lax.ppermute(mine, RING, off_chip)

    def near_swap(mine):
        return lax.ppermute(mine, RING, on_chip)

    def ready(piece, done):
        return [
            t for t in every if t not in done and max(spanned(t, channels, width)) <= piece[-1]
        ]

    def keep(done, _, outs):
        outs[0][...] = done[0]

    def needed(todo, piece):
        return sorted({n for t in todo for n in spanned(t, channels, width)} - set(piece))

    xs, sent = load_first(positions, first_pieces[0])
    fars = [far_swap(sent)]
    lists, more_x, more_own, owns = make_lists(
        tile_rows, tile_cols, tile_count, positions, first_pieces[1], sent, slots, tile, ring_index
    )
    xs, owns = [*xs, *more_x], [*owns, *more_own]
    others = [near_swap(r) for r in owns]
    base, mixing = first_base(xs, momenta, same, spread, channel_coupling, channels)
    near, sent = near_fields(
        lists, tile_values, owns, others, None, more_own, [mixing], 0, "near_first"
    )
    fars.append(far_swap(sent[0]))

    fields, new_x, new_y, rounded, new_fars = {}, [], [], {}, []
    for p, piece in enumerate(first_pieces):
        last = p == len(first_pieces) - 1
        todo = ready(piece, rounded)
        known = needed(todo, piece)
        assert second_pieces[p] == todo

        def work(done, ins, outs, piece=piece, todo=todo, known=known, last=last):
            held = {n: ins[1 + i][...] for i, n in enumerate(known)}
            done = [field.astype(BF16) for field in done]
            held.update(zip(piece, done))
            rest = ins[1 + len(known) :]
            near = sorted(held)
            mixed = jnp.dot(
                jnp.concatenate([held[n] for n in near], axis=1),
                ins[0][span_lanes(near), span_lanes(todo)],
                preferred_element_type=F32,
            )
            for i, t in enumerate(todo):
                x_new, y_new = updated(mixed[:, lanes(i)], rest[2 * i][...], rest[2 * i + 1][...])
                r_new = x_new.astype(BF16)
                outs[0][:, lanes(i)] = r_new
                outs[1 + i][...] = r_new
                if not last:
                    outs[1 + len(todo) + len(piece) + 2 * i][...] = x_new
                    outs[2 + len(todo) + len(piece) + 2 * i][...] = y_new
            for i, field in enumerate(done):
                outs[1 + len(todo) + i][...] = field

        results = far_fields(
            lists,
            tile_values,
            [near[n] for n in piece],
            fars[p],
            [mixing] + [fields[n] for n in known] + [a for t in todo for a in (base[t], xs[t])],
            [((cells, len(todo) * LANES), BF16)]
            + [(wide, BF16)] * (len(todo) + len(piece))
            + ([] if last else [(wide, F32)] * (2 * len(todo))),
            work,
            f"far_first_{p}",
        )
        new_fars.append(far_swap(results[0]))
        rounded.update(zip(todo, results[1:]))
        fields.update(zip(piece, results[1 + len(todo) :]))
        new_x += results[1 + len(todo) + len(piece) :: 2]
        new_y += results[2 + len(todo) + len(piece) :: 2]

    owns = [rounded[g] for g in every]
    others = [near_swap(r) for r in owns]
    (part,) = far_fields(
        lists, tile_values, [], new_fars[0], [], [(wide, F32)], keep, "far_second_0", NEAR_FLOPS
    )
    near, _ = near_fields(lists, tile_values, owns, others, part, [], [], 0, "near_second")
    later = second_pieces[1]
    base, weights, more_x = second_base(
        new_x,
        new_y,
        later,
        [fields[g] for g in every],
        [base[t] for t in later],
        [xs[t] for t in later],
        owns,
        same,
        mixing,
        channels,
    )
    xs = [*new_x, *more_x]
    piece = second_pieces[1]

    def last_work(done, ins, outs):
        held = [ins[groups][...]] + [field.astype(BF16) for field in done]
        for out, field in zip(outs, held[1:]):
            out[...] = field
        row = jnp.concatenate(
            [
                jnp.sum(field.astype(F32) * ref[...], axis=0, keepdims=True)
                for field, ref in zip(held, ins[:groups])
            ],
            axis=1,
        )
        row = jnp.broadcast_to(row, (replicas, width))
        lane = lax.broadcasted_iota(jnp.int32, (replicas, width), 1)
        first = lax.broadcasted_iota(jnp.int32, (replicas, width), 0) * channels
        inside = (lane >= first) & (lane < first + channels)
        total = jnp.sum(jnp.where(inside, row, 0.0), axis=1, keepdims=True)
        place = lax.broadcasted_iota(jnp.int32, (replicas, LANES), 1)
        which = lax.broadcasted_iota(jnp.int32, (replicas, LANES), 0)
        flat = jnp.sum(jnp.where(place == which, total, 0.0), axis=0, keepdims=True)
        spread_out(outs[len(piece) :], jnp.broadcast_to(flat, (8, LANES)))

    results = far_fields(
        lists,
        tile_values,
        near[1:],
        new_fars[1],
        weights,
        [(wide, BF16)] * len(piece) + copies_of(8),
        last_work,
        "far_second_1",
        through=[near[0], *xs, *base, mixing],
    )
    sent = len(piece) + len(copies_of(8))
    fields, partials, kept = results[: len(piece)], results[len(piece) : sent], results[sent:]
    fields, kept = [kept[0], *fields], kept[1:]

    x_new, y_new, token = finish(
        fields, kept[:groups], kept[groups : 2 * groups], kept[2 * groups], channels
    )
    total = sum_over_ring(partials, ring, token)
    energy = total[0, :replicas] / jnp.sqrt(jnp.float32(cells * ring * channels))
    return (x_new, y_new, energy)


def solution(mesh):
    cells = P(("groups", "row", "col"), None)
    slots = P(("groups", "row", "col"))
    return jax.shard_map(
        local,
        mesh=mesh,
        in_specs=(cells, cells, P(("groups", "row", "col"), None, None), slots, slots, slots, P()),
        out_specs=(cells, cells, P("groups")),
        check_vma=False,
    )
```

```python
import jax
import jax.numpy as jnp
import ml_dtypes
import numpy as np
from jax import lax
from jax.experimental import pallas as pl
from jax.experimental.pallas import tpu as pltpu
from jax.sharding import PartitionSpec as P

STEPS = 2
LANES = 128
LONG, SHORT = 20, 4
VMEM_LIMIT = 14 * 1024 * 1024
NEAR_FLOPS = 4 * 10**9
F32 = jnp.float32
BF16 = jnp.bfloat16
RING = ("row", "col")


def call(body, ins, outs, scratch, name, flops=0, aliases=()):
    return pl.pallas_call(
        body,
        in_specs=[pl.BlockSpec(memory_space=pl.ANY if s is pltpu.HBM else s) for _, s in ins],
        out_specs=[pl.BlockSpec(memory_space=pl.ANY if s is pltpu.HBM else s) for *_, s in outs],
        out_shape=[
            jax.ShapeDtypeStruct(dims, kind) if s is pltpu.HBM else s(dims, kind)
            for dims, kind, s in outs
        ],
        scratch_shapes=scratch,
        input_output_aliases=dict(aliases),
        compiler_params=pltpu.CompilerParams(vmem_limit_bytes=VMEM_LIMIT),
        cost_estimate=pl.CostEstimate(
            flops=int(flops) or 1000, bytes_accessed=1000, transcendentals=0
        ),
        name=name,
    )(*[pltpu.with_memory_space_constraint(a, s) for a, s in ins])


def vmem(*arrays):
    return [(a, pltpu.VMEM) for a in arrays]


def lanes(group):
    return slice(group * LANES, (group + 1) * LANES)


def spanned(group, channels, width):
    first = group * LANES // channels * channels
    last = -(-(group + 1) * LANES // channels) * channels
    return list(range(first // LANES, -(-min(last, width) // LANES)))


def span_lanes(near):
    return slice(near[0] * LANES, (near[-1] + 1) * LANES)


def split(x):
    high = x.astype(BF16)
    return high, (x - high.astype(F32)).astype(BF16)


def bases_into(outs, xs, ys, same, step, channels):
    groups = len(xs)
    width = groups * LANES
    detune = 1.0 - (step + 1.0) / (STEPS + 1.0)
    parts = [split(x) for x in xs]
    for g in range(groups):
        near = spanned(g, channels, width)
        ones = same[span_lanes(near), lanes(g)]
        totals = sum(
            jnp.dot(
                jnp.concatenate([parts[n][k] for n in near], axis=1),
                ones,
                preferred_element_type=F32,
            )
            for k in range(2)
        )
        penalty = 0.02 * (totals - (2.0 - channels))
        outs[g][...] = ys[g] + 0.5 * (-detune * xs[g] - 0.4 * penalty)


def mixed_of(fields, mixing, group, channels):
    near = spanned(group, channels, mixing.shape[0])
    return jnp.dot(
        jnp.concatenate([fields[n] for n in near], axis=1),
        mixing[span_lanes(near), lanes(group)],
        preferred_element_type=F32,
    )


def load_first(positions, groups_of):
    cells = positions.shape[0]
    n = len(groups_of)

    def body(x_ref, *refs):
        x_outs, r_outs, sent, sems = refs[:n], refs[n : 2 * n], refs[2 * n], refs[-1]
        copies = [
            pltpu.make_async_copy(x_ref.at[:, lanes(g)], x_outs[i], sems.at[i])
            for i, g in enumerate(groups_of)
        ]
        for copy in copies:
            copy.start()
        for i, copy in enumerate(copies):
            copy.wait()
            rounded = x_outs[i][...].astype(BF16)
            r_outs[i][...] = rounded
            sent[:, lanes(i)] = rounded

    outs = call(
        body,
        [(positions, pltpu.HBM)],
        [((cells, LANES), F32, pltpu.VMEM)] * n
        + [((cells, LANES), BF16, pltpu.VMEM)] * n
        + [((cells, n * LANES), BF16, pltpu.VMEM)],
        [pltpu.SemaphoreType.DMA((n,))],
        "load_first",
    )
    return outs[:n], outs[n : 2 * n], outs[2 * n]


def section(slots, per):
    return -(-(slots + per) // (2 * LONG)) * LONG


def make_lists(rows, cols, count, positions, groups_of, after, slots, tile, ring_index):
    cells = positions.shape[0]
    per = cells // tile
    pairs = section(slots, per)
    n = len(groups_of)

    def body(rows_hbm, cols_hbm, count_hbm, x_ref, _, list_ref, *refs):
        x_outs, r_outs = refs[:n], refs[n : 2 * n]
        rows_ref, cols_ref, count_ref, held, sems = refs[2 * n :]
        copies = [
            pltpu.make_async_copy(*ends, sems.at[k])
            for k, ends in enumerate(
                [(rows_hbm, rows_ref), (cols_hbm, cols_ref), (count_hbm, count_ref)]
                + [(x_ref.at[:, lanes(g)], x_outs[i]) for i, g in enumerate(groups_of)]
            )
        ]
        for copy in copies:
            copy.start()
        for k in range(2 * per):
            held[k] = -1
        far_third = jnp.where(lax.rem(ring_index(), 2) == 1, 2, 0)
        for copy in copies[:3]:
            copy.wait()

        def visit(slot, totals):
            near_pairs, far_pairs = totals
            row, col = rows_ref[slot], cols_ref[slot]
            third = jnp.where(col >= 2 * per, 2, jnp.where(col >= per, 1, 0))
            source = col - third * per
            far = third == far_third
            source = jnp.where(far | (third == 1), source, source + per)
            key = row + jnp.where(far, per, 0)
            place = 2 * jnp.where(far, far_pairs + pairs, near_pairs)
            entry = slot * 65536 + source * 256 + row
            other = held[key]
            full = other >= 0
            list_ref[place] = other
            list_ref[place + 1] = entry
            held[key] = jnp.where(full, -1, entry)
            one = full.astype(jnp.int32)
            far_one = jnp.where(far, one, 0)
            return near_pairs + one - far_one, far_pairs + far_one

        totals = lax.fori_loop(0, count_ref[0], visit, (jnp.int32(0), jnp.int32(0)))
        for part, zero in enumerate((2 * per, per)):
            total = totals[part]
            start = part * pairs
            for k in range(per):
                other = held[part * per + k]
                list_ref[2 * (start + total)] = other
                list_ref[2 * (start + total) + 1] = zero * 256 + k
                total = total + (other >= 0).astype(jnp.int32)
            rest = total % LONG
            padded = rest > 2 * SHORT
            long_turns = total // LONG + padded.astype(jnp.int32)
            short_turns = jnp.where(padded, 0, (rest + SHORT - 1) // SHORT)

            def pad(pair, carry, start=start, zero=zero):
                for e in range(2):
                    list_ref[2 * (start + pair) + e] = zero * 256 + per
                return carry

            lax.fori_loop(total, long_turns * LONG + short_turns * SHORT, pad, 0)
            list_ref[4 * pairs + 2 * part] = long_turns
            list_ref[4 * pairs + 2 * part + 1] = short_turns
        for i, copy in enumerate(copies[3:]):
            copy.wait()
            r_outs[i][...] = x_outs[i][...].astype(BF16)

    outs = call(
        body,
        [(a, pl.ANY) for a in (rows, cols, count)] + [(positions, pltpu.HBM)] + vmem(after),
        [((4 * pairs + 4 + 2,), jnp.int32, pltpu.SMEM)]
        + [((cells, LANES), F32, pltpu.VMEM)] * n
        + [((cells, LANES), BF16, pltpu.VMEM)] * n,
        [
            pltpu.SMEM(rows.shape, jnp.int32),
            pltpu.SMEM(cols.shape, jnp.int32),
            pltpu.SMEM(count.shape, jnp.int32),
            pltpu.SMEM((2 * per,), jnp.int32),
            pltpu.SemaphoreType.DMA((3 + n,)),
        ],
        "make_lists",
    )
    return outs[0], outs[1 : 1 + n], outs[1 + n :]


def add_pairs(part, list_ref, tiles, field, window, pairs):
    def turn(first, length):
        for u in range(length):
            place = 2 * (part * pairs + first + u)
            entries = [list_ref[place + e] for e in range(2)]
            left = jnp.concatenate([tiles[n >> 16] for n in entries], axis=1)
            right = jnp.concatenate([window[(n >> 8) & 255] for n in entries], axis=0)
            field[entries[1] & 255] += jnp.dot(left, right, preferred_element_type=F32)

    def long(i, carry):
        turn(i * LONG, LONG)
        return carry

    def short(i, carry):
        turn(long_turns * LONG + i * SHORT, SHORT)
        return carry

    long_turns = list_ref[4 * pairs + 2 * part]
    lax.fori_loop(0, long_turns, long, 0)
    lax.fori_loop(0, list_ref[4 * pairs + 2 * part + 1], short, 0)


def near_fields(lists, tiles, owns, others, far_part, sent, after, flops, name):
    slots, tile, _ = tiles.shape
    cells = owns[0].shape[0]
    groups = len(owns)
    width = groups * LANES
    per = cells // tile
    pairs = section(slots, per)
    start = [] if far_part is None else [far_part]

    def body(list_ref, tiles_ref, *refs):
        own_refs, other_refs, refs = refs[:groups], refs[groups : 2 * groups], refs[2 * groups :]
        start_refs, refs = refs[: len(start)], refs[len(start) :]
        sent_refs, refs = refs[: len(sent)], refs[len(sent) + len(after) :]
        field_outs, sent_outs, (field, window) = refs[:groups], refs[groups:-2], refs[-2:]
        for out, ref in zip(sent_outs, sent_refs):
            out[...] = ref[...]
        for g in range(groups):
            window[:per, :, lanes(g)] = own_refs[g][...].reshape(per, tile, LANES)
            window[per : 2 * per, :, lanes(g)] = other_refs[g][...].reshape(per, tile, LANES)
        window[2 * per] = jnp.zeros((tile, width), BF16)
        field[:per] = jnp.zeros((per, tile, width), F32)
        for ref in start_refs:
            field[:per, :, lanes(0)] = ref[...].reshape(per, tile, LANES)
        add_pairs(0, list_ref, tiles_ref, field, window, pairs)
        for g, out in enumerate(field_outs):
            out[...] = field[:per, :, lanes(g)].reshape(cells, LANES).astype(out.dtype)

    outs = call(
        body,
        [(lists, pltpu.SMEM)] + vmem(tiles, *owns, *others, *start, *sent, *after),
        [
            ((cells, LANES), BF16 if start and g == 0 else F32, pltpu.VMEM)
            for g in range(groups)
        ]
        + [(a.shape, BF16, pltpu.VMEM) for a in sent],
        [
            pltpu.VMEM((per + 1, tile, width), F32),
            pltpu.VMEM((2 * per + 1, tile, width), BF16),
        ],
        name,
        flops,
    )
    return outs[:groups], outs[groups:]


def far_fields(lists, tiles, nears, far, extra, outs_of, work, name, flops=0, through=()):
    slots, tile, _ = tiles.shape
    cells, width = far.shape
    per = cells // tile
    pairs = section(slots, per)
    n = width // LANES
    m = len(nears)

    def body(list_ref, tiles_ref, far_ref, *refs):
        near_refs, extra_refs = refs[:m], refs[m : m + len(extra)]
        through_refs = refs[m + len(extra) : m + len(extra) + len(through)]
        out_refs, (field, window) = refs[m + len(extra) + len(through) : -2], refs[-2:]
        window[:per] = far_ref[...].reshape(per, tile, width)
        window[per] = jnp.zeros((tile, width), BF16)
        if not near_refs:
            field[:per] = jnp.zeros((per, tile, width), F32)
        for i, ref in enumerate(near_refs):
            field[:per, :, lanes(i)] = ref[...].reshape(per, tile, LANES)
        add_pairs(1, list_ref, tiles_ref, field, window, pairs)
        done = [field[:per, :, lanes(i)].reshape(cells, LANES) for i in range(n)]
        work(done, [*extra_refs, *through_refs], out_refs[: len(outs_of)])

    return call(
        body,
        [(lists, pltpu.SMEM)] + vmem(tiles, far, *nears, *extra, *through),
        [(*out, pltpu.VMEM) for out in outs_of] + [(a.shape, a.dtype, pltpu.VMEM) for a in through],
        [pltpu.VMEM((per + 1, tile, width), F32), pltpu.VMEM((per + 1, tile, width), BF16)],
        name,
        flops,
        [(3 + m + len(extra) + i, len(outs_of) + i) for i in range(len(through))],
    )


def first_base(xs, momenta, same, spread, coupling, channels):
    cells, width = momenta.shape
    groups = len(xs)

    def body(*refs):
        x_refs, (y_ref, same_ref, spread_ref, coupling_ref) = refs[:groups], refs[groups : groups + 4]
        outs = refs[groups + 4 :]
        tall = jnp.dot(spread_ref[...], coupling_ref[...], preferred_element_type=F32).astype(BF16)
        wide = lax.dot_general(
            tall, spread_ref[...], (((1,), (1,)), ((), ())), preferred_element_type=F32
        )
        outs[groups][...] = (wide * same_ref[...].astype(F32)).astype(BF16)
        x = [ref[...] for ref in x_refs]
        y = [y_ref[:, lanes(g)] for g in range(groups)]
        bases_into(outs[:groups], x, y, same_ref, 0, channels)

    outs = call(
        body,
        vmem(*xs, momenta, same, spread, coupling),
        [((cells, LANES), F32, pltpu.VMEM)] * groups + [((width, width), BF16, pltpu.VMEM)],
        [],
        "first_base",
    )
    return outs[:groups], outs[groups]


def updated(field_mixed, base, x):
    y_new = base - 0.2 * field_mixed
    return jnp.clip(x + 0.5 * y_new, -1.0, 1.0), y_new


def second_base(xs, ys, later, fields, first_base, first_x, rounded, same, mixing, channels):
    groups = len(rounded)
    cells = rounded[0].shape[0]
    width = groups * LANES
    done, m = len(xs), len(later)

    def body(*refs):
        refs = list(refs)

        def take(n):
            taken = refs[:n]
            del refs[:n]
            return taken

        x = [ref[...] for ref in take(done)]
        y = [ref[...] for ref in take(done)]
        held = [ref[...] for ref in take(groups)]
        base_refs, x_refs = take(m), take(m)
        r = [ref[...] for ref in take(groups)]
        same_ref, mixing_ref = take(2)
        for i, t in enumerate(later):
            x_new, y_new = updated(
                mixed_of(held, mixing_ref, t, channels), base_refs[i][...], x_refs[i][...]
            )
            x.append(x_new)
            y.append(y_new)
            refs[2 * groups + i][...] = x_new
        bases_into(refs[:groups], x, y, same_ref, 1, channels)
        for g in range(groups):
            near = spanned(g, channels, width)
            refs[groups + g][...] = lax.dot_general(
                jnp.concatenate([r[n] for n in near], axis=1),
                mixing_ref[lanes(g), span_lanes(near)],
                (((1,), (1,)), ((), ())),
                preferred_element_type=F32,
            )

    outs = call(
        body,
        vmem(*xs, *ys, *fields, *first_base, *first_x, *rounded, same, mixing),
        [((cells, LANES), F32, pltpu.VMEM)] * (2 * groups + m),
        [],
        "second_base",
    )
    return outs[:groups], outs[groups : 2 * groups], outs[2 * groups :]


def finish(fields, xs, bases, mixing, channels):
    groups = len(xs)
    cells = xs[0].shape[0]
    width = groups * LANES

    def body(*refs):
        field_refs, x_refs, base_refs = [refs[k * groups : (k + 1) * groups] for k in range(3)]
        mixing_ref, x_out, y_out, token, x_buf, y_buf, sems = refs[3 * groups :]
        held = [ref[...] for ref in field_refs]
        copies = []
        for g in range(groups):
            y_new = base_refs[g][...] - 0.2 * mixed_of(held, mixing_ref, g, channels)
            y_buf[g] = y_new
            x_buf[g] = jnp.clip(x_refs[g][...] + 0.5 * y_new, -1.0, 1.0)
            for k, (buf, out) in enumerate(((y_buf, y_out), (x_buf, x_out))):
                copies.append(
                    pltpu.make_async_copy(buf.at[g], out.at[:, lanes(g)], sems.at[g, k])
                )
                copies[-1].start()
        token[...] = jnp.zeros_like(token)
        for copy in copies:
            copy.wait()

    return call(
        body,
        vmem(*fields, *xs, *bases, mixing),
        [((cells, width), F32, pltpu.HBM)] * 2 + [((8, LANES), F32, pltpu.VMEM)],
        [
            pltpu.VMEM((groups, cells, LANES), F32),
            pltpu.VMEM((groups, cells, LANES), F32),
            pltpu.SemaphoreType.DMA((groups, 2)),
        ],
        "finish",
    )


def copies_of(rows):
    return [((rows * n, LANES), F32) for n in (1, 2, 3)]


def spread_out(outs, value):
    for out in outs:
        out[...] = jnp.concatenate([value] * (out.shape[0] // value.shape[0]), axis=0)


def add_up(arrays, token, name):
    rows = arrays[0].shape[0]

    def body(*refs):
        total = refs[0][...]
        for ref in refs[1 : len(arrays)]:
            total = total + ref[:rows, :]
        spread_out(refs[len(arrays) + len(token) :], total)

    return call(
        body,
        vmem(*arrays, *token),
        [(*size, pltpu.VMEM) for size in copies_of(rows)],
        [],
        name,
    )


def sum_over_ring(values, ring, token):
    if ring & (ring - 1):
        return lax.psum(values[0], RING)
    rounds, size = [], 1
    while size < ring:
        digits = (1, 2, 3) if 4 * size <= ring else (1,)
        rounds.append([size * d for d in digits])
        size *= len(digits) + 1
    for i, bits in enumerate(reversed(rounds)):
        received = [
            lax.ppermute(value, RING, [(j, j ^ bit) for j in range(ring)])
            for value, bit in zip(values, bits)
        ]
        if i == len(rounds) - 1:
            rows = values[0].shape[0]
            return values[0] + sum(part[:rows] for part in received)
        values = add_up([values[0], *received], [token] if i == 0 else [], f"add_up_{i}")
    return values[0]


def local(positions, momenta, tile_values, tile_rows, tile_cols, tile_count, channel_coupling):
    cells, width = positions.shape
    slots, tile, _ = tile_values.shape
    channels = channel_coupling.shape[0]
    replicas = width // channels
    groups = width // LANES
    ring = lax.axis_size("row") * lax.axis_size("col")
    where = np.arange(width)
    same = jnp.asarray(
        (where[:, None] // channels == where[None] // channels).astype(ml_dtypes.bfloat16)
    )
    spread = jnp.asarray(
        (where[:, None] % channels == np.arange(channels)[None]).astype(ml_dtypes.bfloat16)
    )
    on_chip = [(i, i ^ 1) for i in range(ring)]
    off_chip = [(i, (i + 1) % ring if i % 2 else (i - 1) % ring) for i in range(ring)]
    wide = (cells, LANES)
    every = list(range(groups))
    first_pieces = [every[:-1], every[-1:]]
    second_pieces = [every[:1], every[1:]]

    def ring_index():
        return lax.axis_index("row") * lax.axis_size("col") + lax.axis_index("col")

    def far_swap(mine):
        return lax.ppermute(mine, RING, off_chip)

    def near_swap(mine):
        return lax.ppermute(mine, RING, on_chip)

    def ready(piece, done):
        return [
            t for t in every if t not in done and max(spanned(t, channels, width)) <= piece[-1]
        ]

    def keep(done, _, outs):
        outs[0][...] = done[0]

    def needed(todo, piece):
        return sorted({n for t in todo for n in spanned(t, channels, width)} - set(piece))

    xs, owns, sent = load_first(positions, first_pieces[0])
    fars = [far_swap(sent)]
    lists, more_x, more_own = make_lists(
        tile_rows, tile_cols, tile_count, positions, first_pieces[1], sent, slots, tile, ring_index
    )
    xs, owns = [*xs, *more_x], [*owns, *more_own]
    others = [near_swap(r) for r in owns]
    base, mixing = first_base(xs, momenta, same, spread, channel_coupling, channels)
    near, sent = near_fields(
        lists, tile_values, owns, others, None, more_own, [mixing], 0, "near_first"
    )
    fars.append(far_swap(sent[0]))

    fields, new_x, new_y, rounded, new_fars = {}, [], [], {}, []
    for p, piece in enumerate(first_pieces):
        last = p == len(first_pieces) - 1
        todo = ready(piece, rounded)
        known = needed(todo, piece)
        assert second_pieces[p] == todo

        def work(done, ins, outs, piece=piece, todo=todo, known=known, last=last):
            held = {n: ins[1 + i][...] for i, n in enumerate(known)}
            done = [field.astype(BF16) for field in done]
            held.update(zip(piece, done))
            rest = ins[1 + len(known) :]
            near = sorted(held)
            mixed = jnp.dot(
                jnp.concatenate([held[n] for n in near], axis=1),
                ins[0][span_lanes(near), span_lanes(todo)],
                preferred_element_type=F32,
            )
            for i, t in enumerate(todo):
                x_new, y_new = updated(mixed[:, lanes(i)], rest[2 * i][...], rest[2 * i + 1][...])
                r_new = x_new.astype(BF16)
                outs[0][:, lanes(i)] = r_new
                outs[1 + i][...] = r_new
                if not last:
                    outs[1 + len(todo) + len(piece) + 2 * i][...] = x_new
                    outs[2 + len(todo) + len(piece) + 2 * i][...] = y_new
            for i, field in enumerate(done):
                outs[1 + len(todo) + i][...] = field

        results = far_fields(
            lists,
            tile_values,
            [near[n] for n in piece],
            fars[p],
            [mixing] + [fields[n] for n in known] + [a for t in todo for a in (base[t], xs[t])],
            [((cells, len(todo) * LANES), BF16)]
            + [(wide, BF16)] * (len(todo) + len(piece))
            + ([] if last else [(wide, F32)] * (2 * len(todo))),
            work,
            f"far_first_{p}",
        )
        new_fars.append(far_swap(results[0]))
        rounded.update(zip(todo, results[1:]))
        fields.update(zip(piece, results[1 + len(todo) :]))
        new_x += results[1 + len(todo) + len(piece) :: 2]
        new_y += results[2 + len(todo) + len(piece) :: 2]

    owns = [rounded[g] for g in every]
    others = [near_swap(r) for r in owns]
    (part,) = far_fields(
        lists, tile_values, [], new_fars[0], [], [(wide, F32)], keep, "far_second_0", NEAR_FLOPS
    )
    near, _ = near_fields(lists, tile_values, owns, others, part, [], [], 0, "near_second")
    later = second_pieces[1]
    base, weights, more_x = second_base(
        new_x,
        new_y,
        later,
        [fields[g] for g in every],
        [base[t] for t in later],
        [xs[t] for t in later],
        owns,
        same,
        mixing,
        channels,
    )
    xs = [*new_x, *more_x]
    piece = second_pieces[1]

    def last_work(done, ins, outs):
        held = [ins[groups][...]] + [field.astype(BF16) for field in done]
        for out, field in zip(outs, held[1:]):
            out[...] = field
        row = jnp.concatenate(
            [
                jnp.sum(field.astype(F32) * ref[...], axis=0, keepdims=True)
                for field, ref in zip(held, ins[:groups])
            ],
            axis=1,
        )
        row = jnp.broadcast_to(row, (replicas, width))
        lane = lax.broadcasted_iota(jnp.int32, (replicas, width), 1)
        first = lax.broadcasted_iota(jnp.int32, (replicas, width), 0) * channels
        inside = (lane >= first) & (lane < first + channels)
        total = jnp.sum(jnp.where(inside, row, 0.0), axis=1, keepdims=True)
        place = lax.broadcasted_iota(jnp.int32, (replicas, LANES), 1)
        which = lax.broadcasted_iota(jnp.int32, (replicas, LANES), 0)
        flat = jnp.sum(jnp.where(place == which, total, 0.0), axis=0, keepdims=True)
        spread_out(outs[len(piece) :], jnp.broadcast_to(flat, (8, LANES)))

    results = far_fields(
        lists,
        tile_values,
        near[1:],
        new_fars[1],
        weights,
        [(wide, BF16)] * len(piece) + copies_of(8),
        last_work,
        "far_second_1",
        through=[near[0], *xs, *base, mixing],
    )
    sent = len(piece) + len(copies_of(8))
    fields, partials, kept = results[: len(piece)], results[len(piece) : sent], results[sent:]
    fields, kept = [kept[0], *fields], kept[1:]

    x_new, y_new, token = finish(
        fields, kept[:groups], kept[groups : 2 * groups], kept[2 * groups], channels
    )
    total = sum_over_ring(partials, ring, token)
    energy = total[0, :replicas] / jnp.sqrt(jnp.float32(cells * ring * channels))
    return (x_new, y_new, energy)


def solution(mesh):
    cells = P(("groups", "row", "col"), None)
    slots = P(("groups", "row", "col"))
    return jax.shard_map(
        local,
        mesh=mesh,
        in_specs=(cells, cells, P(("groups", "row", "col"), None, None), slots, slots, slots, P()),
        out_specs=(cells, cells, P("groups")),
        check_vma=False,
    )
```
